32 devices in a mesh: section: 2 (over core), dp: 16 (over z, y, x).
Axes of the slice: x: 2, y: 2, z: 4, core: 2. Of those that a mesh axis runs over, the one named last changes fastest.
Arguments:
- tokens: bfloat16 [2, 10240, 768], P(None, 'dp'), may hold values from -6 to 6
- segment_ids: int32 [2, 10240], P(None, 'dp'), may hold values from 0 to 7, as said below
- keep_masks: int32 [2, 2, 2, 128], P('section', None, None, 'dp'), may hold values 0 or 1
- cotangent: bfloat16 [2, 10240, 768], P(None, 'dp'), may hold values from -6 to 6
- norm1_gain: float32 [2, 768], P('section'), may hold values from 0.5 to 1.5
- norm1_bias: float32 [2, 768], P('section'), may hold values from -1.25 to 1.25
- qkv_weight: bfloat16 [2, 768, 2304], P('section'), may hold values from -0.21875 to 0.21875
- qv_bias: float32 [2, 1536], P('section'), may hold values from -1.25 to 1.25
- out_weight: bfloat16 [2, 768, 768], P('section'), may hold values from -0.875 to 0.875
- out_bias: float32 [2, 768], P('section'), may hold values from -1.25 to 1.25
- norm2_gain: float32 [2, 768], P('section'), may hold values from 0.5 to 1.5
- norm2_bias: float32 [2, 768], P('section'), may hold values from -1.25 to 1.25
- fc1_weight: bfloat16 [2, 768, 3072], P('section'), may hold values from -0.21875 to 0.21875
- fc1_bias: float32 [2, 3072], P('section'), may hold values from -1.25 to 1.25
- fc2_weight: bfloat16 [2, 3072, 768], P('section'), may hold values from -0.109375 to 0.109375
- fc2_bias: float32 [2, 768], P('section'), may hold values from -1.25 to 1.25
Outputs:
- layer_out: bfloat16 [2, 2, 10240, 768], P('section', None, 'dp')
- input_grad: bfloat16 [2, 2, 10240, 768], P('section', None, 'dp')
- grad_norm1_gain: float32 [2, 768], P('section', 'dp')
- grad_norm1_bias: float32 [2, 768], P('section', 'dp')
- grad_qkv_weight: float32 [2, 768, 2304], P('section', 'dp')
- grad_qv_bias: float32 [2, 1536], P('section', 'dp')
- grad_out_weight: float32 [2, 768, 768], P('section', 'dp')
- grad_out_bias: float32 [2, 768], P('section', 'dp')
- grad_norm2_gain: float32 [2, 768], P('section', 'dp')
- grad_norm2_bias: float32 [2, 768], P('section', 'dp')
- grad_fc1_weight: float32 [2, 768, 3072], P('section', 'dp')
- grad_fc1_bias: float32 [2, 3072], P('section', 'dp')
- grad_fc2_weight: float32 [2, 3072, 768], P('section', 'dp')
- grad_fc2_bias: float32 [2, 768], P('section', 'dp')
The draws below stay inside these ranges and needn't reach their ends.
Inputs may be any that keep to these rules, and one draw needn't show every extreme that they name: `segment_ids`: within each aligned block of 640 slots the ids never fall; from the block's start it holds one image of 578 tokens, or three of 198, or six of 102, or two of 198 then two of 102, or one of 198 then four of 102, numbered from 0; the remaining slots of the block carry id 7.
All inputs are finite; a program needn't handle non-finite values. No bound on the sum of `keep_masks` on one device may be relied on, other than what follows from the above.
Results may differ from the reference program's by a relative error of at most 0.014.
Values may be sent and summed in bfloat16 or wider, within the bound.
A program may use at most 384 MiB of HBM per device.

```python
import jax
import jax.numpy as jnp
from jax import lax

D = 768
FF = 3072
HEADS = 12
HEAD_DIM = 64
MB_TOK = 640
MICRO = 2
IMG_SMALL = 102
IMG_MID = 198
IMG_LARGE = 578
SEGS = 8
TOKENS_MB = 10240
N_DP = 16


def draw_segment_ids(key, part):
    key = jax.random.fold_in(key, 11)
    blocks = MICRO * (TOKENS_MB // MB_TOK)
    layouts = jnp.array([[IMG_LARGE, 0, 0, 0, 0, 0, 0], [IMG_MID, IMG_MID, IMG_MID, 0, 0, 0, 0], [IMG_SMALL, IMG_SMALL, IMG_SMALL, IMG_SMALL, IMG_SMALL, IMG_SMALL, 0], [IMG_MID, IMG_MID, IMG_SMALL, IMG_SMALL, 0, 0, 0], [IMG_MID, IMG_SMALL, IMG_SMALL, IMG_SMALL, IMG_SMALL, 0, 0]], dtype=jnp.int32)
    chosen = jax.random.randint(key, (blocks,), 0, 5)
    lengths = layouts[chosen]
    ends = jnp.cumsum(lengths, axis=1)
    places = jnp.arange(MB_TOK, dtype=jnp.int32)
    numbers = jnp.sum((places[None, :, None] >= ends[:, None, :]).astype(jnp.int32), axis=2)
    return numbers.reshape(MICRO, TOKENS_MB).astype(jnp.int32)


def place_ends(result, key, least, high):
    longest = result.shape.index(max(result.shape))
    spots = []
    for shift in (0, 1):
        where = [jax.random.randint(jax.random.fold_in(key, axis), (), 0, length) for axis, length in enumerate(result.shape)]
        where[longest] = (where[longest] + shift) % result.shape[longest]
        spots.append(tuple(where))
    return result.at[spots[0]].set(least).at[spots[1]].set(high)


def with_spikes(values, rng, source, target, shards_of, factor):
    owner, partner = [(jnp.arange(values.shape[dim]) // (values.shape[dim] // shards_of)).reshape([-1 if axis == dim else 1 for axis in range(values.ndim)]) for dim in (source, target)]
    chosen = jax.random.permutation(rng, shards_of)[partner]
    strong = (owner == chosen) | (owner == (partner + shards_of // 2) % shards_of)
    return jnp.where(strong, factor * values, values)


def steps_of(rng, shape, split, smallest, top_value):
    factor_of = 1.0
    for position, shards_of in split:
        heights = jax.random.uniform(jax.random.fold_in(jax.random.fold_in(rng, 6), position), (shards_of,), jnp.float32, smallest / len(split), top_value / len(split))
        factor_of = factor_of * jnp.repeat(jnp.exp(heights), shape[position] // shards_of).reshape((-1,) + (1,) * (len(shape) - 1 - position))
    return factor_of


def gaussian(rng, dims, scale, bound, cuts=(), kind=jnp.bfloat16):
    level = steps_of(rng, dims, cuts, -0.22, 0.18) if cuts else 1.0
    entries = jax.random.normal(rng, dims, jnp.float32) * scale * level
    return jnp.minimum(jnp.maximum(entries, -bound), bound).astype(kind)


def bell_draw_with(rng, extent, scale, bound, split, heavy, held_as=jnp.bfloat16):
    drawn = scale * jax.random.normal(rng, extent, jnp.float32)
    if split:
        drawn = drawn * steps_of(rng, extent, split, -0.22, 0.18)
    return jnp.clip(with_spikes(drawn, jax.random.fold_in(rng, 3), *heavy), -bound, bound).astype(held_as)


def setup_inputs(seed: int = 0) -> dict:
    seeds = jax.random.split(jax.random.key(seed), 17)
    tokens = bell_draw_with(seeds[0], (MICRO, TOKENS_MB, D), 1.0, 6.0, ((1, 16),), (1, 2, 16, 2.0))
    segment_ids = draw_segment_ids(jax.random.fold_in(seeds[16], 71), 0)
    keep_masks = place_ends((jax.random.randint(seeds[2], (2, MICRO, 2, SEGS * N_DP), 0, 10) < 9).astype(jnp.int32), jax.random.fold_in(seeds[2], 1), 0, 1)
    cotangent = bell_draw_with(seeds[3], (MICRO, TOKENS_MB, D), 1.0, 6.0, ((1, 16),), (1, 2, 16, 2.0))
    norm1_gain = jnp.clip(1.0 + 0.1 * jax.random.normal(seeds[4], (2, D), jnp.float32), 0.5, 1.5)
    norm1_bias = gaussian(seeds[5], (2, D), 0.2, 1.25, ((0, 2),), jnp.float32)
    qkv_weight = gaussian(seeds[6], (2, D, 3 * D), D ** -0.5, 0.21875, ((0, 2),))
    qv_bias = gaussian(seeds[7], (2, 2 * D), 0.2, 1.25, ((0, 2),), jnp.float32)
    out_weight = gaussian(seeds[8], (2, D, D), (D // 16) ** -0.5, 0.875, ((0, 2),))
    out_bias = gaussian(seeds[9], (2, D), 0.2, 1.25, ((0, 2),), jnp.float32)
    norm2_gain = jnp.clip(1.0 + 0.1 * jax.random.normal(seeds[10], (2, D), jnp.float32), 0.5, 1.5)
    norm2_bias = gaussian(seeds[11], (2, D), 0.2, 1.25, ((0, 2),), jnp.float32)
    fc1_weight = gaussian(seeds[12], (2, D, FF), D ** -0.5, 0.21875, ((0, 2),))
    fc1_bias = gaussian(seeds[13], (2, FF), 0.2, 1.25, ((0, 2),), jnp.float32)
    fc2_weight = gaussian(seeds[14], (2, FF, D), FF ** -0.5, 0.109375, ((0, 2),))
    fc2_bias = gaussian(seeds[15], (2, D), 0.2, 1.25, ((0, 2),), jnp.float32)
    return dict(tokens=tokens, segment_ids=segment_ids, keep_masks=keep_masks, cotangent=cotangent, norm1_gain=norm1_gain, norm1_bias=norm1_bias, qkv_weight=qkv_weight, qv_bias=qv_bias, out_weight=out_weight, out_bias=out_bias, norm2_gain=norm2_gain, norm2_bias=norm2_bias, fc1_weight=fc1_weight, fc1_bias=fc1_bias, fc2_weight=fc2_weight, fc2_bias=fc2_bias)


keep_rate = 0.9
norm_eps = 1e-06

@jax.custom_vjp
def low(v):
    return lax.optimization_barrier(v.astype(jnp.bfloat16)).astype(jnp.float32)

@jax.custom_vjp
def low_back(v):
    return v

def low_keep(v):
    return (low(v), None)

def low_pass(kept, grad):
    return (grad,)

def back_keep(v):
    return (v, None)

def back_low(kept, grad):
    return (low(grad),)
low.defvjp(low_keep, low_pass)
low_back.defvjp(back_keep, back_low)

def product(left, right):
    return jnp.dot(left, right, precision=lax.Precision.HIGHEST, preferred_element_type=jnp.float32)

def layer_norm(values, gain, shift):
    center = values - lax.optimization_barrier(jnp.mean(values, axis=-1, keepdims=True))
    scale = lax.rsqrt(lax.optimization_barrier(jnp.mean(center * center, axis=-1, keepdims=True)) + norm_eps)
    return center * scale * gain + shift

def attend_block(parts):
    queries, keys, values, segment = parts
    scores = jnp.einsum('qhd,khd->hqk', queries, keys, precision=lax.Precision.HIGHEST) * HEAD_DIM ** (-0.5)
    scores = low_back(scores)
    same = segment[:, None] == segment[None, :]
    scores = jnp.where(same[None], scores, -1000000000.0)
    weights = low(jax.nn.softmax(scores, axis=-1))
    return jnp.einsum('hqk,khd->qhd', weights, values, precision=lax.Precision.HIGHEST)

def block_layer(inputs, params, keep_tok, seg_blocks):
    gain_one, shift_one, w_qkv, bias_qv, w_out, bias_out, gain_two, shift_two, w_up, bias_up, w_down, bias_down = params
    blocks = seg_blocks.shape[0]
    normed = low(layer_norm(inputs, gain_one, shift_one))
    mixed = product(normed, w_qkv)
    queries = low(low_back(mixed[:, :D] + bias_qv[:D]))
    keys = low(low_back(mixed[:, D:2 * D]))
    values = low(low_back(mixed[:, 2 * D:] + bias_qv[D:]))

    def shaped(array):
        return array.reshape(blocks, MB_TOK, HEADS, HEAD_DIM)
    attended = lax.map(jax.checkpoint(attend_block), (shaped(queries), shaped(keys), shaped(values), seg_blocks))
    attended = low(low_back(attended.reshape(-1, D)))
    branch = low_back(product(attended, w_out) + bias_out)
    middle = inputs + keep_tok[:, 0:1] * branch / keep_rate
    second = low(layer_norm(middle, gain_two, shift_two))
    hidden = low_back(product(second, w_up) + bias_up)
    active = low(jax.nn.gelu(hidden, approximate=False))
    branch_two = low_back(product(active, w_down) + bias_down)
    return middle + keep_tok[:, 1:2] * branch_two / keep_rate

def reference(tokens, segment_ids, keep_masks, cotangent, norm1_gain, norm1_bias, qkv_weight, qv_bias, out_weight, out_bias, norm2_gain, norm2_bias, fc1_weight, fc1_bias, fc2_weight, fc2_bias):
    floats = [weight.astype(jnp.float32) for weight in (norm1_gain, norm1_bias, qkv_weight, qv_bias, out_weight, out_bias, norm2_gain, norm2_bias, fc1_weight, fc1_bias, fc2_weight, fc2_bias)]
    params_first = tuple((weight[0] for weight in floats))
    params_second = tuple((weight[1] for weight in floats))
    rows = MICRO * TOKENS_MB
    seg_blocks = segment_ids.reshape(rows // MB_TOK, MB_TOK)
    owner = jnp.arange(TOKENS_MB, dtype=jnp.int32) // MB_TOK * SEGS
    slot = (segment_ids + owner[None, :]).astype(jnp.int32)

    def token_keep(layer):
        table = keep_masks[layer].astype(jnp.float32)
        index = jnp.broadcast_to(slot[:, None, :], (MICRO, 2, TOKENS_MB))
        picked = jnp.take_along_axis(table, index, axis=2)
        return jnp.transpose(picked, (0, 2, 1)).reshape(rows, 2)
    keep_first = token_keep(0)
    keep_second = token_keep(1)
    inputs = tokens.astype(jnp.float32).reshape(rows, D)

    def forward(inputs, first_params, second_params, delta):
        first = block_layer(inputs, first_params, keep_first, seg_blocks)
        entry = low_back(low(first) + delta)
        return (first, block_layer(entry, second_params, keep_second, seg_blocks))
    delta = jnp.zeros((rows, D), jnp.float32)
    (first, last), pullback = jax.vjp(forward, inputs, params_first, params_second, delta)
    back = cotangent.astype(jnp.float32).reshape(rows, D)
    grad_in, grads_first, grads_second, grad_mid = pullback((jnp.zeros_like(first), back))
    layer_out = jnp.stack([first, last]).reshape(2, MICRO, TOKENS_MB, D).astype(jnp.bfloat16)
    input_grad = jnp.stack([grad_in, grad_mid]).reshape(2, MICRO, TOKENS_MB, D).astype(jnp.bfloat16)
    grads = [jnp.stack([one, two]) for one, two in zip(grads_first, grads_second)]
    return (layer_out, input_grad, grads[0], grads[1], grads[2], grads[3], grads[4], grads[5], grads[6], grads[7], grads[8], grads[9], grads[10], grads[11])
```

```python
import functools
import jax
import jax.numpy as jnp
from jax import lax
from jax.experimental import pallas as pl
from jax.experimental.pallas import tpu as pltpu
from jax.sharding import PartitionSpec as P

HEAD_DIM = 64
LANES = 128
keep_rate = 0.9
norm_eps = 1e-06
root_half = 0.7071067811865476
inverse_root = 0.3989422804014327
BIG = 2.0**30
f32, bf16 = jnp.float32, jnp.bfloat16
NN = (((1,), (0,)), ((), ()))
NT = (((1,), (1,)), ((), ()))
TN = (((0,), (0,)), ((), ()))


def dot(a, b, dims=NN):
    return lax.dot_general(a, b, dims, preferred_element_type=f32)


def layer_unit(x):
    center = x - jnp.mean(x, axis=-1, keepdims=True)
    scale = lax.rsqrt(jnp.mean(center * center, axis=-1, keepdims=True) + norm_eps)
    return center * scale, scale


def unit_back(grad, unit, scale, gain):
    scaled = grad * gain
    inner = jnp.mean(scaled, axis=-1, keepdims=True)
    along = jnp.mean(scaled * unit, axis=-1, keepdims=True)
    return scale * (scaled - inner - unit * along)


def gelu_pair(h):
    e = jnp.exp(h * h * -0.5)
    t = 1.0 / (jnp.abs(h) * (0.3275911 * root_half) + 1.0)
    poly = t * (0.5 * 0.254829592 + t * (0.5 * -0.284496736 + t * (0.5 * 1.421413741 + t * (0.5 * -1.453152027 + t * (0.5 * 1.061405429)))))
    tail = poly * e
    phi = jnp.where(h < 0, tail, 1.0 - tail)
    return h * phi, phi + h * e * inverse_root


def split3(v):
    a = v.astype(bf16)
    r = v - a.astype(f32)
    b = r.astype(bf16)
    c = (r - b.astype(f32)).astype(bf16)
    return a, b, c


def feature_base(odd):
    return 0 if odd else HEAD_DIM


def lanes_of(rows):
    return lax.broadcasted_iota(jnp.int32, (rows, LANES), 1)


def seg_feature(seg, rows, odd):
    base = feature_base(odd)
    lane = lanes_of(rows)
    inside = (lane >= base) & (lane < base + 8)
    same = (lane - base).astype(f32) == seg
    qf = jnp.where(inside & same, BIG, 0.0)
    kf = jnp.where(inside & jnp.logical_not(same), -1.0, 0.0)
    kf = jnp.where((lane >= base + 8) & (lane < base + 11), 1.0, kf)
    return qf.astype(bf16), kf.astype(bf16)


def own_lanes(rows, odd):
    lane = lanes_of(rows)
    return (lane >= HEAD_DIM) if odd else (lane < HEAD_DIM)


def forward_kernel(l, x_ref, cols_ref, par_ref, wqkv_ref, wo_ref, w1_ref, w2_ref,
                   y_ref, qkv_ref, lse_ref, att_ref, mid_ref, act_ref, slope_ref,
                   norm_s, second_s, feat_s):
    T, D = x_ref.shape
    FF = w1_ref.shape[1]
    W = 256

    RC = 128

    @pl.loop(0, T // RC)
    def _(i):
        rows = pl.ds(i * RC, RC)
        unit, _s = layer_unit(x_ref[rows, :].astype(f32))
        norm_s[rows, :] = (unit * par_ref[0:1, :D] + par_ref[1:2, :D]).astype(bf16)
        for odd in (0, 1):
            qf, kf = seg_feature(cols_ref[rows, 0:1], RC, odd)
            feat_s[2 * odd, rows, :] = qf
            feat_s[2 * odd + 1, rows, :] = kf

    @pl.loop(0, 3 * D // W)
    def _(n):
        cs = pl.ds(pl.multiple_of(n * W, W), W)
        acc = dot(norm_s[...], wqkv_ref[:, cs]) + par_ref[2:3, cs]
        qkv_ref[:, cs] = (acc * jnp.where(n < D // W, 0.125, 1.0)).astype(bf16)

    heads2 = D // LANES

    @pl.loop(0, heads2)
    def _(p):
        off = pl.multiple_of(p * LANES, LANES)
        qp = qkv_ref[:, pl.ds(off, LANES)]
        kp = qkv_ref[:, pl.ds(off + D, LANES)]
        vp = qkv_ref[:, pl.ds(off + 2 * D, LANES)]
        outs = []
        for odd in (0, 1):
            own = own_lanes(T, odd)
            base = feature_base(odd)
            q = jnp.where(own, qp, feat_s[2 * odd])
            k = jnp.where(own, kp, feat_s[2 * odd + 1])
            v = jnp.where(own, vp, jnp.ones_like(vp))
            s = dot(q, k, NT)
            m = jnp.max(s, axis=1, keepdims=True)
            e = jnp.exp(s - m).astype(bf16)
            o = dot(e, v)
            total = o[:, base:base + 1]
            outs.append(o / total)
            lse_ref[p, :, odd:odd + 1] = m + jnp.log(total)
        att_ref[:, pl.ds(off, LANES)] = jnp.where(own_lanes(T, 0), outs[0], outs[1]).astype(bf16)

    @pl.loop(0, D // W)
    def _(n):
        cs = pl.ds(pl.multiple_of(n * W, W), W)
        acc = dot(att_ref[...], wo_ref[:, cs]) + par_ref[3:4, cs]
        mid_ref[:, cs] = x_ref[:, cs].astype(f32) + cols_ref[:, 1 + 2 * l:2 + 2 * l] * acc

    @pl.loop(0, T // RC)
    def _(i):
        rows = pl.ds(i * RC, RC)
        unit, _s = layer_unit(mid_ref[rows, :])
        second_s[rows, :] = (unit * par_ref[4:5, :D] + par_ref[5:6, :D]).astype(bf16)

    @pl.loop(0, FF // W)
    def _(n):
        cs = pl.ds(pl.multiple_of(n * W, W), W)
        h = dot(second_s[...], w1_ref[:, cs]) + par_ref[6:7, cs]
        a, s = gelu_pair(h)
        act_ref[:, cs] = a.astype(bf16)
        slope_ref[:, cs] = s.astype(bf16)

    @pl.loop(0, D // W)
    def _(n):
        cs = pl.ds(pl.multiple_of(n * W, W), W)
        acc = dot(act_ref[...], w2_ref[:, cs]) + par_ref[7:8, cs]
        y_ref[:, cs] = (mid_ref[:, cs] + cols_ref[:, 2 + 2 * l:3 + 2 * l] * acc).astype(bf16)


VM = pl.BlockSpec(memory_space=pltpu.VMEM)
LIMIT = 60 * 2**20


def forward_call(l, x, cols, par, wqkv, wo, w1, w2):
    T, D = x.shape
    FF = w1.shape[1]
    sd = jax.ShapeDtypeStruct
    return pl.pallas_call(
        functools.partial(forward_kernel, l),
        out_shape=(sd((T, D), bf16), sd((T, 3 * D), bf16), sd((D // LANES, T, 2), f32), sd((T, D), bf16),
                   sd((T, D), f32), sd((T, FF), bf16), sd((T, FF), bf16)),
        in_specs=[VM] * 7, out_specs=(VM,) * 7,
        scratch_shapes=[pltpu.VMEM((T, D), bf16), pltpu.VMEM((T, D), bf16), pltpu.VMEM((4, T, LANES), bf16)],
        compiler_params=pltpu.CompilerParams(vmem_limit_bytes=LIMIT), name="fwd_layer",
    )(x, cols, par, wqkv, wo, w1, w2)


def mlp_back_kernel(l, g_ref, cols_ref, par_ref, mid_ref, act_ref, slope_ref, w1_ref, w2_ref,
                    gmid_ref, dw1_ref, dw2_ref, vec_ref, gd_s, second_s, gh_s, gs_s):
    T, D = g_ref.shape
    FF = w1_ref.shape[1]
    W = 256
    RC = 128
    vec_ref[...] = jnp.zeros_like(vec_ref)

    @pl.loop(0, T // RC)
    def _(i):
        rows = pl.ds(i * RC, RC)
        gd = (g_ref[rows, :].astype(f32) * cols_ref[rows, 2 + 2 * l:3 + 2 * l]).astype(bf16)
        gd_s[rows, :] = gd
        vec_ref[3:4, :D] += jnp.sum(gd.astype(f32), axis=0, keepdims=True)
        unit, _s = layer_unit(mid_ref[rows, :])
        second_s[rows, :] = (unit * par_ref[4:5, :D] + par_ref[5:6, :D]).astype(bf16)

    shard1 = dw1_ref.shape[2]
    per_half = dw1_ref.shape[3] // W

    @pl.loop(0, FF // W)
    def _(n):
        cs = pl.ds(pl.multiple_of(n * W, W), W)
        ga = dot(gd_s[...], w2_ref[cs, :], NT)
        gh = (ga * slope_ref[:, cs].astype(f32)).astype(bf16)
        gh_s[:, cs] = gh
        vec_ref[2:3, cs] = jnp.sum(gh.astype(f32), axis=0, keepdims=True)
        d1 = dot(second_s[...], gh, TN).astype(bf16)
        dw1_ref[n // per_half, :, :, pl.ds(pl.multiple_of((n % per_half) * W, W), W)] = d1.reshape(-1, shard1, W)
        d2 = dot(act_ref[:, cs], gd_s[...], TN).astype(bf16)
        dw2_ref[0, cs, :] = d2[:, :D // 2]
        dw2_ref[1, cs, :] = d2[:, D // 2:]

    @pl.loop(0, D // W)
    def _(n):
        cs = pl.ds(pl.multiple_of(n * W, W), W)
        gs_s[:, cs] = dot(gh_s[...], w1_ref[cs, :], NT)

    @pl.loop(0, T // RC)
    def _(i):
        rows = pl.ds(i * RC, RC)
        unit, scale = layer_unit(mid_ref[rows, :])
        gs = gs_s[rows, :]
        vec_ref[0:1, :D] += jnp.sum(gs * unit, axis=0, keepdims=True)
        vec_ref[1:2, :D] += jnp.sum(gs, axis=0, keepdims=True)
        gmid_ref[rows, :] = g_ref[rows, :].astype(f32) + unit_back(gs, unit, scale, par_ref[4:5, :D])


def mlp_back_call(l, n_dp, g, cols, par, mid, act, slope, w1, w2):
    T, D = g.shape
    FF = w1.shape[1]
    sd = jax.ShapeDtypeStruct
    return pl.pallas_call(
        functools.partial(mlp_back_kernel, l),
        out_shape=(sd((T, D), f32), sd((2, n_dp, D // n_dp, FF // 2), bf16), sd((2, FF, D // 2), bf16), sd((8, FF), f32)),
        in_specs=[VM] * 8, out_specs=(VM,) * 4,
        scratch_shapes=[pltpu.VMEM((T, D), bf16), pltpu.VMEM((T, D), bf16), pltpu.VMEM((T, FF), bf16), pltpu.VMEM((T, D), f32)],
        compiler_params=pltpu.CompilerParams(vmem_limit_bytes=LIMIT), name="mlp_back",
    )(g, cols, par, mid, act, slope, w1, w2)


def attn_back_kernel(l, gmid_ref, cols_ref, par_ref, x_ref, qkv_ref, lse_ref, att_ref, wqkv_ref, wo_ref,
                     gin_ref, dqkv_ref, dwo_ref, vec_ref, gb_s, norm_s, ga_s, gm_s, feat_s, gn_s):
    T, D = x_ref.shape
    W = 256
    RC = 128
    vec_ref[...] = jnp.zeros_like(vec_ref)

    @pl.loop(0, T // RC)
    def _(i):
        rows = pl.ds(i * RC, RC)
        gb = (gmid_ref[rows, :] * cols_ref[rows, 1 + 2 * l:2 + 2 * l]).astype(bf16)
        gb_s[rows, :] = gb
        vec_ref[3:4, :D] += jnp.sum(gb.astype(f32), axis=0, keepdims=True)
        unit, _s = layer_unit(x_ref[rows, :].astype(f32))
        norm_s[rows, :] = (unit * par_ref[0:1, :D] + par_ref[1:2, :D]).astype(bf16)
        for odd in (0, 1):
            qf, kf = seg_feature(cols_ref[rows, 0:1], RC, odd)
            feat_s[2 * odd, rows, :] = qf
            feat_s[2 * odd + 1, rows, :] = kf

    @pl.loop(0, D // W)
    def _(n):
        cs = pl.ds(pl.multiple_of(n * W, W), W)
        ga_s[:, cs] = dot(gb_s[...], wo_ref[cs, :], NT).astype(bf16)

    heads2 = D // LANES
    low_lane = own_lanes(T, 0)

    @pl.loop(0, heads2)
    def _(p):
        off = pl.multiple_of(p * LANES, LANES)
        qp = qkv_ref[:, pl.ds(off, LANES)]
        kp = qkv_ref[:, pl.ds(off + D, LANES)]
        vp = qkv_ref[:, pl.ds(off + 2 * D, LANES)]
        gp = ga_s[:, pl.ds(off, LANES)]
        prod = gp.astype(f32) * att_ref[:, pl.ds(off, LANES)].astype(f32)
        dq, dk, dv = [], [], []
        for odd in (0, 1):
            own = own_lanes(T, odd)
            base = feature_base(odd)
            lane = lanes_of(T)
            row_d = jnp.sum(jnp.where(own, prod, 0.0), axis=1, keepdims=True)
            l3 = split3(-lse_ref[p, :, odd:odd + 1])
            d3 = split3(-row_d)
            qf = feat_s[2 * odd]
            gf = jnp.zeros_like(gp)
            for j in range(3):
                qf = jnp.where(lane == base + 8 + j, l3[j], qf)
                gf = jnp.where(lane == base + j, d3[j], gf)
            q = jnp.where(own, qp, qf)
            k = jnp.where(own, kp, feat_s[2 * odd + 1])
            v = jnp.where(own, vp, jnp.ones_like(vp))
            g = jnp.where(own, gp, gf)
            prob = jnp.exp(dot(k, q, NT))
            gs = (prob * dot(v, g, NT)).astype(bf16)
            dv.append(dot(prob.astype(bf16), g))
            dk.append(dot(gs, q))
            dq.append(dot(gs, k, TN))
        gm_s[:, pl.ds(off, LANES)] = (jnp.where(low_lane, dq[0], dq[1]) * 0.125).astype(bf16)
        gm_s[:, pl.ds(off + D, LANES)] = jnp.where(low_lane, dk[0], dk[1]).astype(bf16)
        gm_s[:, pl.ds(off + 2 * D, LANES)] = jnp.where(low_lane, dv[0], dv[1]).astype(bf16)

    shard = dwo_ref.shape[2]

    @pl.loop(0, D // LANES)
    def _(n):
        half = n // (D // LANES // 2)
        o = pl.multiple_of(n * LANES, LANES)
        ho = pl.multiple_of((n % (D // LANES // 2)) * LANES, LANES)
        dwo_ref[half, :, :, pl.ds(ho, LANES)] = dot(att_ref[...], gb_s[:, pl.ds(o, LANES)], TN).astype(bf16).reshape(-1, shard, LANES)

    W3 = 3 * D // 6

    @pl.loop(0, 6)
    def _(n):
        o = pl.multiple_of(n * W3, LANES)
        ho = pl.multiple_of((n % 3) * W3, LANES)
        gm = gm_s[:, pl.ds(o, W3)]
        dqkv_ref[n // 3, :, :, pl.ds(ho, W3)] = dot(norm_s[...], gm, TN).astype(bf16).reshape(-1, shard, W3)
        vec_ref[2:3, pl.ds(o, W3)] = jnp.sum(gm.astype(f32), axis=0, keepdims=True)

    @pl.loop(0, D // W)
    def _(n):
        cs = pl.ds(pl.multiple_of(n * W, W), W)
        gn_s[:, cs] = dot(gm_s[...], wqkv_ref[cs, :], NT)

    @pl.loop(0, T // RC)
    def _(i):
        rows = pl.ds(i * RC, RC)
        unit, scale = layer_unit(x_ref[rows, :].astype(f32))
        gn = gn_s[rows, :]
        vec_ref[0:1, :D] += jnp.sum(gn * unit, axis=0, keepdims=True)
        vec_ref[1:2, :D] += jnp.sum(gn, axis=0, keepdims=True)
        gin_ref[rows, :] = (gmid_ref[rows, :] + unit_back(gn, unit, scale, par_ref[0:1, :D])).astype(bf16)


def attn_back_call(l, n_dp, gmid, cols, par, x, qkv, lse, att, wqkv, wo):
    T, D = x.shape
    sd = jax.ShapeDtypeStruct
    return pl.pallas_call(
        functools.partial(attn_back_kernel, l),
        out_shape=(sd((T, D), bf16), sd((2, n_dp, D // n_dp, 3 * D // 2), bf16), sd((2, n_dp, D // n_dp, D // 2), bf16), sd((8, 4 * D), f32)),
        in_specs=[VM] * 9, out_specs=(VM,) * 4,
        scratch_shapes=[pltpu.VMEM((T, D), bf16), pltpu.VMEM((T, D), bf16), pltpu.VMEM((T, D), bf16), pltpu.VMEM((T, 3 * D), bf16),
                        pltpu.VMEM((4, T, LANES), bf16), pltpu.VMEM((T, D), f32)],
        compiler_params=pltpu.CompilerParams(vmem_limit_bytes=LIMIT), name="attn_back",
    )(gmid, cols, par, x, qkv, lse, att, wqkv, wo)


MESH = pl.DeviceIdType.MESH
ANY = pl.BlockSpec(memory_space=pl.ANY)


def peers(X, Y, Z):
    me = lax.axis_index("dp")
    mx, my, mz = me % X, (me // X) % Y, me // (X * Y)
    return me, mx, my, mz


def greet(X, Y, Z):
    me, mx, my, mz = peers(X, Y, Z)
    sec = lax.axis_index("section")
    bar = pltpu.get_barrier_semaphore()
    ids = [{"section": 1 - sec}, {"dp": me + 1 - 2 * mx}, {"dp": me + X * (1 - 2 * my)}]
    ids += [{"dp": lax.rem(mz + j, Z) * (X * Y) + me % (X * Y)} for j in range(1, Z)]
    for i in ids:
        pl.semaphore_signal(bar, inc=1, device_id=i, device_id_type=MESH)
    pl.semaphore_wait(bar, len(ids))


def swap_kernel(n, *refs):
    mine, theirs, send, recv = refs[:n], refs[n:2 * n], refs[2 * n], refs[2 * n + 1]
    other = {"section": 1 - lax.axis_index("section")}
    bar = pltpu.get_barrier_semaphore()
    pl.semaphore_signal(bar, inc=1, device_id=other, device_id_type=MESH)
    pl.semaphore_wait(bar, 1)
    copies = [
        pltpu.make_async_remote_copy(mine[i], theirs[i], send.at[i], recv.at[i], device_id=other, device_id_type=MESH)
        for i in range(n)
    ]
    for c in copies:
        c.start()
    for c in copies:
        c.wait()


def swap_call(arrays):
    n = len(arrays)
    return pl.pallas_call(
        functools.partial(swap_kernel, n),
        out_shape=tuple(jax.ShapeDtypeStruct(a.shape, a.dtype) for a in arrays),
        in_specs=[ANY] * n, out_specs=(ANY,) * n,
        scratch_shapes=[pltpu.SemaphoreType.DMA((n,)), pltpu.SemaphoreType.DMA((n,))],
        compiler_params=pltpu.CompilerParams(collective_id=0, has_side_effects=True), name="swap_weights",
    )(*arrays)


def reduce_kernel(dims, units, n_src, n_out, *refs):
    X, Y, Z = dims
    N = len(units)
    srcs, outs = refs[:n_src], refs[n_src:n_src + n_out]
    rest = refs[n_src + n_out:]
    own, r0, r1, r2, r3, fin = (rest[i * N:(i + 1) * N] for i in range(6))
    send, recv, lsem = rest[6 * N:]
    sec = lax.axis_index("section")
    me, mx, my, mz = peers(X, Y, Z)
    other = {"section": 1 - sec}
    greet(X, Y, Z)

    def remote(u, k, src, dst, dev):
        return pltpu.make_async_remote_copy(src, dst, send.at[u, k], recv.at[u, k], device_id=dev, device_id_type=MESH)

    def view(u, half):
        src, row, rows, col, cols = units[u][:5]
        return srcs[src].at[half, :, :, :, pl.ds(row, rows), pl.ds(col, cols)]

    loads = [pltpu.make_async_copy(view(u, sec), own[u], lsem.at[u]) for u in range(N)]
    c0 = [remote(u, 0, view(u, 1 - sec), r0[u], other) for u in range(N)]
    for u in range(N):
        c0[u].start()
        loads[u].start()

    def stage1(u):
        loads[u].wait()
        c0[u].wait()
        dt = own[u].dtype

        @pl.loop(0, Z)
        def _(z):
            for y in range(Y):
                for x in range(X):
                    own[u][z, y, x] = (own[u][z, y, x].astype(f32) + r0[u][z, y, x].astype(f32)).astype(dt)
        if units[u][5] == "xy":
            c = remote(u, 1, own[u].at[:, :, 1 - mx], r1[u], {"dp": me + 1 - 2 * mx})
        else:
            c = remote(u, 1, own[u].at[:, 1 - my], r1[u], {"dp": me + X * (1 - 2 * my)})
        c.start()
        return [c]

    def stage2(u, pend):
        pend[0].wait()
        dt = own[u].dtype

        @pl.loop(0, Z)
        def _(z):
            for w in range(2):
                y, x = (w, mx) if units[u][5] == "xy" else (my, w)
                own[u][z, y, x] = (own[u][z, y, x].astype(f32) + r1[u][z, w].astype(f32)).astype(dt)
        if units[u][5] == "xy":
            c = remote(u, 2, own[u].at[:, 1 - my, mx], r2[u], {"dp": me + X * (1 - 2 * my)})
        else:
            c = remote(u, 2, own[u].at[:, my, 1 - mx], r2[u], {"dp": me + 1 - 2 * mx})
        c.start()
        return [c]

    def stage3(u, pend):
        pend[0].wait()
        dt = own[u].dtype

        @pl.loop(0, Z)
        def _(z):
            own[u][z, my, mx] = (own[u][z, my, mx].astype(f32) + r2[u][z].astype(f32)).astype(dt)
        cs = []
        for j in range(1, Z):
            to = lax.rem(mz + j, Z)
            c = remote(u, 2 + j, own[u].at[to, my, mx], r3[u].at[j - 1], {"dp": to * (X * Y) + me % (X * Y)})
            c.start()
            cs.append(c)
        return cs

    def stage4(u, pend):
        for c in pend:
            c.wait()
        total = own[u][mz, my, mx].astype(f32)
        for j in range(1, Z):
            total += r3[u][j - 1].astype(f32)
        fin[u][...] = total

    pend = {}
    for step in range(N + 3):
        for u, fn in ((step, stage1), (step - 1, stage2), (step - 2, stage3), (step - 3, stage4)):
            if 0 <= u < N:
                pend[u] = fn(u) if fn is stage1 else fn(u, pend[u])
    last = []
    for u in range(N):
        layer, out, row, rows, col, cols, width = units[u][6:]
        if layer is None:
            c = pltpu.make_async_copy(fin[u], outs[out], lsem.at[u])
            c.start()
            c.wait()
            continue
        dst = outs[out].at[pl.ds(row, rows), pl.ds(pl.multiple_of(sec * width + col, LANES), cols)]
        local = pltpu.make_async_copy(fin[u], dst, lsem.at[u])
        away = remote(u, Z + 2, fin[u], dst, other)

        @pl.when(sec == layer)
        def _():
            local.start()

        @pl.when(sec != layer)
        def _():
            away.start()
        last.append((layer, local, away))
    for layer, local, away in last:
        @pl.when(sec == layer)
        def _():
            local.wait()
            away.wait_recv()

        @pl.when(sec != layer)
        def _():
            away.wait_send()


def reduce_call(dims, srcs, units, outs, cid):
    X, Y, Z = dims
    N = len(units)
    dts = [srcs[u[0]].dtype for u in units]
    shp = [(u[2], u[4]) for u in units]
    scr = [pltpu.VMEM((Z, Y, X) + s, d) for s, d in zip(shp, dts)] * 2
    scr += [pltpu.VMEM((Z, 2) + s, d) for s, d in zip(shp, dts)]
    scr += [pltpu.VMEM((Z,) + s, d) for s, d in zip(shp, dts)]
    scr += [pltpu.VMEM((Z - 1,) + s, d) for s, d in zip(shp, dts)]
    scr += [pltpu.VMEM(s, f32) for s in shp]
    scr += [pltpu.SemaphoreType.DMA((N, Z + 3)), pltpu.SemaphoreType.DMA((N, Z + 3)), pltpu.SemaphoreType.DMA((N,))]
    return pl.pallas_call(
        functools.partial(reduce_kernel, dims, units, len(srcs), len(outs)),
        out_shape=tuple(jax.ShapeDtypeStruct(o, f32) for o in outs),
        in_specs=[ANY] * len(srcs), out_specs=(ANY,) * len(outs), scratch_shapes=scr,
        compiler_params=pltpu.CompilerParams(collective_id=cid, has_side_effects=True, vmem_limit_bytes=LIMIT), name="reduce_grads",
    )(*srcs)


def dp_dims(n):
    return {16: (2, 2, 4)}.get(n)


def shards(
    tokens, segment_ids, keep_masks, cotangent,
    norm1_gain, norm1_bias, qkv_weight, qv_bias, out_weight, out_bias,
    norm2_gain, norm2_bias, fc1_weight, fc1_bias, fc2_weight, fc2_bias,
):
    sec = lax.axis_index("section")
    n_dp = lax.axis_size("dp")
    dims = dp_dims(n_dp)
    T, D = tokens.shape[1:]
    FF = fc1_weight.shape[2]
    pad = lambda v: jnp.pad(v, (0, FF - v.shape[0]))
    bq = jnp.concatenate([qv_bias[0, :D], jnp.zeros((D,), f32), qv_bias[0, D:]])
    par = jnp.stack([pad(v) for v in (norm1_gain[0], norm1_bias[0], bq, out_bias[0], norm2_gain[0], norm2_bias[0], fc1_bias[0], fc2_bias[0])])
    keep = jnp.pad(keep_masks[0].astype(f32).reshape(4, -1), ((0, 4), (0, LANES - keep_masks.shape[3])))
    own = (qkv_weight[0], out_weight[0], fc1_weight[0], fc2_weight[0], par, keep)
    other = swap_call(own)
    layers = [[jnp.where(sec == l, a, b) for a, b in zip(own, other)] for l in range(2)]
    seg = lax.dynamic_index_in_dim(segment_ids, sec, 0, keepdims=False)
    onehot = (seg[:, None] == jnp.arange(LANES, dtype=jnp.int32)[None]).astype(f32)
    flags = []
    for l in range(2):
        table = lax.dynamic_slice_in_dim(layers[l][5], sec * 2, 2, 0)
        flags.append(jnp.sum(onehot[:, None, :] * table[None], axis=2) / keep_rate)
    cols = jnp.concatenate([seg[:, None].astype(f32)] + flags + [jnp.zeros((T, LANES - 5), f32)], axis=1)
    x = lax.dynamic_index_in_dim(tokens, sec, 0, keepdims=False)
    g = lax.dynamic_index_in_dim(cotangent, sec, 0, keepdims=False)
    saved, ys, gs, grads, vecs = [], [], [], [None, None], [None, None]
    for l in range(2):
        wqkv, wo, w1, w2, par_l, _ = layers[l]
        y, qkv, lse, att, mid, act, slope = forward_call(l, x, cols, par_l, wqkv, wo, w1, w2)
        saved.append((x, qkv, lse, att, mid, act, slope))
        x = y
        ys.append(y)
    for l in (1, 0):
        wqkv, wo, w1, w2, par_l, _ = layers[l]
        x, qkv, lse, att, mid, act, slope = saved[l]
        gmid, dw1, dw2, vm = mlp_back_call(l, n_dp, g, cols, par_l, mid, act, slope, w1, w2)
        g, dqkv, dwo, va = attn_back_call(l, n_dp, gmid, cols, par_l, x, qkv, lse, att, wqkv, wo)
        gs.append(g)
        grads[l] = (dqkv, dwo, dw1, dw2)
        parts = (va[0, :D], va[1, :D], jnp.concatenate([va[2, :D], va[2, 2 * D:3 * D]]), va[3, :D], vm[0, :D], vm[1, :D], vm[2], vm[3, :D])
        vecs[l] = jnp.concatenate([v.reshape(n_dp, -1) for v in parts], axis=1)
    mine = jnp.where(sec == 0, ys[0], ys[1]), jnp.where(sec == 0, gs[1], gs[0])
    away = jnp.where(sec == 0, ys[1], ys[0]), jnp.where(sec == 0, gs[0], gs[1])
    got = [lax.ppermute(a, "section", [(0, 1), (1, 0)]) for a in away]
    both = [jnp.where(sec == 0, jnp.stack([m, o]), jnp.stack([o, m]))[None] for m, o in zip(mine, got)]
    width = vecs[0].shape[1]
    vrows = -(-width // LANES)
    vrows = -(-vrows // 8) * 8
    vec = jnp.pad(jnp.stack(vecs), ((0, 0), (0, 0), (0, vrows * LANES - width)))
    if dims:
        X, Y, Z = dims
        srcs = [a.reshape(2, Z, Y, X, -1, a.shape[-1]) for l in (1, 0) for a in (grads[l][3], grads[l][2], grads[l][0], grads[l][1])]
        srcs.append(vec.reshape(2, Z, Y, X, vrows, LANES))
        units = []
        for i, l in enumerate((1, 0)):
            b = 4 * i
            r2, r = FF // n_dp, D // n_dp
            h2 = r2 // 2
            units += [
                (b, 0, h2, 0, D // 2, "xy", l, 3, 0, h2, 0, D // 2, D // 2),
                (b, h2, h2, 0, D // 2, "yx", l, 3, h2, h2, 0, D // 2, D // 2),
            ]
            for src, out, C, cut in ((1, 2, FF // 2, FF // 4), (2, 0, 3 * D // 2, 640), (3, 1, D // 2, 128)):
                units += [
                    (b + src, 0, r, 0, cut, "xy", l, out, 0, r, 0, cut, C),
                    (b + src, 0, r, cut, C - cut, "yx", l, out, 0, r, cut, C - cut, C),
                ]
        units.append((8, 0, vrows, 0, LANES, "xy", None, 4, 0, 0, 0, 0, 0))
        outs = [(D // n_dp, 3 * D), (D // n_dp, D), (D // n_dp, FF), (FF // n_dp, D), (vrows, LANES)]
        dqkv, dwo, dw1, dw2, v = reduce_call(dims, srcs, units, outs, 1)
        v = v.reshape(-1)
    else:
        full = [jnp.stack([jnp.concatenate([grads[l][i][0], grads[l][i][1]], axis=-1).astype(f32).reshape(n_dp, -1) for l in range(2)]) for i in range(4)]
        full.append(vec)
        res = []
        for a in full:
            a = lax.psum_scatter(a, "section", scatter_dimension=0, tiled=False)
            res.append(lax.psum_scatter(a, "dp", scatter_dimension=0, tiled=False))
        dqkv, dwo, dw1, dw2 = (a.reshape(-1, c) for a, c in zip(res, (3 * D, D, FF, D)))
        v = res[4].reshape(-1)
    d, f = D // n_dp, FF // n_dp
    cuts = [0, d, 2 * d, 4 * d, 5 * d, 6 * d, 7 * d, 7 * d + f, 8 * d + f]
    n1g, n1b, qv, ob, n2g, n2b, b1, b2 = (v[None, a:b] for a, b in zip(cuts[:-1], cuts[1:]))
    return (both[0], both[1], n1g, n1b, dqkv[None], qv, dwo[None], ob, n2g, n2b, dw1[None], b1, dw2[None], b2)


def solution(mesh):
    in_specs = (
        P(None, "dp", None), P(None, "dp"), P("section", None, None, "dp"), P(None, "dp", None),
        P("section", None), P("section", None), P("section", None, None), P("section", None),
        P("section", None, None), P("section", None), P("section", None), P("section", None),
        P("section", None, None), P("section", None), P("section", None, None), P("section", None),
    )
    out_specs = (
        P("section", None, "dp", None), P("section", None, "dp", None),
        P("section", "dp"), P("section", "dp"), P("section", "dp", None), P("section", "dp"),
        P("section", "dp", None), P("section", "dp"), P("section", "dp"), P("section", "dp"),
        P("section", "dp", None), P("section", "dp"), P("section", "dp", None), P("section", "dp"),
    )
    return jax.shard_map(shards, mesh=mesh, in_specs=in_specs, out_specs=out_specs, check_vma=False)
```

```python
import functools
import jax
import jax.numpy as jnp
from jax import lax
from jax.experimental import pallas as pl
from jax.experimental.pallas import tpu as pltpu
from jax.sharding import PartitionSpec as P

HEAD_DIM = 64
LANES = 128
keep_rate = 0.9
norm_eps = 1e-06
root_half = 0.7071067811865476
inverse_root = 0.3989422804014327
BIG = 2.0**30
f32, bf16 = jnp.float32, jnp.bfloat16
NN = (((1,), (0,)), ((), ()))
NT = (((1,), (1,)), ((), ()))
TN = (((0,), (0,)), ((), ()))
MESH = pl.DeviceIdType.MESH
ANY = pl.BlockSpec(memory_space=pl.ANY)
DMA = pltpu.SemaphoreType.DMA
LIMIT = 61 * 2**20
RC = 128
W = 256
sds = jax.ShapeDtypeStruct


def dot(a, b, dims=NN):
    return lax.dot_general(a, b, dims, preferred_element_type=f32)


def layer_unit(x):
    center = x - jnp.mean(x, axis=-1, keepdims=True)
    scale = lax.rsqrt(jnp.mean(center * center, axis=-1, keepdims=True) + norm_eps)
    return center * scale, scale


def unit_back(grad, unit, scale, gain):
    scaled = grad * gain
    inner = jnp.mean(scaled, axis=-1, keepdims=True)
    along = jnp.mean(scaled * unit, axis=-1, keepdims=True)
    return scale * (scaled - inner - unit * along)


def gelu_pair(h):
    e = jnp.exp(h * h * -0.5)
    t = 1.0 / (jnp.abs(h) * (0.3275911 * root_half) + 1.0)
    poly = t * (0.5 * 0.254829592 + t * (0.5 * -0.284496736 + t * (0.5 * 1.421413741 + t * (0.5 * -1.453152027 + t * (0.5 * 1.061405429)))))
    tail = poly * e
    phi = jnp.where(h < 0, tail, 1.0 - tail)
    return h * phi, phi + h * e * inverse_root


def split3(v):
    a = v.astype(bf16)
    r = v - a.astype(f32)
    b = r.astype(bf16)
    c = (r - b.astype(f32)).astype(bf16)
    return a, b, c


def feature_base(odd):
    return 0 if odd else HEAD_DIM


def lanes_of(rows):
    return lax.broadcasted_iota(jnp.int32, (rows, LANES), 1)


def seg_feature(seg, rows, odd):
    base = feature_base(odd)
    lane = lanes_of(rows)
    inside = (lane >= base) & (lane < base + 8)
    same = (lane - base).astype(f32) == seg
    qf = jnp.where(inside & same, BIG, 0.0)
    kf = jnp.where(inside & jnp.logical_not(same), -1.0, 0.0)
    kf = jnp.where((lane >= base + 8) & (lane < base + 11), 1.0, kf)
    return qf.astype(bf16), kf.astype(bf16)


def own_lanes(rows, odd):
    lane = lanes_of(rows)
    return (lane >= HEAD_DIM) if odd else (lane < HEAD_DIM)


def tile(n, width):
    return pl.ds(pl.multiple_of(n * width, LANES), width)


def fetch(src, dst, sem):
    c = pltpu.make_async_copy(src, dst, sem)
    c.start()
    return c


def fetch_layer(sec, layer, own, other, dst, sem):
    c = pltpu.make_async_copy(own, dst, sem)

    @pl.when(sec == layer)
    def _():
        c.start()

    @pl.when(sec != layer)
    def _():
        pltpu.make_async_copy(other, dst, sem).start()
    return c


def partner():
    return {"section": 1 - lax.axis_index("section")}


def greet_partner():
    bar = pltpu.get_barrier_semaphore()
    pl.semaphore_signal(bar, inc=1, device_id=partner(), device_id_type=MESH)
    pl.semaphore_wait(bar, 1)


def send_copy(src, dst, send, recv, dev):
    return pltpu.make_async_remote_copy(src, dst, send, recv, device_id=dev, device_id_type=MESH)


class Reducer:
    def __init__(self, dims, units):
        self.dims, self.units = dims, units
        self.n = len(units)

    def remote_count(self):
        return sum(d - 1 for d in self.dims)

    def buffers(self):
        X, Y, Z = self.dims
        size = dict(x=X, y=Y, z=Z)
        own, inc, parts, fin = [], [], [], []
        for _, _, rows, _, cols, order, _ in self.units:
            own.append(pltpu.VMEM((Z, Y, X, rows, cols), bf16))
            inc.append(pltpu.VMEM((Z, Y, X, rows, cols), bf16))
            for k, a in enumerate(order):
                rest = tuple(size[b] for b in "zyx" if b in order[k + 1:])
                parts.append(pltpu.VMEM((size[a] - 1,) + rest + (rows, cols), bf16))
            fin.append(pltpu.VMEM((rows, cols), f32))
        m = self.remote_count() + 1
        return own + inc + parts + fin + [DMA((self.n, m)), DMA((self.n, m)), DMA((self.n, 2))]

    def outs(self):
        return [sds((2, u[2], u[4]), f32) for u in self.units]

    def bind(self, mine, recv, outs, scratch):
        n = self.n
        self.mine, self.recv, self.outs_ = mine, recv, outs
        self.own, self.inc = scratch[:n], scratch[n:2 * n]
        self.parts = [scratch[2 * n + 3 * i:2 * n + 3 * i + 3] for i in range(n)]
        self.fin = scratch[5 * n:6 * n]
        self.send, self.rsem, self.lsem = scratch[6 * n:]
        X, Y, Z = self.dims
        me = lax.axis_index("dp")
        self.sec = lax.axis_index("section")
        self.size = dict(x=X, y=Y, z=Z)
        self.at = dict(x=me % X, y=(me // X) % Y, z=me // (X * Y))

    def peer(self, axis, t):
        c = dict(self.at)
        c[axis] = t
        X, Y, Z = self.dims
        return {"dp": (c["z"] * Y + c["y"]) * X + c["x"]}

    def greet(self):
        bar = pltpu.get_barrier_semaphore()
        ids = [partner()]
        for a in "xyz":
            ids += [self.peer(a, lax.rem(self.at[a] + j, self.size[a])) for j in range(1, self.size[a])]
        for i in ids:
            pl.semaphore_signal(bar, inc=1, device_id=i, device_id_type=MESH)
        pl.semaphore_wait(bar, len(ids))

    def view(self, ref, u):
        _, row, rows, col, cols = self.units[u][:5]
        return ref.at[:, :, :, pl.ds(row, rows), pl.ds(col, cols)]

    def loads(self, u):
        src = self.units[u][0]
        return (
            pltpu.make_async_copy(self.view(self.mine[src], u), self.own[u], self.lsem.at[u, 0]),
            pltpu.make_async_copy(self.view(self.recv[src], u), self.inc[u], self.lsem.at[u, 1]),
        )

    def prefetch(self):
        for u in range(self.n):
            for c in self.loads(u):
                c.start()

    def index(self, order, k, t):
        done = order[:k]
        return tuple(self.at[a] if a in done else (t if a == order[k] else slice(None)) for a in "zyx")

    def stage_copies(self, u, k):
        order = self.units[u][5]
        a = order[k]
        base = sum(self.size[b] - 1 for b in order[:k])
        out = []
        for j in range(1, self.size[a]):
            t = lax.rem(self.at[a] + j, self.size[a])
            out.append(send_copy(
                self.own[u].at[self.index(order, k, t)], self.parts[u][k].at[j - 1],
                self.send.at[u, base + j - 1], self.rsem.at[u, base + j - 1], self.peer(a, t)))
        return out

    def spots(self, order, k):
        free = [b for b in "zyx" if b in order[k + 1:]]
        combos = [()]
        for b in free:
            combos = [c + (i,) for c in combos for i in range(self.size[b])]
        for c in combos:
            got = dict(zip(free, c))
            yield tuple(got[b] if b in got else self.at[b] for b in "zyx"), c

    def start_unit(self, u):
        for c in self.loads(u):
            c.wait()
        own, inc = self.own[u], self.inc[u]
        X, Y, Z = self.dims

        @pl.loop(0, Z)
        def _(z):
            for y in range(Y):
                for x in range(X):
                    own[z, y, x] = (own[z, y, x].astype(f32) + inc[z, y, x].astype(f32)).astype(bf16)
        for c in self.stage_copies(u, 0):
            c.start()

    def next_stage(self, u, k):
        order = self.units[u][5]
        for c in self.stage_copies(u, k):
            c.wait()
        own, part = self.own[u], self.parts[u][k]
        for i, c in self.spots(order, k):
            total = own[i].astype(f32)
            for j in range(self.size[order[k]] - 1):
                total += part[(j,) + c].astype(f32)
            if k == 2:
                self.fin[u][...] = total
            else:
                own[i] = total.astype(bf16)
        if k < 2:
            for c in self.stage_copies(u, k + 1):
                c.start()
            return
        layer = self.units[u][6]

        @pl.when(self.sec == layer)
        def _():
            self.result(u)[0].start()

        @pl.when(self.sec != layer)
        def _():
            self.result(u)[1].start()

    def result(self, u):
        dst = self.outs_[u].at[self.sec]
        local = pltpu.make_async_copy(self.fin[u], dst, self.lsem.at[u, 0])
        m = self.remote_count()
        away = send_copy(self.fin[u], dst, self.send.at[u, m], self.rsem.at[u, m], partner())
        return local, away

    def finish(self):
        for u in range(self.n):
            layer = self.units[u][6]

            @pl.when(self.sec == layer)
            def _():
                local, away = self.result(u)
                local.wait()
                away.wait_recv()

            @pl.when(self.sec != layer)
            def _():
                self.result(u)[1].wait_send()

    def steps(self, ahead):
        out = []
        for s in range(self.n + 3 * ahead):
            calls = []
            for k in (2, 1, 0):
                u = s - (k + 1) * ahead
                if 0 <= u < self.n:
                    calls.append(functools.partial(self.next_stage, u, k))
            if s < self.n:
                calls.append(functools.partial(self.start_unit, s))
            out.append(calls)
        return out


class Ticker:
    def __init__(self, steps):
        self.left = list(steps)

    def take(self, count):
        now, self.left = self.left[:count], self.left[count:]
        return [c for s in now for c in s]

    def run(self, count):
        for c in self.take(count):
            c()

    def in_loop(self, i, plan):
        for at, count in enumerate(plan):
            calls = self.take(count)
            if calls:
                @pl.when(i == at)
                def _(calls=calls):
                    for c in calls:
                        c()


def layer_scratch(T, D, FF):
    return dict(
        x=pltpu.VMEM((T, D), bf16), wqkv=pltpu.VMEM((D, 3 * D), bf16), wo=pltpu.VMEM((D, D), bf16),
        w1=pltpu.VMEM((D, FF), bf16), w2=pltpu.VMEM((FF, D), bf16),
        norm=pltpu.VMEM((T, D), bf16), second=pltpu.VMEM((T, D), bf16), feat=pltpu.VMEM((4, T, LANES), bf16),
        qkv=pltpu.VMEM((T, 3 * D), bf16), lse=pltpu.VMEM((D // LANES, T, 2), f32), att=pltpu.VMEM((T, D), bf16),
        mid=pltpu.VMEM((T, D), f32), act=pltpu.VMEM((T, FF), bf16), slope=pltpu.VMEM((T, FF), bf16),
        acc=pltpu.VMEM((T, D), f32), ha=pltpu.VMEM((T, W), f32), hb=pltpu.VMEM((T, W), f32), y=pltpu.VMEM((T, D), bf16),
    )


def forward_body(l, s, cols, par, ready, store):
    T, D = s["x"].shape
    FF = s["act"].shape[1]
    k1 = 1 + 2 * l

    @pl.loop(0, T // RC)
    def _(i):
        rows = pl.ds(i * RC, RC)
        unit, _s = layer_unit(s["x"][rows, :].astype(f32))
        s["norm"][rows, :] = (unit * par[l, 0:1, :D] + par[l, 1:2, :D]).astype(bf16)
        for odd in (0, 1):
            qf, kf = seg_feature(cols[rows, 0:1], RC, odd)
            s["feat"][2 * odd, rows, :] = qf
            s["feat"][2 * odd + 1, rows, :] = kf

    for part in range(3):
        ready(f"wqkv{part}")

        @pl.loop(0, D // W)
        def _(n):
            cs = pl.ds(pl.multiple_of(part * D + n * W, W), W)
            acc = dot(s["norm"][...], s["wqkv"][:, cs]) + par[l, 2:3, cs]
            s["qkv"][:, cs] = (acc * 0.125 if part == 0 else acc).astype(bf16)
    store("qkv")

    @pl.loop(0, D // LANES)
    def _(p):
        off = pl.multiple_of(p * LANES, LANES)
        qp = s["qkv"][:, pl.ds(off, LANES)]
        kp = s["qkv"][:, pl.ds(off + D, LANES)]
        vp = s["qkv"][:, pl.ds(off + 2 * D, LANES)]
        outs = []
        for odd in (0, 1):
            own = own_lanes(T, odd)
            base = feature_base(odd)
            q = jnp.where(own, qp, s["feat"][2 * odd])
            k = jnp.where(own, kp, s["feat"][2 * odd + 1])
            v = jnp.where(own, vp, jnp.ones_like(vp))
            sc = dot(q, k, NT)
            m = jnp.max(sc, axis=1, keepdims=True)
            e = jnp.exp(sc - m).astype(bf16)
            o = dot(e, v)
            total = o[:, base:base + 1]
            outs.append(o / total)
            s["lse"][p, :, odd:odd + 1] = m + jnp.log(total)
        s["att"][:, pl.ds(off, LANES)] = jnp.where(own_lanes(T, 0), outs[0], outs[1]).astype(bf16)
    store("lse")
    store("att")
    ready("wo")

    @pl.loop(0, D // W)
    def _(n):
        cs = tile(n, W)
        acc = dot(s["att"][...], s["wo"][:, cs]) + par[l, 3:4, cs]
        s["mid"][:, cs] = s["x"][:, cs].astype(f32) + cols[:, k1:k1 + 1] * acc
    store("mid")

    @pl.loop(0, T // RC)
    def _(i):
        rows = pl.ds(i * RC, RC)
        unit, _s = layer_unit(s["mid"][rows, :])
        s["second"][rows, :] = (unit * par[l, 4:5, :D] + par[l, 5:6, :D]).astype(bf16)
    ready("w1")

    def up(n, h):
        h[...] = dot(s["second"][...], s["w1"][:, tile(n, W)]) + par[l, 6:7, tile(n, W)]

    def bend(n, h):
        a, sl = gelu_pair(h[...])
        s["act"][:, tile(n, W)] = a.astype(bf16)
        s["slope"][:, tile(n, W)] = sl.astype(bf16)

    def down(n):
        return dot(s["act"][:, tile(n, 2 * W)], s["w2"][tile(n, 2 * W), :])

    pairs = FF // (2 * W)
    up(0, s["ha"])
    up(1, s["hb"])
    bend(0, s["ha"])
    up(2, s["ha"])
    bend(1, s["hb"])
    ready("w2")
    s["acc"][...] = jnp.zeros_like(s["acc"])

    @pl.loop(1, pairs)
    def _(i):
        up(2 * i + 1, s["hb"])
        bend(2 * i, s["ha"])
        up(jnp.minimum(2 * i + 2, 2 * pairs - 1), s["ha"])
        bend(2 * i + 1, s["hb"])
        s["acc"][...] += down(i - 1)
    store("act")
    store("slope")
    total = s["acc"][...] + down(pairs - 1) + par[l, 7:8, :D]
    s["y"][...] = (s["mid"][...] + cols[:, k1 + 1:k1 + 2] * total).astype(bf16)
    store("y")


SAVED = ("qkv", "lse", "att", "mid", "act", "slope")


def saved_shapes(T, D, FF):
    return [sds((T, 3 * D), bf16), sds((D // LANES, T, 2), f32), sds((T, D), bf16), sds((T, D), f32), sds((T, FF), bf16), sds((T, FF), bf16)]


VEC_SPOTS = (0, 1, 2, 3, 4, 5, 6, 7)


def first_kernel(names, tokens, segf, keep, *refs):
    vec_in, (wqkv, wo, w1, w2) = refs[:8], refs[8:12]
    o_w = refs[12:16]
    o_par, o_cols, o_y = refs[16:19]
    o_saved = dict(zip(SAVED, refs[19:25]))
    scratch = refs[25:]
    s = dict(zip(names, scratch))
    par, cols, keep_s, seg_s, send, recv, lsem, osem = scratch[len(names):]
    sec = lax.axis_index("section")
    T, D = s["x"].shape
    other = partner()
    greet_partner()
    par[:, 2:3, D:2 * D] = jnp.zeros((2, 1, D), f32)
    small, local = [], []

    def both(src, dst):
        n = len(small)
        small.append(send_copy(src, dst, send.at[n], recv.at[n], other))
        local.append(pltpu.make_async_copy(src, dst, lsem.at[n]))
    both(keep, keep_s.at[sec])
    for row, v in enumerate(vec_in):
        n = v.shape[1]
        if row == 2:
            both(v.at[:, pl.ds(0, D)], par.at[sec, pl.ds(2, 1), pl.ds(0, D)])
            both(v.at[:, pl.ds(D, D)], par.at[sec, pl.ds(2, 1), pl.ds(2 * D, D)])
        else:
            both(v, par.at[sec, pl.ds(row, 1), pl.ds(0, n)])
    for c in small:
        c.start()
    ns = len(small)
    chunks = [(f"wqkv{i}", wqkv.at[0, :, pl.ds(i * D, D)], o_w[0].at[:, pl.ds(i * D, D)], s["wqkv"].at[:, pl.ds(i * D, D)]) for i in range(3)]
    chunks += [(n, w.at[0], o, s[n]) for n, w, o in (("wo", wo, o_w[1]), ("w1", w1, o_w[2]), ("w2", w2, o_w[3]))]
    big = {}
    for i, (n, src, dst, vm) in enumerate(chunks):
        big[n] = send_copy(src, dst, send.at[ns + i], recv.at[ns + i], other)
        big[n].start()
    x_in = fetch(tokens.at[sec], s["x"], lsem.at[ns + 6])
    g_in = fetch(segf, seg_s, lsem.at[ns + 7])
    for c in local:
        c.start()
    loads = {}
    for i, (n, src, dst, vm) in enumerate(chunks):
        loads[n] = (pltpu.make_async_copy(src, vm, lsem.at[ns + i]), pltpu.make_async_copy(dst, vm, lsem.at[ns + i]))

    @pl.when(sec == 0)
    def _():
        for n in loads:
            loads[n][0].start()
    for c in local:
        c.wait()
    for c in small:
        c.wait()
    x_in.wait()
    g_in.wait()

    @pl.loop(0, T // RC)
    def _(i):
        rows = pl.ds(i * RC, RC)
        lane = lanes_of(RC)
        seg = seg_s[rows, :]
        hot = lane.astype(f32) == seg
        out = jnp.where(lane == 0, seg, 0.0)
        for l in range(2):
            for b in range(2):
                flag = jnp.sum(jnp.where(hot, keep_s[l, pl.ds(2 * sec + b, 1), :], 0.0), axis=1, keepdims=True) / keep_rate
                out = jnp.where(lane == 1 + 2 * l + b, flag, out)
        cols[rows, :] = out
    outs = [fetch(par, o_par, osem.at[7]), fetch(cols, o_cols, osem.at[8])]
    o_saved["y"] = o_y
    spots = list(SAVED) + ["y"]

    def arrive(n):
        @pl.when(sec == 1)
        def _():
            big[n].wait_recv()
            loads[n][1].start()

    before = {"wqkv0": ["wqkv0"], "wqkv1": ["wqkv1"], "wqkv2": ["wqkv2"], "wo": ["w1"], "w1": ["w2"], "w2": []}

    def ready(n):
        for a in before[n]:
            arrive(a)
        loads[n][0].wait()
        if n == "wqkv2":
            arrive("wo")

    def store(n):
        outs.append(fetch(s[n], o_saved[n], osem.at[spots.index(n)]))

    forward_body(0, s, cols, par, ready, store)

    @pl.when(sec == 0)
    def _():
        for n in big:
            big[n].wait_recv()
    for n in big:
        big[n].wait_send()
    for c in outs:
        c.wait()


def first_call(tokens, segf, keep, vecs, weights, cid):
    _, T, D = tokens.shape
    FF = weights[2].shape[2]
    sc = layer_scratch(T, D, FF)
    names = tuple(sc)
    ns = 10
    shapes = [sds(w.shape[1:], bf16) for w in weights] + [sds((2, 8, FF), f32), sds((T, LANES), f32), sds((T, D), bf16)] + saved_shapes(T, D, FF)
    return pl.pallas_call(
        functools.partial(first_kernel, names), out_shape=tuple(shapes),
        in_specs=[ANY] * 15, out_specs=(ANY,) * len(shapes),
        scratch_shapes=list(sc.values()) + [
            pltpu.VMEM((2, 8, FF), f32), pltpu.VMEM((T, LANES), f32), pltpu.VMEM((2, 8, LANES), f32), pltpu.VMEM((T, LANES), f32),
            DMA((ns + 6,)), DMA((ns + 6,)), DMA((ns + 8,)), DMA((9,))],
        compiler_params=pltpu.CompilerParams(collective_id=cid, has_side_effects=True, vmem_limit_bytes=LIMIT), name="forward_first",
    )(tokens, segf, keep, *vecs, *weights)


def second_kernel(names, x_hbm, cols_hbm, par_hbm, *refs):
    own, oth = refs[:4], refs[4:8]
    o_out = refs[8]
    o_saved = dict(zip(SAVED, refs[9:15]))
    scratch = refs[15:]
    s = dict(zip(names, scratch))
    par, cols, lsem, osem, esem = scratch[len(names):]
    sec = lax.axis_index("section")
    greet_partner()
    first = [fetch(x_hbm, s["x"], lsem.at[4]), fetch(cols_hbm, cols, lsem.at[5]), fetch(par_hbm, par, lsem.at[6])]
    loads = {n: fetch_layer(sec, 1, own[i].at[0], oth[i], s[n], lsem.at[i]) for i, n in enumerate(("wqkv", "wo", "w1", "w2"))}
    for c in first:
        c.wait()
    outs = []

    def ready(n):
        if n == "wqkv0":
            loads["wqkv"].wait()
        elif n in loads:
            loads[n].wait()

    swap = {}

    def store(n):
        if n != "y":
            outs.append(fetch(s[n], o_saved[n], osem.at[SAVED.index(n)]))

    to_other = lambda src: send_copy(src, o_out.at[0, sec], esem.at[0], esem.at[1], partner())
    to_own = lambda src: pltpu.make_async_copy(src, o_out.at[0, sec], esem.at[2])

    forward_body(1, s, cols, par, ready, store)

    @pl.when(sec == 0)
    def _():
        to_own(s["x"]).start()
        to_other(s["y"]).start()

    @pl.when(sec == 1)
    def _():
        to_own(s["y"]).start()
        to_other(s["x"]).start()
    to_own(s["x"]).wait()
    to_other(s["x"]).wait()
    for c in outs:
        c.wait()


def second_call(x, cols, par, own, oth, cid):
    T, D = x.shape
    FF = own[2].shape[2]
    sc = layer_scratch(T, D, FF)
    shapes = [sds((1, 2, T, D), bf16)] + saved_shapes(T, D, FF)
    return pl.pallas_call(
        functools.partial(second_kernel, tuple(sc)), out_shape=tuple(shapes),
        in_specs=[ANY] * 11, out_specs=(ANY,) * len(shapes),
        scratch_shapes=list(sc.values()) + [pltpu.VMEM((2, 8, FF), f32), pltpu.VMEM((T, LANES), f32), DMA((7,)), DMA((6,)), DMA((3,))],
        compiler_params=pltpu.CompilerParams(collective_id=cid, has_side_effects=True, vmem_limit_bytes=LIMIT), name="forward_second",
    )(x, cols, par, *own, *oth)


def slots(dims):
    return (dims[2], dims[1], dims[0]) if dims else (1, 1, 1)


def mlp_kernel(l, red, n_src, plan, g_hbm, cols_hbm, par_hbm, mid_hbm, act_hbm, slope_hbm, w1_own, w2_own, w1_oth, w2_oth, *refs):
    r_in, refs = refs[:2 * n_src], refs[2 * n_src:]
    o_gmid, o_mine1, o_recv1, o_mine2, o_recv2, o_vec = refs[:6]
    n_red = red.n if red else 0
    r_out, refs = refs[6:6 + n_red], refs[6 + n_red:]
    (g, cols, par, mid, act, slope, w1, w2, gd, second_t, gh, gs, gmid, dw1, dw2, vec, lsem, send, recv, osem), r_scr = refs[:20], refs[20:]
    sec = lax.axis_index("section")
    T, D = g.shape
    FF = act.shape[1]
    Z, Y, X, r1 = dw1.shape[1:5]
    g_src = g_hbm.at[sec] if len(g_hbm.shape) == 3 else g_hbm
    loads = dict(
        g=fetch(g_src, g, lsem.at[0]), cols=fetch(cols_hbm, cols, lsem.at[1]), par=fetch(par_hbm, par, lsem.at[2]), mid=fetch(mid_hbm, mid, lsem.at[3]),
        w2=fetch_layer(sec, l, w2_own.at[0], w2_oth, w2, lsem.at[4]))
    if red:
        red.bind(r_in[:n_src], r_in[n_src:], r_out, r_scr)
        red.prefetch()
        red.greet()
        ticks = Ticker(red.steps(plan["ahead"]))
        ticks.run(plan["start"])
    else:
        greet_partner()
    loads["slope"] = fetch(slope_hbm, slope, lsem.at[5])
    loads["act"] = fetch(act_hbm, act, lsem.at[6])
    loads["w1"] = fetch_layer(sec, l, w1_own.at[0], w1_oth, w1, lsem.at[7])
    vec[...] = jnp.zeros_like(vec)
    for n in ("g", "cols", "par", "mid"):
        loads[n].wait()
    k2 = 2 + 2 * l
    down_row = 7 + FF // D

    @pl.loop(0, T // RC)
    def _(i):
        rows = pl.ds(i * RC, RC)
        low = (g[rows, :].astype(f32) * cols[rows, k2:k2 + 1]).astype(bf16)
        gd[rows, :] = low
        vec[down_row:down_row + 1, :] += jnp.sum(low.astype(f32), axis=0, keepdims=True)
        unit, _s = layer_unit(mid[rows, :])
        second_t[:, rows] = (unit * par[l, 4:5, :D] + par[l, 5:6, :D]).astype(bf16).T
    for n in ("w2", "slope", "act"):
        loads[n].wait()
    tiles = FF // D
    half = tiles // 2
    r2 = FF // (Z * Y * X)

    def rows2(ref, h, n):
        return ref.at[h, n] if Z > 1 else ref.at[h, 0, 0, 0, pl.ds(n * D, D)]

    def hbm2(ref, n):
        return ref.at[n] if Z > 1 else ref.at[0, 0, 0, pl.ds(n * D, D)]

    def copy2(n, i):
        away = send_copy(rows2(dw2, 1 - sec, n), hbm2(o_recv2, n), send.at[2 + i], recv.at[2 + i], partner())
        near = pltpu.make_async_copy(rows2(dw2, sec, n), hbm2(o_mine2, n), osem.at[2 + i])
        return away, near

    def part1(ref, n):
        return ref.at[:, :, :, :, tile(n % half, D)]

    def copy1(n, i):
        away = send_copy(part1(dw1.at[1 - sec], n), part1(o_recv1, n), send.at[i], recv.at[i], partner())
        near = pltpu.make_async_copy(part1(dw1.at[sec], n), part1(o_mine1, n), osem.at[i])
        return away, near

    @pl.loop(0, tiles)
    def _(i):
        n = lax.rem(i + half * (1 - sec), tiles)
        cs = tile(n, D)
        ga = dot(gd[...], w2[cs, :], NT)
        low = (ga * slope[:, cs].astype(f32)).astype(bf16)
        gh[:, cs] = low
        vec[pl.ds(7 + n, 1), :] = jnp.sum(low.astype(f32), axis=0, keepdims=True)
        d2 = dot(act[:, cs], gd[...], TN).astype(bf16)
        for h in range(2):
            piece = d2[:, h * (D // 2):(h + 1) * (D // 2)]
            if Z > 1:
                dw2[h, n] = piece.reshape(Y, X, r2, D // 2)
            else:
                dw2[h, 0, 0, 0, pl.ds(n * D, D), :] = piece
        away, near = copy2(n, i)
        away.start()
        near.start()
        d1 = dot(second_t[...], low).astype(bf16)
        dw1[n // half, :, :, :, :, tile(n % half, D)] = d1.reshape(Z, Y, X, r1, D)

        @pl.when(i < half)
        def _():
            copy1(n, i)[0].start()

        @pl.when(i >= half)
        def _():
            copy1(n, i - half)[1].start()
        if red:
            ticks.in_loop(i, plan["loop"])
    loads["w1"].wait()

    @pl.loop(0, D // W)
    def _(n):
        cs = tile(n, W)
        gs[:, cs] = dot(gh[...], w1[cs, :], NT)
    if red:
        ticks.run(plan["late"])

    @pl.loop(0, T // RC)
    def _(i):
        rows = pl.ds(i * RC, RC)
        unit, scale = layer_unit(mid[rows, :])
        low = gs[rows, :]
        vec[5:6, :] += jnp.sum(low * unit, axis=0, keepdims=True)
        vec[6:7, :] += jnp.sum(low, axis=0, keepdims=True)
        gmid[rows, :] = g[rows, :].astype(f32) + unit_back(low, unit, scale, par[l, 4:5, :D])
    outs = [fetch(gmid, o_gmid, lsem.at[0]), fetch(vec, o_vec, lsem.at[1])]
    if red:
        ticks.run(10**6)
        red.finish()
    for c in outs:
        c.wait()
    for i in range(half):
        away, near = copy1(i, i)
        away.wait()
        near.wait()
    for i in range(tiles):
        away, near = copy2(i, i)
        away.wait()
        near.wait()


def mlp_call(l, dims, red, r_src, plan, g, cols, par, mid, act, slope, own, oth, cid):
    T, D = mid.shape
    FF = act.shape[1]
    sl = slots(dims)
    N = sl[0] * sl[1] * sl[2]
    h1, h2 = sl + (D // N, FF // 2), sl + (FF // N, D // 2)
    shapes = [sds((T, D), f32), sds(h1, bf16), sds(h1, bf16), sds(h2, bf16), sds(h2, bf16), sds((16, D), f32)]
    if red:
        shapes += red.outs()
    V = pltpu.VMEM
    scratch = [V((T, D), bf16), V((T, LANES), f32), V((2, 8, FF), f32), V((T, D), f32), V((T, FF), bf16), V((T, FF), bf16), V((D, FF), bf16), V((FF, D), bf16),
               V((T, D), bf16), V((D, T), bf16), V((T, FF), bf16), V((T, D), f32), V((T, D), f32), V((2,) + h1, bf16), V((2,) + h2, bf16), V((16, D), f32),
               DMA((8,)), DMA((6,)), DMA((6,)), DMA((6,))]
    if red:
        scratch += red.buffers()
    return pl.pallas_call(
        functools.partial(mlp_kernel, l, red, len(r_src) // 2, plan), out_shape=tuple(shapes),
        in_specs=[ANY] * (10 + len(r_src)), out_specs=(ANY,) * len(shapes), scratch_shapes=scratch,
        compiler_params=pltpu.CompilerParams(collective_id=cid, has_side_effects=True, vmem_limit_bytes=LIMIT), name=f"mlp_back_{l}",
    )(g, cols, par, mid, act, slope, own[2], own[3], oth[2], oth[3], *r_src)


def attn_kernel(l, red, n_src, plan, swap_out, gmid_hbm, vec_hbm, cols_hbm, par_hbm, x_hbm, qkv_hbm, lse_hbm, att_hbm, wqkv_own, wo_own, wqkv_oth, wo_oth, *refs):
    if swap_out:
        g_prev, refs = refs[0], refs[1:]
    r_in, refs = refs[:2 * n_src], refs[2 * n_src:]
    o_gin, o_mine1, o_recv1, o_mine2, o_recv2, o_vec = refs[:6]
    refs = refs[6:]
    n_red = red.n if red else 0
    r_out, refs = refs[:n_red], refs[n_red:]
    (gmid, vec, cols, par, x, qkv, lse, att, wqkv, wo, gb, norm_t, att_t, ga, gm, gn, feat, gin, dqkv, dwo, lsem, send, recv, osem, esem), r_scr = refs[:25], refs[25:]
    sec = lax.axis_index("section")
    T, D = x.shape
    Z, Y, X, r = dwo.shape[1:5]
    x_src = x_hbm.at[sec] if len(x_hbm.shape) == 3 else x_hbm
    loads = dict(
        gmid=fetch(gmid_hbm, gmid, lsem.at[0]), cols=fetch(cols_hbm, cols, lsem.at[1]), par=fetch(par_hbm, par, lsem.at[2]), x=fetch(x_src, x, lsem.at[3]),
        att=fetch(att_hbm, att, lsem.at[4]), wo=fetch_layer(sec, l, wo_own.at[0], wo_oth, wo, lsem.at[5]), vec=fetch(vec_hbm, vec, lsem.at[6]))
    if red:
        red.bind(r_in[:n_src], r_in[n_src:], r_out, r_scr)
        red.prefetch()
        red.greet()
        ticks = Ticker(red.steps(plan["ahead"]))
        ticks.run(plan["start"])
    else:
        greet_partner()
    loads["qkv"] = fetch(qkv_hbm, qkv, lsem.at[7])
    loads["lse"] = fetch(lse_hbm, lse, lsem.at[8])
    loads["wqkv"] = fetch_layer(sec, l, wqkv_own.at[0], wqkv_oth, wqkv, lsem.at[9])
    for n in ("gmid", "cols", "par", "x", "att", "vec"):
        loads[n].wait()
    k1 = 1 + 2 * l
    vec[0:5, :] = jnp.zeros((5, D), f32)

    @pl.loop(0, T // RC)
    def _(i):
        rows = pl.ds(i * RC, RC)
        low = (gmid[rows, :] * cols[rows, k1:k1 + 1]).astype(bf16)
        gb[rows, :] = low
        vec[4:5, :] += jnp.sum(low.astype(f32), axis=0, keepdims=True)
        unit, _s = layer_unit(x[rows, :].astype(f32))
        norm_t[:, rows] = (unit * par[l, 0:1, :D] + par[l, 1:2, :D]).astype(bf16).T
        att_t[:, rows] = att[rows, :].T
        for odd in (0, 1):
            qf, kf = seg_feature(cols[rows, 0:1], RC, odd)
            feat[2 * odd, rows, :] = qf
            feat[2 * odd + 1, rows, :] = kf
    loads["wo"].wait()

    @pl.loop(0, D // W)
    def _(n):
        cs = tile(n, W)
        ga[:, cs] = dot(gb[...], wo[cs, :], NT).astype(bf16)

    def pair(buf, mine, got, i):
        away = send_copy(buf.at[1 - sec], got, send.at[i], recv.at[i], partner())
        near = pltpu.make_async_copy(buf.at[sec], mine, osem.at[i])
        return away, near

    @pl.loop(0, 2)
    def _(h):
        dwo[h] = dot(att_t[...], gb[:, tile(h, D // 2)]).astype(bf16).reshape(Z, Y, X, r, D // 2)
    for c in pair(dwo, o_mine2, o_recv2, 1):
        c.start()
    loads["qkv"].wait()
    loads["lse"].wait()
    if red:
        ticks.run(plan["early"])

    low_lane = own_lanes(T, 0)

    @pl.loop(0, D // LANES)
    def _(p):
        off = pl.multiple_of(p * LANES, LANES)
        qp = qkv[:, pl.ds(off, LANES)]
        kp = qkv[:, pl.ds(off + D, LANES)]
        vp = qkv[:, pl.ds(off + 2 * D, LANES)]
        gp = ga[:, pl.ds(off, LANES)]
        prod = gp.astype(f32) * att[:, pl.ds(off, LANES)].astype(f32)
        dq, dk, dv = [], [], []
        for odd in (0, 1):
            own = own_lanes(T, odd)
            base = feature_base(odd)
            lane = lanes_of(T)
            row_d = jnp.sum(jnp.where(own, prod, 0.0), axis=1, keepdims=True)
            l3 = split3(-lse[p, :, odd:odd + 1])
            d3 = split3(-row_d)
            qf = feat[2 * odd]
            gf = jnp.zeros_like(gp)
            for j in range(3):
                qf = jnp.where(lane == base + 8 + j, l3[j], qf)
                gf = jnp.where(lane == base + j, d3[j], gf)
            q = jnp.where(own, qp, qf)
            k = jnp.where(own, kp, feat[2 * odd + 1])
            v = jnp.where(own, vp, jnp.ones_like(vp))
            gg = jnp.where(own, gp, gf)
            prob = jnp.exp(dot(k, q, NT))
            gs = (prob * dot(v, gg, NT)).astype(bf16)
            dv.append(dot(prob.astype(bf16), gg))
            dk.append(dot(gs, q))
            dq.append(dot(gs, k, TN))
        gm[:, pl.ds(off, LANES)] = (jnp.where(low_lane, dq[0], dq[1]) * 0.125).astype(bf16)
        gm[:, pl.ds(off + D, LANES)] = jnp.where(low_lane, dk[0], dk[1]).astype(bf16)
        gm[:, pl.ds(off + 2 * D, LANES)] = jnp.where(low_lane, dv[0], dv[1]).astype(bf16)
        if red:
            ticks.in_loop(p, plan["loop"])

    wide = 3 * D // 2

    @pl.loop(0, 2)
    def _(i):
        h = lax.rem(i + 1 + sec, 2)
        dqkv[h] = dot(norm_t[...], gm[:, tile(h, wide)]).astype(bf16).reshape(Z, Y, X, r, wide)
        away, near = pair(dqkv, o_mine1, o_recv1, 0)

        @pl.when(i == 0)
        def _():
            away.start()

        @pl.when(i == 1)
        def _():
            near.start()
        if red:
            ticks.in_loop(i, plan["mid"])
    vec[2:3, :] = jnp.sum(gm[:, 0:D].astype(f32), axis=0, keepdims=True)
    vec[3:4, :] = jnp.sum(gm[:, 2 * D:].astype(f32), axis=0, keepdims=True)
    loads["wqkv"].wait()

    @pl.loop(0, D // W)
    def _(n):
        cs = tile(n, W)
        gn[:, cs] = dot(gm[...], wqkv[cs, :], NT)
    if red:
        ticks.run(plan["late"])

    @pl.loop(0, T // RC)
    def _(i):
        rows = pl.ds(i * RC, RC)
        unit, scale = layer_unit(x[rows, :].astype(f32))
        low = gn[rows, :]
        vec[0:1, :] += jnp.sum(low * unit, axis=0, keepdims=True)
        vec[1:2, :] += jnp.sum(low, axis=0, keepdims=True)
        gin[rows, :] = (gmid[rows, :] + unit_back(low, unit, scale, par[l, 0:1, :D])).astype(bf16)
    outs = [fetch(vec, o_vec, lsem.at[1])]
    if swap_out:
        to_other = lambda src: send_copy(src, o_gin.at[0, sec], esem.at[0], esem.at[1], partner())
        to_own = lambda src: pltpu.make_async_copy(src, o_gin.at[0, sec], esem.at[2])

        @pl.when(sec == 0)
        def _():
            to_own(gin).start()
            to_other(g_prev).start()

        @pl.when(sec == 1)
        def _():
            to_own(g_prev).start()
            to_other(gin).start()
        to_own(gin).wait()
        to_other(gin).wait()
    else:
        outs.append(fetch(gin, o_gin, lsem.at[0]))
    if red:
        ticks.run(10**6)
        red.finish()
    for c in outs:
        c.wait()
    for buf, mine, got, i in ((dqkv, o_mine1, o_recv1, 0), (dwo, o_mine2, o_recv2, 1)):
        for c in pair(buf, mine, got, i):
            c.wait()


def attn_call(l, dims, red, r_src, plan, gmid, vec, cols, par, x, qkv, lse, att, own, oth, g_prev, cid):
    T, D = gmid.shape
    sl = slots(dims)
    N = sl[0] * sl[1] * sl[2]
    h1, h2 = sl + (D // N, 3 * D // 2), sl + (D // N, D // 2)
    swap_out = g_prev is not None
    shapes = [sds((1, 2, T, D), bf16) if swap_out else sds((T, D), bf16), sds(h1, bf16), sds(h1, bf16), sds(h2, bf16), sds(h2, bf16), sds((16, D), f32)]
    if red:
        shapes += red.outs()
    V = pltpu.VMEM
    FF = par.shape[2]
    scratch = [V((T, D), f32), V((16, D), f32), V((T, LANES), f32), V((2, 8, FF), f32), V((T, D), bf16), V((T, 3 * D), bf16), V((D // LANES, T, 2), f32), V((T, D), bf16),
               V((D, 3 * D), bf16), V((D, D), bf16), V((T, D), bf16), V((D, T), bf16), V((D, T), bf16), V((T, D), bf16), V((T, 3 * D), bf16), V((T, D), f32),
               V((4, T, LANES), bf16), V((T, D), bf16), V((2,) + h1, bf16), V((2,) + h2, bf16),
               DMA((10,)), DMA((2,)), DMA((2,)), DMA((2,)), DMA((3,))]
    if red:
        scratch += red.buffers()
    extra = ([g_prev] if swap_out else []) + list(r_src)
    return pl.pallas_call(
        functools.partial(attn_kernel, l, red, len(r_src) // 2, plan, swap_out), out_shape=tuple(shapes),
        in_specs=[ANY] * (12 + len(extra)), out_specs=(ANY,) * len(shapes), scratch_shapes=scratch,
        compiler_params=pltpu.CompilerParams(collective_id=cid, has_side_effects=True, vmem_limit_bytes=LIMIT), name=f"attn_back_{l}",
    )(gmid, vec, cols, par, x, qkv, lse, att, own[0], own[1], oth[0], oth[1], *extra)


def tail_kernel(red, n_src, n_done, done, places, widths, vec0, vec1, *refs):
    r_in, refs = refs[:2 * n_src], refs[2 * n_src:]
    d_in, refs = refs[:n_done], refs[n_done:]
    o_big, o_vec, r_out, refs = refs[:4], refs[4:12], refs[12:12 + red.n], refs[12 + red.n:]
    va, vown, vgot, lsem, csem, vsend, vrecv = refs[:7]
    r_scr = refs[7:]
    sec = lax.axis_index("section")
    me = lax.axis_index("dp")
    red.bind(r_in[:n_src], r_in[n_src:], r_out, r_scr)
    red.prefetch()
    load = [fetch(v, va.at[i], lsem.at[i]) for i, v in enumerate((vec0, vec1))]
    red.greet()
    def done_copies():
        for i, (out, row, rows, col, cols, width, layer) in enumerate(done):
            for h in range(2):
                yield layer, pltpu.make_async_copy(d_in[i].at[h], o_big[out].at[pl.ds(row, rows), pl.ds(h * width + col, cols)], csem.at[i, h])
    for layer in range(2):
        @pl.when(sec == layer)
        def _():
            for l, c in done_copies():
                if l == layer:
                    c.start()
    for c in load:
        c.wait()
    R = va.shape[1]
    X, Y, Z = red.dims
    hops = [("s", None)] + [(a, j) for a in "xyz" for j in range(1, red.size[a])]

    def hop(n):
        a, j = hops[n]
        if a == "s":
            return send_copy(va.at[1 - sec], vgot.at[0], vsend.at[0], vrecv.at[0], partner())
        return send_copy(vown.at["xyz".index(a)], vgot.at[n], vsend.at[n], vrecv.at[n], red.peer(a, lax.rem(red.at[a] + j, red.size[a])))
    hop(0).start()
    steps = Ticker(red.steps(2))
    steps.run(1)
    hop(0).wait()
    vown[0] = va[sec] + vgot[0]
    n = 1
    for k, a in enumerate("xyz"):
        ids = range(n, n + red.size[a] - 1)
        for i in ids:
            hop(i).start()
        steps.run(1)
        for i in ids:
            hop(i).wait()
        total = vown[k]
        for i in ids:
            total += vgot[i]
        n += len(ids)
        vown[k + 1] = total
    D = va.shape[2]
    n_dp = X * Y * Z
    for o, (row, width) in zip(o_vec, widths):
        size = width // n_dp
        at = me * size
        line = vown[3, pl.ds(row + at // D, 1), :]
        line = pltpu.roll(jnp.broadcast_to(line, (8, D)), lax.rem(D - at % D, D), 1)
        o[...] = line[0:1, :size]
    steps.run(10**6)
    red.finish()

    def last():
        for u in range(red.n):
            src, row, rows, col, cols = red.units[u][:5]
            out, width = places[src]
            for h in range(2):
                yield pltpu.make_async_copy(r_out[u].at[h], o_big[out].at[pl.ds(row, rows), pl.ds(h * width + col, cols)], csem.at[n_done + u, h])

    for layer in range(2):
        @pl.when(sec == layer)
        def _():
            mine = [c for u, c in zip([u for u in range(red.n) for _ in range(2)], last()) if red.units[u][6] == layer]
            for c in mine:
                c.start()
            for l, c in done_copies():
                if l == layer:
                    c.wait()
            for c in mine:
                c.wait()


def tail_call(red, r_src, places, done_refs, done, vec0, vec1, outs, widths, cid):
    n_dp = red.dims[0] * red.dims[1] * red.dims[2]
    D = vec0.shape[1]
    shapes = [sds(o, f32) for o in outs] + [sds((1, w // n_dp), f32) for _, w in widths] + red.outs()
    VM = pl.BlockSpec(memory_space=pltpu.VMEM)
    m = 1 + red.remote_count()
    scratch = [pltpu.VMEM((2, 16, D), f32), pltpu.VMEM((4, 16, D), f32), pltpu.VMEM((m, 16, D), f32), DMA((2,)), DMA((len(done) + red.n, 2)), DMA((m,)), DMA((m,))]
    scratch += red.buffers()
    return pl.pallas_call(
        functools.partial(tail_kernel, red, len(r_src) // 2, len(done), done, places, widths), out_shape=tuple(shapes),
        in_specs=[ANY] * (2 + len(r_src) + len(done)), out_specs=(ANY,) * 4 + (VM,) * 8 + (ANY,) * red.n, scratch_shapes=scratch,
        compiler_params=pltpu.CompilerParams(collective_id=cid, has_side_effects=True, vmem_limit_bytes=LIMIT), name="reduce_last",
    )(vec0, vec1, *r_src, *done_refs)


def dp_dims(n):
    return {16: (2, 2, 4)}.get(n)


def shards(
    tokens, segment_ids, keep_masks, cotangent,
    norm1_gain, norm1_bias, qkv_weight, qv_bias, out_weight, out_bias,
    norm2_gain, norm2_bias, fc1_weight, fc1_bias, fc2_weight, fc2_bias,
):
    sec = lax.axis_index("section")
    n_dp = lax.axis_size("dp")
    dims = dp_dims(n_dp)
    T, D = tokens.shape[1:]
    FF = fc1_weight.shape[2]
    seg = lax.dynamic_index_in_dim(segment_ids, sec, 0, keepdims=False)
    segf = jnp.broadcast_to(seg.astype(f32)[:, None], (T, LANES))
    keep = jnp.pad(keep_masks[0].astype(f32).reshape(4, -1), ((0, 4), (0, LANES - keep_masks.shape[3])))
    own = (qkv_weight, out_weight, fc1_weight, fc2_weight)
    vecs = (norm1_gain, norm1_bias, qv_bias, out_bias, norm2_gain, norm2_bias, fc1_bias, fc2_bias)
    res = first_call(tokens, segf, keep, vecs, own, 0)
    oth, par, cols, y0, saved0 = res[:4], res[4], res[5], res[6], dict(zip(SAVED, res[7:]))
    res = second_call(y0, cols, par, own, oth, 1)
    layer_out, saved1 = res[0], dict(zip(SAVED, res[1:]))
    r, r2 = D // n_dp, FF // n_dp
    if dims:
        cycle = ("xyz", "yxz", "xzy", "yzx", "xyz", "yxz")

        def mlp_units(a, b, l):
            one = [(a, 0, r, W * i, W, cycle[i], l) for i in range(6)]
            two = [(b, r2 // 6 * i, r2 // 6, 0, D // 2, cycle[i], l) for i in range(6)]
            return two + one

        def attn_units(a, b, l):
            return [(b, 0, r, 0, W, "yxz", l), (b, 0, r, W, LANES, "xyz", l)] + [
                (a, 0, r, W * i, W, ("xyz", "yxz", "xzy", "yzx")[i], l) for i in range(4)] + [(a, 0, r, 4 * W, LANES, "xyz", l)]
        red_a1, red_m0, red_a0, red_t = (Reducer(dims, u) for u in (mlp_units(0, 1, 1), attn_units(0, 1, 1), mlp_units(0, 1, 0), attn_units(0, 1, 0)))
    else:
        red_a1 = red_m0 = red_a0 = None
    plan_a = dict(ahead=3, start=3, early=1, loop=(1, 1, 1, 1, 1, 1), mid=(1, 1), late=1)
    plan_m = dict(ahead=2, start=2, loop=(1, 1, 1, 1), late=1)
    m1 = mlp_call(1, dims, None, (), None, cotangent, cols, par, saved1["mid"], saved1["act"], saved1["slope"], own, oth, 2)
    src = (m1[1], m1[3], m1[2], m1[4])
    a1 = attn_call(1, dims, red_a1, src if dims else (), plan_a, m1[0], m1[5], cols, par, y0, saved1["qkv"], saved1["lse"], saved1["att"], own, oth, None, 3)
    src = (a1[1], a1[3], a1[2], a1[4])
    m0 = mlp_call(0, dims, red_m0, src if dims else (), plan_m, a1[0], cols, par, saved0["mid"], saved0["act"], saved0["slope"], own, oth, 4)
    src = (m0[1], m0[3], m0[2], m0[4])
    a0 = attn_call(0, dims, red_a0, src if dims else (), plan_a, m0[0], m0[5], cols, par, tokens, saved0["qkv"], saved0["lse"], saved0["att"], own, oth, a1[0], 5)
    input_grad = a0[0]
    widths = ((0, D), (1, D), (2, 2 * D), (4, D), (5, D), (6, D), (7, FF), (7 + FF // D, D))
    if dims:
        places_m, places_a = ((2, FF // 2), (3, D // 2)), ((0, 3 * D // 2), (1, D // 2))
        done, done_refs = [], []
        for red, places, outs in ((red_a1, places_m, a1[6:]), (red_m0, places_a, m0[6:]), (red_a0, places_m, a0[6:])):
            for u, o in zip(red.units, outs):
                out, width = places[u[0]]
                done.append((out, u[1], u[2], u[3], u[4], width, u[6]))
                done_refs.append(o)
        src = (a0[1], a0[3], a0[2], a0[4])
        outs = ((r, 3 * D), (r, D), (r, FF), (r2, D))
        t = tail_call(red_t, src, places_a, done_refs, tuple(done), a0[5], a1[5], outs, widths, 6)
        dqkv, dwo, dw1, dw2 = t[:4]
        n1g, n1b, qv, ob, n2g, n2b, b1, b2 = t[4:12]
    else:
        res = []
        for a, m, i in ((a0, a1, 1), (a0, a1, 3), (m0, m1, 1), (m0, m1, 3)):
            both = []
            for k in (a, m):
                part = (k[i].astype(f32) + k[i + 1].astype(f32)).reshape(-1, k[i].shape[-1])
                both.append(lax.psum_scatter(part, "dp", scatter_dimension=0, tiled=True))
            halves = lax.all_gather(jnp.stack(both), "section")
            mine = lax.dynamic_index_in_dim(halves, sec, 1, keepdims=False)
            res.append(jnp.concatenate([mine[0], mine[1]], axis=-1))
        dqkv, dwo, dw1, dw2 = res
        v = lax.psum(jnp.stack([a0[5], a1[5]]), ("section", "dp"))
        v = lax.dynamic_index_in_dim(v, sec, 0, keepdims=False)
        at = lax.axis_index("dp")
        cut = [lax.dynamic_slice_in_dim(v[row:row + -(-w // D)].reshape(-1), at * (w // n_dp), w // n_dp)[None] for row, w in widths]
        n1g, n1b, qv, ob, n2g, n2b, b1, b2 = cut
    return (layer_out, input_grad, n1g, n1b, dqkv[None], qv, dwo[None], ob, n2g, n2b, dw1[None], b1, dw2[None], b2)


def solution(mesh):
    in_specs = (
        P(None, "dp", None), P(None, "dp"), P("section", None, None, "dp"), P(None, "dp", None),
        P("section", None), P("section", None), P("section", None, None), P("section", None),
        P("section", None, None), P("section", None), P("section", None), P("section", None),
        P("section", None, None), P("section", None), P("section", None, None), P("section", None),
    )
    out_specs = (
        P("section", None, "dp", None), P("section", None, "dp", None),
        P("section", "dp"), P("section", "dp"), P("section", "dp", None), P("section", "dp"),
        P("section", "dp", None), P("section", "dp"), P("section", "dp"), P("section", "dp"),
        P("section", "dp", None), P("section", "dp"), P("section", "dp", None), P("section", "dp"),
    )
    return jax.shard_map(shards, mesh=mesh, in_specs=in_specs, out_specs=out_specs, check_vma=False)
```

```python
import functools
import jax
import jax.numpy as jnp
from jax import lax
from jax.experimental import pallas as pl
from jax.experimental.pallas import tpu as pltpu
from jax.sharding import PartitionSpec as P

HEAD_DIM = 64
LANES = 128
keep_rate = 0.9
norm_eps = 1e-06
root_half = 0.7071067811865476
inverse_root = 0.3989422804014327
BIG = 2.0**30
f32, bf16 = jnp.float32, jnp.bfloat16
NN = (((1,), (0,)), ((), ()))
NT = (((1,), (1,)), ((), ()))
TN = (((0,), (0,)), ((), ()))
MESH = pl.DeviceIdType.MESH
ANY = pl.BlockSpec(memory_space=pl.ANY)
DMA = pltpu.SemaphoreType.DMA
LIMIT = 61 * 2**20
RC = 128
W = 256
sds = jax.ShapeDtypeStruct


def dot(a, b, dims=NN):
    return lax.dot_general(a, b, dims, preferred_element_type=f32)


def layer_unit(x):
    center = x - jnp.mean(x, axis=-1, keepdims=True)
    scale = lax.rsqrt(jnp.mean(center * center, axis=-1, keepdims=True) + norm_eps)
    return center * scale, scale


def unit_back(grad, unit, scale, gain):
    scaled = grad * gain
    inner = jnp.mean(scaled, axis=-1, keepdims=True)
    along = jnp.mean(scaled * unit, axis=-1, keepdims=True)
    return scale * (scaled - inner - unit * along)


def gelu_pair(h):
    phi = 0.5 * (1.0 + lax.erf(h * root_half))
    return h * phi, phi + h * jnp.exp(-0.5 * h * h) * inverse_root


def split3(v):
    a = v.astype(bf16)
    r = v - a.astype(f32)
    b = r.astype(bf16)
    c = (r - b.astype(f32)).astype(bf16)
    return a, b, c


def feature_base(odd):
    return 0 if odd else HEAD_DIM


def lanes_of(rows):
    return lax.broadcasted_iota(jnp.int32, (rows, LANES), 1)


def seg_feature(seg, rows, odd):
    base = feature_base(odd)
    lane = lanes_of(rows)
    inside = (lane >= base) & (lane < base + 8)
    same = (lane - base).astype(f32) == seg
    qf = jnp.where(inside & same, BIG, 0.0)
    kf = jnp.where(inside & jnp.logical_not(same), -1.0, 0.0)
    kf = jnp.where((lane >= base + 8) & (lane < base + 11), 1.0, kf)
    return qf.astype(bf16), kf.astype(bf16)


def own_lanes(rows, odd):
    lane = lanes_of(rows)
    return (lane >= HEAD_DIM) if odd else (lane < HEAD_DIM)


def tile(n, width):
    return pl.ds(pl.multiple_of(n * width, LANES), width)


def fetch(src, dst, sem):
    c = pltpu.make_async_copy(src, dst, sem)
    c.start()
    return c


def fetch_layer(sec, layer, own, other, dst, sem):
    c = pltpu.make_async_copy(own, dst, sem)

    @pl.when(sec == layer)
    def _():
        c.start()

    @pl.when(sec != layer)
    def _():
        pltpu.make_async_copy(other, dst, sem).start()
    return c


def partner():
    return {"section": 1 - lax.axis_index("section")}


def greet_partner():
    bar = pltpu.get_barrier_semaphore()
    pl.semaphore_signal(bar, inc=1, device_id=partner(), device_id_type=MESH)
    pl.semaphore_wait(bar, 1)


def send_copy(src, dst, send, recv, dev):
    return pltpu.make_async_remote_copy(src, dst, send, recv, device_id=dev, device_id_type=MESH)


def layer_scratch(T, D, FF):
    return dict(
        x=pltpu.VMEM((T, D), bf16), wqkv=pltpu.VMEM((D, 3 * D), bf16), wo=pltpu.VMEM((D, D), bf16),
        w1=pltpu.VMEM((D, FF), bf16), w2=pltpu.VMEM((FF, D), bf16),
        norm=pltpu.VMEM((T, D), bf16), second=pltpu.VMEM((T, D), bf16), feat=pltpu.VMEM((4, T, LANES), bf16),
        qkv=pltpu.VMEM((T, 3 * D), bf16), lse=pltpu.VMEM((D // LANES, T, 2), f32), att=pltpu.VMEM((T, D), bf16),
        mid=pltpu.VMEM((T, D), f32), act=pltpu.VMEM((T, FF), bf16), slope=pltpu.VMEM((T, FF), bf16),
        acc=pltpu.VMEM((T, D), f32), ha=pltpu.VMEM((T, W), f32), hb=pltpu.VMEM((T, W), f32), y=pltpu.VMEM((T, D), bf16),
    )


def forward_body(l, s, cols, par, ready, store):
    T, D = s["x"].shape
    FF = s["act"].shape[1]
    k1 = 1 + 2 * l

    @pl.loop(0, T // RC)
    def _(i):
        rows = pl.ds(i * RC, RC)
        unit, _s = layer_unit(s["x"][rows, :].astype(f32))
        s["norm"][rows, :] = (unit * par[l, 0:1, :D] + par[l, 1:2, :D]).astype(bf16)
        for odd in (0, 1):
            qf, kf = seg_feature(cols[rows, 0:1], RC, odd)
            s["feat"][2 * odd, rows, :] = qf
            s["feat"][2 * odd + 1, rows, :] = kf

    for part in range(3):
        ready(f"wqkv{part}")

        @pl.loop(0, D // W)
        def _(n):
            cs = pl.ds(pl.multiple_of(part * D + n * W, W), W)
            acc = dot(s["norm"][...], s["wqkv"][:, cs]) + par[l, 2:3, cs]
            s["qkv"][:, cs] = (acc * 0.125 if part == 0 else acc).astype(bf16)
    store("qkv")

    @pl.loop(0, D // LANES)
    def _(p):
        off = pl.multiple_of(p * LANES, LANES)
        qp = s["qkv"][:, pl.ds(off, LANES)]
        kp = s["qkv"][:, pl.ds(off + D, LANES)]
        vp = s["qkv"][:, pl.ds(off + 2 * D, LANES)]
        outs = []
        for odd in (0, 1):
            own = own_lanes(T, odd)
            base = feature_base(odd)
            q = jnp.where(own, qp, s["feat"][2 * odd])
            k = jnp.where(own, kp, s["feat"][2 * odd + 1])
            v = jnp.where(own, vp, jnp.ones_like(vp))
            sc = dot(q, k, NT)
            m = jnp.max(sc, axis=1, keepdims=True)
            e = jnp.exp(sc - m).astype(bf16)
            o = dot(e, v)
            total = o[:, base:base + 1]
            outs.append(o / total)
            s["lse"][p, :, odd:odd + 1] = m + jnp.log(total)
        s["att"][:, pl.ds(off, LANES)] = jnp.where(own_lanes(T, 0), outs[0], outs[1]).astype(bf16)
    store("lse")
    store("att")
    ready("wo")

    @pl.loop(0, D // W)
    def _(n):
        cs = tile(n, W)
        acc = dot(s["att"][...], s["wo"][:, cs]) + par[l, 3:4, cs]
        s["mid"][:, cs] = s["x"][:, cs].astype(f32) + cols[:, k1:k1 + 1] * acc
    store("mid")

    @pl.loop(0, T // RC)
    def _(i):
        rows = pl.ds(i * RC, RC)
        unit, _s = layer_unit(s["mid"][rows, :])
        s["second"][rows, :] = (unit * par[l, 4:5, :D] + par[l, 5:6, :D]).astype(bf16)
    ready("w1")

    def up(n, h):
        h[...] = dot(s["second"][...], s["w1"][:, tile(n, W)]) + par[l, 6:7, tile(n, W)]

    def bend(n, h):
        a, sl = gelu_pair(h[...])
        s["act"][:, tile(n, W)] = a.astype(bf16)
        s["slope"][:, tile(n, W)] = sl.astype(bf16)

    def down(n):
        return dot(s["act"][:, tile(n, 2 * W)], s["w2"][tile(n, 2 * W), :])

    pairs = FF // (2 * W)
    up(0, s["ha"])
    up(1, s["hb"])
    bend(0, s["ha"])
    up(2, s["ha"])
    bend(1, s["hb"])
    ready("w2")
    s["acc"][...] = jnp.zeros_like(s["acc"])

    @pl.loop(1, pairs)
    def _(i):
        up(2 * i + 1, s["hb"])
        bend(2 * i, s["ha"])
        up(jnp.minimum(2 * i + 2, 2 * pairs - 1), s["ha"])
        bend(2 * i + 1, s["hb"])
        s["acc"][...] += down(i - 1)
    store("act")
    store("slope")
    total = s["acc"][...] + down(pairs - 1) + par[l, 7:8, :D]
    s["y"][...] = (s["mid"][...] + cols[:, k1 + 1:k1 + 2] * total).astype(bf16)
    store("y")


SAVED = ("qkv", "lse", "att", "mid", "act", "slope")


def saved_shapes(T, D, FF):
    return [sds((T, 3 * D), bf16), sds((D // LANES, T, 2), f32), sds((T, D), bf16), sds((T, D), f32), sds((T, FF), bf16), sds((T, FF), bf16)]


def first_kernel(names, tokens, segf, keep, *refs):
    vec_in, (wqkv, wo, w1, w2) = refs[:8], refs[8:12]
    o_w = refs[12:16]
    o_par, o_cols, o_y = refs[16:19]
    o_saved = dict(zip(SAVED, refs[19:25]))
    scratch = refs[25:]
    s = dict(zip(names, scratch))
    par, cols, keep_s, seg_s, send, recv, lsem, osem = scratch[len(names):]
    sec = lax.axis_index("section")
    T, D = s["x"].shape
    other = partner()
    greet_partner()
    par[:, 2:3, D:2 * D] = jnp.zeros((2, 1, D), f32)
    small, local = [], []

    def both(src, dst):
        n = len(small)
        small.append(send_copy(src, dst, send.at[n], recv.at[n], other))
        local.append(pltpu.make_async_copy(src, dst, lsem.at[n]))
    both(keep, keep_s.at[sec])
    for row, v in enumerate(vec_in):
        n = v.shape[1]
        if row == 2:
            both(v.at[:, pl.ds(0, D)], par.at[sec, pl.ds(2, 1), pl.ds(0, D)])
            both(v.at[:, pl.ds(D, D)], par.at[sec, pl.ds(2, 1), pl.ds(2 * D, D)])
        else:
            both(v, par.at[sec, pl.ds(row, 1), pl.ds(0, n)])
    for c in small:
        c.start()
    ns = len(small)
    chunks = [(f"wqkv{i}", wqkv.at[0, :, pl.ds(i * D, D)], o_w[0].at[:, pl.ds(i * D, D)], s["wqkv"].at[:, pl.ds(i * D, D)]) for i in range(3)]
    chunks += [(n, w.at[0], o, s[n]) for n, w, o in (("wo", wo, o_w[1]), ("w1", w1, o_w[2]), ("w2", w2, o_w[3]))]
    big = {}
    for i, (n, src, dst, vm) in enumerate(chunks):
        big[n] = send_copy(src, dst, send.at[ns + i], recv.at[ns + i], other)
        big[n].start()
    x_in = fetch(tokens.at[sec], s["x"], lsem.at[ns + 6])
    g_in = fetch(segf, seg_s, lsem.at[ns + 7])
    for c in local:
        c.start()
    loads = {}
    for i, (n, src, dst, vm) in enumerate(chunks):
        loads[n] = (pltpu.make_async_copy(src, vm, lsem.at[ns + i]), pltpu.make_async_copy(dst, vm, lsem.at[ns + i]))

    @pl.when(sec == 0)
    def _():
        for n in loads:
            loads[n][0].start()
    for c in local:
        c.wait()
    for c in small:
        c.wait()
    x_in.wait()
    g_in.wait()

    @pl.loop(0, T // RC)
    def _(i):
        rows = pl.ds(i * RC, RC)
        lane = lanes_of(RC)
        seg = seg_s[rows, :]
        hot = lane.astype(f32) == seg
        out = jnp.where(lane == 0, seg, 0.0)
        for l in range(2):
            for b in range(2):
                flag = jnp.sum(jnp.where(hot, keep_s[l, pl.ds(2 * sec + b, 1), :], 0.0), axis=1, keepdims=True) / keep_rate
                out = jnp.where(lane == 1 + 2 * l + b, flag, out)
        cols[rows, :] = out
    outs = [fetch(par, o_par, osem.at[7]), fetch(cols, o_cols, osem.at[8])]
    o_saved["y"] = o_y
    spots = list(SAVED) + ["y"]

    def arrive(n):
        @pl.when(sec == 1)
        def _():
            big[n].wait_recv()
            loads[n][1].start()

    before = {"wqkv0": ["wqkv0"], "wqkv1": ["wqkv1"], "wqkv2": ["wqkv2"], "wo": ["w1"], "w1": ["w2"], "w2": []}

    def ready(n):
        for a in before[n]:
            arrive(a)
        loads[n][0].wait()
        if n == "wqkv2":
            arrive("wo")

    def store(n):
        outs.append(fetch(s[n], o_saved[n], osem.at[spots.index(n)]))

    forward_body(0, s, cols, par, ready, store)

    @pl.when(sec == 0)
    def _():
        for n in big:
            big[n].wait_recv()
    for n in big:
        big[n].wait_send()
    for c in outs:
        c.wait()


def first_call(tokens, segf, keep, vecs, weights, cid):
    _, T, D = tokens.shape
    FF = weights[2].shape[2]
    sc = layer_scratch(T, D, FF)
    names = tuple(sc)
    ns = 10
    shapes = [sds(w.shape[1:], bf16) for w in weights] + [sds((2, 8, FF), f32), sds((T, LANES), f32), sds((T, D), bf16)] + saved_shapes(T, D, FF)
    return pl.pallas_call(
        functools.partial(first_kernel, names), out_shape=tuple(shapes),
        in_specs=[ANY] * 15, out_specs=(ANY,) * len(shapes),
        scratch_shapes=list(sc.values()) + [
            pltpu.VMEM((2, 8, FF), f32), pltpu.VMEM((T, LANES), f32), pltpu.VMEM((2, 8, LANES), f32), pltpu.VMEM((T, LANES), f32),
            DMA((ns + 6,)), DMA((ns + 6,)), DMA((ns + 8,)), DMA((9,))],
        compiler_params=pltpu.CompilerParams(collective_id=cid, has_side_effects=True, vmem_limit_bytes=LIMIT), name="forward_first",
    )(tokens, segf, keep, *vecs, *weights)


def second_kernel(names, x_hbm, cols_hbm, par_hbm, *refs):
    own, oth = refs[:4], refs[4:8]
    o_out = refs[8]
    o_saved = dict(zip(SAVED, refs[9:15]))
    scratch = refs[15:]
    s = dict(zip(names, scratch))
    par, cols, lsem, osem, esem = scratch[len(names):]
    sec = lax.axis_index("section")
    greet_partner()
    first = [fetch(x_hbm, s["x"], lsem.at[4]), fetch(cols_hbm, cols, lsem.at[5]), fetch(par_hbm, par, lsem.at[6])]
    loads = {n: fetch_layer(sec, 1, own[i].at[0], oth[i], s[n], lsem.at[i]) for i, n in enumerate(("wqkv", "wo", "w1", "w2"))}
    for c in first:
        c.wait()
    outs = []

    def ready(n):
        if n == "wqkv0":
            loads["wqkv"].wait()
        elif n in loads:
            loads[n].wait()

    def store(n):
        if n != "y":
            outs.append(fetch(s[n], o_saved[n], osem.at[SAVED.index(n)]))

    to_other = lambda src: send_copy(src, o_out.at[0, sec], esem.at[0], esem.at[1], partner())
    to_own = lambda src: pltpu.make_async_copy(src, o_out.at[0, sec], esem.at[2])

    forward_body(1, s, cols, par, ready, store)

    @pl.when(sec == 0)
    def _():
        to_own(s["x"]).start()
        to_other(s["y"]).start()

    @pl.when(sec == 1)
    def _():
        to_own(s["y"]).start()
        to_other(s["x"]).start()
    to_own(s["x"]).wait()
    to_other(s["x"]).wait()
    for c in outs:
        c.wait()


def second_call(x, cols, par, own, oth, cid):
    T, D = x.shape
    FF = own[2].shape[2]
    sc = layer_scratch(T, D, FF)
    shapes = [sds((1, 2, T, D), bf16)] + saved_shapes(T, D, FF)
    return pl.pallas_call(
        functools.partial(second_kernel, tuple(sc)), out_shape=tuple(shapes),
        in_specs=[ANY] * 11, out_specs=(ANY,) * len(shapes),
        scratch_shapes=list(sc.values()) + [pltpu.VMEM((2, 8, FF), f32), pltpu.VMEM((T, LANES), f32), DMA((7,)), DMA((6,)), DMA((3,))],
        compiler_params=pltpu.CompilerParams(collective_id=cid, has_side_effects=True, vmem_limit_bytes=LIMIT), name="forward_second",
    )(x, cols, par, *own, *oth)


GRID = (4, 2, 2)
UR, UC = 48, 256
CYCLE = ("xyz", "yxz", "xzy", "yzx", "xyz", "yxz")
RING, INCS, FINS, AHEAD = 12, 4, 4, 3


class Stream:
    def __init__(self, dims, units):
        self.dims, self.units, self.n = dims, units, len(units)
        self.head = [0, 0, 0, 0]
        self.loaded = 0
        self.limit = 0

    def scratch(self):
        X, Y, Z = self.dims
        size = dict(x=X, y=Y, z=Z)
        parts = []
        for j in range(RING):
            order = CYCLE[j % len(CYCLE)]
            for k, a in enumerate(order):
                rest = tuple(size[b] for b in "zyx" if b in order[k + 1:])
                parts.append(pltpu.VMEM((size[a] - 1,) + rest + (UR, UC), bf16))
        hops = sum(d - 1 for d in self.dims)
        return [pltpu.VMEM((RING,) + GRID + (UR, UC), bf16), pltpu.VMEM((INCS,) + GRID + (UR, UC), bf16), pltpu.VMEM((FINS, UR, UC), f32),
                DMA((RING, hops)), DMA((RING, hops)), DMA((RING, 2)), DMA((FINS, 2)), DMA((self.n, 2))] + parts

    def bind(self, scratch, arrive, outs):
        self.own, self.inc, self.fin, self.send, self.rsem, self.lsem, self.fsend, self.frecv = scratch[:8]
        self.parts = [scratch[8 + 3 * j:11 + 3 * j] for j in range(RING)]
        self.arrive, self.outs = arrive, outs
        X, Y, Z = self.dims
        me = lax.axis_index("dp")
        self.sec = lax.axis_index("section")
        self.size = dict(x=X, y=Y, z=Z)
        self.at = dict(x=me % X, y=(me // X) % Y, z=me // (X * Y))

    def peer(self, axis, t):
        c = dict(self.at)
        c[axis] = t
        X, Y, Z = self.dims
        return {"dp": (c["z"] * Y + c["y"]) * X + c["x"]}

    def greet(self):
        bar = pltpu.get_barrier_semaphore()
        ids = [partner()]
        for a in "xyz":
            ids += [self.peer(a, lax.rem(self.at[a] + j, self.size[a])) for j in range(1, self.size[a])]
        for i in ids:
            pl.semaphore_signal(bar, inc=1, device_id=i, device_id_type=MESH)
        pl.semaphore_wait(bar, len(ids))

    def order(self, u):
        return CYCLE[(u % RING) % len(CYCLE)]

    def loads(self, u):
        mine, recv = self.units[u]["src"]
        return (pltpu.make_async_copy(mine, self.own.at[u % RING], self.lsem.at[u % RING, 0]),
                pltpu.make_async_copy(recv, self.inc.at[u % INCS], self.lsem.at[u % RING, 1]))

    def load(self, u):
        self.loaded = u + 1
        assert u < RING or self.head[3] > u - RING
        self.arrive(self.units[u]["need"])
        for c in self.loads(u):
            c.start()

    def index(self, order, k, t):
        done = order[:k]
        return tuple(self.at[a] if a in done else (t if a == order[k] else slice(None)) for a in "zyx")

    def hop(self, u, k):
        order = self.order(u)
        a = order[k]
        base = sum(self.size[b] - 1 for b in order[:k])
        j0 = u % RING
        out = []
        for j in range(1, self.size[a]):
            t = lax.rem(self.at[a] + j, self.size[a])
            out.append(send_copy(
                self.own.at[(j0,) + self.index(order, k, t)], self.parts[j0][k].at[j - 1],
                self.send.at[j0, base + j - 1], self.rsem.at[j0, base + j - 1], self.peer(a, t)))
        return out

    def start(self, u):
        if self.loaded <= u:
            self.load(u)
        for c in self.loads(u):
            c.wait()
        own, inc = self.own.at[u % RING], self.inc.at[u % INCS]

        @pl.loop(0, GRID[0])
        def _(z):
            for y in range(GRID[1]):
                for x in range(GRID[2]):
                    own[z, y, x] = own[z, y, x] + inc[z, y, x]
        for c in self.hop(u, 0):
            c.start()
        if u + 1 < self.limit and (u + 1 < RING or self.head[3] > u + 1 - RING):
            self.load(u + 1)

    def move(self, u, k):
        order = self.order(u)
        for c in self.hop(u, k):
            c.wait()
        own, part = self.own.at[u % RING], self.parts[u % RING][k]
        count = self.size[order[k]] - 1
        free = [b for b in "zyx" if b in order[k + 1:]]

        def add(pos):
            got = dict(zip(free, pos))
            i = tuple(got[b] if b in got else self.at[b] for b in "zyx")
            if count == 1 and k < 2:
                own[i] = own[i] + part[(0,) + tuple(pos)]
                return
            total = own[i].astype(f32)
            for j in range(count):
                total += part[(j,) + tuple(pos)].astype(f32)
            if k < 2:
                own[i] = total.astype(bf16)
            else:
                self.fin[u % FINS] = total
        if k == 2:
            if u >= FINS:
                self.sent(u - FINS)
            add(())
            self.deliver(u)
            return

        @pl.loop(0, self.size[free[0]])
        def _(i):
            if len(free) == 1:
                add((i,))
            else:
                for j in range(self.size[free[1]]):
                    add((i, j))
        for c in self.hop(u, k + 1):
            c.start()

    def results(self, u):
        for i, (out, row, rows, col, cols, c0) in enumerate(self.units[u]["dst"](self.sec)):
            dst = self.outs[out].at[pl.ds(row, rows), pl.ds(pl.multiple_of(col, LANES), cols)]
            src = self.fin.at[u % FINS, :, pl.ds(c0, cols)]
            yield (pltpu.make_async_copy(src, dst, self.fsend.at[u % FINS, i]),
                   send_copy(src, dst, self.fsend.at[u % FINS, i], self.frecv.at[u, i], partner()))

    def by_layer(self, u, same, other):
        @pl.when(self.sec == self.units[u]["layer"])
        def _():
            for near, away in self.results(u):
                same(near, away)

        @pl.when(self.sec != self.units[u]["layer"])
        def _():
            for near, away in self.results(u):
                other(near, away)

    def deliver(self, u):
        self.by_layer(u, lambda near, away: near.start(), lambda near, away: away.start())

    def sent(self, u):
        self.by_layer(u, lambda near, away: near.wait(), lambda near, away: away.wait_send())

    def tick(self):
        h = self.head
        todo = []
        can = h[0] < self.limit and (h[0] < RING or h[3] > h[0] - RING)
        for k in (2, 1, 0):
            if h[k + 1] < h[k] and (h[k] - h[k + 1] >= AHEAD or not can):
                todo.append((k, h[k + 1]))
        for k, u in todo:
            self.move(u, k)
            h[k + 1] += 1
        if can:
            self.start(h[0])
            h[0] += 1
        return bool(todo) or can

    def ticks(self, count):
        for _ in range(count):
            self.tick()

    def in_loop(self, i, plan):
        for at, (limit, count) in enumerate(plan):
            self.limit = max(self.limit, limit)
            if count:
                @pl.when(i == at)
                def _(count=count):
                    self.ticks(count)

    def finish(self):
        while self.tick():
            pass
        assert self.head == [self.n] * 4
        for u in range(self.n - FINS, self.n):
            self.sent(u)
        for u in range(self.n):
            @pl.when(self.sec == self.units[u]["layer"])
            def _():
                for _n, away in self.results(u):
                    away.wait_recv()


def gradient_units(bufs):
    Z, Y, X = GRID
    units = []
    for l in (1, 0):
        up, down, attn = bufs[l]
        for c in range(6):
            cut = lambda ref: ref.at[:, :, :, :, pl.ds(c * UC, UC)]
            units.append(dict(layer=l, src=tuple(map(cut, up)), need=(l, "up", c // 3),
                              dst=lambda sec, c=c: [(2, 0, UR, sec * 6 * UC + c * UC, UC, 0)]))
        for g in range(2):
            for c in range(3):
                cut = lambda ref: ref.at[:, g, :, :, :, pl.ds(c * UC, UC)]
                units.append(dict(layer=l, src=tuple(map(cut, down)), need=(l, "down", 0),
                                  dst=lambda sec, c=c, g=g: [(3, pl.multiple_of(sec * 2 * UR + g * UR, 16), UR, c * UC, UC, 0)]))
        for c in range(6):
            cut = lambda ref: ref.at[:, :, :, :, pl.ds(c * UC, UC)]
            def dst(sec, c=c):
                spots, a = [], c * UC
                lo, hi = min(a, 1152), min(a + UC, 1152)
                if hi > lo:
                    spots.append((0, 0, UR, sec * 1152 + lo, hi - lo, 0))
                lo2, hi2 = max(a, 1152), max(a + UC, 1152)
                if hi2 > lo2:
                    spots.append((1, 0, UR, sec * 384 + lo2 - 1152, hi2 - lo2, hi - lo if hi > lo else 0))
                return spots
            units.append(dict(layer=l, src=tuple(map(cut, attn)), need=(l, "attn", 0), dst=dst))
    return units


PLAN = {
    1: dict(norm=0, tile=((0, 0), (3, 1), (3, 1), (6, 1)), gs=((6, 0), (6, 1), (6, 0)), mid=1, gb=0, ga=1,
            pairs=((12, 1),) * 6, dqkv=((12, 1), (12, 1)), gn=((18, 0), (18, 1), (18, 0)), end=1),
    0: dict(norm=1, tile=((18, 1), (21, 1), (21, 1), (24, 1)), gs=((24, 1), (24, 1), (24, 0)), mid=1, gb=1, ga=1,
            pairs=((30, 1),) * 6, dqkv=((30, 1), (30, 1)), gn=((36, 1), (36, 1), (36, 1)), end=1),
}


def backward_kernel(dims, names, cot, tokens, y0, cols_h, par_h, *refs):
    saved = [dict(zip(SAVED, refs[:6])), dict(zip(SAVED, refs[6:12]))]
    own = dict(zip(("wqkv", "wo", "w1", "w2"), refs[12:16]))
    oth = dict(zip(("wqkv", "wo", "w1", "w2"), refs[16:20]))
    refs = refs[20:]
    o_gin, refs = refs[0], refs[1:]
    bufs = {}
    for l in (1, 0):
        bufs[l], refs = ((refs[0], refs[1]), (refs[2], refs[3]), (refs[4], refs[5])), refs[6:]
    if dims:
        o_big, o_vec, refs = refs[:4], refs[4:12], refs[12:]
    else:
        o_vec, refs = refs[0], refs[1:]
    s = dict(zip(names, refs))
    lsem, csend, crecv, cnear, esem, vsend, vrecv = refs[len(names):len(names) + 7]
    st_refs = refs[len(names) + 7:]
    g, mid, gs, gmid, act, slope, w1, w2, gd, tr, gh, x, att, att_t, ga, feat, lse, cols, par, vec, stage = (s[n] for n in names[:21])
    sec = lax.axis_index("section")
    me = lax.axis_index("dp")
    T, D = g.shape
    FF = act.shape[1]
    Z, Y, X = GRID
    tiles, half = FF // D, FF // D // 2

    ld = {}

    def get(n, src, dst):
        keys = tuple(names) + ("w2b", "w2c", "w2d")
        ld[n] = fetch(src, dst, lsem.at[keys.index(n)])

    def get_w(n, layer, name, src_of, dst):
        keys = tuple(names) + ("w2b", "w2c", "w2d")
        ld[n] = fetch_layer(sec, layer, src_of(own[name].at[0]), src_of(oth[name]), dst, lsem.at[keys.index(n)])

    def need(*ns):
        for n in ns:
            ld.pop(n).wait()

    W2 = ("w2", "w2b", "w2c", "w2d")

    def load_w2(l):
        for i, n in enumerate(W2):
            get_w(n, l, "w2", lambda r, i=i: r.at[pl.ds(i * D, D), :], w2.at[pl.ds(i * D, D), :])

    def load_attn_weights(l):
        for i in range(3):
            get_w(W2[i], l, "wqkv", lambda r, i=i: r.at[:, pl.ds(i * D, D)], w2.at[pl.ds(i * D, D), :])
        get_w(W2[3], l, "wo", lambda r: r, w2.at[pl.ds(3 * D, D), :])

    def up_copy(l, i):
        buf = stage.at[lax.rem(i, 2), :, :, :, :, pl.ds(0, D)]
        t = i // 2
        mine, recv = (r.at[:, :, :, :, tile(t, D)] for r in bufs[l][0])
        return (send_copy(buf, recv, csend.at[l, t], crecv.at[l, t], partner()), pltpu.make_async_copy(buf, mine, cnear.at[l, t]))

    def down_copy(l, i, n):
        mine, recv = (r.at[n] for r in bufs[l][1])
        buf = lambda h: stage.at[lax.rem(i, 2), pl.ds(2 * h, 2), :, :, :, pl.ds(D, D)]
        return (send_copy(buf(1 - sec), recv, csend.at[l, 2 + i], crecv.at[l, 2 + i], partner()),
                pltpu.make_async_copy(buf(sec), mine, cnear.at[l, 2 + i]))

    def attn_copy(l):
        mine, recv = bufs[l][2]
        return (send_copy(stage.at[1 - sec], recv, csend.at[l, 6], crecv.at[l, 6], partner()),
                pltpu.make_async_copy(stage.at[sec], mine, cnear.at[l, 6]))

    arrived = set()

    def arrive(key):
        if key in arrived:
            return
        arrived.add(key)
        l, kind, t = key
        if kind == "up":
            up_copy(l, 2 * t)[0].wait_recv()
            up_copy(l, 2 * t + 1)[1].wait()
        elif kind == "down":
            for i in range(tiles):
                down_copy(l, i, i)[0].wait_recv()
        else:
            attn_copy(l)[0].wait_recv()

    get("g", cot.at[sec], g)
    get("cols", cols_h, cols)
    get("par", par_h, par)
    get("mid", saved[1]["mid"], mid)
    load_w2(1)
    get("slope", saved[1]["slope"], slope)
    get("act", saved[1]["act"], act)
    get_w("w1", 1, "w1", lambda r: r, w1)
    get("x", y0, x)
    get("att", saved[1]["att"], att)
    get("lse", saved[1]["lse"], lse)
    if dims:
        st = Stream(dims, gradient_units(bufs))
        st.bind(st_refs, arrive, o_big)
        st.greet()
    else:
        st = None
        greet_partner()
    need("cols", "par")
    vec[...] = jnp.zeros_like(vec)

    @pl.loop(0, T // RC)
    def _(i):
        rows = pl.ds(i * RC, RC)
        for odd in (0, 1):
            qf, kf = seg_feature(cols[rows, 0:1], RC, odd)
            feat[2 * odd, rows, :] = qf
            feat[2 * odd + 1, rows, :] = kf

    def ticks(n):
        if st:
            st.ticks(n)

    def loop_ticks(i, plan):
        if st:
            st.in_loop(i, plan)

    down_row = 7 + FF // D
    low_lane = own_lanes(T, 0)
    for l in (1, 0):
        plan = PLAN[l]
        k1, k2 = 1 + 2 * l, 2 + 2 * l
        need(*(("g",) if l == 1 else ()), "mid")

        @pl.loop(0, T // RC)
        def _(i):
            rows = pl.ds(i * RC, RC)
            low = (g[rows, :].astype(f32) * cols[rows, k2:k2 + 1]).astype(bf16)
            gd[rows, :] = low
            vec[l, down_row:down_row + 1, :] += jnp.sum(low.astype(f32), axis=0, keepdims=True)
            unit, _s = layer_unit(mid[rows, :])
            tr[:, rows] = (unit * par[l, 4:5, :D] + par[l, 5:6, :D]).astype(bf16).T
        if l == 0:
            attn_copy(1)[0].wait_send()
        ticks(plan["norm"])
        need(*W2, "slope", "act")

        @pl.loop(0, tiles)
        def _(i):
            mine = lax.rem(i, 2)
            n = lax.rem(sec + 1 + mine, 2) * half + i // 2
            cs = tile(n, D)
            low = (dot(gd[...], w2[cs, :], NT) * slope[:, cs].astype(f32)).astype(bf16)
            gh[:, cs] = low
            vec[l, pl.ds(7 + n, 1), :] = jnp.sum(low.astype(f32), axis=0, keepdims=True)

            @pl.when(i == 2)
            def _():
                up_copy(l, 0)[0].wait_send()

            @pl.when(i >= 2)
            def _():
                a, b = down_copy(l, i - 2, n)
                a.wait_send()
                b.wait()
            d1 = dot(tr[...], low).astype(bf16)
            stage[mine, :, :, :, :, 0:D] = d1.reshape(Z, Y, X, UR, D)
            away, near = up_copy(l, i)

            @pl.when(mine == 0)
            def _():
                away.start()

            @pl.when(mine == 1)
            def _():
                near.start()
            d2 = dot(act[:, cs], gd[...], TN).astype(bf16).reshape(Y, X, 4, UR, D)
            for q in range(4):
                stage[mine, q, :, :, :, D:2 * D] = d2[:, :, q]
            for c in down_copy(l, i, n):
                c.start()
            loop_ticks(i, plan["tile"])
        load_attn_weights(l)
        get("qkv", saved[l]["qkv"], slope.at[:, pl.ds(0, 3 * D)])
        if l == 1:
            get("act", saved[0]["act"], act)
        need("w1")

        @pl.loop(0, D // W)
        def _(n):
            cs = tile(n, W)
            gs[:, cs] = dot(gh[...], w1[cs, :], NT)
            loop_ticks(n, plan["gs"])
        if l == 1:
            get_w("w1", 0, "w1", lambda r: r, w1)
        up_copy(l, 2)[0].wait_send()
        for i in (2, 3):
            a, b = down_copy(l, i, i)
            a.wait_send()
            b.wait()
        if st:
            st.limit = 12 + (1 - l) * 18

        @pl.loop(0, T // RC)
        def _(i):
            rows = pl.ds(i * RC, RC)
            unit, scale = layer_unit(mid[rows, :])
            low = gs[rows, :]
            vec[l, 5:6, :] += jnp.sum(low * unit, axis=0, keepdims=True)
            vec[l, 6:7, :] += jnp.sum(low, axis=0, keepdims=True)
            gmid[rows, :] = g[rows, :].astype(f32) + unit_back(low, unit, scale, par[l, 4:5, :D])
        ticks(plan["mid"])
        if l == 1:
            get("mid", saved[0]["mid"], mid)
        need("x", "att")

        @pl.loop(0, T // RC)
        def _(i):
            rows = pl.ds(i * RC, RC)
            low = (gmid[rows, :] * cols[rows, k1:k1 + 1]).astype(bf16)
            gd[rows, :] = low
            vec[l, 4:5, :] += jnp.sum(low.astype(f32), axis=0, keepdims=True)
            unit, _s = layer_unit(x[rows, :].astype(f32))
            tr[:, rows] = (unit * par[l, 0:1, :D] + par[l, 1:2, :D]).astype(bf16).T
            att_t[:, rows] = att[rows, :].T
        ticks(plan["gb"])
        need(*W2)

        @pl.loop(0, D // W)
        def _(n):
            cs = tile(n, W)
            ga[:, cs] = dot(gd[...], w2[pl.ds(pl.multiple_of(3 * D + n * W, W), W), :], NT).astype(bf16)
        for k in (0, 1):
            if st:
                assert (l, "up", k) in arrived
        if not st:
            arrive((l, "up", 0))
            arrive((l, "up", 1))
            arrive((l, "down", 0))

        @pl.loop(0, 2)
        def _(h):
            stage[h, :, :, :, :, 3 * D // 2:2 * D] = dot(att_t[...], gd[:, tile(h, D // 2)]).astype(bf16).reshape(Z, Y, X, UR, D // 2)
        ticks(plan["ga"])
        need("qkv", "lse")

        @pl.loop(0, D // LANES)
        def _(p):
            off = pl.multiple_of(p * LANES, LANES)
            qp = slope[:, pl.ds(off, LANES)]
            kp = slope[:, pl.ds(off + D, LANES)]
            vp = slope[:, pl.ds(off + 2 * D, LANES)]
            gp = ga[:, pl.ds(off, LANES)]
            prod = gp.astype(f32) * att[:, pl.ds(off, LANES)].astype(f32)
            dq, dk, dv = [], [], []
            for odd in (0, 1):
                own_l = own_lanes(T, odd)
                base = feature_base(odd)
                lane = lanes_of(T)
                row_d = jnp.sum(jnp.where(own_l, prod, 0.0), axis=1, keepdims=True)
                l3 = split3(-lse[p, :, odd:odd + 1])
                d3 = split3(-row_d)
                qf = feat[2 * odd]
                gf = jnp.zeros_like(gp)
                for j in range(3):
                    qf = jnp.where(lane == base + 8 + j, l3[j], qf)
                    gf = jnp.where(lane == base + j, d3[j], gf)
                q = jnp.where(own_l, qp, qf)
                k = jnp.where(own_l, kp, feat[2 * odd + 1])
                v = jnp.where(own_l, vp, jnp.ones_like(vp))
                gg = jnp.where(own_l, gp, gf)
                prob = jnp.exp(dot(k, q, NT))
                gsc = (prob * dot(v, gg, NT)).astype(bf16)
                dv.append(dot(prob.astype(bf16), gg))
                dk.append(dot(gsc, q))
                dq.append(dot(gsc, k, TN))
            gh[:, pl.ds(off, LANES)] = (jnp.where(low_lane, dq[0], dq[1]) * 0.125).astype(bf16)
            gh[:, pl.ds(off + D, LANES)] = jnp.where(low_lane, dk[0], dk[1]).astype(bf16)
            gh[:, pl.ds(off + 2 * D, LANES)] = jnp.where(low_lane, dv[0], dv[1]).astype(bf16)
            loop_ticks(p, plan["pairs"])
        if l == 1:
            get("slope", saved[0]["slope"], slope)
            get("att", saved[0]["att"], att)
            get("lse", saved[0]["lse"], lse)
        wide = 3 * D // 2

        @pl.loop(0, 2)
        def _(i):
            h = lax.rem(i + 1 + sec, 2)
            stage[h, :, :, :, :, 0:wide] = dot(tr[...], gh[:, tile(h, wide)]).astype(bf16).reshape(Z, Y, X, UR, wide)
            away, near = attn_copy(l)

            @pl.when(i == 0)
            def _():
                away.start()

            @pl.when(i == 1)
            def _():
                near.start()
            loop_ticks(i, plan["dqkv"])
        attn_copy(l)[1].wait()
        if st:
            st.limit = 18 + (1 - l) * 18
        vec[l, 2:3, :] = jnp.sum(gh[:, 0:D].astype(f32), axis=0, keepdims=True)
        vec[l, 3:4, :] = jnp.sum(gh[:, 2 * D:3 * D].astype(f32), axis=0, keepdims=True)

        @pl.loop(0, D // W)
        def _(n):
            cs = tile(n, W)
            acc = jnp.zeros((T, W), f32)
            for c in range(3):
                acc += dot(gh[:, c * D:(c + 1) * D], w2[pl.ds(pl.multiple_of(c * D + n * W, W), W), :], NT)
            gs[:, cs] = acc
            loop_ticks(n, plan["gn"])
        if l == 1:
            load_w2(0)

        @pl.loop(0, T // RC)
        def _(i):
            rows = pl.ds(i * RC, RC)
            unit, scale = layer_unit(x[rows, :].astype(f32))
            low = gs[rows, :]
            vec[l, 0:1, :] += jnp.sum(low * unit, axis=0, keepdims=True)
            vec[l, 1:2, :] += jnp.sum(low, axis=0, keepdims=True)
            res = (gmid[rows, :] + unit_back(low, unit, scale, par[l, 0:1, :D])).astype(bf16)
            if l == 1:
                g[rows, :] = res
            else:
                x[rows, :] = res
        if l == 1:
            get("x", tokens.at[sec], x)
        if l == 1:
            ticks(plan["end"])

    to_other = lambda src: send_copy(src, o_gin.at[0, sec], esem.at[0], esem.at[1], partner())
    to_own = lambda src: pltpu.make_async_copy(src, o_gin.at[0, sec], esem.at[2])

    @pl.when(sec == 0)
    def _():
        to_own(x).start()
        to_other(g).start()

    @pl.when(sec == 1)
    def _():
        to_own(g).start()
        to_other(x).start()
    if st:
        vown, vgot = s["vown"], s["vgot"]
        hops = [("s", None)] + [(a, j) for a in "xyz" for j in range(1, st.size[a])]

        def hop(n):
            a, j = hops[n]
            if a == "s":
                return send_copy(vec.at[1 - sec], vgot.at[0], vsend.at[0], vrecv.at[0], partner())
            return send_copy(vown.at["xyz".index(a)], vgot.at[n], vsend.at[n], vrecv.at[n], st.peer(a, lax.rem(st.at[a] + j, st.size[a])))
        hop(0).start()
        st.ticks(1)
        hop(0).wait()
        vown[0] = vec[sec] + vgot[0]
        n = 1
        for k, a in enumerate("xyz"):
            ids = range(n, n + st.size[a] - 1)
            for i in ids:
                hop(i).start()
            st.ticks(2)
            for i in ids:
                hop(i).wait()
            total = vown[k]
            for i in ids:
                total += vgot[i]
            n += len(ids)
            vown[k + 1] = total
        n_dp = dims[0] * dims[1] * dims[2]
        for o, (row, width) in zip(o_vec, small_spots(D, FF)):
            size = width // n_dp
            at = me * size
            line = vown[3, pl.ds(row + at // D, 1), :]
            line = pltpu.roll(jnp.broadcast_to(line, (8, D)), lax.rem(D - at % D, D), 1)
            o[...] = line[0:1, :size]
        st.finish()
    else:
        arrive((1, "attn", 0))
        arrive((0, "attn", 0))
        c = pltpu.make_async_copy(vec, o_vec, vsend.at[0])
        c.start()
        c.wait()
    attn_copy(0)[0].wait_send()
    to_own(x).wait()
    to_other(x).wait()


def small_spots(D, FF):
    return ((0, D), (1, D), (2, 2 * D), (4, D), (5, D), (6, D), (7, FF), (7 + FF // D, D))


def backward_call(dims, n_dp, cot, tokens, y0, cols, par, saved0, saved1, own, oth, cid):
    T, D = y0.shape
    FF = own[2].shape[2]
    V = pltpu.VMEM
    sc = dict(
        g=V((T, D), bf16), mid=V((T, D), f32), gs=V((T, D), f32), gmid=V((T, D), f32), act=V((T, FF), bf16), slope=V((T, FF), bf16),
        w1=V((D, FF), bf16), w2=V((FF, D), bf16), gd=V((T, D), bf16), tr=V((D, T), bf16), gh=V((T, FF), bf16), x=V((T, D), bf16), att=V((T, D), bf16),
        att_t=V((D, T), bf16), ga=V((T, D), bf16), feat=V((4, T, LANES), bf16), lse=V((D // LANES, T, 2), f32), cols=V((T, LANES), f32),
        par=V((2, 8, FF), f32), vec=V((2, 16, D), f32), stage=V((2,) + GRID + (UR, 2 * D), bf16))
    sc["qkv"] = V((8, LANES), f32)
    hops = 1 + (sum(d - 1 for d in dims) if dims else 0)
    if dims:
        sc.update(vown=V((4, 16, D), f32), vgot=V((hops, 16, D), f32))
    wide = sds(GRID + (UR, 2 * D), bf16)
    tall = sds((GRID[0], 2) + GRID[1:] + (UR, D), bf16)
    shapes = [sds((1, 2, T, D), bf16)] + [wide, wide, tall, tall, wide, wide] * 2
    specs = [ANY] * len(shapes)
    if dims:
        shapes += [sds((D // n_dp, 3 * D), f32), sds((D // n_dp, D), f32), sds((D // n_dp, FF), f32), sds((FF // n_dp, D), f32)]
        shapes += [sds((1, w // n_dp), f32) for _, w in small_spots(D, FF)]
        specs += [ANY] * 4 + [pl.BlockSpec(memory_space=pltpu.VMEM)] * 8
        stream = Stream(dims, [None] * 36).scratch()
    else:
        shapes += [sds((2, 16, D), f32)]
        specs += [ANY]
        stream = []
    scratch = list(sc.values()) + [DMA((len(sc) + 3,)), DMA((2, 7)), DMA((2, 7)), DMA((2, 7)), DMA((3,)), DMA((hops,)), DMA((hops,))] + stream
    return pl.pallas_call(
        functools.partial(backward_kernel, dims, tuple(sc)), out_shape=tuple(shapes),
        in_specs=[ANY] * 25, out_specs=tuple(specs), scratch_shapes=scratch,
        compiler_params=pltpu.CompilerParams(collective_id=cid, has_side_effects=True, vmem_limit_bytes=LIMIT), name="backward",
    )(cot, tokens, y0, cols, par, *saved0, *saved1, *own, *oth)


def dp_dims(n):
    return {16: (2, 2, 4)}.get(n)


def shards(
    tokens, segment_ids, keep_masks, cotangent,
    norm1_gain, norm1_bias, qkv_weight, qv_bias, out_weight, out_bias,
    norm2_gain, norm2_bias, fc1_weight, fc1_bias, fc2_weight, fc2_bias,
):
    sec = lax.axis_index("section")
    n_dp = lax.axis_size("dp")
    dims = dp_dims(n_dp)
    T, D = tokens.shape[1:]
    FF = fc1_weight.shape[2]
    seg = lax.dynamic_index_in_dim(segment_ids, sec, 0, keepdims=False)
    segf = jnp.broadcast_to(seg.astype(f32)[:, None], (T, LANES))
    keep = jnp.pad(keep_masks[0].astype(f32).reshape(4, -1), ((0, 4), (0, LANES - keep_masks.shape[3])))
    own = (qkv_weight, out_weight, fc1_weight, fc2_weight)
    vecs = (norm1_gain, norm1_bias, qv_bias, out_bias, norm2_gain, norm2_bias, fc1_bias, fc2_bias)
    res = first_call(tokens, segf, keep, vecs, own, 0)
    oth, par, cols, y0, saved0 = res[:4], res[4], res[5], res[6], res[7:]
    res = second_call(y0, cols, par, own, oth, 1)
    layer_out, saved1 = res[0], res[1:]
    res = backward_call(dims, n_dp, cotangent, tokens, y0, cols, par, saved0, saved1, own, oth, 2)
    input_grad = res[0]
    if dims:
        dqkv, dwo, dw1, dw2 = res[13:17]
        n1g, n1b, qv, ob, n2g, n2b, b1, b2 = res[17:25]
    else:
        sums = {}
        for i, l in enumerate((1, 0)):
            up, down, attn = (res[1 + 6 * i + 2 * j].astype(f32) + res[2 + 6 * i + 2 * j].astype(f32) for j in range(3))
            up, attn = up.reshape(D, -1), attn.reshape(D, -1)
            down = lax.all_gather(down, "section")
            down = down.transpose(1, 3, 4, 0, 2, 5, 6).reshape(FF, D)
            sums[l] = [lax.psum_scatter(a, "dp", scatter_dimension=0, tiled=True) for a in (attn, up, down)]
        attn, up, down = (jnp.stack([sums[0][i], sums[1][i]]) for i in range(3))
        attn, up = (lax.dynamic_index_in_dim(lax.all_gather(a, "section"), sec, 1, keepdims=False) for a in (attn, up))
        dw2 = lax.dynamic_index_in_dim(down, sec, 0, keepdims=False)
        cut = 3 * D // 2
        dqkv = jnp.concatenate([attn[0, :, :cut], attn[1, :, :cut]], axis=1)
        dwo = jnp.concatenate([attn[0, :, cut:], attn[1, :, cut:]], axis=1)
        dw1 = jnp.concatenate([up[0], up[1]], axis=1)
        v = lax.dynamic_index_in_dim(lax.psum(res[13], ("section", "dp")), sec, 0, keepdims=False)
        at = lax.axis_index("dp")
        n1g, n1b, qv, ob, n2g, n2b, b1, b2 = (
            lax.dynamic_slice_in_dim(v[row:row + -(-w // D)].reshape(-1), at * (w // n_dp), w // n_dp)[None] for row, w in small_spots(D, FF))
    return (layer_out, input_grad, n1g, n1b, dqkv[None], qv, dwo[None], ob, n2g, n2b, dw1[None], b1, dw2[None], b2)


def solution(mesh):
    in_specs = (
        P(None, "dp", None), P(None, "dp"), P("section", None, None, "dp"), P(None, "dp", None),
        P("section", None), P("section", None), P("section", None, None), P("section", None),
        P("section", None, None), P("section", None), P("section", None), P("section", None),
        P("section", None, None), P("section", None), P("section", None, None), P("section", None),
    )
    out_specs = (
        P("section", None, "dp", None), P("section", None, "dp", None),
        P("section", "dp"), P("section", "dp"), P("section", "dp", None), P("section", "dp"),
        P("section", "dp", None), P("section", "dp"), P("section", "dp"), P("section", "dp"),
        P("section", "dp", None), P("section", "dp"), P("section", "dp", None), P("section", "dp"),
    )
    return jax.shard_map(shards, mesh=mesh, in_specs=in_specs, out_specs=out_specs, check_vma=False)
```

```python
import functools
import jax
import jax.numpy as jnp
from jax import lax
from jax.experimental import pallas as pl
from jax.experimental.pallas import tpu as pltpu
from jax.sharding import PartitionSpec as P

HEAD_DIM = 64
LANES = 128
keep_rate = 0.9
norm_eps = 1e-06
root_half = 0.7071067811865476
inverse_root = 0.3989422804014327
BIG = 2.0**30
f32, bf16 = jnp.float32, jnp.bfloat16
NN = (((1,), (0,)), ((), ()))
NT = (((1,), (1,)), ((), ()))
TN = (((0,), (0,)), ((), ()))
MESH = pl.DeviceIdType.MESH
ANY = pl.BlockSpec(memory_space=pl.ANY)
DMA = pltpu.SemaphoreType.DMA
LIMIT = 61 * 2**20
RC = 128
W = 256
sds = jax.ShapeDtypeStruct


def dot(a, b, dims=NN):
    return lax.dot_general(a, b, dims, preferred_element_type=f32)


def layer_unit(x):
    center = x - jnp.mean(x, axis=-1, keepdims=True)
    scale = lax.rsqrt(jnp.mean(center * center, axis=-1, keepdims=True) + norm_eps)
    return center * scale, scale


def unit_back(grad, unit, scale, gain):
    scaled = grad * gain
    inner = jnp.mean(scaled, axis=-1, keepdims=True)
    along = jnp.mean(scaled * unit, axis=-1, keepdims=True)
    return scale * (scaled - inner - unit * along)


def gelu_pair(h):
    phi = 0.5 * (1.0 + lax.erf(h * root_half))
    return h * phi, phi + h * jnp.exp(-0.5 * h * h) * inverse_root


def split3(v):
    a = v.astype(bf16)
    r = v - a.astype(f32)
    b = r.astype(bf16)
    c = (r - b.astype(f32)).astype(bf16)
    return a, b, c


def feature_base(odd):
    return 0 if odd else HEAD_DIM


def lanes_of(rows):
    return lax.broadcasted_iota(jnp.int32, (rows, LANES), 1)


def seg_feature(seg, rows, odd):
    base = feature_base(odd)
    lane = lanes_of(rows)
    inside = (lane >= base) & (lane < base + 8)
    same = (lane - base).astype(f32) == seg
    qf = jnp.where(inside & same, BIG, 0.0)
    kf = jnp.where(inside & jnp.logical_not(same), -1.0, 0.0)
    kf = jnp.where((lane >= base + 8) & (lane < base + 11), 1.0, kf)
    return qf.astype(bf16), kf.astype(bf16)


def own_lanes(rows, odd):
    lane = lanes_of(rows)
    return (lane >= HEAD_DIM) if odd else (lane < HEAD_DIM)


def tile(n, width):
    return pl.ds(pl.multiple_of(n * width, LANES), width)


def fetch(src, dst, sem):
    c = pltpu.make_async_copy(src, dst, sem)
    c.start()
    return c


def fetch_layer(sec, layer, own, other, dst, sem):
    c = pltpu.make_async_copy(own, dst, sem)

    @pl.when(sec == layer)
    def _():
        c.start()

    @pl.when(sec != layer)
    def _():
        pltpu.make_async_copy(other, dst, sem).start()
    return c


def partner():
    return {"section": 1 - lax.axis_index("section")}


def greet_partner():
    bar = pltpu.get_barrier_semaphore()
    pl.semaphore_signal(bar, inc=1, device_id=partner(), device_id_type=MESH)
    pl.semaphore_wait(bar, 1)


def send_copy(src, dst, send, recv, dev):
    return pltpu.make_async_remote_copy(src, dst, send, recv, device_id=dev, device_id_type=MESH)


def layer_scratch(T, D, FF):
    return dict(
        x=pltpu.VMEM((T, D), bf16), wqkv=pltpu.VMEM((D, 3 * D), bf16), wo=pltpu.VMEM((D, D), bf16),
        w1=pltpu.VMEM((D, FF), bf16), w2=pltpu.VMEM((FF, D), bf16),
        norm=pltpu.VMEM((T, D), bf16), second=pltpu.VMEM((T, D), bf16), feat=pltpu.VMEM((4, T, LANES), bf16),
        qkv=pltpu.VMEM((T, 3 * D), bf16), lse=pltpu.VMEM((D // LANES, T, 2), f32), att=pltpu.VMEM((T, D), bf16),
        mid=pltpu.VMEM((T, D), f32), act=pltpu.VMEM((T, FF), bf16), slope=pltpu.VMEM((T, FF), bf16),
        y=pltpu.VMEM((T, D), bf16),
    )


def forward_body(l, s, cols, par, ready, store):
    T, D = s["x"].shape
    FF = s["act"].shape[1]
    k1 = 1 + 2 * l

    @pl.loop(0, T // RC)
    def _(i):
        rows = pl.ds(i * RC, RC)
        unit, _s = layer_unit(s["x"][rows, :].astype(f32))
        s["norm"][rows, :] = (unit * par[l, 0:1, :D] + par[l, 1:2, :D]).astype(bf16)
        for odd in (0, 1):
            qf, kf = seg_feature(cols[rows, 0:1], RC, odd)
            s["feat"][2 * odd, rows, :] = qf
            s["feat"][2 * odd + 1, rows, :] = kf

    for part in range(3):
        ready(f"wqkv{part}")

        @pl.loop(0, D // W)
        def _(n):
            cs = pl.ds(pl.multiple_of(part * D + n * W, W), W)
            acc = dot(s["norm"][...], s["wqkv"][:, cs]) + par[l, 2:3, cs]
            s["qkv"][:, cs] = (acc * 0.125 if part == 0 else acc).astype(bf16)
    store("qkv")

    def one_pair(p):
        off = pl.multiple_of(p * LANES, LANES)
        qp = s["qkv"][:, pl.ds(off, LANES)]
        kp = s["qkv"][:, pl.ds(off + D, LANES)]
        vp = s["qkv"][:, pl.ds(off + 2 * D, LANES)]
        outs, scs, vs = [], [], []
        for odd in (0, 1):
            own = own_lanes(T, odd)
            q = jnp.where(own, qp, s["feat"][2 * odd])
            k = jnp.where(own, kp, s["feat"][2 * odd + 1])
            vs.append(jnp.where(own, vp, jnp.ones_like(vp)))
            scs.append(dot(q, k, NT))
        ms = [jnp.max(sc, axis=1, keepdims=True) for sc in scs]
        es = [jnp.exp(sc - m).astype(bf16) for sc, m in zip(scs, ms)]
        for odd in (0, 1):
            base = feature_base(odd)
            o = dot(es[odd], vs[odd])
            total = o[:, base:base + 1]
            outs.append(o / total)
            s["lse"][p, :, odd:odd + 1] = ms[odd] + jnp.log(total)
        s["att"][:, pl.ds(off, LANES)] = jnp.where(own_lanes(T, 0), outs[0], outs[1]).astype(bf16)

    @pl.loop(0, D // LANES // 2)
    def _(pp):
        one_pair(2 * pp)
        one_pair(2 * pp + 1)
    store("lse")
    store("att")
    ready("wo")

    @pl.loop(0, D // W)
    def _(n):
        cs = tile(n, W)
        acc = dot(s["att"][...], s["wo"][:, cs]) + par[l, 3:4, cs]
        s["mid"][:, cs] = s["x"][:, cs].astype(f32) + cols[:, k1:k1 + 1] * acc
    store("mid")

    @pl.loop(0, T // RC)
    def _(i):
        rows = pl.ds(i * RC, RC)
        unit, _s = layer_unit(s["mid"][rows, :])
        s["second"][rows, :] = (unit * par[l, 4:5, :D] + par[l, 5:6, :D]).astype(bf16)
    ready("w1")

    ready("w2")

    @pl.loop(0, FF // D)
    def _(n):
        cs = tile(n, D)
        a, sl = gelu_pair(dot(s["second"][...], s["w1"][:, cs]) + par[l, 6:7, cs])
        s["act"][:, cs] = a.astype(bf16)
        s["slope"][:, cs] = sl.astype(bf16)
    store("act")
    store("slope")

    @pl.loop(0, D // W)
    def _(n):
        cs = tile(n, W)
        acc = dot(s["act"][...], s["w2"][:, cs]) + par[l, 7:8, cs]
        s["y"][:, cs] = (s["mid"][:, cs] + cols[:, k1 + 1:k1 + 2] * acc).astype(bf16)
    store("y")


SAVED = ("qkv", "lse", "att", "mid", "act", "slope")


def saved_shapes(T, D, FF):
    return [sds((T, 3 * D), bf16), sds((D // LANES, T, 2), f32), sds((T, D), bf16), sds((T, D), f32), sds((T, FF), bf16), sds((T, FF), bf16)]


def first_kernel(names, tokens, segf, keep, *refs):
    vec_in, (wqkv, wo, w1, w2) = refs[:8], refs[8:12]
    o_w = refs[12:16]
    o_par, o_cols, o_y = refs[16:19]
    o_saved = dict(zip(SAVED, refs[19:25]))
    scratch = refs[25:]
    s = dict(zip(names, scratch))
    par, cols, keep_s, seg_s, send, recv, lsem, osem = scratch[len(names):]
    sec = lax.axis_index("section")
    T, D = s["x"].shape
    other = partner()
    greet_partner()
    par[:, 2:3, D:2 * D] = jnp.zeros((2, 1, D), f32)
    small, local = [], []

    def both(src, dst):
        n = len(small)
        small.append(send_copy(src, dst, send.at[n], recv.at[n], other))
        local.append(pltpu.make_async_copy(src, dst, lsem.at[n]))
    both(keep, keep_s.at[sec])
    for row, v in enumerate(vec_in):
        n = v.shape[1]
        if row == 2:
            both(v.at[:, pl.ds(0, D)], par.at[sec, pl.ds(2, 1), pl.ds(0, D)])
            both(v.at[:, pl.ds(D, D)], par.at[sec, pl.ds(2, 1), pl.ds(2 * D, D)])
        else:
            both(v, par.at[sec, pl.ds(row, 1), pl.ds(0, n)])
    for c in small:
        c.start()
    ns = len(small)
    chunks = [(f"wqkv{i}", wqkv.at[0, :, pl.ds(i * D, D)], o_w[0].at[:, pl.ds(i * D, D)], s["wqkv"].at[:, pl.ds(i * D, D)]) for i in range(3)]
    chunks += [(n, w.at[0], o, s[n]) for n, w, o in (("wo", wo, o_w[1]), ("w1", w1, o_w[2]), ("w2", w2, o_w[3]))]
    big = {}
    for i, (n, src, dst, vm) in enumerate(chunks):
        big[n] = send_copy(src, dst, send.at[ns + i], recv.at[ns + i], other)
        big[n].start()
    x_in = fetch(tokens.at[sec], s["x"], lsem.at[ns + 6])
    g_in = fetch(segf, seg_s, lsem.at[ns + 7])
    for c in local:
        c.start()
    loads = {}
    for i, (n, src, dst, vm) in enumerate(chunks):
        loads[n] = (pltpu.make_async_copy(src, vm, lsem.at[ns + i]), pltpu.make_async_copy(dst, vm, lsem.at[ns + i]))

    @pl.when(sec == 0)
    def _():
        for n in loads:
            loads[n][0].start()
    for c in local:
        c.wait()
    for c in small:
        c.wait()
    x_in.wait()
    g_in.wait()

    @pl.loop(0, T // RC)
    def _(i):
        rows = pl.ds(i * RC, RC)
        lane = lanes_of(RC)
        seg = seg_s[rows, :]
        hot = lane.astype(f32) == seg
        out = jnp.where(lane == 0, seg, 0.0)
        for l in range(2):
            for b in range(2):
                flag = jnp.sum(jnp.where(hot, keep_s[l, pl.ds(2 * sec + b, 1), :], 0.0), axis=1, keepdims=True) / keep_rate
                out = jnp.where(lane == 1 + 2 * l + b, flag, out)
        cols[rows, :] = out
    outs = [fetch(par, o_par, osem.at[7]), fetch(cols, o_cols, osem.at[8])]
    o_saved["y"] = o_y
    spots = list(SAVED) + ["y"]

    def arrive(n):
        @pl.when(sec == 1)
        def _():
            big[n].wait_recv()
            loads[n][1].start()

    before = {"wqkv0": ["wqkv0"], "wqkv1": ["wqkv1"], "wqkv2": ["wqkv2"], "wo": ["w1"], "w1": ["w2"], "w2": []}

    def ready(n):
        for a in before[n]:
            arrive(a)
        loads[n][0].wait()
        if n == "wqkv2":
            arrive("wo")

    def store(n):
        outs.append(fetch(s[n], o_saved[n], osem.at[spots.index(n)]))

    forward_body(0, s, cols, par, ready, store)

    @pl.when(sec == 0)
    def _():
        for n in big:
            big[n].wait_recv()
    for n in big:
        big[n].wait_send()
    for c in outs:
        c.wait()


def first_call(tokens, segf, keep, vecs, weights, cid):
    _, T, D = tokens.shape
    FF = weights[2].shape[2]
    sc = layer_scratch(T, D, FF)
    names = tuple(sc)
    ns = 10
    shapes = [sds(w.shape[1:], bf16) for w in weights] + [sds((2, 8, FF), f32), sds((T, LANES), f32), sds((T, D), bf16)] + saved_shapes(T, D, FF)
    return pl.pallas_call(
        functools.partial(first_kernel, names), out_shape=tuple(shapes),
        in_specs=[ANY] * 15, out_specs=(ANY,) * len(shapes),
        scratch_shapes=list(sc.values()) + [
            pltpu.VMEM((2, 8, FF), f32), pltpu.VMEM((T, LANES), f32), pltpu.VMEM((2, 8, LANES), f32), pltpu.VMEM((T, LANES), f32),
            DMA((ns + 6,)), DMA((ns + 6,)), DMA((ns + 8,)), DMA((9,))],
        compiler_params=pltpu.CompilerParams(collective_id=cid, has_side_effects=True, vmem_limit_bytes=LIMIT), name="forward_first",
    )(tokens, segf, keep, *vecs, *weights)


def second_kernel(names, x_hbm, cols_hbm, par_hbm, *refs):
    own, oth = refs[:4], refs[4:8]
    o_out = refs[8]
    o_saved = dict(zip(SAVED, refs[9:15]))
    scratch = refs[15:]
    s = dict(zip(names, scratch))
    par, cols, lsem, osem, esem = scratch[len(names):]
    sec = lax.axis_index("section")
    greet_partner()
    first = [fetch(x_hbm, s["x"], lsem.at[4]), fetch(cols_hbm, cols, lsem.at[5]), fetch(par_hbm, par, lsem.at[6])]
    loads = {n: fetch_layer(sec, 1, own[i].at[0], oth[i], s[n], lsem.at[i]) for i, n in enumerate(("wqkv", "wo", "w1", "w2"))}
    for c in first:
        c.wait()
    outs = []

    def ready(n):
        if n == "wqkv0":
            loads["wqkv"].wait()
        elif n in loads:
            loads[n].wait()

    def store(n):
        if n != "y":
            outs.append(fetch(s[n], o_saved[n], osem.at[SAVED.index(n)]))

    to_other = lambda src: send_copy(src, o_out.at[0, sec], esem.at[0], esem.at[1], partner())
    to_own = lambda src: pltpu.make_async_copy(src, o_out.at[0, sec], esem.at[2])

    forward_body(1, s, cols, par, ready, store)

    @pl.when(sec == 0)
    def _():
        to_own(s["x"]).start()
        to_other(s["y"]).start()

    @pl.when(sec == 1)
    def _():
        to_own(s["y"]).start()
        to_other(s["x"]).start()
    to_own(s["x"]).wait()
    to_other(s["x"]).wait()
    for c in outs:
        c.wait()


def second_call(x, cols, par, own, oth, cid):
    T, D = x.shape
    FF = own[2].shape[2]
    sc = layer_scratch(T, D, FF)
    shapes = [sds((1, 2, T, D), bf16)] + saved_shapes(T, D, FF)
    return pl.pallas_call(
        functools.partial(second_kernel, tuple(sc)), out_shape=tuple(shapes),
        in_specs=[ANY] * 11, out_specs=(ANY,) * len(shapes),
        scratch_shapes=list(sc.values()) + [pltpu.VMEM((2, 8, FF), f32), pltpu.VMEM((T, LANES), f32), DMA((7,)), DMA((6,)), DMA((3,))],
        compiler_params=pltpu.CompilerParams(collective_id=cid, has_side_effects=True, vmem_limit_bytes=LIMIT), name="forward_second",
    )(x, cols, par, *own, *oth)


GRID = (4, 2, 2)
UR, UC = 48, 256
CYCLE = ("xyz", "yxz", "xzy", "yzx", "xyz", "yxz")
RING, INCS, FINS = 12, 4, 4
HOP_US, PACE_US = 10.0, 2.8


class Stream:
    def __init__(self, dims, units):
        self.dims, self.units, self.n = dims, units, len(units)
        self.head = [0, 0, 0, 0]
        self.loaded = 0
        self.limit = 0
        self.due = 0.0
        self.born = {}
        self.seen = set()

    def scratch(self):
        X, Y, Z = self.dims
        size = dict(x=X, y=Y, z=Z)
        parts = []
        for j in range(RING):
            order = CYCLE[j % len(CYCLE)]
            for k, a in enumerate(order):
                rest = tuple(size[b] for b in "zyx" if b in order[k + 1:])
                parts.append(pltpu.VMEM((size[a] - 1,) + rest + (UR, UC), bf16))
        hops = sum(d - 1 for d in self.dims)
        return [pltpu.VMEM((RING,) + GRID + (UR, UC), bf16), pltpu.VMEM((INCS,) + GRID + (UR, UC), bf16), pltpu.VMEM((FINS, UR, UC), f32),
                DMA((RING, hops)), DMA((RING, hops)), DMA((RING, 2)), DMA((FINS, 2)), DMA((self.n, 2))] + parts

    def bind(self, scratch, arrive, outs):
        self.own, self.inc, self.fin, self.send, self.rsem, self.lsem, self.fsend, self.frecv = scratch[:8]
        self.parts = [scratch[8 + 3 * j:11 + 3 * j] for j in range(RING)]
        self.arrive, self.outs = arrive, outs
        X, Y, Z = self.dims
        me = lax.axis_index("dp")
        self.sec = lax.axis_index("section")
        self.size = dict(x=X, y=Y, z=Z)
        self.at = dict(x=me % X, y=(me // X) % Y, z=me // (X * Y))

    def peer(self, axis, t):
        c = dict(self.at)
        c[axis] = t
        X, Y, Z = self.dims
        return {"dp": (c["z"] * Y + c["y"]) * X + c["x"]}

    def greet(self):
        bar = pltpu.get_barrier_semaphore()
        ids = [partner()]
        for a in "xyz":
            ids += [self.peer(a, lax.rem(self.at[a] + j, self.size[a])) for j in range(1, self.size[a])]
        for i in ids:
            pl.semaphore_signal(bar, inc=1, device_id=i, device_id_type=MESH)
        pl.semaphore_wait(bar, len(ids))

    def order(self, u):
        return CYCLE[(u % RING) % len(CYCLE)]

    def loads(self, u):
        mine, recv = self.units[u]["src"]
        return (pltpu.make_async_copy(mine, self.own.at[u % RING], self.lsem.at[u % RING, 0]),
                pltpu.make_async_copy(recv, self.inc.at[u % INCS], self.lsem.at[u % RING, 1]))

    def load(self, u):
        for c in self.loads(u):
            c.start()

    def index(self, order, k, t):
        done = order[:k]
        return tuple(self.at[a] if a in done else (t if a == order[k] else slice(None)) for a in "zyx")

    def hop(self, u, k):
        order = self.order(u)
        a = order[k]
        base = sum(self.size[b] - 1 for b in order[:k])
        j0 = u % RING
        out = []
        for j in range(1, self.size[a]):
            t = lax.rem(self.at[a] + j, self.size[a])
            out.append(send_copy(
                self.own.at[(j0,) + self.index(order, k, t)], self.parts[j0][k].at[j - 1],
                self.send.at[j0, base + j - 1], self.rsem.at[j0, base + j - 1], self.peer(a, t)))
        return out

    def start(self, u):
        for c in self.loads(u):
            c.wait()
        own, inc = self.own.at[u % RING], self.inc.at[u % INCS]

        @pl.loop(0, GRID[0])
        def _(z):
            for y in range(GRID[1]):
                for x in range(GRID[2]):
                    own[z, y, x] = own[z, y, x] + inc[z, y, x]
        for c in self.hop(u, 0):
            c.start()

    def move(self, u, k):
        order = self.order(u)
        for c in self.hop(u, k):
            c.wait()
        own, part = self.own.at[u % RING], self.parts[u % RING][k]
        count = self.size[order[k]] - 1
        free = [b for b in "zyx" if b in order[k + 1:]]

        def add(pos):
            got = dict(zip(free, pos))
            i = tuple(got[b] if b in got else self.at[b] for b in "zyx")
            if count == 1 and k < 2:
                own[i] = own[i] + part[(0,) + tuple(pos)]
                return
            total = own[i].astype(f32)
            for j in range(count):
                total += part[(j,) + tuple(pos)].astype(f32)
            if k < 2:
                own[i] = total.astype(bf16)
            else:
                self.fin[u % FINS] = total
        if k == 2:
            if u >= FINS:
                self.sent(u - FINS)
            add(())
            self.deliver(u)
            return

        @pl.loop(0, self.size[free[0]])
        def _(i):
            if len(free) == 1:
                add((i,))
            else:
                for j in range(self.size[free[1]]):
                    add((i, j))
        for c in self.hop(u, k + 1):
            c.start()

    def results(self, u):
        for i, (out, row, rows, col, cols, c0) in enumerate(self.units[u]["dst"](self.sec)):
            dst = self.outs[out].at[pl.ds(row, rows), pl.ds(pl.multiple_of(col, LANES), cols)]
            src = self.fin.at[u % FINS, :, pl.ds(c0, cols)]
            yield (pltpu.make_async_copy(src, dst, self.fsend.at[u % FINS, i]),
                   send_copy(src, dst, self.fsend.at[u % FINS, i], self.frecv.at[u, i], partner()))

    def by_layer(self, u, same, other):
        @pl.when(self.sec == self.units[u]["layer"])
        def _():
            for near, away in self.results(u):
                same(near, away)

        @pl.when(self.sec != self.units[u]["layer"])
        def _():
            for near, away in self.results(u):
                other(near, away)

    def deliver(self, u):
        self.by_layer(u, lambda near, away: near.start(), lambda near, away: away.start())

    def sent(self, u):
        self.by_layer(u, lambda near, away: near.wait(), lambda near, away: away.wait_send())

    def plan(self, now, limit=None):
        h, calls = self.head, []
        if limit is not None:
            self.limit = max(self.limit, limit)
        drain = now is None
        for k in (2, 1, 0):
            count = 0
            while h[k + 1] < h[k] and (count < 1 if drain else now - self.born[k, h[k + 1]] >= HOP_US):
                u = h[k + 1]
                calls.append(functools.partial(self.move, u, k))
                self.born[k + 1, u] = now
                h[k + 1] += 1
                count += 1
        count = 0
        while h[0] < self.loaded and (drain or now >= self.due) and count < 2:
            u = h[0]
            calls.append(functools.partial(self.start, u))
            self.born[0, u] = now
            h[0] += 1
            count += 1
            if not drain:
                self.due = max(self.due, now - PACE_US) + PACE_US
        while self.loaded < min(self.limit, h[0] + INCS - 1) and (self.loaded < RING or h[3] > self.loaded - RING):
            key = self.units[self.loaded]["need"]
            if key not in self.seen:
                self.seen.add(key)
                calls.append(functools.partial(self.arrive, key))
            calls.append(functools.partial(self.load, self.loaded))
            self.loaded += 1
        return calls

    def tick(self, now, limit=None):
        for c in self.plan(now, limit):
            c()

    def in_loop(self, i, calls):
        for at, todo in enumerate(calls):
            if todo:
                @pl.when(i == at)
                def _(todo=todo):
                    for c in todo:
                        c()

    def finish(self):
        self.limit = self.n
        while self.head[3] < self.n:
            self.tick(None)
        assert self.head == [self.n] * 4
        for u in range(self.n - FINS, self.n):
            self.sent(u)
        for u in range(self.n):
            @pl.when(self.sec == self.units[u]["layer"])
            def _():
                for _n, away in self.results(u):
                    away.wait_recv()


ATTN_SPOTS = (
    ((1, 0, 384, 256, 0),),
    ((1, 256, 640, 128, 0), (0, 0, 896, 128, 128)),
    ((0, 128, 1536, 128, 0), (0, 768, 1664, 128, 128)),
    ((0, 256, 1280, 256, 0),),
    ((0, 512, 1792, 256, 0),),
    ((0, 1024, 2048, 256, 0),),
)
QKV_CUTS = ((0, 0, 0, 256), (0, 256, 768, 256), (0, 512, 1536, 256), (1, 0, 256, 512), (1, 512, 1024, 256), (2, 0, 1280, 256), (2, 256, 1792, 512))


def gradient_units(bufs):
    Z, Y, X = GRID
    units = []
    for l in (1, 0):
        up, down, attn = bufs[l]
        for c in range(6):
            cut = lambda ref: ref.at[:, :, :, :, pl.ds(c * UC, UC)]
            units.append(dict(layer=l, src=tuple(map(cut, up)), need=(l, "up", c // 3),
                              dst=lambda sec, c=c: [(2, 0, UR, sec * 6 * UC + c * UC, UC, 0)]))
        for g in range(2):
            for c in range(3):
                cut = lambda ref: ref.at[:, g, :, :, :, pl.ds(c * UC, UC)]
                units.append(dict(layer=l, src=tuple(map(cut, down)), need=(l, "down", 0),
                                  dst=lambda sec, c=c, g=g: [(3, pl.multiple_of(sec * 2 * UR + g * UR, 16), UR, c * UC, UC, 0)]))
        for c, spots in enumerate(ATTN_SPOTS):
            cut = lambda ref: ref.at[:, :, :, :, pl.ds(c * UC, UC)]
            units.append(dict(layer=l, src=tuple(map(cut, attn)), need=(l, "attn", c // 3),
                              dst=lambda sec, spots=spots: [(out, 0, UR, a + sec * (b - a), n, c0) for out, a, b, n, c0 in spots]))
    return units


LAYER_US = 56.5
TIMES = dict(norm=1.6, tile=(4.0, 6.4, 8.6, 11.0, 13.2, 15.6, 17.8, 20.2), gs=(20.9, 21.7, 22.5), mid=24.2, gb=26.1, ga=27.3, dwo=28.8,
             pairs=(31.4, 34.0, 38.4, 41.1, 43.8, 46.5), early=35.7, dqkv=(47.5, 48.5), gn=(49.6, 50.7, 51.8), end=53.6)


def backward_kernel(dims, names, cot, tokens, y0, cols_h, par_h, *refs):
    saved = [dict(zip(SAVED, refs[:6])), dict(zip(SAVED, refs[6:12]))]
    own = dict(zip(("wqkv", "wo", "w1", "w2"), refs[12:16]))
    oth = dict(zip(("wqkv", "wo", "w1", "w2"), refs[16:20]))
    refs = refs[20:]
    o_gin, refs = refs[0], refs[1:]
    bufs = {}
    for l in (1, 0):
        bufs[l], refs = ((refs[0], refs[1]), (refs[2], refs[3]), (refs[4], refs[5])), refs[6:]
    if dims:
        o_big, o_vec, refs = refs[:4], refs[4:12], refs[12:]
    else:
        o_vec, refs = refs[0], refs[1:]
    s = dict(zip(names, refs))
    lsem, csend, crecv, cnear, esem, vsend, vrecv = refs[len(names):len(names) + 7]
    st_refs = refs[len(names) + 7:]
    g, mid, gs, gmid, act, slope, w1, w2, gd, tr, gh, x, att, att_t, ga, feat, lse, cols, par, vec, stage = (s[n] for n in names[:21])
    sec = lax.axis_index("section")
    me = lax.axis_index("dp")
    T, D = g.shape
    FF = act.shape[1]
    Z, Y, X = GRID
    tiles, half = FF // D, FF // D // 2

    ld = {}
    W2 = ("w2", "w2b", "w2c", "w2d")
    CUTS = tuple(f"c{i}" for i in range(len(QKV_CUTS)))

    def get(n, src, dst):
        keys = tuple(names) + W2[1:] + CUTS
        ld[n] = fetch(src, dst, lsem.at[keys.index(n)])

    def get_w(n, layer, name, src_of, dst):
        keys = tuple(names) + W2[1:] + CUTS
        ld[n] = fetch_layer(sec, layer, src_of(own[name].at[0]), src_of(oth[name]), dst, lsem.at[keys.index(n)])

    def need(*ns):
        for n in ns:
            ld.pop(n).wait()

    def load_w2(l):
        for i, n in enumerate(W2):
            get_w(n, l, "w2", lambda r, i=i: r.at[pl.ds(i * D, D), :], w2.at[pl.ds(i * D, D), :])

    def load_attn_weights(l):
        for n, (block, col, src, cols_n) in zip(CUTS, QKV_CUTS):
            get_w(n, l, "wqkv", lambda r, src=src, cols_n=cols_n: r.at[:, pl.ds(src, cols_n)], w2.at[pl.ds(block * D, D), pl.ds(col, cols_n)])
        get_w(W2[3], l, "wo", lambda r: r, w2.at[pl.ds(3 * D, D), :])

    def up_copy(l, i):
        buf = stage.at[lax.rem(i, 2), :, :, :, :, pl.ds(0, D)]
        t = i // 2
        mine, recv = (r.at[:, :, :, :, tile(t, D)] for r in bufs[l][0])
        return (send_copy(buf, recv, csend.at[l, t], crecv.at[l, t], partner()), pltpu.make_async_copy(buf, mine, cnear.at[l, t]))

    def down_copy(l, i, n):
        mine, recv = (r.at[n] for r in bufs[l][1])
        buf = lambda h: stage.at[lax.rem(i, 2), pl.ds(2 * h, 2), :, :, :, pl.ds(D, D)]
        return (send_copy(buf(1 - sec), recv, csend.at[l, 2 + i], crecv.at[l, 2 + i], partner()),
                pltpu.make_async_copy(buf(sec), mine, cnear.at[l, 2 + i]))

    def attn_copy(l, part):
        mine, recv = (r.at[:, :, :, :, pl.ds(part * D, D)] for r in bufs[l][2])
        buf = lambda h: stage.at[h, :, :, :, :, pl.ds(part * D, D)]
        return (send_copy(buf(1 - sec), recv, csend.at[l, 6 + part], crecv.at[l, 6 + part], partner()),
                pltpu.make_async_copy(buf(sec), mine, cnear.at[l, 6 + part]))

    def arrive(key):
        l, kind, t = key
        if kind == "up":
            up_copy(l, 2 * t)[0].wait_recv()
            up_copy(l, 2 * t + 1)[1].wait()
        elif kind == "down":
            for i in range(tiles):
                down_copy(l, i, i)[0].wait_recv()
        else:
            attn_copy(l, t)[0].wait_recv()

    get("g", cot.at[sec], g)
    get("cols", cols_h, cols)
    get("par", par_h, par)
    get("mid", saved[1]["mid"], mid)
    load_w2(1)
    get("slope", saved[1]["slope"], slope)
    get("act", saved[1]["act"], act)
    get_w("w1", 1, "w1", lambda r: r, w1)
    get("x", y0, x)
    get("att", saved[1]["att"], att)
    get("lse", saved[1]["lse"], lse)
    if dims:
        st = Stream(dims, gradient_units(bufs))
        st.bind(st_refs, arrive, o_big)
        st.greet()
    else:
        st = None
        greet_partner()
    need("cols", "par")
    vec[...] = jnp.zeros_like(vec)

    @pl.loop(0, T // RC)
    def _(i):
        rows = pl.ds(i * RC, RC)
        for odd in (0, 1):
            qf, kf = seg_feature(cols[rows, 0:1], RC, odd)
            feat[2 * odd, rows, :] = qf
            feat[2 * odd + 1, rows, :] = kf

    start_us = 4.0

    def tick(spot, limit):
        if st:
            st.tick(start_us + (1 - l) * LAYER_US + TIMES[spot], limit + (1 - l) * 18)

    def loop_plan(*spots):
        table = [[] for _ in spots]
        for i in range(len(spots[0][0])):
            for calls, (times, limits) in zip(table, spots):
                now = start_us + (1 - l) * LAYER_US + times[i]
                calls.append(st.plan(now, limits[i] + (1 - l) * 18) if st else [])
        return table

    def loop_tick(i, calls):
        if st:
            st.in_loop(i, calls)

    down_row = 7 + FF // D
    low_lane = own_lanes(T, 0)
    for l in (1, 0):
        k1, k2 = 1 + 2 * l, 2 + 2 * l
        need(*(("g",) if l == 1 else ()), "mid")

        @pl.loop(0, T // RC)
        def _(i):
            rows = pl.ds(i * RC, RC)
            low = (g[rows, :].astype(f32) * cols[rows, k2:k2 + 1]).astype(bf16)
            gd[rows, :] = low
            vec[l, down_row:down_row + 1, :] += jnp.sum(low.astype(f32), axis=0, keepdims=True)
            unit, _s = layer_unit(mid[rows, :])
            tr[:, rows] = (unit * par[l, 4:5, :D] + par[l, 5:6, :D]).astype(bf16).T
        if l == 0:
            attn_copy(1, 0)[0].wait_send()
            attn_copy(1, 1)[0].wait_send()
        tick("norm", 0)
        need(*W2, "slope", "act")
        early, late = loop_plan((TIMES["tile"][0::2], (0, 0, 3, 3)), (TIMES["tile"][1::2], (0, 3, 3, 6)))

        @pl.loop(0, tiles)
        def _(i):
            mine = lax.rem(i, 2)
            n = lax.rem(sec + 1 + mine, 2) * half + i // 2
            cs = tile(n, D)
            low = (dot(gd[...], w2[cs, :], NT) * slope[:, cs].astype(f32)).astype(bf16)
            gh[:, cs] = low
            vec[l, pl.ds(7 + n, 1), :] = jnp.sum(low.astype(f32), axis=0, keepdims=True)

            @pl.when(i == 2)
            def _():
                up_copy(l, 0)[0].wait_send()

            @pl.when(i >= 2)
            def _():
                a, b = down_copy(l, i - 2, n)
                a.wait_send()
                b.wait()
            d1 = dot(tr[...], low).astype(bf16)
            stage[mine, :, :, :, :, 0:D] = d1.reshape(Z, Y, X, UR, D)
            away, near = up_copy(l, i)

            @pl.when(mine == 0)
            def _():
                away.start()

            @pl.when(mine == 1)
            def _():
                near.start()
            loop_tick(i, early)
            d2 = dot(act[:, cs], gd[...], TN).astype(bf16).reshape(Y, X, 4, UR, D)
            for q in range(4):
                stage[mine, q, :, :, :, D:2 * D] = d2[:, :, q]
            for c in down_copy(l, i, n):
                c.start()
            loop_tick(i, late)
        load_attn_weights(l)
        get("qkv", saved[l]["qkv"], slope.at[:, pl.ds(0, 3 * D)])
        if l == 1:
            get("act", saved[0]["act"], act)
        need("w1")
        calls, = loop_plan((TIMES["gs"], (6, 6, 6)))

        @pl.loop(0, D // W)
        def _(n):
            cs = tile(n, W)
            gs[:, cs] = dot(gh[...], w1[cs, :], NT)
            loop_tick(n, calls)
        if l == 1:
            get_w("w1", 0, "w1", lambda r: r, w1)
        up_copy(l, 2)[0].wait_send()
        for i in (2, 3):
            a, b = down_copy(l, i, i)
            a.wait_send()
            b.wait()

        @pl.loop(0, T // RC)
        def _(i):
            rows = pl.ds(i * RC, RC)
            unit, scale = layer_unit(mid[rows, :])
            low = gs[rows, :]
            vec[l, 5:6, :] += jnp.sum(low * unit, axis=0, keepdims=True)
            vec[l, 6:7, :] += jnp.sum(low, axis=0, keepdims=True)
            gmid[rows, :] = g[rows, :].astype(f32) + unit_back(low, unit, scale, par[l, 4:5, :D])
        tick("mid", 12)
        if l == 1:
            get("mid", saved[0]["mid"], mid)
        need("x", "att")

        @pl.loop(0, T // RC)
        def _(i):
            rows = pl.ds(i * RC, RC)
            low = (gmid[rows, :] * cols[rows, k1:k1 + 1]).astype(bf16)
            gd[rows, :] = low
            vec[l, 4:5, :] += jnp.sum(low.astype(f32), axis=0, keepdims=True)
            unit, _s = layer_unit(x[rows, :].astype(f32))
            tr[:, rows] = (unit * par[l, 0:1, :D] + par[l, 1:2, :D]).astype(bf16).T
            att_t[:, rows] = att[rows, :].T
        tick("gb", 12)
        need(W2[3])

        @pl.loop(0, D // W)
        def _(n):
            cs = tile(n, W)
            ga[:, cs] = dot(gd[...], w2[pl.ds(pl.multiple_of(3 * D + n * W, W), W), :], NT).astype(bf16)
        tick("ga", 12)
        if st:
            assert {(l, "up", 0), (l, "up", 1)} <= st.seen
        else:
            arrive((l, "up", 0))
            arrive((l, "up", 1))

        @pl.loop(0, 2)
        def _(h):
            stage[h, :, :, :, :, 0:D // 2] = dot(att_t[...], gd[:, tile(h, D // 2)]).astype(bf16).reshape(Z, Y, X, UR, D // 2)
        tick("dwo", 12)
        need("qkv", "lse")

        def pair(p, spots):
            off = pl.multiple_of(p * LANES, LANES)
            qp = slope[:, pl.ds(off, LANES)]
            kp = slope[:, pl.ds(off + D, LANES)]
            vp = slope[:, pl.ds(off + 2 * D, LANES)]
            gp = ga[:, pl.ds(off, LANES)]
            prod = gp.astype(f32) * att[:, pl.ds(off, LANES)].astype(f32)
            dq, dk, dv = [], [], []
            for odd in (0, 1):
                own_l = own_lanes(T, odd)
                base = feature_base(odd)
                lane = lanes_of(T)
                row_d = jnp.sum(jnp.where(own_l, prod, 0.0), axis=1, keepdims=True)
                l3 = split3(-lse[p, :, odd:odd + 1])
                d3 = split3(-row_d)
                qf = feat[2 * odd]
                gf = jnp.zeros_like(gp)
                for j in range(3):
                    qf = jnp.where(lane == base + 8 + j, l3[j], qf)
                    gf = jnp.where(lane == base + j, d3[j], gf)
                q = jnp.where(own_l, qp, qf)
                k = jnp.where(own_l, kp, feat[2 * odd + 1])
                v = jnp.where(own_l, vp, jnp.ones_like(vp))
                gg = jnp.where(own_l, gp, gf)
                prob = jnp.exp(dot(k, q, NT))
                gsc = (prob * dot(v, gg, NT)).astype(bf16)
                dv.append(dot(prob.astype(bf16), gg))
                dk.append(dot(gsc, q))
                dq.append(dot(gsc, k, TN))
            for at, val in zip(spots, ((jnp.where(low_lane, dq[0], dq[1]) * 0.125), jnp.where(low_lane, dk[0], dk[1]), jnp.where(low_lane, dv[0], dv[1]))):
                gh[:, tile(at + p, LANES)] = val.astype(bf16)

        def gradient(part, width, base):
            calls, = loop_plan((TIMES["dqkv"], (15, 15))) if part else (None,)

            @pl.loop(0, 2)
            def _(i):
                h = lax.rem(i + 1 + sec, 2)
                cs = pl.ds(pl.multiple_of(base + h * width, LANES), width)
                stage[h, :, :, :, :, (part + 1) * D - width:(part + 1) * D] = dot(tr[...], gh[:, cs]).astype(bf16).reshape(Z, Y, X, UR, width)
                away, near = attn_copy(l, part)

                @pl.when(i == 0)
                def _():
                    away.start()

                @pl.when(i == 1)
                def _():
                    near.start()
                if part == 1:
                    loop_tick(i, calls)

        calls, = loop_plan((TIMES["pairs"][:2], (12, 12)))

        @pl.loop(0, 2)
        def _(p):
            pair(p, (0, 2, 4))
            loop_tick(p, calls)
        gradient(0, D // 2, 0)
        attn_copy(l, 0)[1].wait()
        tick("early", 12)

        calls, = loop_plan((TIMES["pairs"][2:], (15,) * 4))

        @pl.loop(2, D // LANES)
        def _(p):
            pair(p, (4, 8, 12))
            loop_tick(p - 2, calls)
        if l == 1:
            get("slope", saved[0]["slope"], slope)
            get("att", saved[0]["att"], att)
            get("lse", saved[0]["lse"], lse)
        gradient(1, D, D)
        attn_copy(l, 1)[1].wait()
        for row, to, at, n in ((2, 0, 0, 256), (2, 256, 768, 512), (3, 0, 512, 256), (3, 256, 1792, 512)):
            vec[l, row:row + 1, to:to + n] = jnp.sum(gh[:, at:at + n].astype(f32), axis=0, keepdims=True)

        need(*CUTS)
        calls, = loop_plan((TIMES["gn"], (18, 18, 18)))

        @pl.loop(0, D // W)
        def _(n):
            cs = tile(n, W)
            acc = jnp.zeros((T, W), f32)
            for c in range(3):
                acc += dot(gh[:, c * D:(c + 1) * D], w2[pl.ds(pl.multiple_of(c * D + n * W, W), W), :], NT)
            gs[:, cs] = acc
            loop_tick(n, calls)
        if l == 1:
            load_w2(0)

        @pl.loop(0, T // RC)
        def _(i):
            rows = pl.ds(i * RC, RC)
            unit, scale = layer_unit(x[rows, :].astype(f32))
            low = gs[rows, :]
            vec[l, 0:1, :] += jnp.sum(low * unit, axis=0, keepdims=True)
            vec[l, 1:2, :] += jnp.sum(low, axis=0, keepdims=True)
            res = (gmid[rows, :] + unit_back(low, unit, scale, par[l, 0:1, :D])).astype(bf16)
            if l == 1:
                g[rows, :] = res
            else:
                x[rows, :] = res
        if l == 1:
            get("x", tokens.at[sec], x)
        tick("end", 18)

    to_other = lambda src: send_copy(src, o_gin.at[0, sec], esem.at[0], esem.at[1], partner())
    to_own = lambda src: pltpu.make_async_copy(src, o_gin.at[0, sec], esem.at[2])

    @pl.when(sec == 0)
    def _():
        to_own(x).start()
        to_other(g).start()

    @pl.when(sec == 1)
    def _():
        to_own(g).start()
        to_other(x).start()
    if st:
        vown, vgot = s["vown"], s["vgot"]
        hops = [("s", None)] + [(a, j) for a in "xyz" for j in range(1, st.size[a])]

        def hop(n):
            a, j = hops[n]
            if a == "s":
                return send_copy(vec.at[1 - sec], vgot.at[0], vsend.at[0], vrecv.at[0], partner())
            return send_copy(vown.at["xyz".index(a)], vgot.at[n], vsend.at[n], vrecv.at[n], st.peer(a, lax.rem(st.at[a] + j, st.size[a])))
        hop(0).start()
        st.tick(None)
        hop(0).wait()
        vown[0] = vec[sec] + vgot[0]
        n = 1
        for k, a in enumerate("xyz"):
            ids = range(n, n + st.size[a] - 1)
            for i in ids:
                hop(i).start()
            st.tick(None)
            for i in ids:
                hop(i).wait()
            total = vown[k]
            for i in ids:
                total += vgot[i]
            n += len(ids)
            vown[k + 1] = total
        n_dp = dims[0] * dims[1] * dims[2]
        for o, (row, width) in zip(o_vec, small_spots(D, FF)):
            size = width // n_dp
            at = me * size
            line = vown[3, pl.ds(row + at // D, 1), :]
            line = pltpu.roll(jnp.broadcast_to(line, (8, D)), lax.rem(D - at % D, D), 1)
            o[...] = line[0:1, :size]
        st.finish()
    else:
        for l in (1, 0):
            arrive((l, "down", 0))
            arrive((l, "attn", 0))
            arrive((l, "attn", 1))
        c = pltpu.make_async_copy(vec, o_vec, vsend.at[0])
        c.start()
        c.wait()
    attn_copy(0, 0)[0].wait_send()
    attn_copy(0, 1)[0].wait_send()
    to_own(x).wait()
    to_other(x).wait()


def small_spots(D, FF):
    return ((0, D), (1, D), (2, 2 * D), (4, D), (5, D), (6, D), (7, FF), (7 + FF // D, D))


def backward_call(dims, n_dp, cot, tokens, y0, cols, par, saved0, saved1, own, oth, cid):
    T, D = y0.shape
    FF = own[2].shape[2]
    V = pltpu.VMEM
    sc = dict(
        g=V((T, D), bf16), mid=V((T, D), f32), gs=V((T, D), f32), gmid=V((T, D), f32), act=V((T, FF), bf16), slope=V((T, FF), bf16),
        w1=V((D, FF), bf16), w2=V((FF, D), bf16), gd=V((T, D), bf16), tr=V((D, T), bf16), gh=V((T, FF), bf16), x=V((T, D), bf16), att=V((T, D), bf16),
        att_t=V((D, T), bf16), ga=V((T, D), bf16), feat=V((4, T, LANES), bf16), lse=V((D // LANES, T, 2), f32), cols=V((T, LANES), f32),
        par=V((2, 8, FF), f32), vec=V((2, 16, D), f32), stage=V((2,) + GRID + (UR, 2 * D), bf16))
    sc["qkv"] = V((8, LANES), f32)
    hops = 1 + (sum(d - 1 for d in dims) if dims else 0)
    if dims:
        sc.update(vown=V((4, 16, D), f32), vgot=V((hops, 16, D), f32))
    wide = sds(GRID + (UR, 2 * D), bf16)
    tall = sds((GRID[0], 2) + GRID[1:] + (UR, D), bf16)
    shapes = [sds((1, 2, T, D), bf16)] + [wide, wide, tall, tall, wide, wide] * 2
    specs = [ANY] * len(shapes)
    if dims:
        shapes += [sds((D // n_dp, 3 * D), f32), sds((D // n_dp, D), f32), sds((D // n_dp, FF), f32), sds((FF // n_dp, D), f32)]
        shapes += [sds((1, w // n_dp), f32) for _, w in small_spots(D, FF)]
        specs += [ANY] * 4 + [pl.BlockSpec(memory_space=pltpu.VMEM)] * 8
        stream = Stream(dims, [None] * 36).scratch()
    else:
        shapes += [sds((2, 16, D), f32)]
        specs += [ANY]
        stream = []
    scratch = list(sc.values()) + [DMA((len(sc) + 3 + len(QKV_CUTS),)), DMA((2, 8)), DMA((2, 8)), DMA((2, 8)), DMA((3,)), DMA((hops,)), DMA((hops,))] + stream
    return pl.pallas_call(
        functools.partial(backward_kernel, dims, tuple(sc)), out_shape=tuple(shapes),
        in_specs=[ANY] * 25, out_specs=tuple(specs), scratch_shapes=scratch,
        compiler_params=pltpu.CompilerParams(collective_id=cid, has_side_effects=True, vmem_limit_bytes=LIMIT), name="backward",
    )(cot, tokens, y0, cols, par, *saved0, *saved1, *own, *oth)


def copy_kernel(n, *refs):
    sem = refs[2 * n]
    copies = [pltpu.make_async_copy(refs[i], refs[n + i], sem.at[i]) for i in range(n)]
    for c in copies:
        c.start()
    for c in copies:
        c.wait()


def copy_call(arrays):
    n = len(arrays)
    return pl.pallas_call(
        functools.partial(copy_kernel, n), out_shape=tuple(sds(a.shape, a.dtype) for a in arrays),
        in_specs=[ANY] * n, out_specs=(ANY,) * n, scratch_shapes=[DMA((n,))], name="place_outputs",
    )(*arrays)


def dp_dims(n):
    return {16: (2, 2, 4)}.get(n)


def shards(
    tokens, segment_ids, keep_masks, cotangent,
    norm1_gain, norm1_bias, qkv_weight, qv_bias, out_weight, out_bias,
    norm2_gain, norm2_bias, fc1_weight, fc1_bias, fc2_weight, fc2_bias,
):
    sec = lax.axis_index("section")
    n_dp = lax.axis_size("dp")
    dims = dp_dims(n_dp)
    T, D = tokens.shape[1:]
    FF = fc1_weight.shape[2]
    seg = lax.dynamic_index_in_dim(segment_ids, sec, 0, keepdims=False)
    segf = jnp.broadcast_to(seg.astype(f32)[:, None], (T, LANES))
    keep = jnp.pad(keep_masks[0].astype(f32).reshape(4, -1), ((0, 4), (0, LANES - keep_masks.shape[3])))
    own = (qkv_weight, out_weight, fc1_weight, fc2_weight)
    vecs = (norm1_gain, norm1_bias, qv_bias, out_bias, norm2_gain, norm2_bias, fc1_bias, fc2_bias)
    res = first_call(tokens, segf, keep, vecs, own, 0)
    oth, par, cols, y0, saved0 = res[:4], res[4], res[5], res[6], res[7:]
    res = second_call(y0, cols, par, own, oth, 1)
    layer_out, saved1 = res[0], res[1:]
    res = backward_call(dims, n_dp, cotangent, tokens, y0, cols, par, saved0, saved1, own, oth, 2)
    input_grad = res[0]
    if dims:
        layer_out, input_grad, dqkv, dwo, dw1, dw2, n1g, n1b, qv, ob, n2g, n2b, b1, b2 = copy_call((layer_out, input_grad) + tuple(res[13:25]))
    else:
        sums = {}
        for i, l in enumerate((1, 0)):
            up, down, attn = (res[1 + 6 * i + 2 * j].astype(f32) + res[2 + 6 * i + 2 * j].astype(f32) for j in range(3))
            up, attn = up.reshape(D, -1), attn.reshape(D, -1)
            down = lax.all_gather(down, "section")
            down = down.transpose(1, 3, 4, 0, 2, 5, 6).reshape(FF, D)
            sums[l] = [lax.psum_scatter(a, "dp", scatter_dimension=0, tiled=True) for a in (attn, up, down)]
        attn, up, down = (jnp.stack([sums[0][i], sums[1][i]]) for i in range(3))
        attn, up = (lax.dynamic_index_in_dim(lax.all_gather(a, "section"), sec, 1, keepdims=False) for a in (attn, up))
        dw2 = lax.dynamic_index_in_dim(down, sec, 0, keepdims=False)
        dw1 = jnp.concatenate([up[0], up[1]], axis=1)
        cuts = {}
        for c, spots in enumerate(ATTN_SPOTS):
            for out, a, b, n, c0 in spots:
                for h, col in ((0, a), (1, b)):
                    cuts[out, col] = attn[h, :, c * UC + c0:c * UC + c0 + n]
        dqkv, dwo = (jnp.concatenate([cuts[k] for k in sorted(cuts) if k[0] == out], axis=1) for out in (0, 1))
        v = lax.dynamic_index_in_dim(lax.psum(res[13], ("section", "dp")), sec, 0, keepdims=False)
        at = lax.axis_index("dp")
        n1g, n1b, qv, ob, n2g, n2b, b1, b2 = (
            lax.dynamic_slice_in_dim(v[row:row + -(-w // D)].reshape(-1), at * (w // n_dp), w // n_dp)[None] for row, w in small_spots(D, FF))
    return (layer_out, input_grad, n1g, n1b, dqkv[None], qv, dwo[None], ob, n2g, n2b, dw1[None], b1, dw2[None], b2)


def solution(mesh):
    in_specs = (
        P(None, "dp", None), P(None, "dp"), P("section", None, None, "dp"), P(None, "dp", None),
        P("section", None), P("section", None), P("section", None, None), P("section", None),
        P("section", None, None), P("section", None), P("section", None), P("section", None),
        P("section", None, None), P("section", None), P("section", None, None), P("section", None),
    )
    out_specs = (
        P("section", None, "dp", None), P("section", None, "dp", None),
        P("section", "dp"), P("section", "dp"), P("section", "dp", None), P("section", "dp"),
        P("section", "dp", None), P("section", "dp"), P("section", "dp"), P("section", "dp"),
        P("section", "dp", None), P("section", "dp"), P("section", "dp", None), P("section", "dp"),
    )
    return jax.shard_map(shards, mesh=mesh, in_specs=in_specs, out_specs=out_specs, check_vma=False)
```

```python
import functools
import jax
import jax.numpy as jnp
from jax import lax
from jax.experimental import pallas as pl
from jax.experimental.pallas import tpu as pltpu
from jax.sharding import PartitionSpec as P

HEAD_DIM = 64
LANES = 128
keep_rate = 0.9
norm_eps = 1e-06
root_half = 0.7071067811865476
inverse_root = 0.3989422804014327
BIG = 2.0**30
f32, bf16 = jnp.float32, jnp.bfloat16
NN = (((1,), (0,)), ((), ()))
NT = (((1,), (1,)), ((), ()))
TN = (((0,), (0,)), ((), ()))
MESH = pl.DeviceIdType.MESH
ANY = pl.BlockSpec(memory_space=pl.ANY)
DMA = pltpu.SemaphoreType.DMA
LIMIT = 61 * 2**20
RC = 128
W = 256
sds = jax.ShapeDtypeStruct


def dot(a, b, dims=NN):
    return lax.dot_general(a, b, dims, preferred_element_type=f32)


def layer_unit(x):
    center = x - jnp.mean(x, axis=-1, keepdims=True)
    scale = lax.rsqrt(jnp.mean(center * center, axis=-1, keepdims=True) + norm_eps)
    return center * scale, scale


def unit_back(grad, unit, scale, gain):
    scaled = grad * gain
    inner = jnp.mean(scaled, axis=-1, keepdims=True)
    along = jnp.mean(scaled * unit, axis=-1, keepdims=True)
    return scale * (scaled - inner - unit * along)


def gelu_pair(h):
    phi = 0.5 * (1.0 + lax.erf(h * root_half))
    return h * phi, phi + h * jnp.exp(-0.5 * h * h) * inverse_root


def split3(v):
    a = v.astype(bf16)
    r = v - a.astype(f32)
    b = r.astype(bf16)
    c = (r - b.astype(f32)).astype(bf16)
    return a, b, c


def feature_base(odd):
    return 0 if odd else HEAD_DIM


def lanes_of(rows):
    return lax.broadcasted_iota(jnp.int32, (rows, LANES), 1)


def seg_feature(seg, rows, odd):
    base = feature_base(odd)
    lane = lanes_of(rows)
    inside = (lane >= base) & (lane < base + 8)
    same = (lane - base).astype(f32) == seg
    qf = jnp.where(inside & same, BIG, 0.0)
    kf = jnp.where(inside & jnp.logical_not(same), -1.0, 0.0)
    kf = jnp.where((lane >= base + 8) & (lane < base + 11), 1.0, kf)
    return qf.astype(bf16), kf.astype(bf16)


def own_lanes(rows, odd):
    lane = lanes_of(rows)
    return (lane >= HEAD_DIM) if odd else (lane < HEAD_DIM)


def tile(n, width):
    return pl.ds(pl.multiple_of(n * width, LANES), width)


def fetch(src, dst, sem):
    c = pltpu.make_async_copy(src, dst, sem)
    c.start()
    return c


def fetch_layer(sec, layer, own, other, dst, sem):
    c = pltpu.make_async_copy(own, dst, sem)

    @pl.when(sec == layer)
    def _():
        c.start()

    @pl.when(sec != layer)
    def _():
        pltpu.make_async_copy(other, dst, sem).start()
    return c


def partner():
    return {"section": 1 - lax.axis_index("section")}


def greet_partner():
    bar = pltpu.get_barrier_semaphore()
    pl.semaphore_signal(bar, inc=1, device_id=partner(), device_id_type=MESH)
    pl.semaphore_wait(bar, 1)


def send_copy(src, dst, send, recv, dev):
    return pltpu.make_async_remote_copy(src, dst, send, recv, device_id=dev, device_id_type=MESH)


def layer_scratch(T, D, FF):
    return dict(
        x=pltpu.VMEM((T, D), bf16), wqkv=pltpu.VMEM((D, 3 * D), bf16), wo=pltpu.VMEM((D, D), bf16),
        w1=pltpu.VMEM((D, FF), bf16), w2=pltpu.VMEM((FF, D), bf16),
        norm=pltpu.VMEM((T, D), bf16), second=pltpu.VMEM((T, D), bf16), feat=pltpu.VMEM((4, T, LANES), bf16),
        qkv=pltpu.VMEM((T, 3 * D), bf16), lse=pltpu.VMEM((D // LANES, T, 2), f32), att=pltpu.VMEM((T, D), bf16),
        mid=pltpu.VMEM((T, D), f32), act=pltpu.VMEM((T, FF), bf16), slope=pltpu.VMEM((T, FF), bf16),
        y=pltpu.VMEM((T, D), bf16),
    )


def forward_body(l, s, cols, par, ready, store):
    T, D = s["x"].shape
    FF = s["act"].shape[1]
    k1 = 1 + 2 * l

    @pl.loop(0, T // RC)
    def _(i):
        rows = pl.ds(i * RC, RC)
        unit, _s = layer_unit(s["x"][rows, :].astype(f32))
        s["norm"][rows, :] = (unit * par[l, 0:1, :D] + par[l, 1:2, :D]).astype(bf16)
        for odd in (0, 1):
            qf, kf = seg_feature(cols[rows, 0:1], RC, odd)
            s["feat"][2 * odd, rows, :] = qf
            s["feat"][2 * odd + 1, rows, :] = kf

    for part in range(3):
        ready(f"wqkv{part}")

        @pl.loop(0, D // W)
        def _(n):
            cs = pl.ds(pl.multiple_of(part * D + n * W, W), W)
            acc = dot(s["norm"][...], s["wqkv"][:, cs]) + par[l, 2:3, cs]
            s["qkv"][:, cs] = (acc * 0.125 if part == 0 else acc).astype(bf16)
    store("qkv")

    def one_pair(p):
        off = pl.multiple_of(p * LANES, LANES)
        qp = s["qkv"][:, pl.ds(off, LANES)]
        kp = s["qkv"][:, pl.ds(off + D, LANES)]
        vp = s["qkv"][:, pl.ds(off + 2 * D, LANES)]
        outs, scs, vs = [], [], []
        for odd in (0, 1):
            own = own_lanes(T, odd)
            q = jnp.where(own, qp, s["feat"][2 * odd])
            k = jnp.where(own, kp, s["feat"][2 * odd + 1])
            vs.append(jnp.where(own, vp, jnp.ones_like(vp)))
            scs.append(dot(q, k, NT))
        ms = [jnp.max(sc, axis=1, keepdims=True) for sc in scs]
        es = [jnp.exp(sc - m).astype(bf16) for sc, m in zip(scs, ms)]
        for odd in (0, 1):
            base = feature_base(odd)
            o = dot(es[odd], vs[odd])
            total = o[:, base:base + 1]
            outs.append(o / total)
            s["lse"][p, :, odd:odd + 1] = ms[odd] + jnp.log(total)
        s["att"][:, pl.ds(off, LANES)] = jnp.where(own_lanes(T, 0), outs[0], outs[1]).astype(bf16)

    @pl.loop(0, D // LANES // 2)
    def _(pp):
        one_pair(2 * pp)
        one_pair(2 * pp + 1)
    store("lse")
    store("att")
    ready("wo")

    @pl.loop(0, D // W)
    def _(n):
        cs = tile(n, W)
        acc = dot(s["att"][...], s["wo"][:, cs]) + par[l, 3:4, cs]
        s["mid"][:, cs] = s["x"][:, cs].astype(f32) + cols[:, k1:k1 + 1] * acc
    store("mid")

    @pl.loop(0, T // RC)
    def _(i):
        rows = pl.ds(i * RC, RC)
        unit, _s = layer_unit(s["mid"][rows, :])
        s["second"][rows, :] = (unit * par[l, 4:5, :D] + par[l, 5:6, :D]).astype(bf16)
    ready("w1")

    ready("w2")

    @pl.loop(0, FF // D)
    def _(n):
        cs = tile(n, D)
        a, sl = gelu_pair(dot(s["second"][...], s["w1"][:, cs]) + par[l, 6:7, cs])
        s["act"][:, cs] = a.astype(bf16)
        s["slope"][:, cs] = sl.astype(bf16)
    store("act")
    store("slope")

    @pl.loop(0, D // W)
    def _(n):
        cs = tile(n, W)
        acc = dot(s["act"][...], s["w2"][:, cs]) + par[l, 7:8, cs]
        s["y"][:, cs] = (s["mid"][:, cs] + cols[:, k1 + 1:k1 + 2] * acc).astype(bf16)
    store("y")


SAVED = ("qkv", "lse", "att", "mid", "act", "slope")


def saved_shapes(T, D, FF):
    return [sds((T, 3 * D), bf16), sds((D // LANES, T, 2), f32), sds((T, D), bf16), sds((T, D), f32), sds((T, FF), bf16), sds((T, FF), bf16)]


def first_kernel(names, tokens, segf, keep, *refs):
    vec_in, (wqkv, wo, w1, w2) = refs[:8], refs[8:12]
    o_w = refs[12:16]
    o_par, o_cols, o_y = refs[16:19]
    o_saved = dict(zip(SAVED, refs[19:25]))
    scratch = refs[25:]
    s = dict(zip(names, scratch))
    par, cols, keep_s, seg_s, send, recv, lsem, osem = scratch[len(names):]
    sec = lax.axis_index("section")
    T, D = s["x"].shape
    other = partner()
    greet_partner()
    par[:, 2:3, D:2 * D] = jnp.zeros((2, 1, D), f32)
    small, local = [], []

    def both(src, dst):
        n = len(small)
        small.append(send_copy(src, dst, send.at[n], recv.at[n], other))
        local.append(pltpu.make_async_copy(src, dst, lsem.at[n]))
    both(keep, keep_s.at[sec])
    for row, v in enumerate(vec_in):
        n = v.shape[1]
        if row == 2:
            both(v.at[:, pl.ds(0, D)], par.at[sec, pl.ds(2, 1), pl.ds(0, D)])
            both(v.at[:, pl.ds(D, D)], par.at[sec, pl.ds(2, 1), pl.ds(2 * D, D)])
        else:
            both(v, par.at[sec, pl.ds(row, 1), pl.ds(0, n)])
    for c in small:
        c.start()
    ns = len(small)
    chunks = [(f"wqkv{i}", wqkv.at[0, :, pl.ds(i * D, D)], o_w[0].at[:, pl.ds(i * D, D)], s["wqkv"].at[:, pl.ds(i * D, D)]) for i in range(3)]
    chunks += [(n, w.at[0], o, s[n]) for n, w, o in (("wo", wo, o_w[1]), ("w1", w1, o_w[2]), ("w2", w2, o_w[3]))]
    big = {}
    for i, (n, src, dst, vm) in enumerate(chunks):
        big[n] = send_copy(src, dst, send.at[ns + i], recv.at[ns + i], other)
        big[n].start()
    x_in = fetch(tokens.at[sec], s["x"], lsem.at[ns + 6])
    g_in = fetch(segf, seg_s, lsem.at[ns + 7])
    for c in local:
        c.start()
    loads = {}
    for i, (n, src, dst, vm) in enumerate(chunks):
        loads[n] = (pltpu.make_async_copy(src, vm, lsem.at[ns + i]), pltpu.make_async_copy(dst, vm, lsem.at[ns + i]))

    @pl.when(sec == 0)
    def _():
        for n in loads:
            loads[n][0].start()
    for c in local:
        c.wait()
    for c in small:
        c.wait()
    x_in.wait()
    g_in.wait()

    @pl.loop(0, T // RC)
    def _(i):
        rows = pl.ds(i * RC, RC)
        lane = lanes_of(RC)
        seg = seg_s[rows, :]
        hot = lane.astype(f32) == seg
        out = jnp.where(lane == 0, seg, 0.0)
        for l in range(2):
            for b in range(2):
                flag = jnp.sum(jnp.where(hot, keep_s[l, pl.ds(2 * sec + b, 1), :], 0.0), axis=1, keepdims=True) / keep_rate
                out = jnp.where(lane == 1 + 2 * l + b, flag, out)
        cols[rows, :] = out
    outs = [fetch(par, o_par, osem.at[7]), fetch(cols, o_cols, osem.at[8])]
    o_saved["y"] = o_y
    spots = list(SAVED) + ["y"]

    def arrive(n):
        @pl.when(sec == 1)
        def _():
            big[n].wait_recv()
            loads[n][1].start()

    before = {"wqkv0": ["wqkv0"], "wqkv1": ["wqkv1"], "wqkv2": ["wqkv2"], "wo": ["w1"], "w1": ["w2"], "w2": []}

    def ready(n):
        for a in before[n]:
            arrive(a)
        loads[n][0].wait()
        if n == "wqkv2":
            arrive("wo")

    def store(n):
        outs.append(fetch(s[n], o_saved[n], osem.at[spots.index(n)]))

    forward_body(0, s, cols, par, ready, store)

    @pl.when(sec == 0)
    def _():
        for n in big:
            big[n].wait_recv()
    for n in big:
        big[n].wait_send()
    for c in outs:
        c.wait()


def first_call(tokens, segf, keep, vecs, weights, cid):
    _, T, D = tokens.shape
    FF = weights[2].shape[2]
    sc = layer_scratch(T, D, FF)
    names = tuple(sc)
    ns = 10
    shapes = [sds(w.shape[1:], bf16) for w in weights] + [sds((2, 8, FF), f32), sds((T, LANES), f32), sds((T, D), bf16)] + saved_shapes(T, D, FF)
    return pl.pallas_call(
        functools.partial(first_kernel, names), out_shape=tuple(shapes),
        in_specs=[ANY] * 15, out_specs=(ANY,) * len(shapes),
        scratch_shapes=list(sc.values()) + [
            pltpu.VMEM((2, 8, FF), f32), pltpu.VMEM((T, LANES), f32), pltpu.VMEM((2, 8, LANES), f32), pltpu.VMEM((T, LANES), f32),
            DMA((ns + 6,)), DMA((ns + 6,)), DMA((ns + 8,)), DMA((9,))],
        compiler_params=pltpu.CompilerParams(collective_id=cid, has_side_effects=True, vmem_limit_bytes=LIMIT), name="forward_first",
    )(tokens, segf, keep, *vecs, *weights)


def second_kernel(names, x_hbm, cols_hbm, par_hbm, *refs):
    own, oth = refs[:4], refs[4:8]
    o_out = refs[8]
    o_saved = dict(zip(SAVED, refs[9:15]))
    scratch = refs[15:]
    s = dict(zip(names, scratch))
    par, cols, lsem, osem, esem = scratch[len(names):]
    sec = lax.axis_index("section")
    greet_partner()
    first = [fetch(x_hbm, s["x"], lsem.at[4]), fetch(cols_hbm, cols, lsem.at[5]), fetch(par_hbm, par, lsem.at[6])]
    loads = {n: fetch_layer(sec, 1, own[i].at[0], oth[i], s[n], lsem.at[i]) for i, n in enumerate(("wqkv", "wo", "w1", "w2"))}
    for c in first:
        c.wait()
    outs = []

    def ready(n):
        if n == "wqkv0":
            loads["wqkv"].wait()
        elif n in loads:
            loads[n].wait()

    def store(n):
        if n != "y":
            outs.append(fetch(s[n], o_saved[n], osem.at[SAVED.index(n)]))

    to_other = lambda src: send_copy(src, o_out.at[0, sec], esem.at[0], esem.at[1], partner())
    to_own = lambda src: pltpu.make_async_copy(src, o_out.at[0, sec], esem.at[2])

    forward_body(1, s, cols, par, ready, store)

    @pl.when(sec == 0)
    def _():
        to_own(s["x"]).start()
        to_other(s["y"]).start()

    @pl.when(sec == 1)
    def _():
        to_own(s["y"]).start()
        to_other(s["x"]).start()
    to_own(s["x"]).wait()
    to_other(s["x"]).wait()
    for c in outs:
        c.wait()


def second_call(x, cols, par, own, oth, cid):
    T, D = x.shape
    FF = own[2].shape[2]
    sc = layer_scratch(T, D, FF)
    shapes = [sds((1, 2, T, D), bf16)] + saved_shapes(T, D, FF)
    return pl.pallas_call(
        functools.partial(second_kernel, tuple(sc)), out_shape=tuple(shapes),
        in_specs=[ANY] * 11, out_specs=(ANY,) * len(shapes),
        scratch_shapes=list(sc.values()) + [pltpu.VMEM((2, 8, FF), f32), pltpu.VMEM((T, LANES), f32), DMA((7,)), DMA((6,)), DMA((3,))],
        compiler_params=pltpu.CompilerParams(collective_id=cid, has_side_effects=True, vmem_limit_bytes=LIMIT), name="forward_second",
    )(x, cols, par, *own, *oth)


GRID = (2, 2, 2, 2)
AXES = "hlyx"
UR, UC = 48, 256
CYCLE = ("xlyh", "ylxh")
RING, INCS, FINS = 18, 4, 4
HOP_US, PACE_US = (9.0, 9.0, 9.0, 9.0), 2.4


class Stream:
    def __init__(self, dims, units):
        self.dims, self.units, self.n = dims, units, len(units)
        self.head = [0] * 5
        self.loaded = 0
        self.limit = 0
        self.due = 0.0
        self.born = {}
        self.seen = set()

    def scratch(self):
        parts = []
        for j in range(RING):
            for k in range(4):
                parts.append(pltpu.VMEM((2,) * (3 - k) + (UR, UC), bf16))
        return [pltpu.VMEM((RING,) + GRID + (UR, UC), bf16), pltpu.VMEM((INCS,) + GRID + (UR, UC), bf16), pltpu.VMEM((FINS, UR, UC), f32),
                DMA((RING, 4)), DMA((RING, 4)), DMA((RING, 2)), DMA((FINS, 2)), DMA((self.n, 2))] + parts

    def bind(self, scratch, arrive, outs):
        self.own, self.inc, self.fin, self.send, self.rsem, self.lsem, self.fsend, self.frecv = scratch[:8]
        self.parts = [scratch[8 + 4 * j:12 + 4 * j] for j in range(RING)]
        self.arrive, self.outs = arrive, outs
        me = lax.axis_index("dp")
        self.sec = lax.axis_index("section")
        self.at = dict(x=me % 2, y=me // 2 % 2, l=me // 4 % 2, h=me // 8)

    def peer(self, axis):
        c = dict(self.at)
        c[axis] = 1 - c[axis]
        return {"dp": ((c["h"] * 2 + c["l"]) * 2 + c["y"]) * 2 + c["x"]}

    def greet(self):
        bar = pltpu.get_barrier_semaphore()
        ids = [partner()] + [self.peer(a) for a in AXES]
        for i in ids:
            pl.semaphore_signal(bar, inc=1, device_id=i, device_id_type=MESH)
        pl.semaphore_wait(bar, len(ids))

    def order(self, u):
        return CYCLE[(u % RING) % len(CYCLE)]

    def loads(self, u):
        mine, recv = self.units[u]["src"]
        return (pltpu.make_async_copy(mine, self.own.at[u % RING], self.lsem.at[u % RING, 0]),
                pltpu.make_async_copy(recv, self.inc.at[u % INCS], self.lsem.at[u % RING, 1]))

    def load(self, u):
        for c in self.loads(u):
            c.start()

    def hop(self, u, k):
        order = self.order(u)
        j = u % RING
        spot = tuple(self.at[a] if a in order[:k] else (1 - self.at[a] if a == order[k] else slice(None)) for a in AXES)
        return send_copy(self.own.at[(j,) + spot], self.parts[j][k], self.send.at[j, k], self.rsem.at[j, k], self.peer(order[k]))

    def combine(self, axes, fn):
        if not axes:
            fn({})
            return

        @pl.loop(0, 2)
        def _(i):
            rest = [{}]
            for a in axes[1:]:
                rest = [dict(r, **{a: v}) for r in rest for v in range(2)]
            for r in rest:
                fn(dict(r, **{axes[0]: i}))

    def start(self, u):
        for c in self.loads(u):
            c.wait()
        own, inc = self.own.at[u % RING], self.inc.at[u % INCS]

        def add(at):
            i = tuple(at[a] for a in AXES)
            own[i] = own[i] + inc[i]
        self.combine(AXES, add)
        self.hop(u, 0).start()

    def move(self, u, k):
        order = self.order(u)
        self.hop(u, k).wait()
        own, part = self.own.at[u % RING], self.parts[u % RING][k]
        free = [a for a in AXES if a in order[k + 1:]]
        if k == 3 and u >= FINS:
            self.sent(u - FINS)

        def add(at):
            i = tuple(at[a] if a in at else self.at[a] for a in AXES)
            got = part[tuple(at[a] for a in free) if free else Ellipsis]
            if k == 3:
                self.fin[u % FINS] = own[i].astype(f32) + got.astype(f32)
            else:
                own[i] = own[i] + got
        self.combine(free, add)
        if k == 3:
            self.deliver(u)
        else:
            self.hop(u, k + 1).start()

    def results(self, u):
        for i, (out, row, rows, col, cols, c0) in enumerate(self.units[u]["dst"](self.sec)):
            dst = self.outs[out].at[pl.ds(row, rows), pl.ds(pl.multiple_of(col, LANES), cols)]
            src = self.fin.at[u % FINS, :, pl.ds(c0, cols)]
            yield (pltpu.make_async_copy(src, dst, self.fsend.at[u % FINS, i]),
                   send_copy(src, dst, self.fsend.at[u % FINS, i], self.frecv.at[u, i], partner()))

    def by_layer(self, u, same, other):
        @pl.when(self.sec == self.units[u]["layer"])
        def _():
            for near, away in self.results(u):
                same(near, away)

        @pl.when(self.sec != self.units[u]["layer"])
        def _():
            for near, away in self.results(u):
                other(near, away)

    def deliver(self, u):
        self.by_layer(u, lambda near, away: near.start(), lambda near, away: away.start())

    def sent(self, u):
        self.by_layer(u, lambda near, away: near.wait(), lambda near, away: away.wait_send())

    def plan(self, now, limit=None):
        h, calls = self.head, []
        if limit is not None:
            self.limit = max(self.limit, limit)
        drain = now is None
        for k in (3, 2, 1, 0):
            count = 0
            while h[k + 1] < h[k] and (count < 1 if drain else now - self.born[k, h[k + 1]] >= HOP_US[k]):
                u = h[k + 1]
                calls.append(functools.partial(self.move, u, k))
                self.born[k + 1, u] = now
                h[k + 1] += 1
                count += 1
        count = 0
        while h[0] < self.loaded and (drain or now >= self.due) and count < 2:
            u = h[0]
            calls.append(functools.partial(self.start, u))
            self.born[0, u] = now
            h[0] += 1
            count += 1
            if not drain:
                self.due = max(self.due, now - PACE_US) + PACE_US
        while self.loaded < min(self.limit, h[0] + INCS - 1) and (self.loaded < RING or h[4] > self.loaded - RING):
            key = self.units[self.loaded]["need"]
            if key not in self.seen:
                self.seen.add(key)
                calls.append(functools.partial(self.arrive, key))
            calls.append(functools.partial(self.load, self.loaded))
            self.loaded += 1
        return calls

    def tick(self, now, limit=None):
        for c in self.plan(now, limit):
            c()

    def in_loop(self, i, calls):
        for at, todo in enumerate(calls):
            if todo:
                @pl.when(i == at)
                def _(todo=todo):
                    for c in todo:
                        c()

    def finish(self):
        self.limit = self.n
        while self.head[4] < self.n:
            self.tick(None)
        assert self.head == [self.n] * 5
        for u in range(self.n - FINS, self.n):
            self.sent(u)
        for u in range(self.n):
            @pl.when(self.sec == self.units[u]["layer"])
            def _():
                for _n, away in self.results(u):
                    away.wait_recv()


ATTN_SPOTS = (
    ((1, 0, 384, 256, 0),),
    ((1, 256, 640, 128, 0), (0, 0, 896, 128, 128)),
    ((0, 128, 1536, 128, 0), (0, 768, 1664, 128, 128)),
    ((0, 256, 1280, 256, 0),),
    ((0, 512, 1792, 256, 0),),
    ((0, 1024, 2048, 256, 0),),
)
QKV_CUTS = ((0, 0, 0, 256), (0, 256, 768, 256), (0, 512, 1536, 256), (1, 0, 256, 512), (1, 512, 1024, 256), (2, 0, 1280, 256), (2, 256, 1792, 512))


def gradient_units(bufs):
    units = []
    for l in (1, 0):
        up, down, attn = bufs[l]
        for c in range(6):
            cut = lambda ref: ref.at[:, :, :, :, :, pl.ds(c * UC, UC)]
            units.append(dict(layer=l, src=tuple(map(cut, down)), need=(l, "down", c // 2),
                              dst=lambda sec, c=c: [(3, pl.multiple_of(sec * 2 * UR + c % 2 * UR, 16), UR, c // 2 * UC, UC, 0)]))
        for c in range(6):
            cut = lambda ref: ref.at[:, :, :, :, :, pl.ds(c * UC, UC)]
            units.append(dict(layer=l, src=tuple(map(cut, up)), need=(l, "up", c // 2),
                              dst=lambda sec, c=c: [(2, 0, UR, sec * 6 * UC + c * UC, UC, 0)]))
        for c, spots in enumerate(ATTN_SPOTS):
            cut = lambda ref: ref.at[:, :, :, :, :, pl.ds(c * UC, UC)]
            units.append(dict(layer=l, src=tuple(map(cut, attn)), need=(l, "attn", c // 3),
                              dst=lambda sec, spots=spots: [(out, 0, UR, a + sec * (b - a), n, c0) for out, a, b, n, c0 in spots]))
    return units


LAYER_US = 55.6
TIMES = dict(norm=1.6, down=(3.9, 6.2, 8.5), up=(9.3, 10.3, 11.0, 12.0, 12.8, 13.8, 14.5, 15.5, 16.3, 17.3, 18.0, 19.0), gs=(20.0, 20.8, 21.6), mid=23.3,
             gb=25.2, ga=26.4, dwo=27.9, pairs=(30.5, 33.1, 37.5, 40.2, 42.9, 45.6), early=34.8, dqkv=(46.6, 47.6), gn=(48.7, 49.8, 50.9), end=52.7)


def backward_kernel(dims, names, cot, tokens, y0, cols_h, par_h, *refs):
    saved = [dict(zip(SAVED, refs[:6])), dict(zip(SAVED, refs[6:12]))]
    own = dict(zip(("wqkv", "wo", "w1", "w2"), refs[12:16]))
    oth = dict(zip(("wqkv", "wo", "w1", "w2"), refs[16:20]))
    refs = refs[20:]
    o_gin, refs = refs[0], refs[1:]
    bufs = {}
    for l in (1, 0):
        bufs[l], refs = ((refs[0], refs[1]), (refs[2], refs[3]), (refs[4], refs[5])), refs[6:]
    if dims:
        o_big, o_vec, refs = refs[:4], refs[4:12], refs[12:]
    else:
        o_vec, refs = refs[0], refs[1:]
    s = dict(zip(names, refs))
    lsem, csend, crecv, cnear, esem, vsend, vrecv = refs[len(names):len(names) + 7]
    st_refs = refs[len(names) + 7:]
    g, mid, gs, gmid, act, slope, w1, w2, gd, tr, gh, x, att, att_t, ga, feat, lse, cols, par, vec, stage = (s[n] for n in names[:21])
    sec = lax.axis_index("section")
    me = lax.axis_index("dp")
    T, D = g.shape
    FF = act.shape[1]

    ld = {}
    W2 = ("w2", "w2b", "w2c", "w2d")
    CUTS = tuple(f"c{i}" for i in range(len(QKV_CUTS)))

    def get(n, src, dst):
        keys = tuple(names) + W2[1:] + CUTS
        ld[n] = fetch(src, dst, lsem.at[keys.index(n)])

    def get_w(n, layer, name, src_of, dst):
        keys = tuple(names) + W2[1:] + CUTS
        ld[n] = fetch_layer(sec, layer, src_of(own[name].at[0]), src_of(oth[name]), dst, lsem.at[keys.index(n)])

    def need(*ns):
        for n in ns:
            ld.pop(n).wait()

    def load_w2(l):
        for i, n in enumerate(W2):
            get_w(n, l, "w2", lambda r, i=i: r.at[pl.ds(i * D, D), :], w2.at[pl.ds(i * D, D), :])

    def load_attn_weights(l):
        for n, (block, col, src, cols_n) in zip(CUTS, QKV_CUTS):
            get_w(n, l, "wqkv", lambda r, src=src, cols_n=cols_n: r.at[:, pl.ds(src, cols_n)], w2.at[pl.ds(block * D, D), pl.ds(col, cols_n)])
        get_w(W2[3], l, "wo", lambda r: r, w2.at[pl.ds(3 * D, D), :])

    def tile_copy(l, kind, t, at):
        cs = tile(t, 2 * UC)
        mine, recv = (r.at[:, :, :, :, :, cs] for r in bufs[l][1 - kind])
        buf = lambda h: stage.at[h, :, :, :, :, :, cs]
        return (send_copy(buf(1 - sec), recv, csend.at[l, 3 * kind + at], crecv.at[l, 3 * kind + at], partner()),
                pltpu.make_async_copy(buf(sec), mine, cnear.at[l, 3 * kind + at]))

    def attn_copy(l, part):
        mine, recv = (r.at[:, :, :, :, :, pl.ds(part * D, D)] for r in bufs[l][2])
        buf = lambda h: stage.at[h, :, :, :, :, :, pl.ds(part * D, D)]
        return (send_copy(buf(1 - sec), recv, csend.at[l, 6 + part], crecv.at[l, 6 + part], partner()),
                pltpu.make_async_copy(buf(sec), mine, cnear.at[l, 6 + part]))

    def arrive(key):
        l, kind, t = key
        if kind == "attn":
            attn_copy(l, t)[0].wait_recv()
        else:
            tile_copy(l, 1 if kind == "up" else 0, t, t)[0].wait_recv()

    get("g", cot.at[sec], g)
    get("cols", cols_h, cols)
    get("par", par_h, par)
    get("mid", saved[1]["mid"], mid)
    load_w2(1)
    get("slope", saved[1]["slope"], slope)
    get("act", saved[1]["act"], act)
    get_w("w1", 1, "w1", lambda r: r, w1)
    get("x", y0, x)
    get("att", saved[1]["att"], att)
    get("lse", saved[1]["lse"], lse)
    if dims:
        st = Stream(dims, gradient_units(bufs))
        st.bind(st_refs, arrive, o_big)
        st.greet()
    else:
        st = None
        greet_partner()
    need("cols", "par")
    vec[...] = jnp.zeros_like(vec)

    @pl.loop(0, T // RC)
    def _(i):
        rows = pl.ds(i * RC, RC)
        for odd in (0, 1):
            qf, kf = seg_feature(cols[rows, 0:1], RC, odd)
            feat[2 * odd, rows, :] = qf
            feat[2 * odd + 1, rows, :] = kf

    start_us = 4.0

    def tick(spot, limit):
        if st:
            st.tick(start_us + (1 - l) * LAYER_US + TIMES[spot], limit + (1 - l) * 18)

    def loop_plan(*spots):
        table = [[] for _ in spots]
        for i in range(len(spots[0][0])):
            for calls, (times, limits) in zip(table, spots):
                now = start_us + (1 - l) * LAYER_US + times[i]
                calls.append(st.plan(now, limits[i] + (1 - l) * 18) if st else [])
        return table

    def loop_tick(i, calls):
        if st:
            st.in_loop(i, calls)

    down_row = 7 + FF // D
    low_lane = own_lanes(T, 0)
    for l in (1, 0):
        k1, k2 = 1 + 2 * l, 2 + 2 * l
        need(*(("g",) if l == 1 else ()), "mid")

        @pl.loop(0, T // RC)
        def _(i):
            rows = pl.ds(i * RC, RC)
            low = (g[rows, :].astype(f32) * cols[rows, k2:k2 + 1]).astype(bf16)
            gd[rows, :] = low
            vec[l, down_row:down_row + 1, :] += jnp.sum(low.astype(f32), axis=0, keepdims=True)
            unit, _s = layer_unit(mid[rows, :])
            tr[:, rows] = (unit * par[l, 4:5, :D] + par[l, 5:6, :D]).astype(bf16).T
        if l == 0:
            attn_copy(1, 0)[0].wait_send()
            attn_copy(1, 1)[0].wait_send()
        tick("norm", 0)
        need("act")
        calls, = loop_plan((TIMES["down"], (0, 2, 4)))

        @pl.loop(0, 3)
        def _(c):
            d2 = dot(act[...], gd[:, tile(c, UC)], TN).astype(bf16).reshape(GRID + (4, UR, UC))
            for q in range(4):
                stage[q // 2, :, :, :, :, :, pl.ds(pl.multiple_of((2 * c + q % 2) * UC, UC), UC)] = d2[:, :, :, :, q]
            for k in tile_copy(l, 0, c, c):
                k.start()

            @pl.when(c > 0)
            def _():
                tile_copy(l, 0, c, c - 1)[1].wait()
            loop_tick(c, calls)
        tile_copy(l, 0, 2, 2)[1].wait()
        need(*W2, "slope")
        early, late = loop_plan((TIMES["up"][0::2], (6, 6, 6, 8, 8, 10)), (TIMES["up"][1::2], (6, 6, 8, 8, 10, 10)))

        @pl.loop(0, 6)
        def _(i):
            mine, t = lax.rem(i, 2), i // 2
            h = lax.rem(sec + 1 + mine, 2)
            n = 3 * h + t
            cs = tile(n, 2 * UC)
            low = (dot(gd[...], w2[cs, :], NT) * slope[:, cs].astype(f32)).astype(bf16)
            gh[:, cs] = low
            total = jnp.sum(low.astype(f32), axis=0, keepdims=True)
            for q in range(2):
                m = 2 * n + q
                vec[l, pl.ds(7 + m // 3, 1), tile(lax.rem(m, 3), UC)] = total[:, q * UC:(q + 1) * UC]

            @pl.when(mine == 0)
            def _():
                tile_copy(l, 0, t, t)[0].wait_send()

            @pl.when((mine == 0) & (i > 0))
            def _():
                tile_copy(l, 1, t, t - 1)[1].wait()
            loop_tick(i, early)
            d1 = dot(tr[...], low).astype(bf16)
            stage[h, :, :, :, :, :, tile(t, 2 * UC)] = d1.reshape(GRID + (UR, 2 * UC))
            away, near = tile_copy(l, 1, t, t)

            @pl.when(mine == 0)
            def _():
                away.start()

            @pl.when(mine == 1)
            def _():
                near.start()
            loop_tick(i, late)
        load_attn_weights(l)
        get("qkv", saved[l]["qkv"], slope.at[:, pl.ds(0, 3 * D)])
        if l == 1:
            get("act", saved[0]["act"], act)
        tile_copy(l, 1, 2, 2)[1].wait()
        need("w1")
        calls, = loop_plan((TIMES["gs"], (10, 12, 12)))

        @pl.loop(0, D // W)
        def _(n):
            cs = tile(n, W)
            gs[:, cs] = dot(gh[...], w1[cs, :], NT)
            loop_tick(n, calls)
        if l == 1:
            get_w("w1", 0, "w1", lambda r: r, w1)
        for t in range(3):
            tile_copy(l, 1, t, t)[0].wait_send()

        @pl.loop(0, T // RC)
        def _(i):
            rows = pl.ds(i * RC, RC)
            unit, scale = layer_unit(mid[rows, :])
            low = gs[rows, :]
            vec[l, 5:6, :] += jnp.sum(low * unit, axis=0, keepdims=True)
            vec[l, 6:7, :] += jnp.sum(low, axis=0, keepdims=True)
            gmid[rows, :] = g[rows, :].astype(f32) + unit_back(low, unit, scale, par[l, 4:5, :D])
        tick("mid", 12)
        if l == 1:
            get("mid", saved[0]["mid"], mid)
        need("x", "att")

        @pl.loop(0, T // RC)
        def _(i):
            rows = pl.ds(i * RC, RC)
            low = (gmid[rows, :] * cols[rows, k1:k1 + 1]).astype(bf16)
            gd[rows, :] = low
            vec[l, 4:5, :] += jnp.sum(low.astype(f32), axis=0, keepdims=True)
            unit, _s = layer_unit(x[rows, :].astype(f32))
            tr[:, rows] = (unit * par[l, 0:1, :D] + par[l, 1:2, :D]).astype(bf16).T
            att_t[:, rows] = att[rows, :].T
        tick("gb", 12)
        need(W2[3])

        @pl.loop(0, D // W)
        def _(n):
            cs = tile(n, W)
            ga[:, cs] = dot(gd[...], w2[pl.ds(pl.multiple_of(3 * D + n * W, W), W), :], NT).astype(bf16)
        tick("ga", 12)
        @pl.loop(0, 2)
        def _(h):
            stage[h, :, :, :, :, :, 0:D // 2] = dot(att_t[...], gd[:, tile(h, D // 2)]).astype(bf16).reshape(GRID + (UR, D // 2))
        tick("dwo", 12)
        need("qkv", "lse")

        def pair(p, spots):
            off = pl.multiple_of(p * LANES, LANES)
            qp = slope[:, pl.ds(off, LANES)]
            kp = slope[:, pl.ds(off + D, LANES)]
            vp = slope[:, pl.ds(off + 2 * D, LANES)]
            gp = ga[:, pl.ds(off, LANES)]
            prod = gp.astype(f32) * att[:, pl.ds(off, LANES)].astype(f32)
            dq, dk, dv = [], [], []
            for odd in (0, 1):
                own_l = own_lanes(T, odd)
                base = feature_base(odd)
                lane = lanes_of(T)
                row_d = jnp.sum(jnp.where(own_l, prod, 0.0), axis=1, keepdims=True)
                l3 = split3(-lse[p, :, odd:odd + 1])
                d3 = split3(-row_d)
                qf = feat[2 * odd]
                gf = jnp.zeros_like(gp)
                for j in range(3):
                    qf = jnp.where(lane == base + 8 + j, l3[j], qf)
                    gf = jnp.where(lane == base + j, d3[j], gf)
                q = jnp.where(own_l, qp, qf)
                k = jnp.where(own_l, kp, feat[2 * odd + 1])
                v = jnp.where(own_l, vp, jnp.ones_like(vp))
                gg = jnp.where(own_l, gp, gf)
                prob = jnp.exp(dot(k, q, NT))
                gsc = (prob * dot(v, gg, NT)).astype(bf16)
                dv.append(dot(prob.astype(bf16), gg))
                dk.append(dot(gsc, q))
                dq.append(dot(gsc, k, TN))
            for at, val in zip(spots, ((jnp.where(low_lane, dq[0], dq[1]) * 0.125), jnp.where(low_lane, dk[0], dk[1]), jnp.where(low_lane, dv[0], dv[1]))):
                gh[:, tile(at + p, LANES)] = val.astype(bf16)

        def gradient(part, width, base):
            calls, = loop_plan((TIMES["dqkv"], (15, 15))) if part else (None,)

            @pl.loop(0, 2)
            def _(i):
                h = lax.rem(i + 1 + sec, 2)
                cs = pl.ds(pl.multiple_of(base + h * width, LANES), width)
                stage[h, :, :, :, :, :, (part + 1) * D - width:(part + 1) * D] = dot(tr[...], gh[:, cs]).astype(bf16).reshape(GRID + (UR, width))
                away, near = attn_copy(l, part)

                @pl.when(i == 0)
                def _():
                    away.start()

                @pl.when(i == 1)
                def _():
                    near.start()
                if part == 1:
                    loop_tick(i, calls)

        calls, = loop_plan((TIMES["pairs"][:2], (12, 12)))

        @pl.loop(0, 2)
        def _(p):
            pair(p, (0, 2, 4))
            loop_tick(p, calls)
        gradient(0, D // 2, 0)
        attn_copy(l, 0)[1].wait()
        tick("early", 12)

        calls, = loop_plan((TIMES["pairs"][2:], (15,) * 4))

        @pl.loop(2, D // LANES)
        def _(p):
            pair(p, (4, 8, 12))
            loop_tick(p - 2, calls)
        if l == 1:
            get("slope", saved[0]["slope"], slope)
            get("att", saved[0]["att"], att)
            get("lse", saved[0]["lse"], lse)
        gradient(1, D, D)
        attn_copy(l, 1)[1].wait()
        for row, to, at, n in ((2, 0, 0, 256), (2, 256, 768, 512), (3, 0, 512, 256), (3, 256, 1792, 512)):
            vec[l, row:row + 1, to:to + n] = jnp.sum(gh[:, at:at + n].astype(f32), axis=0, keepdims=True)

        need(*CUTS)
        calls, = loop_plan((TIMES["gn"], (18, 18, 18)))

        @pl.loop(0, D // W)
        def _(n):
            cs = tile(n, W)
            acc = jnp.zeros((T, W), f32)
            for c in range(3):
                acc += dot(gh[:, c * D:(c + 1) * D], w2[pl.ds(pl.multiple_of(c * D + n * W, W), W), :], NT)
            gs[:, cs] = acc
            loop_tick(n, calls)
        if l == 1:
            load_w2(0)

        @pl.loop(0, T // RC)
        def _(i):
            rows = pl.ds(i * RC, RC)
            unit, scale = layer_unit(x[rows, :].astype(f32))
            low = gs[rows, :]
            vec[l, 0:1, :] += jnp.sum(low * unit, axis=0, keepdims=True)
            vec[l, 1:2, :] += jnp.sum(low, axis=0, keepdims=True)
            res = (gmid[rows, :] + unit_back(low, unit, scale, par[l, 0:1, :D])).astype(bf16)
            if l == 1:
                g[rows, :] = res
            else:
                x[rows, :] = res
        if l == 1:
            get("x", tokens.at[sec], x)
        tick("end", 18)

    to_other = lambda src: send_copy(src, o_gin.at[0, sec], esem.at[0], esem.at[1], partner())
    to_own = lambda src: pltpu.make_async_copy(src, o_gin.at[0, sec], esem.at[2])

    @pl.when(sec == 0)
    def _():
        to_own(x).start()
        to_other(g).start()

    @pl.when(sec == 1)
    def _():
        to_own(g).start()
        to_other(x).start()
    if st:
        vown, vgot = s["vown"], s["vgot"]
        def hop(n):
            if n == 0:
                return send_copy(vec.at[1 - sec], vgot.at[0], vsend.at[0], vrecv.at[0], partner())
            return send_copy(vown.at[n - 1], vgot.at[n], vsend.at[n], vrecv.at[n], st.peer(AXES[n - 1]))
        hop(0).start()
        st.tick(None)
        hop(0).wait()
        vown[0] = vec[sec] + vgot[0]
        for n in range(1, 5):
            hop(n).start()
            st.tick(None)
            hop(n).wait()
            vown[n] = vown[n - 1] + vgot[n]
        n_dp = dims[0] * dims[1] * dims[2]
        for o, (row, width) in zip(o_vec, small_spots(D, FF)):
            size = width // n_dp
            at = me * size
            line = vown[4, pl.ds(row + at // D, 1), :]
            line = pltpu.roll(jnp.broadcast_to(line, (8, D)), lax.rem(D - at % D, D), 1)
            o[...] = line[0:1, :size]
        st.finish()
    else:
        for l in (1, 0):
            for t in range(3):
                arrive((l, "down", t))
                arrive((l, "up", t))
            arrive((l, "attn", 0))
            arrive((l, "attn", 1))
        c = pltpu.make_async_copy(vec, o_vec, vsend.at[0])
        c.start()
        c.wait()
    attn_copy(0, 0)[0].wait_send()
    attn_copy(0, 1)[0].wait_send()
    to_own(x).wait()
    to_other(x).wait()


def small_spots(D, FF):
    return ((0, D), (1, D), (2, 2 * D), (4, D), (5, D), (6, D), (7, FF), (7 + FF // D, D))


def backward_call(dims, n_dp, cot, tokens, y0, cols, par, saved0, saved1, own, oth, cid):
    T, D = y0.shape
    FF = own[2].shape[2]
    V = pltpu.VMEM
    sc = dict(
        g=V((T, D), bf16), mid=V((T, D), f32), gs=V((T, D), f32), gmid=V((T, D), f32), act=V((T, FF), bf16), slope=V((T, FF), bf16),
        w1=V((D, FF), bf16), w2=V((FF, D), bf16), gd=V((T, D), bf16), tr=V((D, T), bf16), gh=V((T, FF), bf16), x=V((T, D), bf16), att=V((T, D), bf16),
        att_t=V((D, T), bf16), ga=V((T, D), bf16), feat=V((4, T, LANES), bf16), lse=V((D // LANES, T, 2), f32), cols=V((T, LANES), f32),
        par=V((2, 8, FF), f32), vec=V((2, 16, D), f32), stage=V((2,) + GRID + (UR, 2 * D), bf16))
    sc["qkv"] = V((8, LANES), f32)
    hops = 5
    if dims:
        sc.update(vown=V((5, 16, D), f32), vgot=V((hops, 16, D), f32))
    wide = sds(GRID + (UR, 2 * D), bf16)
    shapes = [sds((1, 2, T, D), bf16)] + [wide] * 12
    specs = [ANY] * len(shapes)
    if dims:
        shapes += [sds((D // n_dp, 3 * D), f32), sds((D // n_dp, D), f32), sds((D // n_dp, FF), f32), sds((FF // n_dp, D), f32)]
        shapes += [sds((1, w // n_dp), f32) for _, w in small_spots(D, FF)]
        specs += [ANY] * 4 + [pl.BlockSpec(memory_space=pltpu.VMEM)] * 8
        stream = Stream(dims, [None] * 36).scratch()
    else:
        shapes += [sds((2, 16, D), f32)]
        specs += [ANY]
        stream = []
    scratch = list(sc.values()) + [DMA((len(sc) + 3 + len(QKV_CUTS),)), DMA((2, 8)), DMA((2, 8)), DMA((2, 8)), DMA((3,)), DMA((hops,)), DMA((hops,))] + stream
    return pl.pallas_call(
        functools.partial(backward_kernel, dims, tuple(sc)), out_shape=tuple(shapes),
        in_specs=[ANY] * 25, out_specs=tuple(specs), scratch_shapes=scratch,
        compiler_params=pltpu.CompilerParams(collective_id=cid, has_side_effects=True, vmem_limit_bytes=LIMIT), name="backward",
    )(cot, tokens, y0, cols, par, *saved0, *saved1, *own, *oth)


def copy_kernel(n, *refs):
    mid, sem = refs[2 * n:3 * n], refs[3 * n]
    into = [pltpu.make_async_copy(refs[i], mid[i], sem.at[0, i]) for i in range(n)]
    out = [pltpu.make_async_copy(mid[i], refs[n + i], sem.at[1, i]) for i in range(n)]
    for c in into:
        c.start()
    for c, o in zip(into, out):
        c.wait()
        o.start()
    for o in out:
        o.wait()


def copy_call(arrays):
    n = len(arrays)
    return pl.pallas_call(
        functools.partial(copy_kernel, n), out_shape=tuple(sds(a.shape, a.dtype) for a in arrays),
        in_specs=[ANY] * n, out_specs=(ANY,) * n, scratch_shapes=[pltpu.VMEM(a.shape, a.dtype) for a in arrays] + [DMA((2, n))],
        compiler_params=pltpu.CompilerParams(vmem_limit_bytes=32 * 2**20), name="place_outputs",
    )(*arrays)


def dp_dims(n):
    return {16: (2, 2, 4)}.get(n)


def shards(
    tokens, segment_ids, keep_masks, cotangent,
    norm1_gain, norm1_bias, qkv_weight, qv_bias, out_weight, out_bias,
    norm2_gain, norm2_bias, fc1_weight, fc1_bias, fc2_weight, fc2_bias,
):
    sec = lax.axis_index("section")
    n_dp = lax.axis_size("dp")
    dims = dp_dims(n_dp)
    T, D = tokens.shape[1:]
    FF = fc1_weight.shape[2]
    seg = lax.dynamic_index_in_dim(segment_ids, sec, 0, keepdims=False)
    segf = jnp.broadcast_to(seg.astype(f32)[:, None], (T, LANES))
    keep = jnp.pad(keep_masks[0].astype(f32).reshape(4, -1), ((0, 4), (0, LANES - keep_masks.shape[3])))
    own = (qkv_weight, out_weight, fc1_weight, fc2_weight)
    vecs = (norm1_gain, norm1_bias, qv_bias, out_bias, norm2_gain, norm2_bias, fc1_bias, fc2_bias)
    res = first_call(tokens, segf, keep, vecs, own, 0)
    oth, par, cols, y0, saved0 = res[:4], res[4], res[5], res[6], res[7:]
    res = second_call(y0, cols, par, own, oth, 1)
    layer_out, saved1 = res[0], res[1:]
    res = backward_call(dims, n_dp, cotangent, tokens, y0, cols, par, saved0, saved1, own, oth, 2)
    input_grad = res[0]
    if dims:
        layer_out, input_grad, dqkv, dwo, dw1, dw2, n1g, n1b, qv, ob, n2g, n2b, b1, b2 = copy_call((layer_out, input_grad) + tuple(res[13:25]))
    else:
        sums = {}
        for i, l in enumerate((1, 0)):
            up, down, attn = (res[1 + 6 * i + 2 * j].astype(f32) + res[2 + 6 * i + 2 * j].astype(f32) for j in range(3))
            up, attn = up.reshape(D, -1), attn.reshape(D, -1)
            down = lax.all_gather(down, "section").reshape((2, 16, UR, 3, 2, UC))
            down = down.transpose(1, 0, 4, 2, 3, 5).reshape(FF, D)
            sums[l] = [lax.psum_scatter(a, "dp", scatter_dimension=0, tiled=True) for a in (attn, up, down)]
        attn, up, down = (jnp.stack([sums[0][i], sums[1][i]]) for i in range(3))
        attn, up = (lax.dynamic_index_in_dim(lax.all_gather(a, "section"), sec, 1, keepdims=False) for a in (attn, up))
        dw2 = lax.dynamic_index_in_dim(down, sec, 0, keepdims=False)
        dw1 = jnp.concatenate([up[0], up[1]], axis=1)
        cuts = {}
        for c, spots in enumerate(ATTN_SPOTS):
            for out, a, b, n, c0 in spots:
                for h, col in ((0, a), (1, b)):
                    cuts[out, col] = attn[h, :, c * UC + c0:c * UC + c0 + n]
        dqkv, dwo = (jnp.concatenate([cuts[k] for k in sorted(cuts) if k[0] == out], axis=1) for out in (0, 1))
        v = lax.dynamic_index_in_dim(lax.psum(res[13], ("section", "dp")), sec, 0, keepdims=False)
        at = lax.axis_index("dp")
        n1g, n1b, qv, ob, n2g, n2b, b1, b2 = (
            lax.dynamic_slice_in_dim(v[row:row + -(-w // D)].reshape(-1), at * (w // n_dp), w // n_dp)[None] for row, w in small_spots(D, FF))
    return (layer_out, input_grad, n1g, n1b, dqkv[None], qv, dwo[None], ob, n2g, n2b, dw1[None], b1, dw2[None], b2)


def solution(mesh):
    in_specs = (
        P(None, "dp", None), P(None, "dp"), P("section", None, None, "dp"), P(None, "dp", None),
        P("section", None), P("section", None), P("section", None, None), P("section", None),
        P("section", None, None), P("section", None), P("section", None), P("section", None),
        P("section", None, None), P("section", None), P("section", None, None), P("section", None),
    )
    out_specs = (
        P("section", None, "dp", None), P("section", None, "dp", None),
        P("section", "dp"), P("section", "dp"), P("section", "dp", None), P("section", "dp"),
        P("section", "dp", None), P("section", "dp"), P("section", "dp"), P("section", "dp"),
        P("section", "dp", None), P("section", "dp"), P("section", "dp", None), P("section", "dp"),
    )
    return jax.shard_map(shards, mesh=mesh, in_specs=in_specs, out_specs=out_specs, check_vma=False)
```

```python
import functools
import jax
import jax.numpy as jnp
from jax import lax
from jax.experimental import pallas as pl
from jax.experimental.pallas import tpu as pltpu
from jax.sharding import PartitionSpec as P

HEAD_DIM = 64
LANES = 128
keep_rate = 0.9
norm_eps = 1e-06
root_half = 0.7071067811865476
inverse_root = 0.3989422804014327
BIG = 2.0**30
f32, bf16 = jnp.float32, jnp.bfloat16
NN = (((1,), (0,)), ((), ()))
NT = (((1,), (1,)), ((), ()))
TN = (((0,), (0,)), ((), ()))
MESH = pl.DeviceIdType.MESH
ANY = pl.BlockSpec(memory_space=pl.ANY)
DMA = pltpu.SemaphoreType.DMA
LIMIT = 61 * 2**20
RC = 128
W = 256
sds = jax.ShapeDtypeStruct


def dot(a, b, dims=NN):
    return lax.dot_general(a, b, dims, preferred_element_type=f32)


def layer_unit(x):
    center = x - jnp.mean(x, axis=-1, keepdims=True)
    scale = lax.rsqrt(jnp.mean(center * center, axis=-1, keepdims=True) + norm_eps)
    return center * scale, scale


def unit_back(grad, unit, scale, gain):
    scaled = grad * gain
    inner = jnp.mean(scaled, axis=-1, keepdims=True)
    along = jnp.mean(scaled * unit, axis=-1, keepdims=True)
    return scale * (scaled - inner - unit * along)


def gelu_pair(h):
    phi = 0.5 * (1.0 + lax.erf(h * root_half))
    return h * phi, phi + h * jnp.exp(-0.5 * h * h) * inverse_root


def split3(v):
    a = v.astype(bf16)
    r = v - a.astype(f32)
    b = r.astype(bf16)
    c = (r - b.astype(f32)).astype(bf16)
    return a, b, c


def feature_base(odd):
    return 0 if odd else HEAD_DIM


def lanes_of(rows):
    return lax.broadcasted_iota(jnp.int32, (rows, LANES), 1)


def seg_feature(seg, rows, odd):
    base = feature_base(odd)
    lane = lanes_of(rows)
    inside = (lane >= base) & (lane < base + 8)
    same = (lane - base).astype(f32) == seg
    qf = jnp.where(inside & same, BIG, 0.0)
    kf = jnp.where(inside & jnp.logical_not(same), -1.0, 0.0)
    kf = jnp.where((lane >= base + 8) & (lane < base + 11), 1.0, kf)
    return qf.astype(bf16), kf.astype(bf16)


def own_lanes(rows, odd):
    lane = lanes_of(rows)
    return (lane >= HEAD_DIM) if odd else (lane < HEAD_DIM)


def tile(n, width):
    return pl.ds(pl.multiple_of(n * width, LANES), width)


def fetch(src, dst, sem):
    c = pltpu.make_async_copy(src, dst, sem)
    c.start()
    return c


def fetch_layer(sec, layer, own, other, dst, sem):
    c = pltpu.make_async_copy(own, dst, sem)

    @pl.when(sec == layer)
    def _():
        c.start()

    @pl.when(sec != layer)
    def _():
        pltpu.make_async_copy(other, dst, sem).start()
    return c


def partner():
    return {"section": 1 - lax.axis_index("section")}


def greet_partner():
    bar = pltpu.get_barrier_semaphore()
    pl.semaphore_signal(bar, inc=1, device_id=partner(), device_id_type=MESH)
    pl.semaphore_wait(bar, 1)


def send_copy(src, dst, send, recv, dev):
    return pltpu.make_async_remote_copy(src, dst, send, recv, device_id=dev, device_id_type=MESH)


def layer_scratch(T, D, FF):
    return dict(
        x=pltpu.VMEM((T, D), bf16), wqkv=pltpu.VMEM((D, 3 * D), bf16), wo=pltpu.VMEM((D, D), bf16),
        w1=pltpu.VMEM((D, FF), bf16), w2=pltpu.VMEM((FF, D), bf16),
        norm=pltpu.VMEM((T, D), bf16), second=pltpu.VMEM((T, D), bf16), feat=pltpu.VMEM((4, T, LANES), bf16),
        qkv=pltpu.VMEM((T, 3 * D), bf16), lse=pltpu.VMEM((D // LANES, T, 2), f32), att=pltpu.VMEM((T, D), bf16),
        mid=pltpu.VMEM((T, D), f32), act=pltpu.VMEM((T, FF), bf16), slope=pltpu.VMEM((T, FF), bf16),
        y=pltpu.VMEM((T, D), bf16),
    )


def forward_body(l, s, cols, par, ready, store):
    T, D = s["x"].shape
    FF = s["act"].shape[1]
    k1 = 1 + 2 * l

    @pl.loop(0, T // RC)
    def _(i):
        rows = pl.ds(i * RC, RC)
        unit, _s = layer_unit(s["x"][rows, :].astype(f32))
        s["norm"][rows, :] = (unit * par[l, 0:1, :D] + par[l, 1:2, :D]).astype(bf16)
        for odd in (0, 1):
            qf, kf = seg_feature(cols[rows, 0:1], RC, odd)
            s["feat"][2 * odd, rows, :] = qf
            s["feat"][2 * odd + 1, rows, :] = kf

    for part in range(3):
        ready(f"wqkv{part}")

        @pl.loop(0, D // W)
        def _(n):
            cs = pl.ds(pl.multiple_of(part * D + n * W, W), W)
            acc = dot(s["norm"][...], s["wqkv"][:, cs]) + par[l, 2:3, cs]
            s["qkv"][:, cs] = (acc * 0.125 if part == 0 else acc).astype(bf16)
    store("qkv")

    def one_pair(p):
        off = pl.multiple_of(p * LANES, LANES)
        qp = s["qkv"][:, pl.ds(off, LANES)]
        kp = s["qkv"][:, pl.ds(off + D, LANES)]
        vp = s["qkv"][:, pl.ds(off + 2 * D, LANES)]
        outs, scs, vs = [], [], []
        for odd in (0, 1):
            own = own_lanes(T, odd)
            q = jnp.where(own, qp, s["feat"][2 * odd])
            k = jnp.where(own, kp, s["feat"][2 * odd + 1])
            vs.append(jnp.where(own, vp, jnp.ones_like(vp)))
            scs.append(dot(q, k, NT))
        ms = [jnp.max(sc, axis=1, keepdims=True) for sc in scs]
        es = [jnp.exp(sc - m).astype(bf16) for sc, m in zip(scs, ms)]
        for odd in (0, 1):
            base = feature_base(odd)
            o = dot(es[odd], vs[odd])
            total = o[:, base:base + 1]
            outs.append(o / total)
            s["lse"][p, :, odd:odd + 1] = ms[odd] + jnp.log(total)
        s["att"][:, pl.ds(off, LANES)] = jnp.where(own_lanes(T, 0), outs[0], outs[1]).astype(bf16)

    @pl.loop(0, D // LANES // 2)
    def _(pp):
        one_pair(2 * pp)
        one_pair(2 * pp + 1)
    store("lse")
    store("att")
    ready("wo")

    @pl.loop(0, D // W)
    def _(n):
        cs = tile(n, W)
        acc = dot(s["att"][...], s["wo"][:, cs]) + par[l, 3:4, cs]
        s["mid"][:, cs] = s["x"][:, cs].astype(f32) + cols[:, k1:k1 + 1] * acc
    store("mid")

    @pl.loop(0, T // RC)
    def _(i):
        rows = pl.ds(i * RC, RC)
        unit, _s = layer_unit(s["mid"][rows, :])
        s["second"][rows, :] = (unit * par[l, 4:5, :D] + par[l, 5:6, :D]).astype(bf16)
    ready("w1")

    ready("w2")

    @pl.loop(0, FF // D)
    def _(n):
        cs = tile(n, D)
        a, sl = gelu_pair(dot(s["second"][...], s["w1"][:, cs]) + par[l, 6:7, cs])
        s["act"][:, cs] = a.astype(bf16)
        s["slope"][:, cs] = sl.astype(bf16)
    store("act")
    store("slope")

    @pl.loop(0, D // W)
    def _(n):
        cs = tile(n, W)
        acc = dot(s["act"][...], s["w2"][:, cs]) + par[l, 7:8, cs]
        s["y"][:, cs] = (s["mid"][:, cs] + cols[:, k1 + 1:k1 + 2] * acc).astype(bf16)
    store("y")


SAVED = ("qkv", "lse", "att", "mid", "act", "slope")


def saved_shapes(T, D, FF):
    return [sds((T, 3 * D), bf16), sds((D // LANES, T, 2), f32), sds((T, D), bf16), sds((T, D), f32), sds((T, FF), bf16), sds((T, FF), bf16)]


def first_kernel(names, tokens, segf, keep, *refs):
    vec_in, (wqkv, wo, w1, w2) = refs[:8], refs[8:12]
    o_w = refs[12:16]
    o_par, o_cols, o_y = refs[16:19]
    o_saved = dict(zip(SAVED, refs[19:25]))
    scratch = refs[25:]
    s = dict(zip(names, scratch))
    par, cols, keep_s, seg_s, send, recv, lsem, osem = scratch[len(names):]
    sec = lax.axis_index("section")
    T, D = s["x"].shape
    other = partner()
    greet_partner()
    par[:, 2:3, D:2 * D] = jnp.zeros((2, 1, D), f32)
    small, local = [], []

    def both(src, dst):
        n = len(small)
        small.append(send_copy(src, dst, send.at[n], recv.at[n], other))
        local.append(pltpu.make_async_copy(src, dst, lsem.at[n]))
    both(keep, keep_s.at[sec])
    for row, v in enumerate(vec_in):
        n = v.shape[1]
        if row == 2:
            both(v.at[:, pl.ds(0, D)], par.at[sec, pl.ds(2, 1), pl.ds(0, D)])
            both(v.at[:, pl.ds(D, D)], par.at[sec, pl.ds(2, 1), pl.ds(2 * D, D)])
        else:
            both(v, par.at[sec, pl.ds(row, 1), pl.ds(0, n)])
    for c in small:
        c.start()
    ns = len(small)
    chunks = [(f"wqkv{i}", wqkv.at[0, :, pl.ds(i * D, D)], o_w[0].at[:, pl.ds(i * D, D)], s["wqkv"].at[:, pl.ds(i * D, D)]) for i in range(3)]
    chunks += [(n, w.at[0], o, s[n]) for n, w, o in (("wo", wo, o_w[1]), ("w1", w1, o_w[2]), ("w2", w2, o_w[3]))]
    to_vmem, to_hbm, keep_w = {}, {}, {}
    for i, (n, src, dst, vm) in enumerate(chunks):
        to_vmem[n] = send_copy(src, vm, send.at[ns + i], recv.at[ns + i], other)
        to_hbm[n] = send_copy(src, dst, send.at[ns + i], recv.at[ns + i], other)
        keep_w[n] = pltpu.make_async_copy(vm, dst, lsem.at[ns + i])

    @pl.when(sec == 0)
    def _():
        for c in to_vmem.values():
            c.start()

    @pl.when(sec == 1)
    def _():
        for c in to_hbm.values():
            c.start()
    x_in = fetch(tokens.at[sec], s["x"], lsem.at[ns + 6])
    g_in = fetch(segf, seg_s, lsem.at[ns + 7])
    for c in local:
        c.start()
    loads = {n: pltpu.make_async_copy(src, vm, lsem.at[ns + i]) for i, (n, src, dst, vm) in enumerate(chunks)}

    @pl.when(sec == 0)
    def _():
        for c in loads.values():
            c.start()
    for c in local:
        c.wait()
    for c in small:
        c.wait()
    x_in.wait()
    g_in.wait()

    @pl.loop(0, T // RC)
    def _(i):
        rows = pl.ds(i * RC, RC)
        lane = lanes_of(RC)
        seg = seg_s[rows, :]
        hot = lane.astype(f32) == seg
        out = jnp.where(lane == 0, seg, 0.0)
        for l in range(2):
            for b in range(2):
                flag = jnp.sum(jnp.where(hot, keep_s[l, pl.ds(2 * sec + b, 1), :], 0.0), axis=1, keepdims=True) / keep_rate
                out = jnp.where(lane == 1 + 2 * l + b, flag, out)
        cols[rows, :] = out
    outs = [fetch(par, o_par, osem.at[7]), fetch(cols, o_cols, osem.at[8])]
    o_saved["y"] = o_y
    spots = list(SAVED) + ["y"]

    def ready(n):
        @pl.when(sec == 0)
        def _():
            loads[n].wait()

        @pl.when(sec == 1)
        def _():
            to_vmem[n].wait_recv()
            keep_w[n].start()

    def store(n):
        outs.append(fetch(s[n], o_saved[n], osem.at[spots.index(n)]))

    forward_body(0, s, cols, par, ready, store)

    @pl.when(sec == 0)
    def _():
        for c in to_hbm.values():
            c.wait_recv()

    @pl.when(sec == 1)
    def _():
        for c in keep_w.values():
            c.wait()
    for c in to_vmem.values():
        c.wait_send()
    for c in outs:
        c.wait()


def first_call(tokens, segf, keep, vecs, weights, cid):
    _, T, D = tokens.shape
    FF = weights[2].shape[2]
    sc = layer_scratch(T, D, FF)
    names = tuple(sc)
    ns = 10
    shapes = [sds(w.shape[1:], bf16) for w in weights] + [sds((2, 8, FF), f32), sds((T, LANES), f32), sds((T, D), bf16)] + saved_shapes(T, D, FF)
    return pl.pallas_call(
        functools.partial(first_kernel, names), out_shape=tuple(shapes),
        in_specs=[ANY] * 15, out_specs=(ANY,) * len(shapes),
        scratch_shapes=list(sc.values()) + [
            pltpu.VMEM((2, 8, FF), f32), pltpu.VMEM((T, LANES), f32), pltpu.VMEM((2, 8, LANES), f32), pltpu.VMEM((T, LANES), f32),
            DMA((ns + 6,)), DMA((ns + 6,)), DMA((ns + 8,)), DMA((9,))],
        compiler_params=pltpu.CompilerParams(collective_id=cid, has_side_effects=True, vmem_limit_bytes=LIMIT), name="forward_first",
    )(tokens, segf, keep, *vecs, *weights)


def second_kernel(names, x_hbm, cols_hbm, par_hbm, *refs):
    own, oth = refs[:4], refs[4:8]
    o_out = refs[8]
    o_saved = dict(zip(SAVED, refs[9:15]))
    scratch = refs[15:]
    s = dict(zip(names, scratch))
    par, cols, lsem, osem, esem = scratch[len(names):]
    sec = lax.axis_index("section")
    greet_partner()
    first = [fetch(x_hbm, s["x"], lsem.at[4]), fetch(cols_hbm, cols, lsem.at[5]), fetch(par_hbm, par, lsem.at[6])]
    loads = {n: fetch_layer(sec, 1, own[i].at[0], oth[i], s[n], lsem.at[i]) for i, n in enumerate(("wqkv", "wo", "w1", "w2"))}
    for c in first:
        c.wait()
    outs = []

    def ready(n):
        if n == "wqkv0":
            loads["wqkv"].wait()
        elif n in loads:
            loads[n].wait()

    def store(n):
        if n != "y":
            outs.append(fetch(s[n], o_saved[n], osem.at[SAVED.index(n)]))

    to_other = lambda src: send_copy(src, o_out.at[0, sec], esem.at[0], esem.at[1], partner())
    to_own = lambda src: pltpu.make_async_copy(src, o_out.at[0, sec], esem.at[2])

    forward_body(1, s, cols, par, ready, store)

    @pl.when(sec == 0)
    def _():
        to_own(s["x"]).start()
        to_other(s["y"]).start()

    @pl.when(sec == 1)
    def _():
        to_own(s["y"]).start()
        to_other(s["x"]).start()
    to_own(s["x"]).wait()
    to_other(s["x"]).wait()
    for c in outs:
        c.wait()


def second_call(x, cols, par, own, oth, cid):
    T, D = x.shape
    FF = own[2].shape[2]
    sc = layer_scratch(T, D, FF)
    shapes = [sds((1, 2, T, D), bf16)] + saved_shapes(T, D, FF)
    return pl.pallas_call(
        functools.partial(second_kernel, tuple(sc)), out_shape=tuple(shapes),
        in_specs=[ANY] * 11, out_specs=(ANY,) * len(shapes),
        scratch_shapes=list(sc.values()) + [pltpu.VMEM((2, 8, FF), f32), pltpu.VMEM((T, LANES), f32), DMA((7,)), DMA((6,)), DMA((3,))],
        compiler_params=pltpu.CompilerParams(collective_id=cid, has_side_effects=True, vmem_limit_bytes=LIMIT), name="forward_second",
    )(x, cols, par, *own, *oth)


GRID = (2, 2, 2, 2)
AXES = "hlyx"
UR, UC = 48, 256
CYCLE = ("xlyh", "ylxh")
RING, INCS, FINS = 18, 4, 4
HOP_US, PACE_US = (8.0, 8.0, 8.0, 8.0), 2.8


class Stream:
    def __init__(self, dims, units):
        self.dims, self.units, self.n = dims, units, len(units)
        self.head = [0] * 5
        self.loaded = 0
        self.limit = 0
        self.due = 0.0
        self.born = {}
        self.seen = set()

    def scratch(self):
        parts = []
        for j in range(RING):
            for k in range(4):
                parts.append(pltpu.VMEM((2,) * (3 - k) + (UR, UC), bf16))
        return [pltpu.VMEM((RING,) + GRID + (UR, UC), bf16), pltpu.VMEM((INCS,) + GRID + (UR, UC), bf16), pltpu.VMEM((FINS, UR, UC), f32),
                DMA((RING, 4)), DMA((RING, 4)), DMA((RING, 2)), DMA((FINS, 2)), DMA((self.n, 2))] + parts

    def bind(self, scratch, arrive, outs):
        self.own, self.inc, self.fin, self.send, self.rsem, self.lsem, self.fsend, self.frecv = scratch[:8]
        self.parts = [scratch[8 + 4 * j:12 + 4 * j] for j in range(RING)]
        self.arrive, self.outs = arrive, outs
        me = lax.axis_index("dp")
        self.sec = lax.axis_index("section")
        self.at = dict(x=me % 2, y=me // 2 % 2, l=me // 4 % 2, h=me // 8)

    def peer(self, axis):
        c = dict(self.at)
        c[axis] = 1 - c[axis]
        return {"dp": ((c["h"] * 2 + c["l"]) * 2 + c["y"]) * 2 + c["x"]}

    def greet(self):
        bar = pltpu.get_barrier_semaphore()
        ids = [partner()] + [self.peer(a) for a in AXES]
        for i in ids:
            pl.semaphore_signal(bar, inc=1, device_id=i, device_id_type=MESH)
        pl.semaphore_wait(bar, len(ids))

    def order(self, u):
        return CYCLE[(u % RING) % len(CYCLE)]

    def loads(self, u):
        mine, recv = self.units[u]["src"]
        return (pltpu.make_async_copy(mine, self.own.at[u % RING], self.lsem.at[u % RING, 0]),
                pltpu.make_async_copy(recv, self.inc.at[u % INCS], self.lsem.at[u % RING, 1]))

    def load(self, u):
        for c in self.loads(u):
            c.start()

    def hop(self, u, k):
        order = self.order(u)
        j = u % RING
        spot = tuple(self.at[a] if a in order[:k] else (1 - self.at[a] if a == order[k] else slice(None)) for a in AXES)
        return send_copy(self.own.at[(j,) + spot], self.parts[j][k], self.send.at[j, k], self.rsem.at[j, k], self.peer(order[k]))

    def combine(self, axes, fn):
        if not axes:
            fn({})
            return

        @pl.loop(0, 2)
        def _(i):
            rest = [{}]
            for a in axes[1:]:
                rest = [dict(r, **{a: v}) for r in rest for v in range(2)]
            for r in rest:
                fn(dict(r, **{axes[0]: i}))

    def start(self, u):
        for c in self.loads(u):
            c.wait()
        own, inc = self.own.at[u % RING], self.inc.at[u % INCS]

        def add(at):
            i = tuple(at[a] for a in AXES)
            own[i] = own[i] + inc[i]
        self.combine(AXES, add)
        self.hop(u, 0).start()

    def move(self, u, k):
        order = self.order(u)
        self.hop(u, k).wait()
        own, part = self.own.at[u % RING], self.parts[u % RING][k]
        free = [a for a in AXES if a in order[k + 1:]]
        if k == 3 and u >= FINS:
            self.sent(u - FINS)

        def add(at):
            i = tuple(at[a] if a in at else self.at[a] for a in AXES)
            got = part[tuple(at[a] for a in free) if free else Ellipsis]
            if k == 3:
                self.fin[u % FINS] = own[i].astype(f32) + got.astype(f32)
            else:
                own[i] = own[i] + got
        self.combine(free, add)
        if k == 3:
            self.deliver(u)
        else:
            self.hop(u, k + 1).start()

    def results(self, u):
        for i, (out, row, rows, col, cols, c0) in enumerate(self.units[u]["dst"](self.sec)):
            dst = self.outs[out].at[pl.ds(row, rows), pl.ds(pl.multiple_of(col, LANES), cols)]
            src = self.fin.at[u % FINS, :, pl.ds(c0, cols)]
            yield (pltpu.make_async_copy(src, dst, self.fsend.at[u % FINS, i]),
                   send_copy(src, dst, self.fsend.at[u % FINS, i], self.frecv.at[u, i], partner()))

    def by_layer(self, u, same, other):
        @pl.when(self.sec == self.units[u]["layer"])
        def _():
            for near, away in self.results(u):
                same(near, away)

        @pl.when(self.sec != self.units[u]["layer"])
        def _():
            for near, away in self.results(u):
                other(near, away)

    def deliver(self, u):
        self.by_layer(u, lambda near, away: near.start(), lambda near, away: away.start())

    def sent(self, u):
        self.by_layer(u, lambda near, away: near.wait(), lambda near, away: away.wait_send())

    def plan(self, now, limit=None):
        h, calls = self.head, []
        if limit is not None:
            self.limit = max(self.limit, limit)
        drain = now is None
        for k in (3, 2, 1, 0):
            count = 0
            while h[k + 1] < h[k] and (count < 1 if drain else now - self.born[k, h[k + 1]] >= HOP_US[k]):
                u = h[k + 1]
                calls.append(functools.partial(self.move, u, k))
                self.born[k + 1, u] = now
                h[k + 1] += 1
                count += 1
        count = 0
        while h[0] < self.loaded and (drain or now >= self.due) and count < 2:
            u = h[0]
            calls.append(functools.partial(self.start, u))
            self.born[0, u] = now
            h[0] += 1
            count += 1
            if not drain:
                self.due = max(self.due, now - PACE_US) + PACE_US
        while self.loaded < min(self.limit, h[0] + INCS - 1) and (self.loaded < RING or h[4] > self.loaded - RING):
            key = self.units[self.loaded]["need"]
            if key not in self.seen:
                self.seen.add(key)
                calls.append(functools.partial(self.arrive, key))
            calls.append(functools.partial(self.load, self.loaded))
            self.loaded += 1
        return calls

    def tick(self, now, limit=None):
        for c in self.plan(now, limit):
            c()

    def in_loop(self, i, calls):
        for at, todo in enumerate(calls):
            if todo:
                @pl.when(i == at)
                def _(todo=todo):
                    for c in todo:
                        c()

    def finish(self):
        self.limit = self.n
        while self.head[4] < self.n:
            self.tick(None)
        assert self.head == [self.n] * 5
        for u in range(self.n - FINS, self.n):
            self.sent(u)
        for u in range(self.n):
            @pl.when(self.sec == self.units[u]["layer"])
            def _():
                for _n, away in self.results(u):
                    away.wait_recv()


ATTN_SPOTS = (
    ((1, 0, 384, 256, 0),),
    ((1, 256, 640, 128, 0), (0, 0, 896, 128, 128)),
    ((0, 128, 1536, 128, 0), (0, 768, 1664, 128, 128)),
    ((0, 256, 1280, 256, 0),),
    ((0, 512, 1792, 256, 0),),
    ((0, 1024, 2048, 256, 0),),
)
QKV_CUTS = ((0, 0, 0, 256), (0, 256, 768, 256), (0, 512, 1536, 256), (1, 0, 256, 512), (1, 512, 1024, 256), (2, 0, 1280, 256), (2, 256, 1792, 512))


def gradient_units(bufs):
    units = []
    for l in (1, 0):
        up, down, attn = bufs[l]
        for c in range(6):
            cut = lambda ref: ref.at[:, :, :, :, :, pl.ds(c * UC, UC)]
            units.append(dict(layer=l, src=tuple(map(cut, down)), need=(l, "down", c // 2),
                              dst=lambda sec, c=c: [(3, pl.multiple_of(sec * 2 * UR + c % 2 * UR, 16), UR, c // 2 * UC, UC, 0)]))
        for c in range(6):
            cut = lambda ref: ref.at[:, :, :, :, :, pl.ds(c * UC, UC)]
            units.append(dict(layer=l, src=tuple(map(cut, up)), need=(l, "up", c // 2),
                              dst=lambda sec, c=c: [(2, 0, UR, sec * 6 * UC + c * UC, UC, 0)]))
        for c, spots in enumerate(ATTN_SPOTS):
            cut = lambda ref: ref.at[:, :, :, :, :, pl.ds(c * UC, UC)]
            units.append(dict(layer=l, src=tuple(map(cut, attn)), need=(l, "attn", c // 3),
                              dst=lambda sec, spots=spots: [(out, 0, UR, a + sec * (b - a), n, c0) for out, a, b, n, c0 in spots]))
    return units


LAYER_US = 55.6
TIMES = dict(norm=1.6, down=(3.9, 6.2, 8.5), up=(9.3, 10.3, 11.0, 12.0, 12.8, 13.8, 14.5, 15.5, 16.3, 17.3, 18.0, 19.0), gs=(20.0, 20.8, 21.6), mid=23.3,
             gb=25.2, ga=26.4, dwo=27.9, pairs=(30.5, 33.1, 37.5, 40.2, 42.9, 45.6), early=34.8, dqkv=(46.6, 47.6), gn=(48.7, 49.8, 50.9), end=52.7)


def backward_kernel(dims, names, cot, tokens, y0, cols_h, par_h, *refs):
    saved = [dict(zip(SAVED, refs[:6])), dict(zip(SAVED, refs[6:12]))]
    own = dict(zip(("wqkv", "wo", "w1", "w2"), refs[12:16]))
    oth = dict(zip(("wqkv", "wo", "w1", "w2"), refs[16:20]))
    refs = refs[20:]
    o_gin, refs = refs[0], refs[1:]
    bufs = {}
    for l in (1, 0):
        bufs[l], refs = ((refs[0], refs[1]), (refs[2], refs[3]), (refs[4], refs[5])), refs[6:]
    if dims:
        o_big, o_vec, refs = refs[:4], refs[4:12], refs[12:]
    else:
        o_vec, refs = refs[0], refs[1:]
    s = dict(zip(names, refs))
    lsem, csend, crecv, cnear, esem, vsend, vrecv = refs[len(names):len(names) + 7]
    st_refs = refs[len(names) + 7:]
    g, mid, gs, gmid, act, slope, w1, w2, gd, tr, gh, x, att, att_t, ga, feat, lse, cols, par, vec, stage = (s[n] for n in names[:21])
    sec = lax.axis_index("section")
    me = lax.axis_index("dp")
    T, D = g.shape
    FF = act.shape[1]

    ld = {}
    W2 = ("w2", "w2b", "w2c", "w2d")
    CUTS = tuple(f"c{i}" for i in range(len(QKV_CUTS)))

    def get(n, src, dst):
        keys = tuple(names) + W2[1:] + CUTS
        ld[n] = fetch(src, dst, lsem.at[keys.index(n)])

    def get_w(n, layer, name, src_of, dst):
        keys = tuple(names) + W2[1:] + CUTS
        ld[n] = fetch_layer(sec, layer, src_of(own[name].at[0]), src_of(oth[name]), dst, lsem.at[keys.index(n)])

    def need(*ns):
        for n in ns:
            ld.pop(n).wait()

    def load_w2(l):
        for i, n in enumerate(W2):
            get_w(n, l, "w2", lambda r, i=i: r.at[pl.ds(i * D, D), :], w2.at[pl.ds(i * D, D), :])

    def load_attn_weights(l):
        for n, (block, col, src, cols_n) in zip(CUTS, QKV_CUTS):
            get_w(n, l, "wqkv", lambda r, src=src, cols_n=cols_n: r.at[:, pl.ds(src, cols_n)], w2.at[pl.ds(block * D, D), pl.ds(col, cols_n)])
        get_w(W2[3], l, "wo", lambda r: r, w2.at[pl.ds(3 * D, D), :])

    def tile_copy(l, kind, t, at):
        cs = tile(t, 2 * UC)
        mine, recv = (r.at[:, :, :, :, :, cs] for r in bufs[l][1 - kind])
        buf = lambda h: stage.at[h, :, :, :, :, :, cs]
        return (send_copy(buf(1 - sec), recv, csend.at[l, 3 * kind + at], crecv.at[l, 3 * kind + at], partner()),
                pltpu.make_async_copy(buf(sec), mine, cnear.at[l, 3 * kind + at]))

    def attn_copy(l, part):
        mine, recv = (r.at[:, :, :, :, :, pl.ds(part * D, D)] for r in bufs[l][2])
        buf = lambda h: stage.at[h, :, :, :, :, :, pl.ds(part * D, D)]
        return (send_copy(buf(1 - sec), recv, csend.at[l, 6 + part], crecv.at[l, 6 + part], partner()),
                pltpu.make_async_copy(buf(sec), mine, cnear.at[l, 6 + part]))

    def arrive(key):
        l, kind, t = key
        if kind == "attn":
            attn_copy(l, t)[0].wait_recv()
        else:
            tile_copy(l, 1 if kind == "up" else 0, t, t)[0].wait_recv()

    get("g", cot.at[sec], g)
    get("cols", cols_h, cols)
    get("par", par_h, par)
    get("mid", saved[1]["mid"], mid)
    load_w2(1)
    get("slope", saved[1]["slope"], slope)
    get("act", saved[1]["act"], act)
    get_w("w1", 1, "w1", lambda r: r, w1)
    get("x", y0, x)
    get("att", saved[1]["att"], att)
    get("lse", saved[1]["lse"], lse)
    if dims:
        st = Stream(dims, gradient_units(bufs))
        st.bind(st_refs, arrive, o_big)
        st.greet()
    else:
        st = None
        greet_partner()
    need("cols", "par")
    vec[...] = jnp.zeros_like(vec)

    @pl.loop(0, T // RC)
    def _(i):
        rows = pl.ds(i * RC, RC)
        for odd in (0, 1):
            qf, kf = seg_feature(cols[rows, 0:1], RC, odd)
            feat[2 * odd, rows, :] = qf
            feat[2 * odd + 1, rows, :] = kf

    start_us = 4.0

    def tick(spot, limit):
        if st:
            st.tick(start_us + (1 - l) * LAYER_US + TIMES[spot], limit + (1 - l) * 18)

    def loop_plan(*spots):
        table = [[] for _ in spots]
        for i in range(len(spots[0][0])):
            for calls, (times, limits) in zip(table, spots):
                now = start_us + (1 - l) * LAYER_US + times[i]
                calls.append(st.plan(now, limits[i] + (1 - l) * 18) if st else [])
        return table

    def loop_tick(i, calls):
        if st:
            st.in_loop(i, calls)

    down_row = 7 + FF // D
    low_lane = own_lanes(T, 0)
    for l in (1, 0):
        k1, k2 = 1 + 2 * l, 2 + 2 * l
        need(*(("g",) if l == 1 else ()), "mid")

        @pl.loop(0, T // RC)
        def _(i):
            rows = pl.ds(i * RC, RC)
            low = (g[rows, :].astype(f32) * cols[rows, k2:k2 + 1]).astype(bf16)
            gd[rows, :] = low
            vec[l, down_row:down_row + 1, :] += jnp.sum(low.astype(f32), axis=0, keepdims=True)
            unit, _s = layer_unit(mid[rows, :])
            tr[:, rows] = (unit * par[l, 4:5, :D] + par[l, 5:6, :D]).astype(bf16).T
        if l == 0:
            attn_copy(1, 0)[0].wait_send()
            attn_copy(1, 1)[0].wait_send()
        tick("norm", 0)
        need("act")
        calls, = loop_plan((TIMES["down"], (0, 2, 4)))

        @pl.loop(0, 3)
        def _(c):
            d2 = dot(act[...], gd[:, tile(c, UC)], TN).astype(bf16).reshape(GRID + (4, UR, UC))
            for q in range(4):
                stage[q // 2, :, :, :, :, :, pl.ds(pl.multiple_of((2 * c + q % 2) * UC, UC), UC)] = d2[:, :, :, :, q]
            for k in tile_copy(l, 0, c, c):
                k.start()

            @pl.when(c > 0)
            def _():
                tile_copy(l, 0, c, c - 1)[1].wait()
            loop_tick(c, calls)
        tile_copy(l, 0, 2, 2)[1].wait()
        need(*W2, "slope")
        early, late = loop_plan((TIMES["up"][0::2], (6, 6, 6, 8, 8, 10)), (TIMES["up"][1::2], (6, 6, 8, 8, 10, 10)))

        @pl.loop(0, 6)
        def _(i):
            mine, t = lax.rem(i, 2), i // 2
            h = lax.rem(sec + 1 + mine, 2)
            n = 3 * h + t
            cs = tile(n, 2 * UC)
            low = (dot(gd[...], w2[cs, :], NT) * slope[:, cs].astype(f32)).astype(bf16)
            gh[:, cs] = low
            total = jnp.sum(low.astype(f32), axis=0, keepdims=True)
            for q in range(2):
                m = 2 * n + q
                vec[l, pl.ds(7 + m // 3, 1), tile(lax.rem(m, 3), UC)] = total[:, q * UC:(q + 1) * UC]

            @pl.when(mine == 0)
            def _():
                tile_copy(l, 0, t, t)[0].wait_send()

            @pl.when((mine == 0) & (i > 0))
            def _():
                tile_copy(l, 1, t, t - 1)[1].wait()
            loop_tick(i, early)
            d1 = dot(tr[...], low).astype(bf16)
            stage[h, :, :, :, :, :, tile(t, 2 * UC)] = d1.reshape(GRID + (UR, 2 * UC))
            away, near = tile_copy(l, 1, t, t)

            @pl.when(mine == 0)
            def _():
                away.start()

            @pl.when(mine == 1)
            def _():
                near.start()
            loop_tick(i, late)
        load_attn_weights(l)
        get("qkv", saved[l]["qkv"], slope.at[:, pl.ds(0, 3 * D)])
        if l == 1:
            get("act", saved[0]["act"], act)
        tile_copy(l, 1, 2, 2)[1].wait()
        need("w1")
        calls, = loop_plan((TIMES["gs"], (10, 12, 12)))

        @pl.loop(0, D // W)
        def _(n):
            cs = tile(n, W)
            gs[:, cs] = dot(gh[...], w1[cs, :], NT)
            loop_tick(n, calls)
        if l == 1:
            get_w("w1", 0, "w1", lambda r: r, w1)
        for t in range(3):
            tile_copy(l, 1, t, t)[0].wait_send()

        @pl.loop(0, T // RC)
        def _(i):
            rows = pl.ds(i * RC, RC)
            unit, scale = layer_unit(mid[rows, :])
            low = gs[rows, :]
            vec[l, 5:6, :] += jnp.sum(low * unit, axis=0, keepdims=True)
            vec[l, 6:7, :] += jnp.sum(low, axis=0, keepdims=True)
            gmid[rows, :] = g[rows, :].astype(f32) + unit_back(low, unit, scale, par[l, 4:5, :D])
        tick("mid", 12)
        if l == 1:
            get("mid", saved[0]["mid"], mid)
        need("x", "att")

        @pl.loop(0, T // RC)
        def _(i):
            rows = pl.ds(i * RC, RC)
            low = (gmid[rows, :] * cols[rows, k1:k1 + 1]).astype(bf16)
            gd[rows, :] = low
            vec[l, 4:5, :] += jnp.sum(low.astype(f32), axis=0, keepdims=True)
            unit, _s = layer_unit(x[rows, :].astype(f32))
            tr[:, rows] = (unit * par[l, 0:1, :D] + par[l, 1:2, :D]).astype(bf16).T
            att_t[:, rows] = att[rows, :].T
        tick("gb", 12)
        need(W2[3])

        @pl.loop(0, D // W)
        def _(n):
            cs = tile(n, W)
            ga[:, cs] = dot(gd[...], w2[pl.ds(pl.multiple_of(3 * D + n * W, W), W), :], NT).astype(bf16)
        tick("ga", 12)
        @pl.loop(0, 2)
        def _(h):
            stage[h, :, :, :, :, :, 0:D // 2] = dot(att_t[...], gd[:, tile(h, D // 2)]).astype(bf16).reshape(GRID + (UR, D // 2))
        tick("dwo", 12)
        need("qkv", "lse")

        def pair(p, spots):
            off = pl.multiple_of(p * LANES, LANES)
            qp = slope[:, pl.ds(off, LANES)]
            kp = slope[:, pl.ds(off + D, LANES)]
            vp = slope[:, pl.ds(off + 2 * D, LANES)]
            gp = ga[:, pl.ds(off, LANES)]
            prod = gp.astype(f32) * att[:, pl.ds(off, LANES)].astype(f32)
            dq, dk, dv = [], [], []
            for odd in (0, 1):
                own_l = own_lanes(T, odd)
                base = feature_base(odd)
                lane = lanes_of(T)
                row_d = jnp.sum(jnp.where(own_l, prod, 0.0), axis=1, keepdims=True)
                l3 = split3(-lse[p, :, odd:odd + 1])
                d3 = split3(-row_d)
                qf = feat[2 * odd]
                gf = jnp.zeros_like(gp)
                for j in range(3):
                    qf = jnp.where(lane == base + 8 + j, l3[j], qf)
                    gf = jnp.where(lane == base + j, d3[j], gf)
                q = jnp.where(own_l, qp, qf)
                k = jnp.where(own_l, kp, feat[2 * odd + 1])
                v = jnp.where(own_l, vp, jnp.ones_like(vp))
                gg = jnp.where(own_l, gp, gf)
                prob = jnp.exp(dot(k, q, NT))
                gsc = (prob * dot(v, gg, NT)).astype(bf16)
                dv.append(dot(prob.astype(bf16), gg))
                dk.append(dot(gsc, q))
                dq.append(dot(gsc, k, TN))
            for at, val in zip(spots, ((jnp.where(low_lane, dq[0], dq[1]) * 0.125), jnp.where(low_lane, dk[0], dk[1]), jnp.where(low_lane, dv[0], dv[1]))):
                gh[:, tile(at + p, LANES)] = val.astype(bf16)

        def gradient(part, width, base):
            calls, = loop_plan((TIMES["dqkv"], (15, 15))) if part else (None,)

            @pl.loop(0, 2)
            def _(i):
                h = lax.rem(i + 1 + sec, 2)
                cs = pl.ds(pl.multiple_of(base + h * width, LANES), width)
                stage[h, :, :, :, :, :, (part + 1) * D - width:(part + 1) * D] = dot(tr[...], gh[:, cs]).astype(bf16).reshape(GRID + (UR, width))
                away, near = attn_copy(l, part)

                @pl.when(i == 0)
                def _():
                    away.start()

                @pl.when(i == 1)
                def _():
                    near.start()
                if part == 1:
                    loop_tick(i, calls)

        calls, = loop_plan((TIMES["pairs"][:2], (12, 12)))

        @pl.loop(0, 2)
        def _(p):
            pair(p, (0, 2, 4))
            loop_tick(p, calls)
        gradient(0, D // 2, 0)
        attn_copy(l, 0)[1].wait()
        tick("early", 15)

        calls, = loop_plan((TIMES["pairs"][2:], (15,) * 4))

        @pl.loop(2, D // LANES)
        def _(p):
            pair(p, (4, 8, 12))
            loop_tick(p - 2, calls)
        if l == 1:
            get("slope", saved[0]["slope"], slope)
            get("att", saved[0]["att"], att)
            get("lse", saved[0]["lse"], lse)
        gradient(1, D, D)
        attn_copy(l, 1)[1].wait()
        for row, to, at, n in ((2, 0, 0, 256), (2, 256, 768, 512), (3, 0, 512, 256), (3, 256, 1792, 512)):
            vec[l, row:row + 1, to:to + n] = jnp.sum(gh[:, at:at + n].astype(f32), axis=0, keepdims=True)

        need(*CUTS)
        calls, = loop_plan((TIMES["gn"], (18, 18, 18)))

        @pl.loop(0, D // W)
        def _(n):
            cs = tile(n, W)
            acc = jnp.zeros((T, W), f32)
            for c in range(3):
                acc += dot(gh[:, c * D:(c + 1) * D], w2[pl.ds(pl.multiple_of(c * D + n * W, W), W), :], NT)
            gs[:, cs] = acc
            loop_tick(n, calls)
        if l == 1:
            load_w2(0)

        @pl.loop(0, T // RC)
        def _(i):
            rows = pl.ds(i * RC, RC)
            unit, scale = layer_unit(x[rows, :].astype(f32))
            low = gs[rows, :]
            vec[l, 0:1, :] += jnp.sum(low * unit, axis=0, keepdims=True)
            vec[l, 1:2, :] += jnp.sum(low, axis=0, keepdims=True)
            res = (gmid[rows, :] + unit_back(low, unit, scale, par[l, 0:1, :D])).astype(bf16)
            if l == 1:
                g[rows, :] = res
            else:
                x[rows, :] = res
        if l == 1:
            get("x", tokens.at[sec], x)
        tick("end", 18)

    to_other = lambda src: send_copy(src, o_gin.at[0, sec], esem.at[0], esem.at[1], partner())
    to_own = lambda src: pltpu.make_async_copy(src, o_gin.at[0, sec], esem.at[2])

    @pl.when(sec == 0)
    def _():
        to_own(x).start()
        to_other(g).start()

    @pl.when(sec == 1)
    def _():
        to_own(g).start()
        to_other(x).start()
    if st:
        vown, vgot = s["vown"], s["vgot"]
        def hop(n):
            if n == 0:
                return send_copy(vec.at[1 - sec], vgot.at[0], vsend.at[0], vrecv.at[0], partner())
            return send_copy(vown.at[n - 1], vgot.at[n], vsend.at[n], vrecv.at[n], st.peer(AXES[n - 1]))
        hop(0).start()
        st.tick(None)
        hop(0).wait()
        vown[0] = vec[sec] + vgot[0]
        for n in range(1, 5):
            hop(n).start()
            st.tick(None)
            hop(n).wait()
            vown[n] = vown[n - 1] + vgot[n]
        n_dp = dims[0] * dims[1] * dims[2]
        for o, (row, width) in zip(o_vec, small_spots(D, FF)):
            size = width // n_dp
            at = me * size
            line = vown[4, pl.ds(row + at // D, 1), :]
            line = pltpu.roll(jnp.broadcast_to(line, (8, D)), lax.rem(D - at % D, D), 1)
            o[...] = line[0:1, :size]
        st.finish()
    else:
        for l in (1, 0):
            for t in range(3):
                arrive((l, "down", t))
                arrive((l, "up", t))
            arrive((l, "attn", 0))
            arrive((l, "attn", 1))
        c = pltpu.make_async_copy(vec, o_vec, vsend.at[0])
        c.start()
        c.wait()
    attn_copy(0, 0)[0].wait_send()
    attn_copy(0, 1)[0].wait_send()
    to_own(x).wait()
    to_other(x).wait()


def small_spots(D, FF):
    return ((0, D), (1, D), (2, 2 * D), (4, D), (5, D), (6, D), (7, FF), (7 + FF // D, D))


def backward_call(dims, n_dp, cot, tokens, y0, cols, par, saved0, saved1, own, oth, cid):
    T, D = y0.shape
    FF = own[2].shape[2]
    V = pltpu.VMEM
    sc = dict(
        g=V((T, D), bf16), mid=V((T, D), f32), gs=V((T, D), f32), gmid=V((T, D), f32), act=V((T, FF), bf16), slope=V((T, FF), bf16),
        w1=V((D, FF), bf16), w2=V((FF, D), bf16), gd=V((T, D), bf16), tr=V((D, T), bf16), gh=V((T, FF), bf16), x=V((T, D), bf16), att=V((T, D), bf16),
        att_t=V((D, T), bf16), ga=V((T, D), bf16), feat=V((4, T, LANES), bf16), lse=V((D // LANES, T, 2), f32), cols=V((T, LANES), f32),
        par=V((2, 8, FF), f32), vec=V((2, 16, D), f32), stage=V((2,) + GRID + (UR, 2 * D), bf16))
    sc["qkv"] = V((8, LANES), f32)
    hops = 5
    if dims:
        sc.update(vown=V((5, 16, D), f32), vgot=V((hops, 16, D), f32))
    wide = sds(GRID + (UR, 2 * D), bf16)
    shapes = [sds((1, 2, T, D), bf16)] + [wide] * 12
    specs = [ANY] * len(shapes)
    if dims:
        shapes += [sds((D // n_dp, 3 * D), f32), sds((D // n_dp, D), f32), sds((D // n_dp, FF), f32), sds((FF // n_dp, D), f32)]
        shapes += [sds((1, w // n_dp), f32) for _, w in small_spots(D, FF)]
        specs += [ANY] * 4 + [pl.BlockSpec(memory_space=pltpu.VMEM)] * 8
        stream = Stream(dims, [None] * 36).scratch()
    else:
        shapes += [sds((2, 16, D), f32)]
        specs += [ANY]
        stream = []
    scratch = list(sc.values()) + [DMA((len(sc) + 3 + len(QKV_CUTS),)), DMA((2, 8)), DMA((2, 8)), DMA((2, 8)), DMA((3,)), DMA((hops,)), DMA((hops,))] + stream
    return pl.pallas_call(
        functools.partial(backward_kernel, dims, tuple(sc)), out_shape=tuple(shapes),
        in_specs=[ANY] * 25, out_specs=tuple(specs), scratch_shapes=scratch,
        compiler_params=pltpu.CompilerParams(collective_id=cid, has_side_effects=True, vmem_limit_bytes=LIMIT), name="backward",
    )(cot, tokens, y0, cols, par, *saved0, *saved1, *own, *oth)


def copy_kernel(n, *refs):
    mid, sem = refs[2 * n:3 * n], refs[3 * n]
    into = [pltpu.make_async_copy(refs[i], mid[i], sem.at[0, i]) for i in range(n)]
    out = [pltpu.make_async_copy(mid[i], refs[n + i], sem.at[1, i]) for i in range(n)]
    for c in into:
        c.start()
    for c, o in zip(into, out):
        c.wait()
        o.start()
    for o in out:
        o.wait()


def copy_call(arrays):
    n = len(arrays)
    return pl.pallas_call(
        functools.partial(copy_kernel, n), out_shape=tuple(sds(a.shape, a.dtype) for a in arrays),
        in_specs=[ANY] * n, out_specs=(ANY,) * n, scratch_shapes=[pltpu.VMEM(a.shape, a.dtype) for a in arrays] + [DMA((2, n))],
        compiler_params=pltpu.CompilerParams(vmem_limit_bytes=LIMIT), name="place_outputs",
    )(*arrays)


def dp_dims(n):
    return {16: (2, 2, 4)}.get(n)


def shards(
    tokens, segment_ids, keep_masks, cotangent,
    norm1_gain, norm1_bias, qkv_weight, qv_bias, out_weight, out_bias,
    norm2_gain, norm2_bias, fc1_weight, fc1_bias, fc2_weight, fc2_bias,
):
    sec = lax.axis_index("section")
    n_dp = lax.axis_size("dp")
    dims = dp_dims(n_dp)
    T, D = tokens.shape[1:]
    FF = fc1_weight.shape[2]
    seg = lax.dynamic_index_in_dim(segment_ids, sec, 0, keepdims=False)
    segf = jnp.broadcast_to(seg.astype(f32)[:, None], (T, LANES))
    keep = jnp.pad(keep_masks[0].astype(f32).reshape(4, -1), ((0, 4), (0, LANES - keep_masks.shape[3])))
    own = (qkv_weight, out_weight, fc1_weight, fc2_weight)
    vecs = (norm1_gain, norm1_bias, qv_bias, out_bias, norm2_gain, norm2_bias, fc1_bias, fc2_bias)
    res = first_call(tokens, segf, keep, vecs, own, 0)
    oth, par, cols, y0, saved0 = res[:4], res[4], res[5], res[6], res[7:]
    res = second_call(y0, cols, par, own, oth, 1)
    layer_out, saved1 = res[0], res[1:]
    res = backward_call(dims, n_dp, cotangent, tokens, y0, cols, par, saved0, saved1, own, oth, 2)
    input_grad = res[0]
    if dims:
        layer_out, input_grad, dqkv, dwo, dw1, dw2, n1g, n1b, qv, ob, n2g, n2b, b1, b2 = copy_call((layer_out, input_grad) + tuple(res[13:25]))
    else:
        sums = {}
        for i, l in enumerate((1, 0)):
            up, down, attn = (res[1 + 6 * i + 2 * j].astype(f32) + res[2 + 6 * i + 2 * j].astype(f32) for j in range(3))
            up, attn = up.reshape(D, -1), attn.reshape(D, -1)
            down = lax.all_gather(down, "section").reshape((2, 16, UR, 3, 2, UC))
            down = down.transpose(1, 0, 4, 2, 3, 5).reshape(FF, D)
            sums[l] = [lax.psum_scatter(a, "dp", scatter_dimension=0, tiled=True) for a in (attn, up, down)]
        attn, up, down = (jnp.stack([sums[0][i], sums[1][i]]) for i in range(3))
        attn, up = (lax.dynamic_index_in_dim(lax.all_gather(a, "section"), sec, 1, keepdims=False) for a in (attn, up))
        dw2 = lax.dynamic_index_in_dim(down, sec, 0, keepdims=False)
        dw1 = jnp.concatenate([up[0], up[1]], axis=1)
        cuts = {}
        for c, spots in enumerate(ATTN_SPOTS):
            for out, a, b, n, c0 in spots:
                for h, col in ((0, a), (1, b)):
                    cuts[out, col] = attn[h, :, c * UC + c0:c * UC + c0 + n]
        dqkv, dwo = (jnp.concatenate([cuts[k] for k in sorted(cuts) if k[0] == out], axis=1) for out in (0, 1))
        v = lax.dynamic_index_in_dim(lax.psum(res[13], ("section", "dp")), sec, 0, keepdims=False)
        at = lax.axis_index("dp")
        n1g, n1b, qv, ob, n2g, n2b, b1, b2 = (
            lax.dynamic_slice_in_dim(v[row:row + -(-w // D)].reshape(-1), at * (w // n_dp), w // n_dp)[None] for row, w in small_spots(D, FF))
    return (layer_out, input_grad, n1g, n1b, dqkv[None], qv, dwo[None], ob, n2g, n2b, dw1[None], b1, dw2[None], b2)


def solution(mesh):
    in_specs = (
        P(None, "dp", None), P(None, "dp"), P("section", None, None, "dp"), P(None, "dp", None),
        P("section", None), P("section", None), P("section", None, None), P("section", None),
        P("section", None, None), P("section", None), P("section", None), P("section", None),
        P("section", None, None), P("section", None), P("section", None, None), P("section", None),
    )
    out_specs = (
        P("section", None, "dp", None), P("section", None, "dp", None),
        P("section", "dp"), P("section", "dp"), P("section", "dp", None), P("section", "dp"),
        P("section", "dp", None), P("section", "dp"), P("section", "dp"), P("section", "dp"),
        P("section", "dp", None), P("section", "dp"), P("section", "dp", None), P("section", "dp"),
    )
    return jax.shard_map(shards, mesh=mesh, in_specs=in_specs, out_specs=out_specs, check_vma=False)
```

```python
import functools
import jax
import jax.numpy as jnp
from jax import lax
from jax.experimental import pallas as pl
from jax.experimental.pallas import tpu as pltpu
from jax.sharding import PartitionSpec as P

HEAD_DIM = 64
LANES = 128
keep_rate = 0.9
norm_eps = 1e-06
root_half = 0.7071067811865476
inverse_root = 0.3989422804014327
BIG = 2.0**30
f32, bf16 = jnp.float32, jnp.bfloat16
NN = (((1,), (0,)), ((), ()))
NT = (((1,), (1,)), ((), ()))
TN = (((0,), (0,)), ((), ()))
MESH = pl.DeviceIdType.MESH
ANY = pl.BlockSpec(memory_space=pl.ANY)
DMA = pltpu.SemaphoreType.DMA
LIMIT = 61 * 2**20
RC = 128
W = 256
sds = jax.ShapeDtypeStruct


def dot(a, b, dims=NN):
    return lax.dot_general(a, b, dims, preferred_element_type=f32)


def layer_unit(x):
    center = x - jnp.mean(x, axis=-1, keepdims=True)
    scale = lax.rsqrt(jnp.mean(center * center, axis=-1, keepdims=True) + norm_eps)
    return center * scale, scale


def unit_back(grad, unit, scale, gain):
    scaled = grad * gain
    inner = jnp.mean(scaled, axis=-1, keepdims=True)
    along = jnp.mean(scaled * unit, axis=-1, keepdims=True)
    return scale * (scaled - inner - unit * along)


def gelu_pair(h):
    phi = 0.5 * (1.0 + lax.erf(h * root_half))
    return h * phi, phi + h * jnp.exp(-0.5 * h * h) * inverse_root


def split3(v):
    a = v.astype(bf16)
    r = v - a.astype(f32)
    b = r.astype(bf16)
    c = (r - b.astype(f32)).astype(bf16)
    return a, b, c


def feature_base(odd):
    return 0 if odd else HEAD_DIM


def lanes_of(rows):
    return lax.broadcasted_iota(jnp.int32, (rows, LANES), 1)


def seg_feature(seg, rows, odd):
    base = feature_base(odd)
    lane = lanes_of(rows)
    inside = (lane >= base) & (lane < base + 8)
    same = (lane - base).astype(f32) == seg
    qf = jnp.where(inside & same, BIG, 0.0)
    kf = jnp.where(inside & jnp.logical_not(same), -1.0, 0.0)
    kf = jnp.where((lane >= base + 8) & (lane < base + 11), 1.0, kf)
    return qf.astype(bf16), kf.astype(bf16)


def own_lanes(rows, odd):
    lane = lanes_of(rows)
    return (lane >= HEAD_DIM) if odd else (lane < HEAD_DIM)


def tile(n, width):
    return pl.ds(pl.multiple_of(n * width, LANES), width)


def fetch(src, dst, sem):
    c = pltpu.make_async_copy(src, dst, sem)
    c.start()
    return c


def fetch_layer(sec, layer, own, other, dst, sem):
    c = pltpu.make_async_copy(own, dst, sem)

    @pl.when(sec == layer)
    def _():
        c.start()

    @pl.when(sec != layer)
    def _():
        pltpu.make_async_copy(other, dst, sem).start()
    return c


def partner():
    return {"section": 1 - lax.axis_index("section")}


def greet_partner():
    bar = pltpu.get_barrier_semaphore()
    pl.semaphore_signal(bar, inc=1, device_id=partner(), device_id_type=MESH)
    pl.semaphore_wait(bar, 1)


def send_copy(src, dst, send, recv, dev):
    return pltpu.make_async_remote_copy(src, dst, send, recv, device_id=dev, device_id_type=MESH)


def layer_scratch(T, D, FF):
    return dict(
        x=pltpu.VMEM((T, D), bf16), wqkv=pltpu.VMEM((D, 3 * D), bf16), wo=pltpu.VMEM((D, D), bf16),
        w1=pltpu.VMEM((D, FF), bf16), w2=pltpu.VMEM((FF, D), bf16),
        norm=pltpu.VMEM((T, D), bf16), second=pltpu.VMEM((T, D), bf16), feat=pltpu.VMEM((4, T, LANES), bf16),
        qkv=pltpu.VMEM((T, 3 * D), bf16), lse=pltpu.VMEM((D // LANES, T, 2), f32), att=pltpu.VMEM((T, D), bf16),
        mid=pltpu.VMEM((T, D), f32), act=pltpu.VMEM((T, FF), bf16), slope=pltpu.VMEM((T, FF), bf16),
        y=pltpu.VMEM((T, D), bf16),
    )


def forward_body(l, s, cols, par, ready, store):
    T, D = s["x"].shape
    FF = s["act"].shape[1]
    k1 = 1 + 2 * l

    @pl.loop(0, T // RC)
    def _(i):
        rows = pl.ds(i * RC, RC)
        unit, _s = layer_unit(s["x"][rows, :].astype(f32))
        s["norm"][rows, :] = (unit * par[l, 0:1, :D] + par[l, 1:2, :D]).astype(bf16)
        for odd in (0, 1):
            qf, kf = seg_feature(cols[rows, 0:1], RC, odd)
            s["feat"][2 * odd, rows, :] = qf
            s["feat"][2 * odd + 1, rows, :] = kf

    for part in range(3):
        ready(f"wqkv{part}")

        @pl.loop(0, D // W)
        def _(n):
            cs = pl.ds(pl.multiple_of(part * D + n * W, W), W)
            acc = dot(s["norm"][...], s["wqkv"][:, cs]) + par[l, 2:3, cs]
            s["qkv"][:, cs] = (acc * 0.125 if part == 0 else acc).astype(bf16)
    store("qkv")

    def one_pair(p):
        off = pl.multiple_of(p * LANES, LANES)
        qp = s["qkv"][:, pl.ds(off, LANES)]
        kp = s["qkv"][:, pl.ds(off + D, LANES)]
        vp = s["qkv"][:, pl.ds(off + 2 * D, LANES)]
        outs, scs, vs = [], [], []
        for odd in (0, 1):
            own = own_lanes(T, odd)
            q = jnp.where(own, qp, s["feat"][2 * odd])
            k = jnp.where(own, kp, s["feat"][2 * odd + 1])
            vs.append(jnp.where(own, vp, jnp.ones_like(vp)))
            scs.append(dot(q, k, NT))
        ms = [jnp.max(sc, axis=1, keepdims=True) for sc in scs]
        es = [jnp.exp(sc - m).astype(bf16) for sc, m in zip(scs, ms)]
        for odd in (0, 1):
            base = feature_base(odd)
            o = dot(es[odd], vs[odd])
            total = o[:, base:base + 1]
            outs.append(o / total)
            s["lse"][p, :, odd:odd + 1] = ms[odd] + jnp.log(total)
        s["att"][:, pl.ds(off, LANES)] = jnp.where(own_lanes(T, 0), outs[0], outs[1]).astype(bf16)

    @pl.loop(0, D // LANES // 2)
    def _(pp):
        one_pair(2 * pp)
        one_pair(2 * pp + 1)
    store("lse")
    store("att")
    ready("wo")

    @pl.loop(0, D // W)
    def _(n):
        cs = tile(n, W)
        acc = dot(s["att"][...], s["wo"][:, cs]) + par[l, 3:4, cs]
        s["mid"][:, cs] = s["x"][:, cs].astype(f32) + cols[:, k1:k1 + 1] * acc
    store("mid")

    @pl.loop(0, T // RC)
    def _(i):
        rows = pl.ds(i * RC, RC)
        unit, _s = layer_unit(s["mid"][rows, :])
        s["second"][rows, :] = (unit * par[l, 4:5, :D] + par[l, 5:6, :D]).astype(bf16)
    ready("w1")

    ready("w2")

    @pl.loop(0, FF // D)
    def _(n):
        cs = tile(n, D)
        a, sl = gelu_pair(dot(s["second"][...], s["w1"][:, cs]) + par[l, 6:7, cs])
        s["act"][:, cs] = a.astype(bf16)
        s["slope"][:, cs] = sl.astype(bf16)
    store("act")
    store("slope")

    @pl.loop(0, D // W)
    def _(n):
        cs = tile(n, W)
        acc = dot(s["act"][...], s["w2"][:, cs]) + par[l, 7:8, cs]
        s["y"][:, cs] = (s["mid"][:, cs] + cols[:, k1 + 1:k1 + 2] * acc).astype(bf16)
    store("y")


SAVED = ("qkv", "lse", "att", "mid", "act", "slope")


def saved_shapes(T, D, FF):
    return [sds((T, 3 * D), bf16), sds((D // LANES, T, 2), f32), sds((T, D), bf16), sds((T, D), f32), sds((T, FF), bf16), sds((T, FF), bf16)]


def first_kernel(names, tokens, segs, keep, *refs):
    vec_in, (wqkv, wo, w1, w2) = refs[:8], refs[8:12]
    o_w = refs[12:16]
    o_par, o_cols, o_y = refs[16:19]
    o_saved = dict(zip(SAVED, refs[19:25]))
    scratch = refs[25:]
    s = dict(zip(names, scratch))
    par, cols, keep_s, seg_s, send, recv, lsem, osem = scratch[len(names):]
    sec = lax.axis_index("section")
    T, D = s["x"].shape
    other = partner()
    greet_partner()
    par[:, 2:3, D:2 * D] = jnp.zeros((2, 1, D), f32)
    small, local = [], []

    def both(src, dst):
        n = len(small)
        small.append(send_copy(src, dst, send.at[n], recv.at[n], other))
        local.append(pltpu.make_async_copy(src, dst, lsem.at[n]))
    both(keep.at[0], keep_s.at[sec])
    for row, v in enumerate(vec_in):
        n = v.shape[1]
        if row == 2:
            both(v.at[:, pl.ds(0, D)], par.at[sec, pl.ds(2, 1), pl.ds(0, D)])
            both(v.at[:, pl.ds(D, D)], par.at[sec, pl.ds(2, 1), pl.ds(2 * D, D)])
        else:
            both(v, par.at[sec, pl.ds(row, 1), pl.ds(0, n)])
    for c in small:
        c.start()
    ns = len(small)
    chunks = [(f"wqkv{i}", wqkv.at[0, :, pl.ds(i * D, D)], o_w[0].at[:, pl.ds(i * D, D)], s["wqkv"].at[:, pl.ds(i * D, D)]) for i in range(3)]
    chunks += [(n, w.at[0], o, s[n]) for n, w, o in (("wo", wo, o_w[1]), ("w1", w1, o_w[2]), ("w2", w2, o_w[3]))]
    to_vmem, to_hbm, keep_w = {}, {}, {}
    for i, (n, src, dst, vm) in enumerate(chunks):
        to_vmem[n] = send_copy(src, vm, send.at[ns + i], recv.at[ns + i], other)
        to_hbm[n] = send_copy(src, dst, send.at[ns + i], recv.at[ns + i], other)
        keep_w[n] = pltpu.make_async_copy(vm, dst, lsem.at[ns + i])

    @pl.when(sec == 0)
    def _():
        for c in to_vmem.values():
            c.start()

    @pl.when(sec == 1)
    def _():
        for c in to_hbm.values():
            c.start()
    x_in = fetch(tokens.at[sec], s["x"], lsem.at[ns + 6])
    g_in = fetch(segs, seg_s, lsem.at[ns + 7])
    for c in local:
        c.start()
    loads = {n: pltpu.make_async_copy(src, vm, lsem.at[ns + i]) for i, (n, src, dst, vm) in enumerate(chunks)}

    @pl.when(sec == 0)
    def _():
        for c in loads.values():
            c.start()
    for c in local:
        c.wait()
    for c in small:
        c.wait()
    x_in.wait()
    g_in.wait()

    cols[...] = jnp.broadcast_to(seg_s[pl.ds(sec, 1), :].astype(f32), (LANES, T)).T

    @pl.loop(0, T // RC)
    def _(i):
        rows = pl.ds(i * RC, RC)
        lane = lanes_of(RC)
        seg = cols[rows, 0:1]
        ids = keep_s.shape[3]
        hot = lax.broadcasted_iota(jnp.int32, (RC, ids), 1).astype(f32) == seg
        out = jnp.where(lane == 0, seg, 0.0)
        for l in range(2):
            for b in range(2):
                flag = jnp.sum(jnp.where(hot, keep_s[l, sec, b:b + 1, :].astype(f32), 0.0), axis=1, keepdims=True) / keep_rate
                out = jnp.where(lane == 1 + 2 * l + b, flag, out)
        cols[rows, :] = out
    outs = [fetch(par, o_par, osem.at[7]), fetch(cols, o_cols, osem.at[8])]
    o_saved["y"] = o_y
    spots = list(SAVED) + ["y"]

    def ready(n):
        @pl.when(sec == 0)
        def _():
            loads[n].wait()

        @pl.when(sec == 1)
        def _():
            to_vmem[n].wait_recv()
            keep_w[n].start()

    def store(n):
        outs.append(fetch(s[n], o_saved[n], osem.at[spots.index(n)]))

    forward_body(0, s, cols, par, ready, store)

    @pl.when(sec == 0)
    def _():
        for c in to_hbm.values():
            c.wait_recv()

    @pl.when(sec == 1)
    def _():
        for c in keep_w.values():
            c.wait()
    for c in to_vmem.values():
        c.wait_send()
    for c in outs:
        c.wait()


def first_call(tokens, segs, keep, vecs, weights, cid):
    _, T, D = tokens.shape
    FF = weights[2].shape[2]
    sc = layer_scratch(T, D, FF)
    names = tuple(sc)
    ns = 10
    shapes = [sds(w.shape[1:], bf16) for w in weights] + [sds((2, 8, FF), f32), sds((T, LANES), f32), sds((T, D), bf16)] + saved_shapes(T, D, FF)
    return pl.pallas_call(
        functools.partial(first_kernel, names), out_shape=tuple(shapes),
        in_specs=[ANY] * 15, out_specs=(ANY,) * len(shapes),
        scratch_shapes=list(sc.values()) + [
            pltpu.VMEM((2, 8, FF), f32), pltpu.VMEM((T, LANES), f32), pltpu.VMEM((2,) + keep.shape[1:], jnp.int32), pltpu.VMEM(segs.shape, jnp.int32),
            DMA((ns + 6,)), DMA((ns + 6,)), DMA((ns + 8,)), DMA((9,))],
        compiler_params=pltpu.CompilerParams(collective_id=cid, has_side_effects=True, vmem_limit_bytes=LIMIT), name="forward_first",
    )(tokens, segs, keep, *vecs, *weights)


def second_kernel(names, x_hbm, cols_hbm, par_hbm, *refs):
    own, oth = refs[:4], refs[4:8]
    o_out = refs[8]
    o_saved = dict(zip(SAVED, refs[9:15]))
    scratch = refs[15:]
    s = dict(zip(names, scratch))
    par, cols, lsem, osem, esem = scratch[len(names):]
    sec = lax.axis_index("section")
    greet_partner()
    first = [fetch(x_hbm, s["x"], lsem.at[4]), fetch(cols_hbm, cols, lsem.at[5]), fetch(par_hbm, par, lsem.at[6])]
    loads = {n: fetch_layer(sec, 1, own[i].at[0], oth[i], s[n], lsem.at[i]) for i, n in enumerate(("wqkv", "wo", "w1", "w2"))}
    for c in first:
        c.wait()
    outs = []

    def ready(n):
        if n == "wqkv0":
            loads["wqkv"].wait()
        elif n in loads:
            loads[n].wait()

    def store(n):
        if n != "y":
            outs.append(fetch(s[n], o_saved[n], osem.at[SAVED.index(n)]))

    to_other = lambda src: send_copy(src, o_out.at[0, sec], esem.at[0], esem.at[1], partner())
    to_own = lambda src: pltpu.make_async_copy(src, o_out.at[0, sec], esem.at[2])

    forward_body(1, s, cols, par, ready, store)

    @pl.when(sec == 0)
    def _():
        to_own(s["x"]).start()
        to_other(s["y"]).start()

    @pl.when(sec == 1)
    def _():
        to_own(s["y"]).start()
        to_other(s["x"]).start()
    to_own(s["x"]).wait()
    to_other(s["x"]).wait()
    for c in outs:
        c.wait()


def second_call(x, cols, par, own, oth, cid):
    T, D = x.shape
    FF = own[2].shape[2]
    sc = layer_scratch(T, D, FF)
    shapes = [sds((1, 2, T, D), bf16)] + saved_shapes(T, D, FF)
    return pl.pallas_call(
        functools.partial(second_kernel, tuple(sc)), out_shape=tuple(shapes),
        in_specs=[ANY] * 11, out_specs=(ANY,) * len(shapes),
        scratch_shapes=list(sc.values()) + [pltpu.VMEM((2, 8, FF), f32), pltpu.VMEM((T, LANES), f32), DMA((7,)), DMA((6,)), DMA((3,))],
        compiler_params=pltpu.CompilerParams(collective_id=cid, has_side_effects=True, vmem_limit_bytes=LIMIT), name="forward_second",
    )(x, cols, par, *own, *oth)


GRID = (2, 2, 2, 2)
AXES = "hlyx"
UR, UC = 48, 256
CYCLE = ("xlyh", "ylxh")
RING, INCS, FINS = 18, 4, 4
HOP_US, PACE_US = 8.0, 2.4


class Stream:
    def __init__(self, dims, units):
        self.dims, self.units, self.n = dims, units, len(units)
        self.head = [0] * 5
        self.loaded = 0
        self.limit = 0
        self.due = 0.0
        self.born = {}
        self.seen = set()

    def scratch(self):
        parts = []
        for j in range(RING):
            for k in range(4):
                parts.append(pltpu.VMEM((2,) * (3 - k) + (UR, UC), bf16))
        return [pltpu.VMEM((RING,) + GRID + (UR, UC), bf16), pltpu.VMEM((INCS,) + GRID + (UR, UC), bf16), pltpu.VMEM((FINS, UR, UC), f32),
                DMA((RING, 4)), DMA((RING, 4)), DMA((RING, 2)), DMA((FINS, 2)), DMA((self.n, 2))] + parts

    def bind(self, scratch, arrive, outs):
        self.own, self.inc, self.fin, self.send, self.rsem, self.lsem, self.fsend, self.frecv = scratch[:8]
        self.parts = [scratch[8 + 4 * j:12 + 4 * j] for j in range(RING)]
        self.arrive, self.outs = arrive, outs
        me = lax.axis_index("dp")
        self.sec = lax.axis_index("section")
        self.at = dict(x=me % 2, y=me // 2 % 2, l=me // 4 % 2, h=me // 8)

    def peer(self, axis):
        c = dict(self.at)
        c[axis] = 1 - c[axis]
        return {"dp": ((c["h"] * 2 + c["l"]) * 2 + c["y"]) * 2 + c["x"]}

    def greet(self):
        bar = pltpu.get_barrier_semaphore()
        ids = [partner()] + [self.peer(a) for a in AXES]
        for i in ids:
            pl.semaphore_signal(bar, inc=1, device_id=i, device_id_type=MESH)
        pl.semaphore_wait(bar, len(ids))

    def order(self, u):
        return CYCLE[(u % RING) % len(CYCLE)]

    def loads(self, u):
        mine, recv = self.units[u]["src"]
        return (pltpu.make_async_copy(mine, self.own.at[u % RING], self.lsem.at[u % RING, 0]),
                pltpu.make_async_copy(recv, self.inc.at[u % INCS], self.lsem.at[u % RING, 1]))

    def load(self, u):
        for c in self.loads(u):
            c.start()

    def hop(self, u, k):
        order = self.order(u)
        j = u % RING
        spot = tuple(self.at[a] if a in order[:k] else (1 - self.at[a] if a == order[k] else slice(None)) for a in AXES)
        return send_copy(self.own.at[(j,) + spot], self.parts[j][k], self.send.at[j, k], self.rsem.at[j, k], self.peer(order[k]))

    def combine(self, axes, fn):
        if not axes:
            fn({})
            return

        @pl.loop(0, 2)
        def _(i):
            rest = [{}]
            for a in axes[1:]:
                rest = [dict(r, **{a: v}) for r in rest for v in range(2)]
            for r in rest:
                fn(dict(r, **{axes[0]: i}))

    def start(self, u):
        for c in self.loads(u):
            c.wait()
        own, inc = self.own.at[u % RING], self.inc.at[u % INCS]

        def add(at):
            i = tuple(at[a] for a in AXES)
            own[i] = own[i] + inc[i]
        self.combine(AXES, add)
        self.hop(u, 0).start()

    def move(self, u, k):
        order = self.order(u)
        self.hop(u, k).wait()
        own, part = self.own.at[u % RING], self.parts[u % RING][k]
        free = [a for a in AXES if a in order[k + 1:]]
        if k == 3 and u >= FINS:
            self.sent(u - FINS)

        def add(at):
            i = tuple(at[a] if a in at else self.at[a] for a in AXES)
            got = part[tuple(at[a] for a in free) if free else Ellipsis]
            if k == 3:
                self.fin[u % FINS] = own[i].astype(f32) + got.astype(f32)
            else:
                own[i] = own[i] + got
        self.combine(free, add)
        if k == 3:
            self.deliver(u)
        else:
            self.hop(u, k + 1).start()

    def results(self, u):
        for i, (out, row, rows, col, cols, c0) in enumerate(self.units[u]["dst"](self.sec)):
            dst = self.outs[out].at[pl.ds(row, rows), pl.ds(pl.multiple_of(col, LANES), cols)]
            src = self.fin.at[u % FINS, :, pl.ds(c0, cols)]
            yield (pltpu.make_async_copy(src, dst, self.fsend.at[u % FINS, i]),
                   send_copy(src, dst, self.fsend.at[u % FINS, i], self.frecv.at[u, i], partner()))

    def by_layer(self, u, same, other):
        @pl.when(self.sec == self.units[u]["layer"])
        def _():
            for near, away in self.results(u):
                same(near, away)

        @pl.when(self.sec != self.units[u]["layer"])
        def _():
            for near, away in self.results(u):
                other(near, away)

    def deliver(self, u):
        self.by_layer(u, lambda near, away: near.start(), lambda near, away: away.start())

    def sent(self, u):
        self.by_layer(u, lambda near, away: near.wait(), lambda near, away: away.wait_send())

    def plan(self, now, limit=None):
        h, calls = self.head, []
        if limit is not None:
            self.limit = max(self.limit, limit)
        drain = now is None
        for k in (3, 2, 1, 0):
            count = 0
            while h[k + 1] < h[k] and (count < 1 if drain else now - self.born[k, h[k + 1]] >= HOP_US):
                u = h[k + 1]
                calls.append(functools.partial(self.move, u, k))
                self.born[k + 1, u] = now
                h[k + 1] += 1
                count += 1
        count = 0
        while h[0] < self.loaded and (drain or now >= self.due) and count < 2:
            u = h[0]
            calls.append(functools.partial(self.start, u))
            self.born[0, u] = now
            h[0] += 1
            count += 1
            if not drain:
                self.due = max(self.due, now - PACE_US) + PACE_US
        while self.loaded < min(self.limit, h[0] + INCS - 1) and (self.loaded < RING or h[4] > self.loaded - RING):
            key = self.units[self.loaded]["need"]
            if key not in self.seen:
                self.seen.add(key)
                calls.append(functools.partial(self.arrive, key))
            calls.append(functools.partial(self.load, self.loaded))
            self.loaded += 1
        return calls

    def tick(self, now, limit=None):
        for c in self.plan(now, limit):
            c()

    def in_loop(self, i, calls):
        for at, todo in enumerate(calls):
            if todo:
                @pl.when(i == at)
                def _(todo=todo):
                    for c in todo:
                        c()

    def finish(self):
        self.limit = self.n
        while self.head[4] < self.n:
            self.tick(None)
        assert self.head == [self.n] * 5
        for u in range(self.n - FINS, self.n):
            self.sent(u)
        for u in range(self.n):
            @pl.when(self.sec == self.units[u]["layer"])
            def _():
                for _n, away in self.results(u):
                    away.wait_recv()


ATTN_SPOTS = (
    ((1, 0, 384, 256, 0),),
    ((1, 256, 640, 128, 0), (0, 0, 896, 128, 128)),
    ((0, 128, 1536, 128, 0), (0, 768, 1664, 128, 128)),
    ((0, 256, 1280, 256, 0),),
    ((0, 512, 1792, 256, 0),),
    ((0, 1024, 2048, 256, 0),),
)
QKV_CUTS = ((0, 0, 0, 256), (0, 256, 768, 256), (0, 512, 1536, 256), (1, 0, 256, 512), (1, 512, 1024, 256), (2, 0, 1280, 256), (2, 256, 1792, 512))


def gradient_units(bufs):
    units = []
    for l in (1, 0):
        up, down, attn = bufs[l]
        for c in range(6):
            cut = lambda ref: ref.at[:, :, :, :, :, pl.ds(c * UC, UC)]
            units.append(dict(layer=l, src=tuple(map(cut, down)), need=(l, "down", c // 2),
                              dst=lambda sec, c=c: [(3, pl.multiple_of(sec * 2 * UR + c % 2 * UR, 16), UR, c // 2 * UC, UC, 0)]))
        for c in range(6):
            cut = lambda ref: ref.at[:, :, :, :, :, pl.ds(c * UC, UC)]
            units.append(dict(layer=l, src=tuple(map(cut, up)), need=(l, "up", c // 2),
                              dst=lambda sec, c=c: [(2, 0, UR, sec * 6 * UC + c * UC, UC, 0)]))
        for c, spots in enumerate(ATTN_SPOTS):
            cut = lambda ref: ref.at[:, :, :, :, :, pl.ds(c * UC, UC)]
            units.append(dict(layer=l, src=tuple(map(cut, attn)), need=(l, "attn", c // 3),
                              dst=lambda sec, spots=spots: [(out, 0, UR, a + sec * (b - a), n, c0) for out, a, b, n, c0 in spots]))
    return units


LAYER_US = 55.6
TIMES = dict(norm=1.6, down=(3.9, 6.2, 8.5), up=(9.3, 10.3, 11.0, 12.0, 12.8, 13.8, 14.5, 15.5, 16.3, 17.3, 18.0, 19.0), gs=(20.0, 20.8, 21.6), mid=23.3,
             gb=25.2, ga=26.4, dwo=27.9, pairs=(30.5, 33.1, 37.5, 40.2, 42.9, 45.6), early=34.8, dqkv=(46.6, 47.6), gn=(48.7, 49.8, 50.9), end=52.7)


def backward_kernel(dims, names, cot, tokens, y0, cols_h, par_h, *refs):
    saved = [dict(zip(SAVED, refs[:6])), dict(zip(SAVED, refs[6:12]))]
    own = dict(zip(("wqkv", "wo", "w1", "w2"), refs[12:16]))
    oth = dict(zip(("wqkv", "wo", "w1", "w2"), refs[16:20]))
    refs = refs[20:]
    o_gin, refs = refs[0], refs[1:]
    bufs = {}
    for l in (1, 0):
        bufs[l], refs = ((refs[0], refs[1]), (refs[2], refs[3]), (refs[4], refs[5])), refs[6:]
    if dims:
        o_big, o_vec, refs = refs[:4], refs[4:12], refs[12:]
    else:
        o_vec, refs = refs[0], refs[1:]
    s = dict(zip(names, refs))
    lsem, csend, crecv, cnear, esem, vsend, vrecv = refs[len(names):len(names) + 7]
    st_refs = refs[len(names) + 7:]
    g, mid, gs, gmid, act, slope, w1, w2, gd, tr, gh, x, att, att_t, ga, feat, lse, cols, par, vec, stage = (s[n] for n in names[:21])
    sec = lax.axis_index("section")
    me = lax.axis_index("dp")
    T, D = g.shape
    FF = act.shape[1]

    ld = {}
    W2 = ("w2", "w2b", "w2c", "w2d")
    CUTS = tuple(f"c{i}" for i in range(len(QKV_CUTS)))

    def get(n, src, dst):
        keys = tuple(names) + W2[1:] + CUTS
        ld[n] = fetch(src, dst, lsem.at[keys.index(n)])

    def get_w(n, layer, name, src_of, dst):
        keys = tuple(names) + W2[1:] + CUTS
        ld[n] = fetch_layer(sec, layer, src_of(own[name].at[0]), src_of(oth[name]), dst, lsem.at[keys.index(n)])

    def need(*ns):
        for n in ns:
            ld.pop(n).wait()

    def load_w2(l):
        for i, n in enumerate(W2):
            get_w(n, l, "w2", lambda r, i=i: r.at[pl.ds(i * D, D), :], w2.at[pl.ds(i * D, D), :])

    def load_attn_weights(l):
        for n, (block, col, src, cols_n) in zip(CUTS, QKV_CUTS):
            get_w(n, l, "wqkv", lambda r, src=src, cols_n=cols_n: r.at[:, pl.ds(src, cols_n)], w2.at[pl.ds(block * D, D), pl.ds(col, cols_n)])
        get_w(W2[3], l, "wo", lambda r: r, w2.at[pl.ds(3 * D, D), :])

    def tile_copy(l, kind, t, at):
        cs = tile(t, 2 * UC)
        mine, recv = (r.at[:, :, :, :, :, cs] for r in bufs[l][1 - kind])
        buf = lambda h: stage.at[h, :, :, :, :, :, cs]
        return (send_copy(buf(1 - sec), recv, csend.at[l, 3 * kind + at], crecv.at[l, 3 * kind + at], partner()),
                pltpu.make_async_copy(buf(sec), mine, cnear.at[l, 3 * kind + at]))

    def attn_copy(l, part):
        mine, recv = (r.at[:, :, :, :, :, pl.ds(part * D, D)] for r in bufs[l][2])
        buf = lambda h: stage.at[h, :, :, :, :, :, pl.ds(part * D, D)]
        return (send_copy(buf(1 - sec), recv, csend.at[l, 6 + part], crecv.at[l, 6 + part], partner()),
                pltpu.make_async_copy(buf(sec), mine, cnear.at[l, 6 + part]))

    def arrive(key):
        l, kind, t = key
        if kind == "attn":
            attn_copy(l, t)[0].wait_recv()
        else:
            tile_copy(l, 1 if kind == "up" else 0, t, t)[0].wait_recv()

    get("g", cot.at[sec], g)
    get("cols", cols_h, cols)
    get("par", par_h, par)
    get("act", saved[1]["act"], act)
    get("mid", saved[1]["mid"], mid)
    get("slope", saved[1]["slope"], slope)
    load_w2(1)
    get_w("w1", 1, "w1", lambda r: r, w1)
    get("x", y0, x)
    get("att", saved[1]["att"], att)
    get("lse", saved[1]["lse"], lse)
    if dims:
        st = Stream(dims, gradient_units(bufs))
        st.bind(st_refs, arrive, o_big)
        st.greet()
    else:
        st = None
        greet_partner()
    need("cols", "par")
    vec[...] = jnp.zeros_like(vec)

    @pl.loop(0, T // RC)
    def _(i):
        rows = pl.ds(i * RC, RC)
        for odd in (0, 1):
            qf, kf = seg_feature(cols[rows, 0:1], RC, odd)
            feat[2 * odd, rows, :] = qf
            feat[2 * odd + 1, rows, :] = kf

    start_us = 4.0

    def tick(spot, limit):
        if st:
            st.tick(start_us + (1 - l) * LAYER_US + TIMES[spot], limit + (1 - l) * 18)

    def loop_plan(*spots):
        table = [[] for _ in spots]
        for i in range(len(spots[0][0])):
            for calls, (times, limits) in zip(table, spots):
                now = start_us + (1 - l) * LAYER_US + times[i]
                calls.append(st.plan(now, limits[i] + (1 - l) * 18) if st else [])
        return table

    def loop_tick(i, calls):
        if st:
            st.in_loop(i, calls)

    down_row = 7 + FF // D
    low_lane = own_lanes(T, 0)
    for l in (1, 0):
        k1, k2 = 1 + 2 * l, 2 + 2 * l
        need(*(("g",) if l == 1 else ()), "mid")

        @pl.loop(0, T // RC)
        def _(i):
            rows = pl.ds(i * RC, RC)
            low = (g[rows, :].astype(f32) * cols[rows, k2:k2 + 1]).astype(bf16)
            gd[rows, :] = low
            vec[l, down_row:down_row + 1, :] += jnp.sum(low.astype(f32), axis=0, keepdims=True)
            unit, _s = layer_unit(mid[rows, :])
            tr[:, rows] = (unit * par[l, 4:5, :D] + par[l, 5:6, :D]).astype(bf16).T
        if l == 0:
            attn_copy(1, 0)[0].wait_send()
            attn_copy(1, 1)[0].wait_send()
        tick("norm", 0)
        need("act")
        calls, = loop_plan((TIMES["down"], (0, 2, 4)))

        @pl.loop(0, 3)
        def _(c):
            d2 = dot(act[...], gd[:, tile(c, UC)], TN).astype(bf16).reshape(GRID + (4, UR, UC))
            for q in range(4):
                stage[q // 2, :, :, :, :, :, pl.ds(pl.multiple_of((2 * c + q % 2) * UC, UC), UC)] = d2[:, :, :, :, q]
            for k in tile_copy(l, 0, c, c):
                k.start()

            @pl.when(c > 0)
            def _():
                tile_copy(l, 0, c, c - 1)[1].wait()
            loop_tick(c, calls)
        tile_copy(l, 0, 2, 2)[1].wait()
        need(*W2, "slope")
        early, late = loop_plan((TIMES["up"][0::2], (6, 6, 6, 8, 8, 10)), (TIMES["up"][1::2], (6, 6, 8, 8, 10, 10)))

        @pl.loop(0, 6)
        def _(i):
            mine, t = lax.rem(i, 2), i // 2
            h = lax.rem(sec + 1 + mine, 2)
            n = 3 * h + t
            cs = tile(n, 2 * UC)
            low = (dot(gd[...], w2[cs, :], NT) * slope[:, cs].astype(f32)).astype(bf16)
            gh[:, cs] = low
            total = jnp.sum(low.astype(f32), axis=0, keepdims=True)
            for q in range(2):
                m = 2 * n + q
                vec[l, pl.ds(7 + m // 3, 1), tile(lax.rem(m, 3), UC)] = total[:, q * UC:(q + 1) * UC]

            @pl.when(mine == 0)
            def _():
                tile_copy(l, 0, t, t)[0].wait_send()

            @pl.when((mine == 0) & (i > 0))
            def _():
                tile_copy(l, 1, t, t - 1)[1].wait()
            loop_tick(i, early)
            d1 = dot(tr[...], low).astype(bf16)
            stage[h, :, :, :, :, :, tile(t, 2 * UC)] = d1.reshape(GRID + (UR, 2 * UC))
            away, near = tile_copy(l, 1, t, t)

            @pl.when(mine == 0)
            def _():
                away.start()

            @pl.when(mine == 1)
            def _():
                near.start()
            loop_tick(i, late)
        load_attn_weights(l)
        get("qkv", saved[l]["qkv"], slope.at[:, pl.ds(0, 3 * D)])
        if l == 1:
            get("act", saved[0]["act"], act)
        tile_copy(l, 1, 2, 2)[1].wait()
        need("w1")
        calls, = loop_plan((TIMES["gs"], (10, 12, 12)))

        @pl.loop(0, D // W)
        def _(n):
            cs = tile(n, W)
            gs[:, cs] = dot(gh[...], w1[cs, :], NT)
            loop_tick(n, calls)
        if l == 1:
            get_w("w1", 0, "w1", lambda r: r, w1)
        for t in range(3):
            tile_copy(l, 1, t, t)[0].wait_send()

        @pl.loop(0, T // RC)
        def _(i):
            rows = pl.ds(i * RC, RC)
            unit, scale = layer_unit(mid[rows, :])
            low = gs[rows, :]
            vec[l, 5:6, :] += jnp.sum(low * unit, axis=0, keepdims=True)
            vec[l, 6:7, :] += jnp.sum(low, axis=0, keepdims=True)
            gmid[rows, :] = g[rows, :].astype(f32) + unit_back(low, unit, scale, par[l, 4:5, :D])
        tick("mid", 12)
        if l == 1:
            get("mid", saved[0]["mid"], mid)
        need("x", "att")

        @pl.loop(0, T // RC)
        def _(i):
            rows = pl.ds(i * RC, RC)
            low = (gmid[rows, :] * cols[rows, k1:k1 + 1]).astype(bf16)
            gd[rows, :] = low
            vec[l, 4:5, :] += jnp.sum(low.astype(f32), axis=0, keepdims=True)
            unit, _s = layer_unit(x[rows, :].astype(f32))
            tr[:, rows] = (unit * par[l, 0:1, :D] + par[l, 1:2, :D]).astype(bf16).T
            att_t[:, rows] = att[rows, :].T
        tick("gb", 12)
        need(W2[3])

        @pl.loop(0, D // W)
        def _(n):
            cs = tile(n, W)
            ga[:, cs] = dot(gd[...], w2[pl.ds(pl.multiple_of(3 * D + n * W, W), W), :], NT).astype(bf16)
        tick("ga", 12)
        @pl.loop(0, 2)
        def _(h):
            stage[h, :, :, :, :, :, 0:D // 2] = dot(att_t[...], gd[:, tile(h, D // 2)]).astype(bf16).reshape(GRID + (UR, D // 2))
        tick("dwo", 12)
        need("qkv", "lse")

        def pair(p, spots):
            off = pl.multiple_of(p * LANES, LANES)
            qp = slope[:, pl.ds(off, LANES)]
            kp = slope[:, pl.ds(off + D, LANES)]
            vp = slope[:, pl.ds(off + 2 * D, LANES)]
            gp = ga[:, pl.ds(off, LANES)]
            prod = gp.astype(f32) * att[:, pl.ds(off, LANES)].astype(f32)
            dq, dk, dv = [], [], []
            for odd in (0, 1):
                own_l = own_lanes(T, odd)
                base = feature_base(odd)
                lane = lanes_of(T)
                row_d = jnp.sum(jnp.where(own_l, prod, 0.0), axis=1, keepdims=True)
                l3 = split3(-lse[p, :, odd:odd + 1])
                d3 = split3(-row_d)
                qf = feat[2 * odd]
                gf = jnp.zeros_like(gp)
                for j in range(3):
                    qf = jnp.where(lane == base + 8 + j, l3[j], qf)
                    gf = jnp.where(lane == base + j, d3[j], gf)
                q = jnp.where(own_l, qp, qf)
                k = jnp.where(own_l, kp, feat[2 * odd + 1])
                v = jnp.where(own_l, vp, jnp.ones_like(vp))
                gg = jnp.where(own_l, gp, gf)
                prob = jnp.exp(dot(k, q, NT))
                gsc = (prob * dot(v, gg, NT)).astype(bf16)
                dv.append(dot(prob.astype(bf16), gg))
                dk.append(dot(gsc, q))
                dq.append(dot(gsc, k, TN))
            for at, val in zip(spots, ((jnp.where(low_lane, dq[0], dq[1]) * 0.125), jnp.where(low_lane, dk[0], dk[1]), jnp.where(low_lane, dv[0], dv[1]))):
                gh[:, tile(at + p, LANES)] = val.astype(bf16)

        def gradient(part, width, base):
            calls, = loop_plan((TIMES["dqkv"], (15, 15))) if part else (None,)

            @pl.loop(0, 2)
            def _(i):
                h = lax.rem(i + 1 + sec, 2)
                cs = pl.ds(pl.multiple_of(base + h * width, LANES), width)
                stage[h, :, :, :, :, :, (part + 1) * D - width:(part + 1) * D] = dot(tr[...], gh[:, cs]).astype(bf16).reshape(GRID + (UR, width))
                away, near = attn_copy(l, part)

                @pl.when(i == 0)
                def _():
                    away.start()

                @pl.when(i == 1)
                def _():
                    near.start()
                if part == 1:
                    loop_tick(i, calls)

        calls, = loop_plan((TIMES["pairs"][:2], (12, 12)))

        @pl.loop(0, 2)
        def _(p):
            pair(p, (0, 2, 4))
            loop_tick(p, calls)
        gradient(0, D // 2, 0)
        attn_copy(l, 0)[1].wait()
        tick("early", 15)

        calls, = loop_plan((TIMES["pairs"][2:], (15,) * 4))

        @pl.loop(2, D // LANES)
        def _(p):
            pair(p, (4, 8, 12))
            loop_tick(p - 2, calls)
        if l == 1:
            get("slope", saved[0]["slope"], slope)
            get("att", saved[0]["att"], att)
            get("lse", saved[0]["lse"], lse)
        gradient(1, D, D)
        attn_copy(l, 1)[1].wait()
        for row, to, at, n in ((2, 0, 0, 256), (2, 256, 768, 512), (3, 0, 512, 256), (3, 256, 1792, 512)):
            vec[l, row:row + 1, to:to + n] = jnp.sum(gh[:, at:at + n].astype(f32), axis=0, keepdims=True)

        need(*CUTS)
        calls, = loop_plan((TIMES["gn"], (18, 18, 18)))

        @pl.loop(0, D // W)
        def _(n):
            cs = tile(n, W)
            acc = jnp.zeros((T, W), f32)
            for c in range(3):
                acc += dot(gh[:, c * D:(c + 1) * D], w2[pl.ds(pl.multiple_of(c * D + n * W, W), W), :], NT)
            gs[:, cs] = acc
            loop_tick(n, calls)
        if l == 1:
            load_w2(0)

        @pl.loop(0, T // RC)
        def _(i):
            rows = pl.ds(i * RC, RC)
            unit, scale = layer_unit(x[rows, :].astype(f32))
            low = gs[rows, :]
            vec[l, 0:1, :] += jnp.sum(low * unit, axis=0, keepdims=True)
            vec[l, 1:2, :] += jnp.sum(low, axis=0, keepdims=True)
            res = (gmid[rows, :] + unit_back(low, unit, scale, par[l, 0:1, :D])).astype(bf16)
            if l == 1:
                g[rows, :] = res
            else:
                x[rows, :] = res
        if l == 1:
            get("x", tokens.at[sec], x)
        tick("end", 18)

    to_other = lambda src: send_copy(src, o_gin.at[0, sec], esem.at[0], esem.at[1], partner())
    to_own = lambda src: pltpu.make_async_copy(src, o_gin.at[0, sec], esem.at[2])

    @pl.when(sec == 0)
    def _():
        to_own(x).start()
        to_other(g).start()

    @pl.when(sec == 1)
    def _():
        to_own(g).start()
        to_other(x).start()
    if st:
        vown, vgot = s["vown"], s["vgot"]
        def hop(n):
            if n == 0:
                return send_copy(vec.at[1 - sec], vgot.at[0], vsend.at[0], vrecv.at[0], partner())
            return send_copy(vown.at[n - 1], vgot.at[n], vsend.at[n], vrecv.at[n], st.peer(AXES[n - 1]))
        hop(0).start()
        st.tick(None)
        hop(0).wait()
        vown[0] = vec[sec] + vgot[0]
        for n in range(1, 5):
            hop(n).start()
            st.tick(None)
            st.tick(None)
            hop(n).wait()
            vown[n] = vown[n - 1] + vgot[n]
        n_dp = dims[0] * dims[1] * dims[2]
        for o, (row, width) in zip(o_vec, small_spots(D, FF)):
            size = width // n_dp
            at = me * size
            line = vown[4, pl.ds(row + at // D, 1), :]
            line = pltpu.roll(jnp.broadcast_to(line, (8, D)), lax.rem(D - at % D, D), 1)
            o[...] = line[0:1, :size]
        st.finish()
    else:
        for l in (1, 0):
            for t in range(3):
                arrive((l, "down", t))
                arrive((l, "up", t))
            arrive((l, "attn", 0))
            arrive((l, "attn", 1))
        c = pltpu.make_async_copy(vec, o_vec, vsend.at[0])
        c.start()
        c.wait()
    attn_copy(0, 0)[0].wait_send()
    attn_copy(0, 1)[0].wait_send()
    to_own(x).wait()
    to_other(x).wait()


def small_spots(D, FF):
    return ((0, D), (1, D), (2, 2 * D), (4, D), (5, D), (6, D), (7, FF), (7 + FF // D, D))


def backward_call(dims, n_dp, cot, tokens, y0, cols, par, saved0, saved1, own, oth, cid):
    T, D = y0.shape
    FF = own[2].shape[2]
    V = pltpu.VMEM
    sc = dict(
        g=V((T, D), bf16), mid=V((T, D), f32), gs=V((T, D), f32), gmid=V((T, D), f32), act=V((T, FF), bf16), slope=V((T, FF), bf16),
        w1=V((D, FF), bf16), w2=V((FF, D), bf16), gd=V((T, D), bf16), tr=V((D, T), bf16), gh=V((T, FF), bf16), x=V((T, D), bf16), att=V((T, D), bf16),
        att_t=V((D, T), bf16), ga=V((T, D), bf16), feat=V((4, T, LANES), bf16), lse=V((D // LANES, T, 2), f32), cols=V((T, LANES), f32),
        par=V((2, 8, FF), f32), vec=V((2, 16, D), f32), stage=V((2,) + GRID + (UR, 2 * D), bf16))
    sc["qkv"] = V((8, LANES), f32)
    hops = 5
    if dims:
        sc.update(vown=V((5, 16, D), f32), vgot=V((hops, 16, D), f32))
    wide = sds(GRID + (UR, 2 * D), bf16)
    shapes = [sds((1, 2, T, D), bf16)] + [wide] * 12
    specs = [ANY] * len(shapes)
    if dims:
        shapes += [sds((D // n_dp, 3 * D), f32), sds((D // n_dp, D), f32), sds((D // n_dp, FF), f32), sds((FF // n_dp, D), f32)]
        shapes += [sds((1, w // n_dp), f32) for _, w in small_spots(D, FF)]
        specs += [ANY] * 4 + [pl.BlockSpec(memory_space=pltpu.VMEM)] * 8
        stream = Stream(dims, [None] * 36).scratch()
    else:
        shapes += [sds((2, 16, D), f32)]
        specs += [ANY]
        stream = []
    scratch = list(sc.values()) + [DMA((len(sc) + 3 + len(QKV_CUTS),)), DMA((2, 8)), DMA((2, 8)), DMA((2, 8)), DMA((3,)), DMA((hops,)), DMA((hops,))] + stream
    return pl.pallas_call(
        functools.partial(backward_kernel, dims, tuple(sc)), out_shape=tuple(shapes),
        in_specs=[ANY] * 25, out_specs=tuple(specs), scratch_shapes=scratch,
        compiler_params=pltpu.CompilerParams(collective_id=cid, has_side_effects=True, vmem_limit_bytes=LIMIT), name="backward",
    )(cot, tokens, y0, cols, par, *saved0, *saved1, *own, *oth)


def copy_kernel(n, *refs):
    mid, sem = refs[2 * n:3 * n], refs[3 * n]
    into = [pltpu.make_async_copy(refs[i], mid[i], sem.at[0, i]) for i in range(n)]
    out = [pltpu.make_async_copy(mid[i], refs[n + i], sem.at[1, i]) for i in range(n)]
    for c in into:
        c.start()
    for c, o in zip(into, out):
        c.wait()
        o.start()
    for o in out:
        o.wait()


def copy_call(arrays):
    n = len(arrays)
    return pl.pallas_call(
        functools.partial(copy_kernel, n), out_shape=tuple(sds(a.shape, a.dtype) for a in arrays),
        in_specs=[ANY] * n, out_specs=(ANY,) * n, scratch_shapes=[pltpu.VMEM(a.shape, a.dtype) for a in arrays] + [DMA((2, n))],
        compiler_params=pltpu.CompilerParams(vmem_limit_bytes=LIMIT), name="place_outputs",
    )(*arrays)


def dp_dims(n):
    return {16: (2, 2, 4)}.get(n)


def shards(
    tokens, segment_ids, keep_masks, cotangent,
    norm1_gain, norm1_bias, qkv_weight, qv_bias, out_weight, out_bias,
    norm2_gain, norm2_bias, fc1_weight, fc1_bias, fc2_weight, fc2_bias,
):
    sec = lax.axis_index("section")
    n_dp = lax.axis_size("dp")
    dims = dp_dims(n_dp)
    T, D = tokens.shape[1:]
    FF = fc1_weight.shape[2]
    own = (qkv_weight, out_weight, fc1_weight, fc2_weight)
    vecs = (norm1_gain, norm1_bias, qv_bias, out_bias, norm2_gain, norm2_bias, fc1_bias, fc2_bias)
    res = first_call(tokens, segment_ids, keep_masks, vecs, own, 0)
    oth, par, cols, y0, saved0 = res[:4], res[4], res[5], res[6], res[7:]
    res = second_call(y0, cols, par, own, oth, 1)
    layer_out, saved1 = res[0], res[1:]
    res = backward_call(dims, n_dp, cotangent, tokens, y0, cols, par, saved0, saved1, own, oth, 2)
    input_grad = res[0]
    if dims:
        layer_out, input_grad, dqkv, dwo, dw1, dw2, n1g, n1b, qv, ob, n2g, n2b, b1, b2 = copy_call((layer_out, input_grad) + tuple(res[13:25]))
    else:
        sums = {}
        for i, l in enumerate((1, 0)):
            up, down, attn = (res[1 + 6 * i + 2 * j].astype(f32) + res[2 + 6 * i + 2 * j].astype(f32) for j in range(3))
            up, attn = up.reshape(D, -1), attn.reshape(D, -1)
            down = lax.all_gather(down, "section").reshape((2, 16, UR, 3, 2, UC))
            down = down.transpose(1, 0, 4, 2, 3, 5).reshape(FF, D)
            sums[l] = [lax.psum_scatter(a, "dp", scatter_dimension=0, tiled=True) for a in (attn, up, down)]
        attn, up, down = (jnp.stack([sums[0][i], sums[1][i]]) for i in range(3))
        attn, up = (lax.dynamic_index_in_dim(lax.all_gather(a, "section"), sec, 1, keepdims=False) for a in (attn, up))
        dw2 = lax.dynamic_index_in_dim(down, sec, 0, keepdims=False)
        dw1 = jnp.concatenate([up[0], up[1]], axis=1)
        cuts = {}
        for c, spots in enumerate(ATTN_SPOTS):
            for out, a, b, n, c0 in spots:
                for h, col in ((0, a), (1, b)):
                    cuts[out, col] = attn[h, :, c * UC + c0:c * UC + c0 + n]
        dqkv, dwo = (jnp.concatenate([cuts[k] for k in sorted(cuts) if k[0] == out], axis=1) for out in (0, 1))
        v = lax.dynamic_index_in_dim(lax.psum(res[13], ("section", "dp")), sec, 0, keepdims=False)
        at = lax.axis_index("dp")
        n1g, n1b, qv, ob, n2g, n2b, b1, b2 = (
            lax.dynamic_slice_in_dim(v[row:row + -(-w // D)].reshape(-1), at * (w // n_dp), w // n_dp)[None] for row, w in small_spots(D, FF))
    return (layer_out, input_grad, n1g, n1b, dqkv[None], qv, dwo[None], ob, n2g, n2b, dw1[None], b1, dw2[None], b2)


def solution(mesh):
    in_specs = (
        P(None, "dp", None), P(None, "dp"), P("section", None, None, "dp"), P(None, "dp", None),
        P("section", None), P("section", None), P("section", None, None), P("section", None),
        P("section", None, None), P("section", None), P("section", None), P("section", None),
        P("section", None, None), P("section", None), P("section", None, None), P("section", None),
    )
    out_specs = (
        P("section", None, "dp", None), P("section", None, "dp", None),
        P("section", "dp"), P("section", "dp"), P("section", "dp", None), P("section", "dp"),
        P("section", "dp", None), P("section", "dp"), P("section", "dp"), P("section", "dp"),
        P("section", "dp", None), P("section", "dp"), P("section", "dp", None), P("section", "dp"),
    )
    return jax.shard_map(shards, mesh=mesh, in_specs=in_specs, out_specs=out_specs, check_vma=False)
```

```python
import functools
import jax
import jax.numpy as jnp
from jax import lax
from jax.experimental import pallas as pl
from jax.experimental.pallas import tpu as pltpu
from jax.sharding import PartitionSpec as P

HEAD_DIM = 64
LANES = 128
keep_rate = 0.9
norm_eps = 1e-06
root_half = 0.7071067811865476
inverse_root = 0.3989422804014327
BIG = 2.0**30
f32, bf16 = jnp.float32, jnp.bfloat16
NN = (((1,), (0,)), ((), ()))
NT = (((1,), (1,)), ((), ()))
TN = (((0,), (0,)), ((), ()))
MESH = pl.DeviceIdType.MESH
ANY = pl.BlockSpec(memory_space=pl.ANY)
DMA = pltpu.SemaphoreType.DMA
LIMIT = 61 * 2**20
RC = 128
W = 256
sds = jax.ShapeDtypeStruct


def dot(a, b, dims=NN):
    return lax.dot_general(a, b, dims, preferred_element_type=f32)


def layer_unit(x):
    center = x - jnp.mean(x, axis=-1, keepdims=True)
    scale = lax.rsqrt(jnp.mean(center * center, axis=-1, keepdims=True) + norm_eps)
    return center * scale, scale


def unit_back(grad, unit, scale, gain):
    scaled = grad * gain
    inner = jnp.mean(scaled, axis=-1, keepdims=True)
    along = jnp.mean(scaled * unit, axis=-1, keepdims=True)
    return scale * (scaled - inner - unit * along)


def gelu_pair(h):
    phi = 0.5 * (1.0 + lax.erf(h * root_half))
    return h * phi, phi + h * jnp.exp(-0.5 * h * h) * inverse_root


def split3(v):
    a = v.astype(bf16)
    r = v - a.astype(f32)
    b = r.astype(bf16)
    c = (r - b.astype(f32)).astype(bf16)
    return a, b, c


def feature_base(odd):
    return 0 if odd else HEAD_DIM


def lanes_of(rows):
    return lax.broadcasted_iota(jnp.int32, (rows, LANES), 1)


def seg_feature(seg, rows, odd):
    base = feature_base(odd)
    lane = lanes_of(rows)
    inside = (lane >= base) & (lane < base + 8)
    same = (lane - base).astype(f32) == seg
    qf = jnp.where(inside & same, BIG, 0.0)
    kf = jnp.where(inside & jnp.logical_not(same), -1.0, 0.0)
    kf = jnp.where((lane >= base + 8) & (lane < base + 11), 1.0, kf)
    return qf.astype(bf16), kf.astype(bf16)


def own_lanes(rows, odd):
    lane = lanes_of(rows)
    return (lane >= HEAD_DIM) if odd else (lane < HEAD_DIM)


def tile(n, width):
    return pl.ds(pl.multiple_of(n * width, LANES), width)


def fetch(src, dst, sem):
    c = pltpu.make_async_copy(src, dst, sem)
    c.start()
    return c


def fetch_layer(sec, layer, own, other, dst, sem):
    c = pltpu.make_async_copy(own, dst, sem)

    @pl.when(sec == layer)
    def _():
        c.start()

    @pl.when(sec != layer)
    def _():
        pltpu.make_async_copy(other, dst, sem).start()
    return c


def partner():
    return {"section": 1 - lax.axis_index("section")}


def greet_partner():
    bar = pltpu.get_barrier_semaphore()
    pl.semaphore_signal(bar, inc=1, device_id=partner(), device_id_type=MESH)
    pl.semaphore_wait(bar, 1)


def send_copy(src, dst, send, recv, dev):
    return pltpu.make_async_remote_copy(src, dst, send, recv, device_id=dev, device_id_type=MESH)


def layer_scratch(T, D, FF):
    return dict(
        x=pltpu.VMEM((T, D), bf16), wqkv=pltpu.VMEM((D, 3 * D), bf16), wo=pltpu.VMEM((D, D), bf16),
        w1=pltpu.VMEM((D, FF), bf16), w2=pltpu.VMEM((FF, D), bf16),
        norm=pltpu.VMEM((T, D), bf16), second=pltpu.VMEM((T, D), bf16), feat=pltpu.VMEM((4, T, LANES), bf16),
        qkv=pltpu.VMEM((T, 3 * D), bf16), lse=pltpu.VMEM((D // LANES, T, 2), f32), att=pltpu.VMEM((T, D), bf16),
        mid=pltpu.VMEM((T, D), f32), act=pltpu.VMEM((T, FF), bf16), slope=pltpu.VMEM((T, FF), bf16),
        y=pltpu.VMEM((T, D), bf16),
    )


def forward_body(l, s, cols, par, ready, store):
    T, D = s["x"].shape
    FF = s["act"].shape[1]
    k1 = 1 + 2 * l

    @pl.loop(0, T // RC)
    def _(i):
        rows = pl.ds(i * RC, RC)
        unit, _s = layer_unit(s["x"][rows, :].astype(f32))
        s["norm"][rows, :] = (unit * par[l, 0:1, :D] + par[l, 1:2, :D]).astype(bf16)
        for odd in (0, 1):
            qf, kf = seg_feature(cols[rows, 0:1], RC, odd)
            s["feat"][2 * odd, rows, :] = qf
            s["feat"][2 * odd + 1, rows, :] = kf

    for part in range(3):
        ready(f"wqkv{part}")

        @pl.loop(0, D // W)
        def _(n):
            cs = pl.ds(pl.multiple_of(part * D + n * W, W), W)
            acc = dot(s["norm"][...], s["wqkv"][:, cs]) + par[l, 2:3, cs]
            s["qkv"][:, cs] = (acc * 0.125 if part == 0 else acc).astype(bf16)
    store("qkv")

    def one_pair(p):
        off = pl.multiple_of(p * LANES, LANES)
        qp = s["qkv"][:, pl.ds(off, LANES)]
        kp = s["qkv"][:, pl.ds(off + D, LANES)]
        vp = s["qkv"][:, pl.ds(off + 2 * D, LANES)]
        outs, scs, vs = [], [], []
        for odd in (0, 1):
            own = own_lanes(T, odd)
            q = jnp.where(own, qp, s["feat"][2 * odd])
            k = jnp.where(own, kp, s["feat"][2 * odd + 1])
            vs.append(jnp.where(own, vp, jnp.ones_like(vp)))
            scs.append(dot(q, k, NT))
        ms = [jnp.max(sc, axis=1, keepdims=True) for sc in scs]
        es = [jnp.exp(sc - m).astype(bf16) for sc, m in zip(scs, ms)]
        for odd in (0, 1):
            base = feature_base(odd)
            o = dot(es[odd], vs[odd])
            total = o[:, base:base + 1]
            outs.append(o / total)
            s["lse"][p, :, odd:odd + 1] = ms[odd] + jnp.log(total)
        s["att"][:, pl.ds(off, LANES)] = jnp.where(own_lanes(T, 0), outs[0], outs[1]).astype(bf16)

    @pl.loop(0, D // LANES // 2)
    def _(pp):
        one_pair(2 * pp)
        one_pair(2 * pp + 1)
    store("lse")
    store("att")
    ready("wo")

    @pl.loop(0, D // W)
    def _(n):
        cs = tile(n, W)
        acc = dot(s["att"][...], s["wo"][:, cs]) + par[l, 3:4, cs]
        s["mid"][:, cs] = s["x"][:, cs].astype(f32) + cols[:, k1:k1 + 1] * acc
    store("mid")

    @pl.loop(0, T // RC)
    def _(i):
        rows = pl.ds(i * RC, RC)
        unit, _s = layer_unit(s["mid"][rows, :])
        s["second"][rows, :] = (unit * par[l, 4:5, :D] + par[l, 5:6, :D]).astype(bf16)
    ready("w1")

    ready("w2")

    @pl.loop(0, FF // D)
    def _(n):
        cs = tile(n, D)
        a, sl = gelu_pair(dot(s["second"][...], s["w1"][:, cs]) + par[l, 6:7, cs])
        s["act"][:, cs] = a.astype(bf16)
        s["slope"][:, cs] = sl.astype(bf16)
    store("act")
    store("slope")

    @pl.loop(0, D // W)
    def _(n):
        cs = tile(n, W)
        acc = dot(s["act"][...], s["w2"][:, cs]) + par[l, 7:8, cs]
        s["y"][:, cs] = (s["mid"][:, cs] + cols[:, k1 + 1:k1 + 2] * acc).astype(bf16)
    store("y")


SAVED = ("qkv", "lse", "att", "mid", "act", "slope")


def saved_shapes(T, D, FF):
    return [sds((T, 3 * D), bf16), sds((D // LANES, T, 2), f32), sds((T, D), bf16), sds((T, D), f32), sds((T, FF), bf16), sds((T, FF), bf16)]


def first_kernel(names, tokens, segs, keep, *refs):
    vec_in, (wqkv, wo, w1, w2) = refs[:8], refs[8:12]
    o_w = refs[12:16]
    o_par, o_cols, o_y = refs[16:19]
    o_saved = dict(zip(SAVED, refs[19:25]))
    scratch = refs[25:]
    s = dict(zip(names, scratch))
    par, cols, keep_s, seg_s, send, recv, lsem, osem = scratch[len(names):]
    sec = lax.axis_index("section")
    T, D = s["x"].shape
    other = partner()
    greet_partner()
    par[:, 2:3, D:2 * D] = jnp.zeros((2, 1, D), f32)
    small, local = [], []

    def both(src, dst):
        n = len(small)
        small.append(send_copy(src, dst, send.at[n], recv.at[n], other))
        local.append(pltpu.make_async_copy(src, dst, lsem.at[n]))
    both(keep.at[0], keep_s.at[sec])
    for row, v in enumerate(vec_in):
        n = v.shape[1]
        if row == 2:
            both(v.at[:, pl.ds(0, D)], par.at[sec, pl.ds(2, 1), pl.ds(0, D)])
            both(v.at[:, pl.ds(D, D)], par.at[sec, pl.ds(2, 1), pl.ds(2 * D, D)])
        else:
            both(v, par.at[sec, pl.ds(row, 1), pl.ds(0, n)])
    for c in small:
        c.start()
    ns = len(small)
    chunks = [(f"wqkv{i}", wqkv.at[0, :, pl.ds(i * D, D)], o_w[0].at[:, pl.ds(i * D, D)], s["wqkv"].at[:, pl.ds(i * D, D)]) for i in range(3)]
    chunks += [(n, w.at[0], o, s[n]) for n, w, o in (("wo", wo, o_w[1]), ("w1", w1, o_w[2]), ("w2", w2, o_w[3]))]
    to_vmem, to_hbm, keep_w = {}, {}, {}
    for i, (n, src, dst, vm) in enumerate(chunks):
        to_vmem[n] = send_copy(src, vm, send.at[ns + i], recv.at[ns + i], other)
        to_hbm[n] = send_copy(src, dst, send.at[ns + i], recv.at[ns + i], other)
        keep_w[n] = pltpu.make_async_copy(vm, dst, lsem.at[ns + i])

    @pl.when(sec == 0)
    def _():
        for c in to_vmem.values():
            c.start()

    @pl.when(sec == 1)
    def _():
        for c in to_hbm.values():
            c.start()
    x_in = fetch(tokens.at[sec], s["x"], lsem.at[ns + 6])
    g_in = fetch(segs, seg_s, lsem.at[ns + 7])
    for c in local:
        c.start()
    loads = {n: pltpu.make_async_copy(src, vm, lsem.at[ns + i]) for i, (n, src, dst, vm) in enumerate(chunks)}

    @pl.when(sec == 0)
    def _():
        for c in loads.values():
            c.start()
    for c in local:
        c.wait()
    for c in small:
        c.wait()
    x_in.wait()
    g_in.wait()

    cols[...] = jnp.broadcast_to(seg_s[pl.ds(sec, 1), :].astype(f32), (LANES, T)).T

    @pl.loop(0, T // RC)
    def _(i):
        rows = pl.ds(i * RC, RC)
        lane = lanes_of(RC)
        seg = cols[rows, 0:1]
        ids = keep_s.shape[3]
        hot = lax.broadcasted_iota(jnp.int32, (RC, ids), 1).astype(f32) == seg
        out = jnp.where(lane == 0, seg, 0.0)
        for l in range(2):
            for b in range(2):
                flag = jnp.sum(jnp.where(hot, keep_s[l, sec, b:b + 1, :].astype(f32), 0.0), axis=1, keepdims=True) / keep_rate
                out = jnp.where(lane == 1 + 2 * l + b, flag, out)
        cols[rows, :] = out
    outs = [fetch(par, o_par, osem.at[7]), fetch(cols, o_cols, osem.at[8])]
    o_saved["y"] = o_y
    spots = list(SAVED) + ["y"]

    def ready(n):
        @pl.when(sec == 0)
        def _():
            loads[n].wait()

        @pl.when(sec == 1)
        def _():
            to_vmem[n].wait_recv()
            keep_w[n].start()

    def store(n):
        outs.append(fetch(s[n], o_saved[n], osem.at[spots.index(n)]))

    forward_body(0, s, cols, par, ready, store)

    @pl.when(sec == 0)
    def _():
        for c in to_hbm.values():
            c.wait_recv()

    @pl.when(sec == 1)
    def _():
        for c in keep_w.values():
            c.wait()
    for c in to_vmem.values():
        c.wait_send()
    for c in outs:
        c.wait()


def first_call(tokens, segs, keep, vecs, weights, cid):
    _, T, D = tokens.shape
    FF = weights[2].shape[2]
    sc = layer_scratch(T, D, FF)
    names = tuple(sc)
    ns = 10
    shapes = [sds(w.shape[1:], bf16) for w in weights] + [sds((2, 8, FF), f32), sds((T, LANES), f32), sds((T, D), bf16)] + saved_shapes(T, D, FF)
    return pl.pallas_call(
        functools.partial(first_kernel, names), out_shape=tuple(shapes),
        in_specs=[ANY] * 15, out_specs=(ANY,) * len(shapes),
        scratch_shapes=list(sc.values()) + [
            pltpu.VMEM((2, 8, FF), f32), pltpu.VMEM((T, LANES), f32), pltpu.VMEM((2,) + keep.shape[1:], jnp.int32), pltpu.VMEM(segs.shape, jnp.int32),
            DMA((ns + 6,)), DMA((ns + 6,)), DMA((ns + 8,)), DMA((9,))],
        compiler_params=pltpu.CompilerParams(collective_id=cid, has_side_effects=True, vmem_limit_bytes=LIMIT), name="forward_first",
    )(tokens, segs, keep, *vecs, *weights)


def second_kernel(names, x_hbm, cols_hbm, par_hbm, *refs):
    own, oth = refs[:4], refs[4:8]
    o_out = refs[8]
    o_saved = dict(zip(SAVED, refs[9:15]))
    scratch = refs[15:]
    s = dict(zip(names, scratch))
    par, cols, lsem, osem, esem = scratch[len(names):]
    sec = lax.axis_index("section")
    greet_partner()
    first = [fetch(x_hbm, s["x"], lsem.at[4]), fetch(cols_hbm, cols, lsem.at[5]), fetch(par_hbm, par, lsem.at[6])]
    loads = {n: fetch_layer(sec, 1, own[i].at[0], oth[i], s[n], lsem.at[i]) for i, n in enumerate(("wqkv", "wo", "w1", "w2"))}
    for c in first:
        c.wait()
    outs = []

    def ready(n):
        if n == "wqkv0":
            loads["wqkv"].wait()
        elif n in loads:
            loads[n].wait()

    def store(n):
        if n != "y":
            outs.append(fetch(s[n], o_saved[n], osem.at[SAVED.index(n)]))

    to_other = lambda src: send_copy(src, o_out.at[0, sec], esem.at[0], esem.at[1], partner())
    to_own = lambda src: pltpu.make_async_copy(src, o_out.at[0, sec], esem.at[2])

    forward_body(1, s, cols, par, ready, store)

    @pl.when(sec == 0)
    def _():
        to_own(s["x"]).start()
        to_other(s["y"]).start()

    @pl.when(sec == 1)
    def _():
        to_own(s["y"]).start()
        to_other(s["x"]).start()
    to_own(s["x"]).wait()
    to_other(s["x"]).wait()
    for c in outs:
        c.wait()


def second_call(x, cols, par, own, oth, cid):
    T, D = x.shape
    FF = own[2].shape[2]
    sc = layer_scratch(T, D, FF)
    shapes = [sds((1, 2, T, D), bf16)] + saved_shapes(T, D, FF)
    return pl.pallas_call(
        functools.partial(second_kernel, tuple(sc)), out_shape=tuple(shapes),
        in_specs=[ANY] * 11, out_specs=(ANY,) * len(shapes),
        scratch_shapes=list(sc.values()) + [pltpu.VMEM((2, 8, FF), f32), pltpu.VMEM((T, LANES), f32), DMA((7,)), DMA((6,)), DMA((3,))],
        compiler_params=pltpu.CompilerParams(collective_id=cid, has_side_effects=True, vmem_limit_bytes=LIMIT), name="forward_second",
    )(x, cols, par, *own, *oth)


GRID = (2, 2, 2, 2)
AXES = "hlyx"
UR, UC = 48, 256
CYCLE = ("xlyh", "ylxh")
RING, INCS, FINS = 18, 4, 4
HOP_US, PACE_US = 8.0, 2.4


class Stream:
    def __init__(self, dims, units):
        self.dims, self.units, self.n = dims, units, len(units)
        self.head = [0] * 5
        self.loaded = 0
        self.limit = 0
        self.due = 0.0
        self.born = {}
        self.seen = set()

    def scratch(self):
        parts = []
        for j in range(RING):
            for k in range(4):
                parts.append(pltpu.VMEM((2,) * (3 - k) + (UR, UC), bf16))
        return [pltpu.VMEM((RING,) + GRID + (UR, UC), bf16), pltpu.VMEM((INCS,) + GRID + (UR, UC), bf16), pltpu.VMEM((FINS, UR, UC), f32),
                DMA((RING, 4)), DMA((RING, 4)), DMA((RING, 2)), DMA((FINS, 2)), DMA((self.n, 2))] + parts

    def bind(self, scratch, arrive, outs):
        self.own, self.inc, self.fin, self.send, self.rsem, self.lsem, self.fsend, self.frecv = scratch[:8]
        self.parts = [scratch[8 + 4 * j:12 + 4 * j] for j in range(RING)]
        self.arrive, self.outs = arrive, outs
        me = lax.axis_index("dp")
        self.sec = lax.axis_index("section")
        self.at = dict(x=me % 2, y=me // 2 % 2, l=me // 4 % 2, h=me // 8)

    def peer(self, axis):
        c = dict(self.at)
        c[axis] = 1 - c[axis]
        return {"dp": ((c["h"] * 2 + c["l"]) * 2 + c["y"]) * 2 + c["x"]}

    def greet(self):
        bar = pltpu.get_barrier_semaphore()
        ids = [partner()] + [self.peer(a) for a in AXES]
        for i in ids:
            pl.semaphore_signal(bar, inc=1, device_id=i, device_id_type=MESH)
        pl.semaphore_wait(bar, len(ids))

    def order(self, u):
        return CYCLE[(u % RING) % len(CYCLE)]

    def loads(self, u):
        mine, recv = self.units[u]["src"]
        return (pltpu.make_async_copy(mine, self.own.at[u % RING], self.lsem.at[u % RING, 0]),
                pltpu.make_async_copy(recv, self.inc.at[u % INCS], self.lsem.at[u % RING, 1]))

    def load(self, u):
        for c in self.loads(u):
            c.start()

    def hop(self, u, k):
        order = self.order(u)
        j = u % RING
        spot = tuple(self.at[a] if a in order[:k] else (1 - self.at[a] if a == order[k] else slice(None)) for a in AXES)
        return send_copy(self.own.at[(j,) + spot], self.parts[j][k], self.send.at[j, k], self.rsem.at[j, k], self.peer(order[k]))

    def combine(self, axes, fn):
        if not axes:
            fn({})
            return

        @pl.loop(0, 2)
        def _(i):
            rest = [{}]
            for a in axes[1:]:
                rest = [dict(r, **{a: v}) for r in rest for v in range(2)]
            for r in rest:
                fn(dict(r, **{axes[0]: i}))

    def start(self, u):
        for c in self.loads(u):
            c.wait()
        own, inc = self.own.at[u % RING], self.inc.at[u % INCS]

        def add(at):
            i = tuple(at[a] for a in AXES)
            own[i] = own[i] + inc[i]
        self.combine(AXES, add)
        self.hop(u, 0).start()

    def move(self, u, k):
        order = self.order(u)
        self.hop(u, k).wait()
        own, part = self.own.at[u % RING], self.parts[u % RING][k]
        free = [a for a in AXES if a in order[k + 1:]]
        if k == 3 and u >= FINS:
            self.sent(u - FINS)

        def add(at):
            i = tuple(at[a] if a in at else self.at[a] for a in AXES)
            got = part[tuple(at[a] for a in free) if free else Ellipsis]
            if k == 3:
                self.fin[u % FINS] = own[i].astype(f32) + got.astype(f32)
            else:
                own[i] = own[i] + got
        self.combine(free, add)
        if k == 3:
            self.deliver(u)
        else:
            self.hop(u, k + 1).start()

    def results(self, u):
        for i, (out, row, rows, col, cols, c0) in enumerate(self.units[u]["dst"](self.sec)):
            dst = self.outs[out].at[pl.ds(row, rows), pl.ds(pl.multiple_of(col, LANES), cols)]
            src = self.fin.at[u % FINS, :, pl.ds(c0, cols)]
            yield (pltpu.make_async_copy(src, dst, self.fsend.at[u % FINS, i]),
                   send_copy(src, dst, self.fsend.at[u % FINS, i], self.frecv.at[u, i], partner()))

    def by_layer(self, u, same, other):
        @pl.when(self.sec == self.units[u]["layer"])
        def _():
            for near, away in self.results(u):
                same(near, away)

        @pl.when(self.sec != self.units[u]["layer"])
        def _():
            for near, away in self.results(u):
                other(near, away)

    def deliver(self, u):
        self.by_layer(u, lambda near, away: near.start(), lambda near, away: away.start())

    def sent(self, u):
        self.by_layer(u, lambda near, away: near.wait(), lambda near, away: away.wait_send())

    def plan(self, now, limit=None):
        h, calls = self.head, []
        if limit is not None:
            self.limit = max(self.limit, limit)
        drain = now is None
        for k in (3, 2, 1, 0):
            count = 0
            while h[k + 1] < h[k] and (count < 1 if drain else now - self.born[k, h[k + 1]] >= HOP_US):
                u = h[k + 1]
                calls.append(functools.partial(self.move, u, k))
                self.born[k + 1, u] = now
                h[k + 1] += 1
                count += 1
        count = 0
        while h[0] < self.loaded and (drain or now >= self.due) and count < 2:
            u = h[0]
            calls.append(functools.partial(self.start, u))
            self.born[0, u] = now
            h[0] += 1
            count += 1
            if not drain:
                self.due = max(self.due, now - PACE_US) + PACE_US
        while self.loaded < min(self.limit, h[0] + INCS - 1) and (self.loaded < RING or h[4] > self.loaded - RING):
            key = self.units[self.loaded]["need"]
            if key not in self.seen:
                self.seen.add(key)
                calls.append(functools.partial(self.arrive, key))
            calls.append(functools.partial(self.load, self.loaded))
            self.loaded += 1
        return calls

    def tick(self, now, limit=None):
        for c in self.plan(now, limit):
            c()

    def in_loop(self, i, calls):
        for at, todo in enumerate(calls):
            if todo:
                @pl.when(i == at)
                def _(todo=todo):
                    for c in todo:
                        c()

    def finish(self):
        self.limit = self.n
        while self.head[4] < self.n:
            self.tick(None)
        assert self.head == [self.n] * 5
        for u in range(self.n - FINS, self.n):
            self.sent(u)
        for u in range(self.n):
            @pl.when(self.sec == self.units[u]["layer"])
            def _():
                for _n, away in self.results(u):
                    away.wait_recv()


ATTN_SPOTS = (
    ((1, 0, 384, 256, 0),),
    ((1, 256, 640, 128, 0), (0, 0, 896, 128, 128)),
    ((0, 128, 1536, 128, 0), (0, 768, 1664, 128, 128)),
    ((0, 256, 1280, 256, 0),),
    ((0, 512, 1792, 256, 0),),
    ((0, 1024, 2048, 256, 0),),
)
QKV_CUTS = ((0, 0, 0, 256), (0, 256, 768, 256), (0, 512, 1536, 256), (1, 0, 256, 512), (1, 512, 1024, 256), (2, 0, 1280, 256), (2, 256, 1792, 512))


def gradient_units(bufs):
    units = []
    for l in (1, 0):
        up, down, attn = bufs[l]
        for c in range(6):
            cut = lambda ref: ref.at[:, :, :, :, :, pl.ds(c * UC, UC)]
            units.append(dict(layer=l, src=tuple(map(cut, down)), need=(l, "down", c // 2),
                              dst=lambda sec, c=c: [(3, pl.multiple_of(sec * 2 * UR + c % 2 * UR, 16), UR, c // 2 * UC, UC, 0)]))
        for c in range(6):
            cut = lambda ref: ref.at[:, :, :, :, :, pl.ds(c * UC, UC)]
            units.append(dict(layer=l, src=tuple(map(cut, up)), need=(l, "up", c // 2),
                              dst=lambda sec, c=c: [(2, 0, UR, sec * 6 * UC + c * UC, UC, 0)]))
        for c, spots in enumerate(ATTN_SPOTS):
            cut = lambda ref: ref.at[:, :, :, :, :, pl.ds(c * UC, UC)]
            units.append(dict(layer=l, src=tuple(map(cut, attn)), need=(l, "attn", c // 3),
                              dst=lambda sec, spots=spots: [(out, 0, UR, a + sec * (b - a), n, c0) for out, a, b, n, c0 in spots]))
    return units


LAYER_US = 55.6
TIMES = dict(norm=0.4, down=(2.7, 5.0, 7.3), unit=8.5, up=(9.3, 10.3, 11.0, 12.0, 12.8, 13.8, 14.5, 15.5, 16.3, 17.3, 18.0, 19.0), gs=(20.0, 20.8, 21.6), mid=23.3,
             gb=25.2, ga=26.4, dwo=27.9, pairs=(30.5, 33.1, 37.5, 40.2, 42.9, 45.6), early=34.8, dqkv=(46.6, 47.6), gn=(48.7, 49.8, 50.9), end=52.7)


def backward_kernel(dims, names, cot, tokens, y0, cols_h, par_h, *refs):
    saved = [dict(zip(SAVED, refs[:6])), dict(zip(SAVED, refs[6:12]))]
    own = dict(zip(("wqkv", "wo", "w1", "w2"), refs[12:16]))
    oth = dict(zip(("wqkv", "wo", "w1", "w2"), refs[16:20]))
    refs = refs[20:]
    o_gin, refs = refs[0], refs[1:]
    bufs = {}
    for l in (1, 0):
        bufs[l], refs = ((refs[0], refs[1]), (refs[2], refs[3]), (refs[4], refs[5])), refs[6:]
    if dims:
        o_big, o_vec, refs = refs[:4], refs[4:12], refs[12:]
    else:
        o_vec, refs = refs[0], refs[1:]
    s = dict(zip(names, refs))
    lsem, csend, crecv, cnear, esem, vsend, vrecv = refs[len(names):len(names) + 7]
    st_refs = refs[len(names) + 7:]
    g, mid, gs, gmid, act, slope, w1, w2, gd, tr, gh, x, att, att_t, ga, feat, lse, cols, par, vec, stage = (s[n] for n in names[:21])
    sec = lax.axis_index("section")
    me = lax.axis_index("dp")
    T, D = g.shape
    FF = act.shape[1]

    ld = {}
    W2 = ("w2", "w2b", "w2c", "w2d")
    CUTS = tuple(f"c{i}" for i in range(len(QKV_CUTS)))

    def get(n, src, dst):
        keys = tuple(names) + W2[1:] + CUTS
        ld[n] = fetch(src, dst, lsem.at[keys.index(n)])

    def get_w(n, layer, name, src_of, dst):
        keys = tuple(names) + W2[1:] + CUTS
        ld[n] = fetch_layer(sec, layer, src_of(own[name].at[0]), src_of(oth[name]), dst, lsem.at[keys.index(n)])

    def need(*ns):
        for n in ns:
            ld.pop(n).wait()

    def load_w2(l):
        for i, n in enumerate(W2):
            get_w(n, l, "w2", lambda r, i=i: r.at[pl.ds(i * D, D), :], w2.at[pl.ds(i * D, D), :])

    def load_attn_weights(l):
        for n, (block, col, src, cols_n) in zip(CUTS, QKV_CUTS):
            get_w(n, l, "wqkv", lambda r, src=src, cols_n=cols_n: r.at[:, pl.ds(src, cols_n)], w2.at[pl.ds(block * D, D), pl.ds(col, cols_n)])
        get_w(W2[3], l, "wo", lambda r: r, w2.at[pl.ds(3 * D, D), :])

    def tile_copy(l, kind, t, at):
        cs = tile(t, 2 * UC)
        mine, recv = (r.at[:, :, :, :, :, cs] for r in bufs[l][1 - kind])
        buf = lambda h: stage.at[h, :, :, :, :, :, cs]
        return (send_copy(buf(1 - sec), recv, csend.at[l, 3 * kind + at], crecv.at[l, 3 * kind + at], partner()),
                pltpu.make_async_copy(buf(sec), mine, cnear.at[l, 3 * kind + at]))

    def attn_copy(l, part):
        mine, recv = (r.at[:, :, :, :, :, pl.ds(part * D, D)] for r in bufs[l][2])
        buf = lambda h: stage.at[h, :, :, :, :, :, pl.ds(part * D, D)]
        return (send_copy(buf(1 - sec), recv, csend.at[l, 6 + part], crecv.at[l, 6 + part], partner()),
                pltpu.make_async_copy(buf(sec), mine, cnear.at[l, 6 + part]))

    def arrive(key):
        l, kind, t = key
        if kind == "attn":
            attn_copy(l, t)[0].wait_recv()
        else:
            tile_copy(l, 1 if kind == "up" else 0, t, t)[0].wait_recv()

    get("g", cot.at[sec], g)
    get("cols", cols_h, cols)
    get("par", par_h, par)
    get("act", saved[1]["act"], act)
    get("mid", saved[1]["mid"], mid)
    get("slope", saved[1]["slope"], slope)
    load_w2(1)
    get_w("w1", 1, "w1", lambda r: r, w1)
    get("x", y0, x)
    get("att", saved[1]["att"], att)
    get("lse", saved[1]["lse"], lse)
    if dims:
        st = Stream(dims, gradient_units(bufs))
        st.bind(st_refs, arrive, o_big)
        st.greet()
    else:
        st = None
        greet_partner()
    need("cols", "par")
    vec[...] = jnp.zeros_like(vec)

    start_us = 3.5

    def tick(spot, limit):
        if st:
            st.tick(start_us + (1 - l) * LAYER_US + TIMES[spot], limit + (1 - l) * 18)

    def loop_plan(*spots):
        table = [[] for _ in spots]
        for i in range(len(spots[0][0])):
            for calls, (times, limits) in zip(table, spots):
                now = start_us + (1 - l) * LAYER_US + times[i]
                calls.append(st.plan(now, limits[i] + (1 - l) * 18) if st else [])
        return table

    def loop_tick(i, calls):
        if st:
            st.in_loop(i, calls)

    down_row = 7 + FF // D
    low_lane = own_lanes(T, 0)
    for l in (1, 0):
        k1, k2 = 1 + 2 * l, 2 + 2 * l
        if l == 1:
            need("g")

        @pl.loop(0, T // RC)
        def _(i):
            rows = pl.ds(i * RC, RC)
            low = (g[rows, :].astype(f32) * cols[rows, k2:k2 + 1]).astype(bf16)
            gd[rows, :] = low
            vec[l, down_row:down_row + 1, :] += jnp.sum(low.astype(f32), axis=0, keepdims=True)
        if l == 0:
            attn_copy(1, 0)[0].wait_send()
            attn_copy(1, 1)[0].wait_send()
        tick("norm", 0)
        need("act")
        calls, = loop_plan((TIMES["down"], (0, 2, 4)))

        @pl.loop(0, 3)
        def _(c):
            d2 = dot(act[...], gd[:, tile(c, UC)], TN).astype(bf16).reshape(GRID + (4, UR, UC))
            for q in range(4):
                stage[q // 2, :, :, :, :, :, pl.ds(pl.multiple_of((2 * c + q % 2) * UC, UC), UC)] = d2[:, :, :, :, q]
            for k in tile_copy(l, 0, c, c):
                k.start()

            @pl.when(c > 0)
            def _():
                tile_copy(l, 0, c, c - 1)[1].wait()
            loop_tick(c, calls)
        tile_copy(l, 0, 2, 2)[1].wait()
        need("mid")

        @pl.loop(0, T // RC)
        def _(i):
            rows = pl.ds(i * RC, RC)
            unit, _s = layer_unit(mid[rows, :])
            tr[:, rows] = (unit * par[l, 4:5, :D] + par[l, 5:6, :D]).astype(bf16).T
            if l == 1:
                for odd in (0, 1):
                    qf, kf = seg_feature(cols[rows, 0:1], RC, odd)
                    feat[2 * odd, rows, :] = qf
                    feat[2 * odd + 1, rows, :] = kf
        tick("unit", 6)
        need(*W2, "slope")
        early, late = loop_plan((TIMES["up"][0::2], (6, 6, 6, 8, 8, 10)), (TIMES["up"][1::2], (6, 6, 8, 8, 10, 10)))

        @pl.loop(0, 6)
        def _(i):
            mine, t = lax.rem(i, 2), i // 2
            h = lax.rem(sec + 1 + mine, 2)
            n = 3 * h + t
            cs = tile(n, 2 * UC)
            low = (dot(gd[...], w2[cs, :], NT) * slope[:, cs].astype(f32)).astype(bf16)
            gh[:, cs] = low
            total = jnp.sum(low.astype(f32), axis=0, keepdims=True)
            for q in range(2):
                m = 2 * n + q
                vec[l, pl.ds(7 + m // 3, 1), tile(lax.rem(m, 3), UC)] = total[:, q * UC:(q + 1) * UC]

            @pl.when(mine == 0)
            def _():
                tile_copy(l, 0, t, t)[0].wait_send()

            @pl.when((mine == 0) & (i > 0))
            def _():
                tile_copy(l, 1, t, t - 1)[1].wait()
            loop_tick(i, early)
            d1 = dot(tr[...], low).astype(bf16)
            stage[h, :, :, :, :, :, tile(t, 2 * UC)] = d1.reshape(GRID + (UR, 2 * UC))
            away, near = tile_copy(l, 1, t, t)

            @pl.when(mine == 0)
            def _():
                away.start()

            @pl.when(mine == 1)
            def _():
                near.start()
            loop_tick(i, late)
        load_attn_weights(l)
        get("qkv", saved[l]["qkv"], slope.at[:, pl.ds(0, 3 * D)])
        if l == 1:
            get("act", saved[0]["act"], act)
        tile_copy(l, 1, 2, 2)[1].wait()
        need("w1")
        calls, = loop_plan((TIMES["gs"], (10, 12, 12)))

        @pl.loop(0, D // W)
        def _(n):
            cs = tile(n, W)
            gs[:, cs] = dot(gh[...], w1[cs, :], NT)
            loop_tick(n, calls)
        if l == 1:
            get_w("w1", 0, "w1", lambda r: r, w1)
        for t in range(3):
            tile_copy(l, 1, t, t)[0].wait_send()

        @pl.loop(0, T // RC)
        def _(i):
            rows = pl.ds(i * RC, RC)
            unit, scale = layer_unit(mid[rows, :])
            low = gs[rows, :]
            vec[l, 5:6, :] += jnp.sum(low * unit, axis=0, keepdims=True)
            vec[l, 6:7, :] += jnp.sum(low, axis=0, keepdims=True)
            gmid[rows, :] = g[rows, :].astype(f32) + unit_back(low, unit, scale, par[l, 4:5, :D])
        tick("mid", 12)
        if l == 1:
            get("mid", saved[0]["mid"], mid)
        need("x", "att")

        @pl.loop(0, T // RC)
        def _(i):
            rows = pl.ds(i * RC, RC)
            low = (gmid[rows, :] * cols[rows, k1:k1 + 1]).astype(bf16)
            gd[rows, :] = low
            vec[l, 4:5, :] += jnp.sum(low.astype(f32), axis=0, keepdims=True)
            unit, _s = layer_unit(x[rows, :].astype(f32))
            tr[:, rows] = (unit * par[l, 0:1, :D] + par[l, 1:2, :D]).astype(bf16).T
            att_t[:, rows] = att[rows, :].T
        tick("gb", 12)
        need(W2[3])

        @pl.loop(0, D // W)
        def _(n):
            cs = tile(n, W)
            ga[:, cs] = dot(gd[...], w2[pl.ds(pl.multiple_of(3 * D + n * W, W), W), :], NT).astype(bf16)
        tick("ga", 12)
        @pl.loop(0, 2)
        def _(h):
            stage[h, :, :, :, :, :, 0:D // 2] = dot(att_t[...], gd[:, tile(h, D // 2)]).astype(bf16).reshape(GRID + (UR, D // 2))
        tick("dwo", 12)
        need("qkv", "lse")

        def pair(p, spots):
            off = pl.multiple_of(p * LANES, LANES)
            qp = slope[:, pl.ds(off, LANES)]
            kp = slope[:, pl.ds(off + D, LANES)]
            vp = slope[:, pl.ds(off + 2 * D, LANES)]
            gp = ga[:, pl.ds(off, LANES)]
            prod = gp.astype(f32) * att[:, pl.ds(off, LANES)].astype(f32)
            dq, dk, dv = [], [], []
            for odd in (0, 1):
                own_l = own_lanes(T, odd)
                base = feature_base(odd)
                lane = lanes_of(T)
                row_d = jnp.sum(jnp.where(own_l, prod, 0.0), axis=1, keepdims=True)
                l3 = split3(-lse[p, :, odd:odd + 1])
                d3 = split3(-row_d)
                qf = feat[2 * odd]
                gf = jnp.zeros_like(gp)
                for j in range(3):
                    qf = jnp.where(lane == base + 8 + j, l3[j], qf)
                    gf = jnp.where(lane == base + j, d3[j], gf)
                q = jnp.where(own_l, qp, qf)
                k = jnp.where(own_l, kp, feat[2 * odd + 1])
                v = jnp.where(own_l, vp, jnp.ones_like(vp))
                gg = jnp.where(own_l, gp, gf)
                prob = jnp.exp(dot(k, q, NT))
                gsc = (prob * dot(v, gg, NT)).astype(bf16)
                dv.append(dot(prob.astype(bf16), gg))
                dk.append(dot(gsc, q))
                dq.append(dot(gsc, k, TN))
            for at, val in zip(spots, ((jnp.where(low_lane, dq[0], dq[1]) * 0.125), jnp.where(low_lane, dk[0], dk[1]), jnp.where(low_lane, dv[0], dv[1]))):
                gh[:, tile(at + p, LANES)] = val.astype(bf16)

        def gradient(part, width, base):
            calls, = loop_plan((TIMES["dqkv"], (15, 15))) if part else (None,)

            @pl.loop(0, 2)
            def _(i):
                h = lax.rem(i + 1 + sec, 2)
                cs = pl.ds(pl.multiple_of(base + h * width, LANES), width)
                stage[h, :, :, :, :, :, (part + 1) * D - width:(part + 1) * D] = dot(tr[...], gh[:, cs]).astype(bf16).reshape(GRID + (UR, width))
                away, near = attn_copy(l, part)

                @pl.when(i == 0)
                def _():
                    away.start()

                @pl.when(i == 1)
                def _():
                    near.start()
                if part == 1:
                    loop_tick(i, calls)

        calls, = loop_plan((TIMES["pairs"][:2], (12, 12)))

        @pl.loop(0, 2)
        def _(p):
            pair(p, (0, 2, 4))
            loop_tick(p, calls)
        gradient(0, D // 2, 0)
        attn_copy(l, 0)[1].wait()
        tick("early", 15)

        calls, = loop_plan((TIMES["pairs"][2:], (15,) * 4))

        @pl.loop(2, D // LANES)
        def _(p):
            pair(p, (4, 8, 12))
            loop_tick(p - 2, calls)
        if l == 1:
            get("slope", saved[0]["slope"], slope)
            get("att", saved[0]["att"], att)
            get("lse", saved[0]["lse"], lse)
        gradient(1, D, D)
        attn_copy(l, 1)[1].wait()
        for row, to, at, n in ((2, 0, 0, 256), (2, 256, 768, 512), (3, 0, 512, 256), (3, 256, 1792, 512)):
            vec[l, row:row + 1, to:to + n] = jnp.sum(gh[:, at:at + n].astype(f32), axis=0, keepdims=True)

        need(*CUTS)
        calls, = loop_plan((TIMES["gn"], (18, 18, 18)))

        @pl.loop(0, D // W)
        def _(n):
            cs = tile(n, W)
            acc = jnp.zeros((T, W), f32)
            for c in range(3):
                acc += dot(gh[:, c * D:(c + 1) * D], w2[pl.ds(pl.multiple_of(c * D + n * W, W), W), :], NT)
            gs[:, cs] = acc
            loop_tick(n, calls)
        if l == 1:
            load_w2(0)

        @pl.loop(0, T // RC)
        def _(i):
            rows = pl.ds(i * RC, RC)
            unit, scale = layer_unit(x[rows, :].astype(f32))
            low = gs[rows, :]
            vec[l, 0:1, :] += jnp.sum(low * unit, axis=0, keepdims=True)
            vec[l, 1:2, :] += jnp.sum(low, axis=0, keepdims=True)
            res = (gmid[rows, :] + unit_back(low, unit, scale, par[l, 0:1, :D])).astype(bf16)
            if l == 1:
                g[rows, :] = res
            else:
                x[rows, :] = res
        if l == 1:
            get("x", tokens.at[sec], x)
        tick("end", 18)

    to_other = lambda src: send_copy(src, o_gin.at[0, sec], esem.at[0], esem.at[1], partner())
    to_own = lambda src: pltpu.make_async_copy(src, o_gin.at[0, sec], esem.at[2])

    @pl.when(sec == 0)
    def _():
        to_own(x).start()
        to_other(g).start()

    @pl.when(sec == 1)
    def _():
        to_own(g).start()
        to_other(x).start()
    if st:
        vown, vgot = s["vown"], s["vgot"]
        def hop(n):
            if n == 0:
                return send_copy(vec.at[1 - sec], vgot.at[0], vsend.at[0], vrecv.at[0], partner())
            return send_copy(vown.at[n - 1], vgot.at[n], vsend.at[n], vrecv.at[n], st.peer(AXES[n - 1]))
        hop(0).start()
        st.tick(None)
        hop(0).wait()
        vown[0] = vec[sec] + vgot[0]
        for n in range(1, 5):
            hop(n).start()
            st.tick(None)
            st.tick(None)
            hop(n).wait()
            vown[n] = vown[n - 1] + vgot[n]
        n_dp = dims[0] * dims[1] * dims[2]
        for o, (row, width) in zip(o_vec, small_spots(D, FF)):
            size = width // n_dp
            at = me * size
            line = vown[4, pl.ds(row + at // D, 1), :]
            line = pltpu.roll(jnp.broadcast_to(line, (8, D)), lax.rem(D - at % D, D), 1)
            o[...] = line[0:1, :size]
        st.finish()
    else:
        for l in (1, 0):
            for t in range(3):
                arrive((l, "down", t))
                arrive((l, "up", t))
            arrive((l, "attn", 0))
            arrive((l, "attn", 1))
        c = pltpu.make_async_copy(vec, o_vec, vsend.at[0])
        c.start()
        c.wait()
    attn_copy(0, 0)[0].wait_send()
    attn_copy(0, 1)[0].wait_send()
    to_own(x).wait()
    to_other(x).wait()


def small_spots(D, FF):
    return ((0, D), (1, D), (2, 2 * D), (4, D), (5, D), (6, D), (7, FF), (7 + FF // D, D))


def backward_call(dims, n_dp, cot, tokens, y0, cols, par, saved0, saved1, own, oth, cid):
    T, D = y0.shape
    FF = own[2].shape[2]
    V = pltpu.VMEM
    sc = dict(
        g=V((T, D), bf16), mid=V((T, D), f32), gs=V((T, D), f32), gmid=V((T, D), f32), act=V((T, FF), bf16), slope=V((T, FF), bf16),
        w1=V((D, FF), bf16), w2=V((FF, D), bf16), gd=V((T, D), bf16), tr=V((D, T), bf16), gh=V((T, FF), bf16), x=V((T, D), bf16), att=V((T, D), bf16),
        att_t=V((D, T), bf16), ga=V((T, D), bf16), feat=V((4, T, LANES), bf16), lse=V((D // LANES, T, 2), f32), cols=V((T, LANES), f32),
        par=V((2, 8, FF), f32), vec=V((2, 16, D), f32), stage=V((2,) + GRID + (UR, 2 * D), bf16))
    sc["qkv"] = V((8, LANES), f32)
    hops = 5
    if dims:
        sc.update(vown=V((5, 16, D), f32), vgot=V((hops, 16, D), f32))
    wide = sds(GRID + (UR, 2 * D), bf16)
    shapes = [sds((1, 2, T, D), bf16)] + [wide] * 12
    specs = [ANY] * len(shapes)
    if dims:
        shapes += [sds((D // n_dp, 3 * D), f32), sds((D // n_dp, D), f32), sds((D // n_dp, FF), f32), sds((FF // n_dp, D), f32)]
        shapes += [sds((1, w // n_dp), f32) for _, w in small_spots(D, FF)]
        specs += [ANY] * 4 + [pl.BlockSpec(memory_space=pltpu.VMEM)] * 8
        stream = Stream(dims, [None] * 36).scratch()
    else:
        shapes += [sds((2, 16, D), f32)]
        specs += [ANY]
        stream = []
    scratch = list(sc.values()) + [DMA((len(sc) + 3 + len(QKV_CUTS),)), DMA((2, 8)), DMA((2, 8)), DMA((2, 8)), DMA((3,)), DMA((hops,)), DMA((hops,))] + stream
    return pl.pallas_call(
        functools.partial(backward_kernel, dims, tuple(sc)), out_shape=tuple(shapes),
        in_specs=[ANY] * 25, out_specs=tuple(specs), scratch_shapes=scratch,
        compiler_params=pltpu.CompilerParams(collective_id=cid, has_side_effects=True, vmem_limit_bytes=LIMIT), name="backward",
    )(cot, tokens, y0, cols, par, *saved0, *saved1, *own, *oth)


def copy_kernel(n, *refs):
    mid, sem = refs[2 * n:3 * n], refs[3 * n]
    into = [pltpu.make_async_copy(refs[i], mid[i], sem.at[0, i]) for i in range(n)]
    out = [pltpu.make_async_copy(mid[i], refs[n + i], sem.at[1, i]) for i in range(n)]
    for c in into:
        c.start()
    for c, o in zip(into, out):
        c.wait()
        o.start()
    for o in out:
        o.wait()


def copy_call(arrays):
    n = len(arrays)
    return pl.pallas_call(
        functools.partial(copy_kernel, n), out_shape=tuple(sds(a.shape, a.dtype) for a in arrays),
        in_specs=[ANY] * n, out_specs=(ANY,) * n, scratch_shapes=[pltpu.VMEM(a.shape, a.dtype) for a in arrays] + [DMA((2, n))],
        compiler_params=pltpu.CompilerParams(vmem_limit_bytes=LIMIT), name="place_outputs",
    )(*arrays)


def dp_dims(n):
    return {16: (2, 2, 4)}.get(n)


def shards(
    tokens, segment_ids, keep_masks, cotangent,
    norm1_gain, norm1_bias, qkv_weight, qv_bias, out_weight, out_bias,
    norm2_gain, norm2_bias, fc1_weight, fc1_bias, fc2_weight, fc2_bias,
):
    sec = lax.axis_index("section")
    n_dp = lax.axis_size("dp")
    dims = dp_dims(n_dp)
    T, D = tokens.shape[1:]
    FF = fc1_weight.shape[2]
    own = (qkv_weight, out_weight, fc1_weight, fc2_weight)
    vecs = (norm1_gain, norm1_bias, qv_bias, out_bias, norm2_gain, norm2_bias, fc1_bias, fc2_bias)
    res = first_call(tokens, segment_ids, keep_masks, vecs, own, 0)
    oth, par, cols, y0, saved0 = res[:4], res[4], res[5], res[6], res[7:]
    res = second_call(y0, cols, par, own, oth, 1)
    layer_out, saved1 = res[0], res[1:]
    res = backward_call(dims, n_dp, cotangent, tokens, y0, cols, par, saved0, saved1, own, oth, 2)
    input_grad = res[0]
    if dims:
        layer_out, input_grad, dqkv, dwo, dw1, dw2, n1g, n1b, qv, ob, n2g, n2b, b1, b2 = copy_call((layer_out, input_grad) + tuple(res[13:25]))
    else:
        sums = {}
        for i, l in enumerate((1, 0)):
            up, down, attn = (res[1 + 6 * i + 2 * j].astype(f32) + res[2 + 6 * i + 2 * j].astype(f32) for j in range(3))
            up, attn = up.reshape(D, -1), attn.reshape(D, -1)
            down = lax.all_gather(down, "section").reshape((2, 16, UR, 3, 2, UC))
            down = down.transpose(1, 0, 4, 2, 3, 5).reshape(FF, D)
            sums[l] = [lax.psum_scatter(a, "dp", scatter_dimension=0, tiled=True) for a in (attn, up, down)]
        attn, up, down = (jnp.stack([sums[0][i], sums[1][i]]) for i in range(3))
        attn, up = (lax.dynamic_index_in_dim(lax.all_gather(a, "section"), sec, 1, keepdims=False) for a in (attn, up))
        dw2 = lax.dynamic_index_in_dim(down, sec, 0, keepdims=False)
        dw1 = jnp.concatenate([up[0], up[1]], axis=1)
        cuts = {}
        for c, spots in enumerate(ATTN_SPOTS):
            for out, a, b, n, c0 in spots:
                for h, col in ((0, a), (1, b)):
                    cuts[out, col] = attn[h, :, c * UC + c0:c * UC + c0 + n]
        dqkv, dwo = (jnp.concatenate([cuts[k] for k in sorted(cuts) if k[0] == out], axis=1) for out in (0, 1))
        v = lax.dynamic_index_in_dim(lax.psum(res[13], ("section", "dp")), sec, 0, keepdims=False)
        at = lax.axis_index("dp")
        n1g, n1b, qv, ob, n2g, n2b, b1, b2 = (
            lax.dynamic_slice_in_dim(v[row:row + -(-w // D)].reshape(-1), at * (w // n_dp), w // n_dp)[None] for row, w in small_spots(D, FF))
    return (layer_out, input_grad, n1g, n1b, dqkv[None], qv, dwo[None], ob, n2g, n2b, dw1[None], b1, dw2[None], b2)


def solution(mesh):
    in_specs = (
        P(None, "dp", None), P(None, "dp"), P("section", None, None, "dp"), P(None, "dp", None),
        P("section", None), P("section", None), P("section", None, None), P("section", None),
        P("section", None, None), P("section", None), P("section", None), P("section", None),
        P("section", None, None), P("section", None), P("section", None, None), P("section", None),
    )
    out_specs = (
        P("section", None, "dp", None), P("section", None, "dp", None),
        P("section", "dp"), P("section", "dp"), P("section", "dp", None), P("section", "dp"),
        P("section", "dp", None), P("section", "dp"), P("section", "dp"), P("section", "dp"),
        P("section", "dp", None), P("section", "dp"), P("section", "dp", None), P("section", "dp"),
    )
    return jax.shard_map(shards, mesh=mesh, in_specs=in_specs, out_specs=out_specs, check_vma=False)
```
